256 devices in a mesh: dp: 32 (over x_lo, z, core), section: 8 (over y, x_hi).
Axes of the slice: x: 4 (x_hi: 2, x_lo: 2; x = x_hi * 2 + x_lo), y: 4, z: 8, core: 2. Of those that a mesh axis runs over, the one named last changes fastest.
Arguments:
- first_input: bfloat16 [4, 1024, 8192], P(None, 'dp'), may hold values from -6 to 6
- example_ids: int32 [32, 4, 8], P('dp'), may hold values from 0 to 7, each once within a row
- out_store: bfloat16 [8, 256, 8, 8192], P('section', 'dp'), may hold values from -6 to 6
- in_store: bfloat16 [8, 256, 8, 8192], P('section', 'dp'), may hold values from -6 to 6
- norm_gain: float32 [8, 8192], P('section'), may hold values from 0.25 to 1.75
- adapter_in: bfloat16 [8, 8192, 128], P('section'), may hold values from -0.0625 to 0.0625
- adapter_out: bfloat16 [8, 128, 8192], P('section'), may hold values from -0.5 to 0.5
Outputs:
- grad_in: float32 [8, 8192, 128], P('section', 'dp')
- grad_out: float32 [8, 128, 8192], P('section', None, 'dp')
The draws below stay inside these ranges and needn't reach their ends.
Inputs may be any that keep to these rules, and one draw needn't show every extreme that they name: Each row of example_ids over its last dimension is a permutation of the 8 stored examples.
All inputs are finite; a program needn't handle non-finite values.
Results may differ from the reference program's by a relative error of at most 0.0045.
Values may be sent and summed in bfloat16 or wider, within the bound.
No kernel may reach another device: no remote copies, remote signals or barrier semaphores. Data moves between devices by JAX's collectives and lax.ppermute only.
A program may use at most 64 MiB of HBM per device.

```python
import jax
import jax.numpy as jnp
from jax import lax

D = 8192
RANK = 128
MICRO = 4
EX = 8
PICK = 4
TOK_EX = 8
EXAMPLES = 256
ROWS = 1024
N_DP = 32
N_SECTION = 8


def level_of(own_key, shape, cuts, low, top_value):
    factor_of = 1.0
    for dim, parts in cuts:
        steps = jax.random.uniform(jax.random.fold_in(jax.random.fold_in(own_key, 6), dim), (parts,), jnp.float32, low / len(cuts), top_value / len(cuts))
        factor_of = factor_of * jnp.repeat(jnp.exp(steps), shape[dim] // parts).reshape((-1,) + (1,) * (len(shape) - 1 - dim))
    return factor_of


def centred(key, extent, deviation, reach, shards=(), kind=jnp.bfloat16):
    result = jax.random.normal(key, extent, jnp.float32) * deviation
    if len(shards) > 0:
        result = level_of(key, extent, shards, -0.22, 0.18) * result
    return jnp.clip(result, min=-reach, max=reach).astype(kind)


def setup_inputs(seed: int = 0) -> dict:
    arg_keys = jax.random.split(jax.random.key(seed), 8)
    return {
        "first_input": centred(arg_keys[0], (MICRO, ROWS, D), 1.0, 6.0, ((1, 32),)),
        "example_ids": jax.vmap(lambda own: jax.random.permutation(own, EX))(jax.random.split(arg_keys[1], N_DP * MICRO)).reshape((N_DP, MICRO, EX)).astype(jnp.int32),
        "out_store": centred(arg_keys[2], (N_SECTION, EXAMPLES, TOK_EX, D), 1.0, 6.0, ((0, 8), (1, 32))),
        "in_store": centred(arg_keys[3], (N_SECTION, EXAMPLES, TOK_EX, D), 1.0, 6.0, ((0, 8), (1, 32))),
        "norm_gain": jnp.clip(1.0 + 0.15 * jax.random.normal(arg_keys[4], (N_SECTION, D), jnp.float32), 0.25, 1.75),
        "adapter_in": centred(arg_keys[5], (N_SECTION, D, RANK), D ** -0.5, 0.0625, ((0, 8),)),
        "adapter_out": centred(arg_keys[6], (N_SECTION, RANK, D), RANK ** -0.5, 0.5, ((0, 8),)),
    }


def layer(entry, gain, w_in, w_out):
    inverse = lax.rsqrt(lax.optimization_barrier(jnp.mean(entry * entry, -1, keepdims=True)) + 1e-05)
    normed = (entry * inverse * gain).astype(jnp.bfloat16)
    inner = jnp.dot(normed, w_in, preferred_element_type=jnp.float32)
    active = jax.nn.silu(inner).astype(jnp.bfloat16)
    output = entry + jnp.dot(active, w_out, preferred_element_type=jnp.float32)
    return (output, inverse, normed, inner, active)

def backward(entry, grad_b, gain, w_in, w_out):
    output, inverse, normed, inner, active = layer(entry, gain, w_in, w_out)
    grad_f = grad_b.astype(jnp.float32)
    d_act = jnp.dot(grad_b, w_out.T, preferred_element_type=jnp.float32)
    sigm = jax.nn.sigmoid(inner)
    d_inner = (d_act * sigm * (1.0 + inner * (1.0 - sigm))).astype(jnp.bfloat16)
    g_out = jnp.dot(active.T, grad_b, preferred_element_type=jnp.float32)
    g_in = jnp.dot(normed.T, d_inner, preferred_element_type=jnp.float32)
    d_norm = jnp.dot(d_inner, w_in.T, preferred_element_type=jnp.float32)
    scaled = gain * d_norm
    d_entry = grad_f + inverse * scaled - entry * inverse ** 3 * lax.optimization_barrier(jnp.mean(entry * scaled, -1, keepdims=True))
    return (d_entry, g_in, g_out)

def pick_rows(store, section, example_ids, micro_idx):
    chosen = example_ids[:, micro_idx, :PICK] + (jnp.arange(N_DP, dtype=jnp.int32) * EX)[:, None]
    picked = store[section][chosen.reshape(-1)]
    return picked.reshape(N_DP * PICK * TOK_EX, D).astype(jnp.float32)

def reference(first_input, example_ids, out_store, in_store, norm_gain, adapter_in, adapter_out):
    grad_in = [jnp.zeros((D, RANK), jnp.float32) for s in range(N_SECTION)]
    grad_out = [jnp.zeros((RANK, D), jnp.float32) for s in range(N_SECTION)]
    for micro_idx in range(MICRO):
        entries = []
        entry = first_input[micro_idx].astype(jnp.float32)
        for section in range(N_SECTION):
            entries.append(entry)
            output = layer(entry, norm_gain[section], adapter_in[section], adapter_out[section])[0]
            if section < N_SECTION - 1:
                delta = (output - pick_rows(out_store, section, example_ids, micro_idx)).astype(jnp.bfloat16)
                entry = pick_rows(in_store, section + 1, example_ids, micro_idx) + delta.astype(jnp.float32)
        grad_b = output.astype(jnp.bfloat16)
        for section in range(N_SECTION - 1, -1, -1):
            d_entry, g_in, g_out = backward(entries[section], grad_b, norm_gain[section], adapter_in[section], adapter_out[section])
            grad_in[section] = grad_in[section] + g_in
            grad_out[section] = grad_out[section] + g_out
            grad_b = d_entry.astype(jnp.bfloat16)
    return (jnp.stack(grad_in), jnp.stack(grad_out))
```

```python
import functools

import jax
import jax.numpy as jnp
from jax import lax
from jax.experimental import pallas as pl
from jax.experimental.pallas import tpu as pltpu
from jax.sharding import Mesh, PartitionSpec as P

F32 = jnp.float32
BF16 = jnp.bfloat16
EPS = 1e-05
PLANE = ("xl", "y", "xh")
SECTION = ("y", "xh")
SWAP = [(0, 1), (1, 0)]
NS = 8
R = 128
TOK = 8
MIC = 4
BLK = 128
PROJ = 29
NORM = 36
START = 37
GRAM = 45
LANES = 81 * BLK


def gram_at(t):
    return sum(NS - i for i in range(t))


def proj_at(s):
    return s * (s - 1) // 2


def dot_t(a, b):
    return lax.dot_general(a, b, (((1,), (1,)), ((), ())), preferred_element_type=F32)


def dot(a, b):
    return jnp.dot(a, b, preferred_element_type=F32)


def split(x):
    high = x.astype(BF16)
    return high, (x - high.astype(F32)).astype(BF16)


def project_kernel(core_ref, got_ref, out_w_ref, in_w_ref, start_ref, send_ref):
    cols = got_ref.shape[2]
    first = got_ref[:, 192:224, :].astype(F32).reshape(16, MIC, TOK, cols)
    running = None
    lane = lax.broadcasted_iota(jnp.int32, (R, BLK), 1)
    norms = jnp.zeros((R, BLK), F32)
    for s in range(1, NS):
        step = jnp.concatenate(
            [
                got_ref[x * NS + s, 0:64, :].astype(F32)
                - got_ref[x * NS + s - 1, 64:128, :].astype(F32)
                for x in range(2)
            ],
            0,
        )
        running = step if running is None else running + step
        rounded = running.astype(BF16)
        count = s if s < NS - 1 else NS
        at = proj_at(s) * BLK
        send_ref[:, at : at + count * BLK] = dot_t(
            rounded, out_w_ref[0:count].reshape(count * R, cols)
        ).astype(BF16)
        at = (PROJ + s - 1) * BLK
        send_ref[:, at : at + BLK] = dot(rounded, in_w_ref[s]).astype(BF16)
        for m in range(MIC):
            part = jnp.sum(
                running * (running + 2.0 * first[:, m].reshape(R, cols)), -1, keepdims=True
            )
            norms = jnp.where(lane == m * NS + s, part, norms)
    high, low = split(norms)
    merged = jnp.where(lane < 32, high.astype(F32), pltpu.roll(low.astype(F32), 32, 1))
    send_ref[:, NORM * BLK : (NORM + 1) * BLK] = merged.astype(BF16)
    send_ref[:, START * BLK : GRAM * BLK] = start_ref[...]

    @pl.when(core_ref[0] == 0)
    def _():
        for t in range(NS):
            at = (GRAM + gram_at(t)) * BLK
            send_ref[:, at : at + (NS - t) * BLK] = dot_t(
                out_w_ref[t], out_w_ref[t:NS].reshape((NS - t) * R, cols)
            ).astype(BF16)

    @pl.when(core_ref[0] != 0)
    def _():
        for t in range(NS):
            for s in range(t, NS):
                at = (GRAM + gram_at(t) + s - t) * BLK
                send_ref[:, at : at + BLK] = dot(out_w_ref[t], in_w_ref[s]).astype(BF16)


def chain_kernel(width, proj_ref, norm_ref, start_ref, mask_ref, oo_ref, oi_ref, send_ref):
    rows = MIC * TOK

    def spread(at, count=1):
        block = proj_ref[:, at * BLK : (at + count) * BLK]
        return jnp.concatenate([block] * MIC, 0)

    def pair(ref, t, s, count=1):
        at = (gram_at(t) + s - t) * BLK
        return ref[:, at : at + count * BLK]

    mask = mask_ref[:, 0:1]
    start_in = [start_ref[s, :, 0:R] for s in range(NS)]
    start_out = [start_ref[s, :, R : 2 * R] for s in range(NS)]
    run_out = [start_out[t] for t in range(NS)]
    run_in = [start_in[t] for t in range(NS)]
    inners, inverses, actives, crossed = [], [], [], []
    for s in range(NS):
        norm = norm_ref[:, s : s + 1]
        entry_out = []
        inner = run_in[s]
        if s > 0:
            inner = inner + spread(PROJ + s - 1)
            total = jnp.zeros((rows, R), F32)
            for t in range(s):
                base = spread(proj_at(s) + t)
                full = base + run_out[t]
                entry_out.append(full)
                total = total + actives[t].astype(F32) * (full + base + start_out[t])
            norm = norm + jnp.sum(total, -1, keepdims=True)
        inverse = lax.rsqrt(jnp.maximum(norm, 0.0) * (1.0 / width) + EPS)
        inner = inner * inverse
        active = (inner * jax.nn.sigmoid(inner) * mask).astype(BF16)
        inners.append(inner)
        inverses.append(inverse)
        actives.append(active)
        crossed.append(entry_out)
        send_ref[:, s * R : (s + 1) * R] = active
        grown = dot(active, pair(oo_ref, s, s, NS - s))
        for t in range(NS):
            if t >= s:
                run_out[t] = run_out[t] + grown[:, (t - s) * R : (t - s + 1) * R]
            else:
                run_out[t] = run_out[t] + dot_t(active, pair(oo_ref, t, s))
        if s < NS - 1:
            grown = dot(active, pair(oi_ref, s, s + 1, NS - 1 - s))
            for t in range(s + 1, NS):
                run_in[t] = run_in[t] + grown[:, (t - s - 1) * R : (t - s) * R]
    grads = [run_out[t] + spread(proj_at(NS - 1) + t) for t in range(NS)]
    lane = lax.broadcasted_iota(jnp.int32, (rows, BLK), 1)
    scalars = jnp.zeros((rows, BLK), F32)
    for s in range(NS - 1, -1, -1):
        inner = inners[s]
        sigm = jax.nn.sigmoid(inner)
        d_inner = (grads[s] * sigm * (1.0 + inner * (1.0 - sigm)) * mask).astype(BF16)
        send_ref[:, (NS + s) * R : (NS + s + 1) * R] = d_inner
        d_wide = d_inner.astype(F32)
        inverse = inverses[s]
        scale = (
            inverse * inverse * jnp.sum(d_wide * inner, -1, keepdims=True) * (1.0 / width)
        )
        for t in range(s):
            grads[t] = (
                grads[t] + inverse * dot_t(d_inner, pair(oi_ref, t, s)) - scale * crossed[s][t]
            )
        high, low = split(inverse)
        scalars = jnp.where(lane == s, high.astype(F32), scalars)
        scalars = jnp.where(lane == NS + s, low.astype(F32), scalars)
        high, low = split(scale)
        scalars = jnp.where(lane == 2 * NS + s, high.astype(F32), scalars)
        scalars = jnp.where(lane == 3 * NS + s, low.astype(F32), scalars)
    send_ref[:, 2 * NS * R : 2 * NS * R + BLK] = scalars.astype(BF16)


def grads_kernel(got_ref, out_w_ref, in_w_ref, chain_ref, g_in_ref, g_out_ref, kept_ref):
    cols = got_ref.shape[2]
    rows = 16 * MIC * TOK
    scalars = chain_ref[:, 2 * NS * R : 2 * NS * R + BLK].astype(F32)
    inverses = [scalars[:, s : s + 1] + scalars[:, NS + s : NS + s + 1] for s in range(NS)]
    scales = [
        scalars[:, 2 * NS + s : 2 * NS + s + 1] + scalars[:, 3 * NS + s : 3 * NS + s + 1]
        for s in range(NS)
    ]

    def active(s):
        return chain_ref[:, s * R : (s + 1) * R]

    def d_inner(s):
        return chain_ref[:, (NS + s) * R : (NS + s + 1) * R]

    def dot_rows(a, b):
        return lax.dot_general(a, b, (((0,), (0,)), ((), ())), preferred_element_type=F32)

    entry = got_ref[:, 192:224, :].astype(F32).reshape(rows, cols)
    for s in range(NS):
        if s > 0:
            step = jnp.concatenate(
                [
                    got_ref[x * NS + s, 0:64, :].astype(F32)
                    - got_ref[x * NS + s - 1, 64:128, :].astype(F32)
                    for x in range(2)
                ],
                0,
            )
            step = jnp.broadcast_to(step.reshape(16, 1, TOK, cols), (16, MIC, TOK, cols))
            entry = entry + step.reshape(rows, cols)
        kept_ref[s] = entry
        normed = (entry * inverses[s]).astype(BF16)
        g_in_ref[0, s] = dot_rows(normed, d_inner(s))
        entry = entry + dot(active(s), out_w_ref[s])
    grad = entry
    for s in range(NS - 1, -1, -1):
        g_out_ref[0, s] = dot_rows(active(s), grad.astype(BF16))
        if s > 0:
            grad = grad + inverses[s] * dot_t(d_inner(s), in_w_ref[s]) - scales[s] * kept_ref[s]


def vmem(n):
    return [pl.BlockSpec(memory_space=pltpu.VMEM)] * n


PARAMS = dict(vmem_limit_bytes=56 * 1024 * 1024)


def body(first_input, example_ids, out_store, in_store, norm_gain, adapter_in, adapter_out):
    width = first_input.shape[2]
    cols = width // 16
    half = cols // 2
    core = lax.axis_index("c")
    xl = lax.axis_index("xl")
    z = lax.axis_index("z")
    section = lax.axis_index(SECTION)
    quarter = xl * 2 + core
    ids = example_ids[0]
    start = first_input.reshape(MIC, 4, TOK, width)
    w_in = adapter_in[0]
    w_out = adapter_out[0]
    gained = (norm_gain[0][:, None] * w_in.astype(F32)).astype(BF16)

    picked = ids[:, :4]
    mine = picked == section
    own = jnp.zeros((MIC, TOK, width), BF16)
    for j in range(4):
        own = jnp.where(mine[:, j, None, None], start[:, j], own)
    own_norm = jnp.sum(jnp.square(own.astype(F32)), -1)
    mask = jnp.any(mine, 1).astype(F32)

    in_part = lax.dynamic_index_in_dim(gained.reshape(16, 4, R, R), quarter, 1, keepdims=False)
    in_part = in_part.reshape(16, 4, 32, R).transpose(2, 0, 1, 3).reshape(32, width)
    out_part = lax.dynamic_slice_in_dim(w_out, quarter * 32, 32, 0)
    send = jnp.concatenate(
        [
            in_store.reshape(64, width),
            out_store.reshape(64, width),
            out_part,
            in_part,
            own.reshape(32, width),
        ],
        0,
    )
    send = send.reshape(224, 16, cols).transpose(1, 0, 2)
    got = lax.all_to_all(send, PLANE, 0, 0, tiled=True)

    weights = got[:, 128:192]
    other = lax.ppermute(weights, "c", SWAP)
    both = jnp.stack(
        [jnp.where(core == 0, weights, other), jnp.where(core == 0, other, weights)]
    ).reshape(2, 2, NS, 64, cols)
    out_w = both[:, :, :, :32].transpose(2, 1, 0, 3, 4).reshape(NS, R, cols)
    in_w = (
        both[:, :, :, 32:]
        .reshape(2, 2, NS, 32, 4, R)
        .transpose(2, 1, 0, 4, 3, 5)
        .reshape(NS, cols, R)
    )

    flat = first_input.reshape(MIC * 32, width)
    start_proj = jnp.concatenate([dot(flat, gained), dot_t(flat, w_out)], 1)
    start_proj = start_proj.reshape(MIC, 4, TOK, 2 * R)
    placed = jnp.zeros((MIC, NS, TOK, 2 * R), F32)
    for j in range(4):
        here = picked[:, j, None] == jnp.arange(NS)[None, :]
        placed = jnp.where(here[:, :, None, None], start_proj[:, j, None], placed)
    placed = placed.transpose(1, 2, 0, 3).reshape(NS * TOK, MIC * 2 * R).astype(BF16)
    placed = jnp.concatenate([placed, placed], 0)

    parts = pl.pallas_call(
        project_kernel,
        out_shape=jax.ShapeDtypeStruct((R, LANES), BF16),
        in_specs=[pl.BlockSpec(memory_space=pltpu.SMEM)] + vmem(4),
        out_specs=pl.BlockSpec(memory_space=pltpu.VMEM),
        compiler_params=pltpu.CompilerParams(**PARAMS),
        name="project",
    )(core.reshape(1), got, out_w, in_w, placed)
    parts = lax.all_to_all(parts.reshape(16, TOK, LANES), PLANE, 0, 0, tiled=True)

    gram = jnp.sum(parts[:, :, GRAM * BLK :].astype(F32), 0).astype(BF16)
    gram = lax.all_to_all(
        jnp.broadcast_to(gram, (16,) + gram.shape), PLANE, 0, 0, tiled=True
    ).reshape(R, 36 * BLK)
    other = lax.ppermute(gram, "c", SWAP)
    oo = jnp.where(core == 0, gram, other)
    oi = jnp.where(core == 0, other, gram)

    proj = jnp.sum(parts[:, :, : START * BLK].astype(F32), 0)
    norm = proj[:, NORM * BLK : NORM * BLK + 64].reshape(TOK, 2, MIC, NS).sum(1)
    norm = norm.transpose(1, 0, 2) + own_norm[:, :, None]
    norm = jnp.pad(norm.reshape(MIC * TOK, NS), ((0, 0), (0, BLK - NS)))
    starts = lax.dynamic_slice_in_dim(parts[:, :, START * BLK : GRAM * BLK], xl * NS, NS, 0)
    starts = starts.reshape(NS, TOK, MIC, 2 * R).transpose(0, 2, 1, 3)
    starts = starts.reshape(NS, MIC * TOK, 2 * R).astype(F32)
    mask = jnp.broadcast_to(mask[:, None, None], (MIC, TOK, BLK)).reshape(MIC * TOK, BLK)
    latent = pl.pallas_call(
        functools.partial(chain_kernel, width),
        out_shape=jax.ShapeDtypeStruct((MIC * TOK, 17 * BLK), BF16),
        in_specs=vmem(6),
        out_specs=pl.BlockSpec(memory_space=pltpu.VMEM),
        compiler_params=pltpu.CompilerParams(**PARAMS),
        name="chain",
    )(proj, norm, starts, mask, oo, oi)

    latent = lax.all_to_all(
        jnp.broadcast_to(latent, (16,) + latent.shape), PLANE, 0, 0, tiled=True
    ).reshape(16 * MIC * TOK, 17 * BLK)

    g_in, g_out = pl.pallas_call(
        grads_kernel,
        grid=(2,),
        out_shape=(
            jax.ShapeDtypeStruct((2, NS, half, R), F32),
            jax.ShapeDtypeStruct((2, NS, R, half), F32),
        ),
        in_specs=[
            pl.BlockSpec((16, 224, half), lambda i: (0, 0, i)),
            pl.BlockSpec((NS, R, half), lambda i: (0, 0, i)),
            pl.BlockSpec((NS, half, R), lambda i: (0, i, 0)),
            pl.BlockSpec((16 * MIC * TOK, 17 * BLK), lambda i: (0, 0)),
        ],
        out_specs=(
            pl.BlockSpec((1, NS, half, R), lambda i: (i, 0, 0, 0)),
            pl.BlockSpec((1, NS, R, half), lambda i: (i, 0, 0, 0)),
        ),
        scratch_shapes=[pltpu.VMEM((NS, 16 * MIC * TOK, half), F32)],
        compiler_params=pltpu.CompilerParams(**PARAMS),
        name="grads",
    )(got, out_w, in_w, latent)

    def keep(x):
        return lax.dynamic_index_in_dim(x, core, 0, keepdims=False)

    def give(x):
        return lax.dynamic_index_in_dim(x, 1 - core, 0, keepdims=False).astype(BF16)

    sent = jnp.concatenate(
        [give(g_in), give(g_out).reshape(NS, R, 2, BLK).transpose(0, 2, 1, 3).reshape(NS, half, R)],
        1,
    )
    kept = jnp.concatenate(
        [keep(g_in), keep(g_out).reshape(NS, R, 2, BLK).transpose(0, 2, 1, 3).reshape(NS, half, R)],
        1,
    )
    total = (kept + lax.ppermute(sent, "c", SWAP).astype(F32)).astype(BF16)
    total = lax.all_to_all(total, "z", 0, 0, tiled=True)
    total = jnp.sum(total.astype(F32), 0)
    turned = [(a * NS + b, b * NS + a) for a in range(NS) for b in range(NS)]
    total = lax.ppermute(total, ("z",) + SECTION, turned)
    block = (xl * NS + z) * 2 + core
    gain = lax.dynamic_slice_in_dim(norm_gain[0], block * half, half, 0)
    grad_in = total[:half] * gain[:, None]
    grad_out = total[half:].reshape(2, R, BLK).transpose(1, 0, 2).reshape(R, half)
    return (grad_in[None], grad_out[None])


def solution(mesh):
    fine = Mesh(mesh.devices.reshape(2, 8, 2, 4, 2), ("xl", "z", "c", "y", "xh"))
    dp = ("xl", "z", "c")
    placed = (
        P(None, dp, None),
        P(dp, None, None),
        P(SECTION, dp, None, None),
        P(SECTION, dp, None, None),
        P(SECTION, None),
        P(SECTION, None, None),
        P(SECTION, None, None),
    )
    return jax.shard_map(
        body,
        mesh=fine,
        in_specs=placed,
        out_specs=(P(SECTION, dp, None), P(SECTION, None, dp)),
        check_vma=False,
    )
```

```python
import functools

import jax
import jax.numpy as jnp
from jax import lax
from jax.experimental import pallas as pl
from jax.experimental.pallas import tpu as pltpu
from jax.sharding import Mesh, PartitionSpec as P

F32 = jnp.float32
BF16 = jnp.bfloat16
EPS = 1e-05
PLANE = ("xl", "y", "xh")
SECTION = ("y", "xh")
SWAP = [(0, 1), (1, 0)]
NS = 8
R = 128
TOK = 8
MIC = 4
BLK = 128
OUT_ROW = 64
W_ROW = 128
X_ROW = 192
SENT = 224
PROJ = 29
NORM = 36
START = 37
GRAM = 45
SPLIT = 41
GRAMS = 36
PARAMS = pltpu.CompilerParams(vmem_limit_bytes=56 * 1024 * 1024)
VMEM = pl.BlockSpec(memory_space=pltpu.VMEM)
SMEM = pl.BlockSpec(memory_space=pltpu.SMEM)


def gram_at(t):
    return sum(NS - i for i in range(t))


def proj_at(s):
    return s * (s - 1) // 2


def dot_t(a, b):
    return lax.dot_general(a, b, (((1,), (1,)), ((), ())), preferred_element_type=F32)


def dot_rows(a, b):
    return lax.dot_general(a, b, (((0,), (0,)), ((), ())), preferred_element_type=F32)


def dot(a, b):
    return jnp.dot(a, b, preferred_element_type=F32)


def split(x):
    high = x.astype(BF16)
    return high, (x - high.astype(F32)).astype(BF16)


def interleave(tiles):
    lane = lax.broadcasted_iota(jnp.int32, tiles[0].shape, 1)
    low = lane < 64
    even = lane % 64 < 32
    a, b, c, d = tiles
    halves = []
    for p, q in ((a, c), (b, d)):
        halves.append(
            (
                jnp.where(low, p, pltpu.roll(q, 64, 1)),
                jnp.where(low, pltpu.roll(p, 64, 1), q),
            )
        )
    result = []
    for p, q in zip(halves[0], halves[1]):
        result.append(jnp.where(even, p, pltpu.roll(q, 32, 1)))
        result.append(jnp.where(even, pltpu.roll(p, 96, 1), q))
    return result


def pack_kernel(
    at_ref, ids_ref, in_ref, out_ref, w_out_ref, w_in_ref, gain_ref, first_ref, send_ref, row_ref
):
    section = at_ref[1]
    gain = gain_ref[...].reshape(8, BLK).T
    for s in range(NS):
        for j in range(4):
            column = 2 * j + s // 4
            scale = gain[(s % 4) * 32 : (s % 4) * 32 + 32, column : column + 1]
            send_ref[s, W_ROW + 32 : X_ROW, j * BLK : (j + 1) * BLK] = (
                w_in_ref[0, j, 0, s].astype(F32) * scale
            ).astype(BF16)
    picks = [[ids_ref[m, j] == section for j in range(4)] for m in range(MIC)]

    def own(at):
        rows = []
        for m in range(MIC):
            block = first_ref[m, :, at : at + BLK].astype(F32).reshape(4, TOK, BLK)
            total = jnp.zeros((TOK, BLK), F32)
            for j in range(4):
                total = jnp.where(picks[m][j], block[j], total)
            rows.append(total)
        return jnp.concatenate(rows, 0)

    squares = jnp.zeros((MIC * TOK, BLK), F32)
    for c in range(2):
        for zq in range(2):
            for h in range(2):
                lanes = [((4 * zq + j) * 4 + c * 2 + h) * BLK for j in range(4)]
                to = (c * 2 + zq) * BLK
                for ref, row, count in (
                    (in_ref, 0, 64),
                    (out_ref, OUT_ROW, 64),
                    (w_out_ref, W_ROW, 32),
                ):
                    tiles = interleave([ref[:, at : at + BLK].astype(F32) for at in lanes])
                    for i in range(4):
                        send_ref[4 * h + i, row : row + count, to : to + BLK] = tiles[i].astype(
                            BF16
                        )
                tiles = [own(at) for at in lanes]
                for tile in tiles:
                    squares = squares + tile * tile
                tiles = interleave(tiles)
                for i in range(4):
                    send_ref[4 * h + i, X_ROW:SENT, to : to + BLK] = tiles[i].astype(BF16)
    norm = jnp.sum(squares, -1, keepdims=True)
    lane = lax.broadcasted_iota(jnp.int32, (TOK, BLK), 1)
    for m in range(MIC):
        valid = picks[m][0] | picks[m][1] | picks[m][2] | picks[m][3]
        rows = slice(m * TOK, (m + 1) * TOK)
        mask = jnp.where(valid, 1.0, 0.0)
        fresh = jnp.where(lane == 1, mask, jnp.where(lane == 0, norm[rows], 0.0))

        @pl.when(pl.program_id(0) == 0)
        def _():
            row_ref[rows, :] = fresh

        @pl.when(pl.program_id(0) != 0)
        def _():
            row_ref[rows, :] = row_ref[rows, :] + jnp.where(lane == 0, fresh, 0.0)


def project_kernel(
    at_ref, got_ref, other_ref, start_ref, send_ref, out_w_ref, in_w_ref, wide_ref
):
    cols = got_ref.shape[2]
    first_core = at_ref[0] == 0
    for s in range(NS):
        for x in range(2):
            mine = got_ref[x * NS + s, W_ROW:X_ROW, :]
            theirs = other_ref[x * NS + s]
            for c in range(2):
                part = jnp.where(first_core == (c == 0), mine, theirs)
                k = 2 * x + c
                out_w_ref[s, 32 * k : 32 * k + 32, :] = part[:32]
                for g in range(4):
                    row = k * BLK + g * 32
                    in_w_ref[s, row : row + 32, :] = part[32:, g * BLK : (g + 1) * BLK]
    first = got_ref[:, X_ROW:SENT, :].astype(F32).reshape(16, MIC, TOK, cols)
    running = None
    lane = lax.broadcasted_iota(jnp.int32, (R, BLK), 1)
    norms = jnp.zeros((R, BLK), F32)
    for s in range(1, NS):
        step = jnp.concatenate(
            [
                got_ref[x * NS + s, 0:OUT_ROW, :].astype(F32)
                - got_ref[x * NS + s - 1, OUT_ROW:W_ROW, :].astype(F32)
                for x in range(2)
            ],
            0,
        )
        running = step if running is None else running + step
        rounded = running.astype(BF16)
        count = s if s < NS - 1 else NS
        at = proj_at(s) * BLK
        wide_ref[:, at : at + count * BLK] = dot_t(
            rounded, out_w_ref[0:count].reshape(count * R, cols)
        )
        at = (PROJ + s - 1) * BLK
        wide_ref[:, at : at + BLK] = dot(rounded, in_w_ref[s])
        for m in range(MIC):
            part = jnp.sum(
                running * (running + 2.0 * first[:, m].reshape(R, cols)), -1, keepdims=True
            )
            norms = jnp.where(lane == m * NS + s, part, norms)
    high = norms.astype(BF16).astype(F32)
    wide_ref[:, NORM * BLK : (NORM + 1) * BLK] = jnp.where(
        lane < 32, high, pltpu.roll(norms - high, 32, 1)
    )
    wide_ref[:, START * BLK : GRAM * BLK] = start_ref[...].astype(F32)
    wide_ref[:, (GRAM + GRAMS) * BLK :] = jnp.zeros((R, BLK), F32)

    @pl.when(first_core)
    def _():
        for t in range(NS):
            at = (GRAM + gram_at(t)) * BLK
            wide_ref[:, at : at + (NS - t) * BLK] = dot_t(
                out_w_ref[t], out_w_ref[t:NS].reshape((NS - t) * R, cols)
            )

    @pl.when(jnp.logical_not(first_core))
    def _():
        for t in range(NS):
            for s in range(t, NS):
                at = (GRAM + gram_at(t) + s - t) * BLK
                wide_ref[:, at : at + BLK] = dot(out_w_ref[t], in_w_ref[s])

    for b in range(SPLIT):
        pair = [
            wide_ref[:, at * BLK : (at + 1) * BLK].reshape(16, TOK, BLK) for at in (b, SPLIT + b)
        ]
        send_ref[:, :, b * BLK : (b + 1) * BLK] = jnp.concatenate(pair, 1).astype(BF16)


def chain_kernel(
    width, at_ref, parts_ref, row_ref, gram_ref, other_ref, send_ref, sum_ref, oo_ref, oi_ref
):
    rows = MIC * TOK
    first_core = at_ref[0] == 0
    for b in range(0, GRAMS, 4):
        at = slice(b * BLK, (b + 4) * BLK)
        mine, theirs = gram_ref[:, at], other_ref[:, at]
        oo_ref[:, at] = jnp.where(first_core, mine, theirs)
        oi_ref[:, at] = jnp.where(first_core, theirs, mine)
    for b in range(START):
        at = slice(b * BLK, (b + 1) * BLK)
        total = parts_ref[0, :, at].astype(F32)
        for q in range(1, 16):
            total = total + parts_ref[q, :, at].astype(F32)
        sum_ref[:, at] = total[:TOK]
    starts = []
    for s in range(NS):
        block = parts_ref[at_ref[2] * NS + s].astype(F32)
        pieces = []
        for m in range(MIC):
            b = START + 2 * m
            if b < SPLIT:
                pieces.append(block[:TOK, b * BLK : (b + 2) * BLK])
            else:
                pieces.append(block[TOK:, (b - SPLIT) * BLK : (b + 2 - SPLIT) * BLK])
        starts.append(jnp.concatenate(pieces, 0))

    def spread(at):
        block = sum_ref[:, at * BLK : (at + 1) * BLK]
        return jnp.concatenate([block] * MIC, 0)

    def pair(ref, t, s, count=1):
        at = (gram_at(t) + s - t) * BLK
        return ref[:, at : at + count * BLK]

    mask = row_ref[:, 1:2]
    own_norm = row_ref[:, 0:1]
    norm_block = sum_ref[:, NORM * BLK : (NORM + 1) * BLK]
    run_in = [start[:, :R] for start in starts]
    start_out = [start[:, R:] for start in starts]
    run_out = list(start_out)
    inners, inverses, actives, crossed = [], [], [], []
    for s in range(NS):
        norm = own_norm
        entry_out = []
        inner = run_in[s]
        if s > 0:
            inner = inner + spread(PROJ + s - 1)
            norm = norm + jnp.concatenate(
                [
                    norm_block[:, m * NS + s : m * NS + s + 1]
                    + norm_block[:, 32 + m * NS + s : 33 + m * NS + s]
                    for m in range(MIC)
                ],
                0,
            )
            total = jnp.zeros((rows, R), F32)
            for t in range(s):
                base = spread(proj_at(s) + t)
                full = base + run_out[t]
                entry_out.append(full)
                total = total + actives[t].astype(F32) * (full + base + start_out[t])
            norm = norm + jnp.sum(total, -1, keepdims=True)
        inverse = lax.rsqrt(jnp.maximum(norm, 0.0) * (1.0 / width) + EPS)
        inner = inner * inverse
        active = (inner * jax.nn.sigmoid(inner) * mask).astype(BF16)
        inners.append(inner)
        inverses.append(inverse)
        actives.append(active)
        crossed.append(entry_out)
        grown = dot(active, pair(oo_ref, s, s, NS - s))
        for t in range(NS):
            if t >= s:
                run_out[t] = run_out[t] + grown[:, (t - s) * R : (t - s + 1) * R]
            else:
                run_out[t] = run_out[t] + dot_t(active, pair(oo_ref, t, s))
        if s < NS - 1:
            grown = dot(active, pair(oi_ref, s, s + 1, NS - 1 - s))
            for t in range(s + 1, NS):
                run_in[t] = run_in[t] + grown[:, (t - s - 1) * R : (t - s) * R]
    grads = [run_out[t] + spread(proj_at(NS - 1) + t) for t in range(NS)]
    lane = lax.broadcasted_iota(jnp.int32, (rows, BLK), 1)
    scalars = jnp.zeros((rows, BLK), F32)
    d_inners = [None] * NS
    for s in range(NS - 1, -1, -1):
        inner = inners[s]
        sigm = jax.nn.sigmoid(inner)
        d_inner = (grads[s] * sigm * (1.0 + inner * (1.0 - sigm)) * mask).astype(BF16)
        d_inners[s] = d_inner
        d_wide = d_inner.astype(F32)
        inverse = inverses[s]
        scale = inverse * inverse * jnp.sum(d_wide * inner, -1, keepdims=True) * (1.0 / width)
        for t in range(s):
            grads[t] = (
                grads[t] + inverse * dot_t(d_inner, pair(oi_ref, t, s)) - scale * crossed[s][t]
            )
        for at, value in ((s, inverse), (2 * NS + s, scale)):
            high, low = split(value)
            scalars = jnp.where(lane == at, high.astype(F32), scalars)
            scalars = jnp.where(lane == at + NS, low.astype(F32), scalars)
    for q in range(16):
        for s in range(NS):
            send_ref[q, :, s * R : (s + 1) * R] = actives[s]
            send_ref[q, :, (NS + s) * R : (NS + s + 1) * R] = d_inners[s]
        send_ref[q, :, 2 * NS * R :] = scalars.astype(BF16)


def grads_kernel(at_ref, got_ref, out_w_ref, in_w_ref, chain_ref, *rest):
    *add, result_ref, kept_ref = rest
    cols = got_ref.shape[2]
    rows = 16 * MIC * TOK
    scalars = chain_ref[:, 2 * NS * R :].astype(F32)
    inverses = [scalars[:, s : s + 1] + scalars[:, NS + s : NS + s + 1] for s in range(NS)]
    scales = [
        scalars[:, 2 * NS + s : 2 * NS + s + 1] + scalars[:, 3 * NS + s : 3 * NS + s + 1]
        for s in range(NS)
    ]

    def active(s):
        return chain_ref[:, s * R : (s + 1) * R]

    def d_inner(s):
        return chain_ref[:, (NS + s) * R : (NS + s + 1) * R]

    def put(s, kind, value):
        value = value.reshape(8, 32, R)
        at = slice(32 * kind, 32 * kind + 32)
        if add:
            value = value + add[0][:, s, at, :].astype(F32)
        result_ref[:, s, at, :] = value.astype(BF16)

    entry = got_ref[:, X_ROW:SENT, :].astype(F32).reshape(rows, cols)
    for s in range(NS):
        if s > 0:
            step = jnp.concatenate(
                [
                    got_ref[x * NS + s, 0:OUT_ROW, :].astype(F32)
                    - got_ref[x * NS + s - 1, OUT_ROW:W_ROW, :].astype(F32)
                    for x in range(2)
                ],
                0,
            )
            step = jnp.broadcast_to(step.reshape(16, 1, TOK, cols), (16, MIC, TOK, cols))
            entry = entry + step.reshape(rows, cols)
        kept_ref[s] = entry
        put(s, 0, dot_rows((entry * inverses[s]).astype(BF16), d_inner(s)))
        entry = entry + dot(active(s), out_w_ref[s])
    grad = entry
    for s in range(NS - 1, -1, -1):
        put(s, 1, dot_rows(grad.astype(BF16), active(s)))
        if s > 0:
            grad = grad + inverses[s] * dot_t(d_inner(s), in_w_ref[s]) - scales[s] * kept_ref[s]


def final_kernel(parts_ref, gain_ref, in_ref, out_ref):
    total = parts_ref[0].astype(F32)
    for i in range(1, 8):
        total = total + parts_ref[i].astype(F32)
    gain = gain_ref[...].T
    for j in range(8):
        scale = gain[(j % 4) * 32 : (j % 4) * 32 + 32, j // 4 : j // 4 + 1]
        in_ref[j * 32 : j * 32 + 32, :] = total[j, :32] * scale
    out = total[:, 32:].reshape(2 * BLK, R)
    for i in range(2):
        out_ref[:, i * BLK : (i + 1) * BLK] = out[i * BLK : (i + 1) * BLK].T


def body(first_input, example_ids, out_store, in_store, norm_gain, adapter_in, adapter_out):
    width = first_input.shape[2]
    cols = width // 16
    half = cols // 2
    core = lax.axis_index("c")
    xl = lax.axis_index("xl")
    z = lax.axis_index("z")
    section = lax.axis_index(SECTION)
    quarter = xl * 2 + core
    at = jnp.stack([core, section, xl, quarter]).astype(jnp.int32)
    ids = example_ids[0]
    w_in = adapter_in[0]
    w_out = adapter_out[0]

    send, row = pl.pallas_call(
        pack_kernel,
        grid_spec=pltpu.PrefetchScalarGridSpec(
            num_scalar_prefetch=2,
            grid=(2,),
            in_specs=[
                pl.BlockSpec((64, width // 2), lambda i, at, ids: (0, i)),
                pl.BlockSpec((64, width // 2), lambda i, at, ids: (0, i)),
                pl.BlockSpec((32, width // 2), lambda i, at, ids: (at[3], i)),
                pl.BlockSpec(
                    (1, 4, 1, 8, 32, R),
                    lambda i, at, ids: (i, at[3] % 2, at[3] // 2, 0, 0, 0),
                ),
                pl.BlockSpec(
                    (1, 4, 1, 2, BLK), lambda i, at, ids: (i, at[3] % 2, at[3] // 2, 0, 0)
                ),
                pl.BlockSpec((MIC, 32, width // 2), lambda i, at, ids: (0, 0, i)),
            ],
            out_specs=[
                pl.BlockSpec((8, SENT, cols), lambda i, at, ids: (i, 0, 0)),
                pl.BlockSpec((MIC * TOK, BLK), lambda i, at, ids: (0, 0)),
            ],
        ),
        out_shape=(
            jax.ShapeDtypeStruct((16, SENT, cols), BF16),
            jax.ShapeDtypeStruct((MIC * TOK, BLK), F32),
        ),
        compiler_params=PARAMS,
        name="pack",
    )(
        at,
        ids,
        in_store.reshape(64, width),
        out_store.reshape(64, width),
        w_out,
        w_in.reshape(2, 8, 2, 8, 32, R),
        norm_gain.reshape(2, 8, 2, 2, BLK),
        first_input,
    )
    got = lax.all_to_all(send, PLANE, 0, 0, tiled=True)

    flat = first_input.reshape(MIC * 32, width)
    gained = (flat.astype(F32) * norm_gain).astype(BF16)
    start_proj = jnp.concatenate([dot(gained, w_in), dot_t(flat, w_out)], 1)
    start_proj = start_proj.reshape(MIC, 4, TOK, 2 * R)
    placed = jnp.zeros((MIC, NS, TOK, 2 * R), F32)
    for j in range(4):
        here = ids[:, j, None] == jnp.arange(NS)[None, :]
        placed = jnp.where(here[:, :, None, None], start_proj[:, j, None], placed)
    placed = placed.transpose(1, 2, 0, 3).reshape(NS * TOK, MIC * 2 * R).astype(BF16)
    placed = jnp.concatenate([placed, placed], 0)

    other = lax.ppermute(got[:, W_ROW:X_ROW], "c", SWAP)
    parts, out_w, in_w = pl.pallas_call(
        project_kernel,
        out_shape=(
            jax.ShapeDtypeStruct((16, 2 * TOK, SPLIT * BLK), BF16),
            jax.ShapeDtypeStruct((NS, R, cols), BF16),
            jax.ShapeDtypeStruct((NS, cols, R), BF16),
        ),
        in_specs=[SMEM, VMEM, VMEM, VMEM],
        out_specs=(VMEM, VMEM, VMEM),
        scratch_shapes=[pltpu.VMEM((R, 2 * SPLIT * BLK), F32)],
        compiler_params=PARAMS,
        name="project",
    )(at, got, other, placed)
    parts = lax.all_to_all(parts, PLANE, 0, 0, tiled=True)

    first_gram = (GRAM - SPLIT) * BLK
    gram = parts[:, TOK:, first_gram : first_gram + GRAMS * BLK].astype(F32)
    gram = jnp.sum(gram, 0).astype(BF16)
    gram = lax.all_to_all(
        jnp.broadcast_to(gram, (16,) + gram.shape), PLANE, 0, 0, tiled=True
    ).reshape(R, GRAMS * BLK)
    other = lax.ppermute(gram, "c", SWAP)

    latent = pl.pallas_call(
        functools.partial(chain_kernel, width),
        out_shape=jax.ShapeDtypeStruct((16, MIC * TOK, 17 * BLK), BF16),
        in_specs=[SMEM, VMEM, VMEM, VMEM, VMEM],
        out_specs=VMEM,
        scratch_shapes=[
            pltpu.VMEM((TOK, START * BLK), F32),
            pltpu.VMEM((R, GRAMS * BLK), BF16),
            pltpu.VMEM((R, GRAMS * BLK), BF16),
        ],
        compiler_params=PARAMS,
        name="chain",
    )(at, parts, row, gram, other)
    latent = lax.all_to_all(latent, PLANE, 0, 0, tiled=True).reshape(16 * MIC * TOK, 17 * BLK)

    def grads(own, *add):
        def side(at):
            return at[0] if own else 1 - at[0]

        return pl.pallas_call(
            grads_kernel,
            grid_spec=pltpu.PrefetchScalarGridSpec(
                num_scalar_prefetch=1,
                grid=(1,),
                in_specs=[
                    pl.BlockSpec((16, SENT, half), lambda i, at: (0, 0, side(at))),
                    pl.BlockSpec((NS, R, half), lambda i, at: (0, 0, side(at))),
                    pl.BlockSpec((NS, half, R), lambda i, at: (0, side(at), 0)),
                    pl.BlockSpec((16 * MIC * TOK, 17 * BLK), lambda i, at: (0, 0)),
                ]
                + [pl.BlockSpec((8, NS, 64, R), lambda i, at: (0, 0, 0, 0))] * len(add),
                out_specs=pl.BlockSpec((8, NS, 64, R), lambda i, at: (0, 0, 0, 0)),
                scratch_shapes=[pltpu.VMEM((NS, 16 * MIC * TOK, half), F32)],
            ),
            out_shape=jax.ShapeDtypeStruct((8, NS, 64, R), BF16),
            compiler_params=PARAMS,
            name="grads_own" if own else "grads_other",
        )(at, got, out_w, in_w, latent, *add)

    swapped = lax.ppermute(grads(False), "c", SWAP)
    total = grads(True, swapped).reshape(64, 64, R)
    total = lax.all_to_all(total, ("z",) + SECTION, 0, 0, tiled=True)
    block = (xl * NS + z) * 2 + core
    gain = lax.dynamic_slice_in_dim(norm_gain[0], block * half, half, 0)
    grad_in, grad_out = pl.pallas_call(
        final_kernel,
        out_shape=(
            jax.ShapeDtypeStruct((half, R), F32),
            jax.ShapeDtypeStruct((R, half), F32),
        ),
        in_specs=[VMEM, VMEM],
        out_specs=(VMEM, VMEM),
        compiler_params=PARAMS,
        name="final",
    )(total.reshape(8, 8, 64, R), gain.reshape(2, BLK))
    return (grad_in[None], grad_out[None])


def solution(mesh):
    fine = Mesh(mesh.devices.reshape(2, 8, 2, 4, 2), ("xl", "z", "c", "y", "xh"))
    dp = ("xl", "z", "c")
    placed = (
        P(None, dp, None),
        P(dp, None, None),
        P(SECTION, dp, None, None),
        P(SECTION, dp, None, None),
        P(SECTION, None),
        P(SECTION, None, None),
        P(SECTION, None, None),
    )
    return jax.shard_map(
        body,
        mesh=fine,
        in_specs=placed,
        out_specs=(P(SECTION, dp, None), P(SECTION, None, dp)),
        check_vma=False,
    )
```

```python
import functools

import jax
import jax.numpy as jnp
from jax import lax
from jax.experimental import pallas as pl
from jax.experimental.pallas import tpu as pltpu
from jax.sharding import Mesh, PartitionSpec as P

F32 = jnp.float32
BF16 = jnp.bfloat16
EPS = 1e-05
PLANE = ("xl", "y", "xh")
SECTION = ("y", "xh")
SWAP = [(0, 1), (1, 0)]
NS = 8
R = 128
TOK = 8
MIC = 4
BLK = 128
HALF = 1024
W_LANE = 2 * HALF
SENT = 3072
PROJ = 29
NORM = 36
START = 37
GRAM = 45
GRAMS = 32
SPLIT = 39
OO = 36
OI = 28
LARGE = pltpu.CompilerParams(vmem_limit_bytes=56 * 1024 * 1024)
PARAMS = pltpu.CompilerParams(vmem_limit_bytes=32 * 1024 * 1024)
VMEM = pl.BlockSpec(memory_space=pltpu.VMEM)
SMEM = pl.BlockSpec(memory_space=pltpu.SMEM)


def gram_at(t):
    return sum(NS - i for i in range(t))


def cross_at(t):
    return sum(NS - 1 - i for i in range(t))


def proj_at(s):
    return s * (s - 1) // 2


def dot_t(a, b):
    return lax.dot_general(a, b, (((1,), (1,)), ((), ())), preferred_element_type=F32)


def dot_rows(a, b):
    return lax.dot_general(a, b, (((0,), (0,)), ((), ())), preferred_element_type=F32)


def dot(a, b):
    return jnp.dot(a, b, preferred_element_type=F32)


def split(x):
    high = x.astype(BF16)
    return high, (x - high.astype(F32)).astype(BF16)


def interleave(tiles):
    lane = lax.broadcasted_iota(jnp.int32, tiles[0].shape, 1)
    low = lane < 64
    even = lane % 64 < 32
    a, b, c, d = tiles
    halves = []
    for p, q in ((a, c), (b, d)):
        halves.append(
            (
                jnp.where(low, p, pltpu.roll(q, 64, 1)),
                jnp.where(low, pltpu.roll(p, 64, 1), q),
            )
        )
    result = []
    for p, q in zip(halves[0], halves[1]):
        result.append(jnp.where(even, p, pltpu.roll(q, 32, 1)))
        result.append(jnp.where(even, pltpu.roll(p, 96, 1), q))
    return result


def pack_kernel(
    at_ref,
    ids_ref,
    in_ref,
    out_ref,
    w_out_ref,
    w_in_ref,
    gain_ref,
    first_ref,
    all_out_ref,
    all_in_ref,
    all_gain_ref,
    send_ref,
    row_ref,
    cols_ref,
    start_ref,
    sum_ref,
):
    section = at_ref[1]
    last = pl.program_id(0) != 0
    gain = gain_ref[...].reshape(8, BLK).T
    for s in range(NS):
        for j in range(4):
            column = 2 * j + s // 4
            scale = gain[(s % 4) * 32 : (s % 4) * 32 + 32, column : column + 1]
            to = W_LANE + 512 + j * BLK
            send_ref[s, :, to : to + BLK] = (w_in_ref[0, j, 0, s].astype(F32) * scale).astype(BF16)

    for c in range(2):
        for zq in range(2):
            for h in range(2):
                lanes = [((4 * zq + j) * 4 + c * 2 + h) * BLK for j in range(4)]
                to = c * 256 + zq * BLK
                for ref, row, at in (
                    (in_ref, 0, c * HALF + zq * BLK),
                    (in_ref, 32, c * HALF + 256 + zq * BLK),
                    (out_ref, 0, c * HALF + 512 + zq * BLK),
                    (out_ref, 32, c * HALF + 768 + zq * BLK),
                    (w_out_ref, 0, W_LANE + c * 256 + zq * BLK),
                ):
                    tiles = interleave(
                        [ref[row : row + 32, lane : lane + BLK].astype(F32) for lane in lanes]
                    )
                    for i in range(4):
                        send_ref[4 * h + i, :, at : at + BLK] = tiles[i].astype(BF16)
            tiles = []
            for j in range(4):
                lane = pl.multiple_of(((4 * zq + j) * 4 + c * 2 + section // 4) * BLK, BLK)
                tiles.append(
                    jnp.concatenate(
                        [first_ref[m, :, pl.ds(lane, BLK)].astype(F32) for m in range(MIC)], 0
                    )
                )
            tiles = interleave(tiles)
            tile = tiles[0]
            for i in range(1, 4):
                tile = jnp.where(section % 4 == i, tiles[i], tile)
            cols_ref[0, :, to : to + BLK] = tile.astype(BF16)

    lane = lax.broadcasted_iota(jnp.int32, (TOK, BLK), 1)
    for m in range(MIC):
        picks = [ids_ref[m, j] == section for j in range(4)]
        block = first_ref[m].astype(F32)
        total = jnp.zeros((TOK, block.shape[1]), F32)
        for j in range(4):
            total = jnp.where(picks[j], block[j * TOK : (j + 1) * TOK], total)
        norm = jnp.sum(total * total, -1, keepdims=True)
        valid = picks[0] | picks[1] | picks[2] | picks[3]
        rows = slice(m * TOK, (m + 1) * TOK)
        before = jnp.where(last, row_ref[rows, :], 0.0)
        fresh = jnp.where(lane == 0, before + norm, jnp.where(valid, 1.0, 0.0))
        row_ref[rows, :] = fresh

    flat = first_ref[...].reshape(R, first_ref.shape[2])
    scaled = (flat.astype(F32) * all_gain_ref[...]).astype(BF16)
    both = jnp.concatenate([dot(scaled, all_in_ref[...]), dot_t(flat, all_out_ref[...])], 1)
    sum_ref[...] = jnp.where(last, sum_ref[...], 0.0) + both

    @pl.when(last)
    def _():
        for m in range(MIC):
            blocks = [sum_ref[(4 * m + j) * TOK : (4 * m + j + 1) * TOK, :] for j in range(4)]
            for e in range(NS):
                total = jnp.zeros((TOK, 2 * R), F32)
                for j in range(4):
                    total = jnp.where(ids_ref[m, j] == e, blocks[j], total)
                start_ref[e * TOK : (e + 1) * TOK, m * 2 * R : (m + 1) * 2 * R] = total


def stores(got_ref, s, at, cols):
    pieces = []
    for x in range(2):
        for i in range(2):
            a, b = at + i * 256, at + 512 + i * 256
            pieces.append(
                got_ref[x * NS + s, :, a : a + cols].astype(F32)
                - got_ref[x * NS + s - 1, :, b : b + cols].astype(F32)
            )
    return jnp.concatenate(pieces, 0)


def project_kernel(
    at_ref,
    ids_ref,
    other_ids_ref,
    got_ref,
    other_ref,
    cols_ref,
    other_cols_ref,
    start_ref,
    send_ref,
    out_w_ref,
    in_w_ref,
    first_ref,
    wide_ref,
):
    cols = cols_ref.shape[1]
    first_core = at_ref[0] == 0
    for s in range(NS):
        for x in range(2):
            mine = got_ref[x * NS + s, :, W_LANE:SENT]
            theirs = other_ref[x * NS + s]
            for c in range(2):
                part = jnp.where(first_core == (c == 0), mine, theirs)
                k = 2 * x + c
                out_w_ref[s, 32 * k : 32 * k + 32, :] = part[:, :cols]
                for g in range(4):
                    row = k * BLK + g * 32
                    lane = cols + g * BLK
                    in_w_ref[s, row : row + 32, :] = part[:, lane : lane + BLK]
    first = [[] for _ in range(MIC)]
    for x in range(2):
        here = at_ref[2] == x
        rows = jnp.where(here, cols_ref[...], other_cols_ref[...]).astype(F32)
        picked = [
            [jnp.where(here, ids_ref[m, j], other_ids_ref[m, j]) for j in range(4)]
            for m in range(MIC)
        ]
        for e in range(NS):
            blocks = []
            for m in range(MIC):
                total = jnp.zeros((TOK, cols), F32)
                for j in range(4):
                    at = (4 * m + j) * TOK
                    total = jnp.where(picked[m][j] == e, rows[at : at + TOK], total)
                blocks.append(total)
                first[m].append(total)
            first_ref[x * NS + e] = jnp.concatenate(blocks, 0).astype(BF16)
    first = [2.0 * jnp.concatenate(blocks, 0) for blocks in first]
    running = None
    lane = lax.broadcasted_iota(jnp.int32, (R, BLK), 1)
    norms = jnp.zeros((R, BLK), F32)
    for s in range(1, NS):
        step = jnp.concatenate(
            [stores(got_ref, s, 0, cols // 2), stores(got_ref, s, HALF, cols // 2)], 1
        )
        running = step if running is None else running + step
        rounded = running.astype(BF16)
        count = s if s < NS - 1 else NS
        at = proj_at(s) * BLK
        wide_ref[:, at : at + count * BLK] = dot_t(
            rounded, out_w_ref[0:count].reshape(count * R, cols)
        )
        at = (PROJ + s - 1) * BLK
        wide_ref[:, at : at + BLK] = dot(rounded, in_w_ref[s])
        for m in range(MIC):
            part = jnp.sum(running * (running + first[m]), -1, keepdims=True)
            norms = jnp.where(lane == m * NS + s, part, norms)
    high = norms.astype(BF16).astype(F32)
    wide_ref[:, NORM * BLK : (NORM + 1) * BLK] = jnp.where(
        lane < 32, high, pltpu.roll(norms - high, 32, 1)
    )
    wide_ref[0:64, START * BLK : GRAM * BLK] = start_ref[...]
    wide_ref[64:128, START * BLK : GRAM * BLK] = start_ref[...]
    wide_ref[:, (GRAM + GRAMS) * BLK :] = jnp.zeros((R, BLK), F32)

    square = [(t, s) for t in range(NS) for s in range(t, NS)]

    @pl.when(first_core)
    def _():
        for t in range(5):
            at = (GRAM + gram_at(t)) * BLK
            wide_ref[:, at : at + (NS - t) * BLK] = dot_t(
                out_w_ref[t], out_w_ref[t:NS].reshape((NS - t) * R, cols)
            )
        for i in range(gram_at(5), GRAMS):
            t, s = square[i]
            at = (GRAM + i) * BLK
            wide_ref[:, at : at + BLK] = dot_t(out_w_ref[t], out_w_ref[s])

    @pl.when(jnp.logical_not(first_core))
    def _():
        for t in range(NS - 1):
            for s in range(t + 1, NS):
                at = (GRAM + cross_at(t) + s - t - 1) * BLK
                wide_ref[:, at : at + BLK] = dot(out_w_ref[t], in_w_ref[s])
        for i in range(GRAMS, OO):
            t, s = square[i]
            at = (GRAM + OI + i - GRAMS) * BLK
            wide_ref[:, at : at + BLK] = dot_t(out_w_ref[t], out_w_ref[s])

    for b in range(SPLIT):
        pair = [
            wide_ref[:, at * BLK : (at + 1) * BLK].reshape(16, TOK, BLK) for at in (b, SPLIT + b)
        ]
        send_ref[:, :, b * BLK : (b + 1) * BLK] = jnp.concatenate(pair, 1).astype(BF16)


def chain_kernel(
    width, at_ref, parts_ref, row_ref, gram_ref, other_ref, send_ref, sum_ref, oo_ref, oi_ref
):
    rows = MIC * TOK
    first_core = at_ref[0] == 0
    for b in range(0, GRAMS, 4):
        at = slice(b * BLK, (b + 4) * BLK)
        mine, theirs = gram_ref[:, at], other_ref[:, at]
        oo_ref[:, at] = jnp.where(first_core, mine, theirs)
        second = jnp.where(first_core, theirs, mine)
        if b < OI:
            oi_ref[:, at] = second
        else:
            oo_ref[:, (b + 4) * BLK : (b + 8) * BLK] = second
    for b in range(START):
        at = slice(b * BLK, (b + 1) * BLK)
        total = parts_ref[0, :, at].astype(F32)
        for q in range(1, 16):
            total = total + parts_ref[q, :, at].astype(F32)
        sum_ref[:, at] = total[:TOK]
    starts = []
    for s in range(NS):
        block = parts_ref[at_ref[2] * NS + s].astype(F32)
        pieces = []
        for m in range(MIC):
            b = START + 2 * m
            if b < SPLIT:
                pieces.append(block[:TOK, b * BLK : (b + 2) * BLK])
            else:
                pieces.append(block[TOK:, (b - SPLIT) * BLK : (b + 2 - SPLIT) * BLK])
        starts.append(jnp.concatenate(pieces, 0))

    def spread(at):
        block = sum_ref[:, at * BLK : (at + 1) * BLK]
        return jnp.concatenate([block] * MIC, 0)

    def square(t, s, count=1):
        at = (gram_at(t) + s - t) * BLK
        return oo_ref[:, at : at + count * BLK]

    def cross(t, s, count=1):
        at = (cross_at(t) + s - t - 1) * BLK
        return oi_ref[:, at : at + count * BLK]

    mask = row_ref[:, 1:2]
    own_norm = row_ref[:, 0:1]
    norm_block = sum_ref[:, NORM * BLK : (NORM + 1) * BLK]
    run_in = [start[:, :R] for start in starts]
    start_out = [start[:, R:] for start in starts]
    run_out = list(start_out)
    inners, inverses, actives, crossed = [], [], [], []
    for s in range(NS):
        norm = own_norm
        entry_out = []
        inner = run_in[s]
        if s > 0:
            inner = inner + spread(PROJ + s - 1)
            norm = norm + jnp.concatenate(
                [
                    norm_block[:, m * NS + s : m * NS + s + 1]
                    + norm_block[:, 32 + m * NS + s : 33 + m * NS + s]
                    for m in range(MIC)
                ],
                0,
            )
            total = jnp.zeros((rows, R), F32)
            for t in range(s):
                base = spread(proj_at(s) + t)
                full = base + run_out[t]
                entry_out.append(full)
                total = total + actives[t].astype(F32) * (full + base + start_out[t])
            norm = norm + jnp.sum(total, -1, keepdims=True)
        inverse = lax.rsqrt(jnp.maximum(norm, 0.0) * (1.0 / width) + EPS)
        inner = inner * inverse
        active = (inner * jax.nn.sigmoid(inner) * mask).astype(BF16)
        inners.append(inner)
        inverses.append(inverse)
        actives.append(active)
        crossed.append(entry_out)
        grown = dot(active, square(s, s, NS - s))
        for t in range(NS):
            if t >= s:
                run_out[t] = run_out[t] + grown[:, (t - s) * R : (t - s + 1) * R]
            else:
                run_out[t] = run_out[t] + dot_t(active, square(t, s))
        if s < NS - 1:
            grown = dot(active, cross(s, s + 1, NS - 1 - s))
            for t in range(s + 1, NS):
                run_in[t] = run_in[t] + grown[:, (t - s - 1) * R : (t - s) * R]
    grads = [run_out[t] + spread(proj_at(NS - 1) + t) for t in range(NS)]
    lane = lax.broadcasted_iota(jnp.int32, (rows, BLK), 1)
    scalars = jnp.zeros((rows, BLK), F32)
    d_inners = [None] * NS
    for s in range(NS - 1, -1, -1):
        inner = inners[s]
        sigm = jax.nn.sigmoid(inner)
        d_inner = (grads[s] * sigm * (1.0 + inner * (1.0 - sigm)) * mask).astype(BF16)
        d_inners[s] = d_inner
        d_wide = d_inner.astype(F32)
        inverse = inverses[s]
        scale = inverse * inverse * jnp.sum(d_wide * inner, -1, keepdims=True) * (1.0 / width)
        for t in range(s):
            grads[t] = (
                grads[t] + inverse * dot_t(d_inner, cross(t, s)) - scale * crossed[s][t]
            )
        for at, value in ((s, inverse), (2 * NS + s, scale)):
            high, low = split(value)
            scalars = jnp.where(lane == at, high.astype(F32), scalars)
            scalars = jnp.where(lane == at + NS, low.astype(F32), scalars)
    for q in range(16):
        for s in range(NS):
            send_ref[q, :, s * R : (s + 1) * R] = actives[s]
            send_ref[q, :, (NS + s) * R : (NS + s + 1) * R] = d_inners[s]
        send_ref[q, :, 2 * NS * R :] = scalars.astype(BF16)


def grads_kernel(at_ref, got_ref, first_ref, out_w_ref, in_w_ref, chain_ref, result_ref, kept_ref):
    cols = first_ref.shape[2]
    rows = 16 * MIC * TOK
    scalars = chain_ref[:, 2 * NS * R :].astype(F32)
    inverses = [scalars[:, s : s + 1] + scalars[:, NS + s : NS + s + 1] for s in range(NS)]
    scales = [
        scalars[:, 2 * NS + s : 2 * NS + s + 1] + scalars[:, 3 * NS + s : 3 * NS + s + 1]
        for s in range(NS)
    ]

    def active(s):
        return chain_ref[:, s * R : (s + 1) * R]

    def d_inner(s):
        return chain_ref[:, (NS + s) * R : (NS + s + 1) * R]

    def put(s, kind, value):
        result_ref[:, s, :, kind * R : (kind + 1) * R] = value.reshape(8, 32, R).astype(
            result_ref.dtype
        )

    entry = first_ref[...].astype(F32).reshape(rows, cols)
    for s in range(NS):
        if s > 0:
            step = stores(got_ref, s, 0, cols)
            step = jnp.broadcast_to(step.reshape(16, 1, TOK, cols), (16, MIC, TOK, cols))
            entry = entry + step.reshape(rows, cols)
        kept_ref[s] = entry
        put(s, 0, dot_rows((entry * inverses[s]).astype(BF16), d_inner(s)))
        entry = entry + dot(active(s), out_w_ref[s])
    grad = entry
    for s in range(NS - 1, -1, -1):
        put(s, 1, dot_rows(grad.astype(BF16), active(s)))
        if s > 0:
            grad = grad + inverses[s] * dot_t(d_inner(s), in_w_ref[s]) - scales[s] * kept_ref[s]


def final_kernel(parts_ref, gain_ref, in_ref, out_ref):
    total = parts_ref[0].astype(F32)
    for i in range(1, 8):
        total = total + parts_ref[i].astype(F32)
    gain = gain_ref[...].T
    for j in range(8):
        scale = gain[(j % 4) * 32 : (j % 4) * 32 + 32, j // 4 : j // 4 + 1]
        in_ref[j * 32 : j * 32 + 32, :] = total[j, :, :R] * scale
    out = total[:, :, R:].reshape(2 * BLK, R)
    for i in range(2):
        out_ref[:, i * BLK : (i + 1) * BLK] = out[i * BLK : (i + 1) * BLK].T


def body(first_input, example_ids, out_store, in_store, norm_gain, adapter_in, adapter_out):
    width = first_input.shape[2]
    cols = width // 16
    half = cols // 2
    wide = width // 2
    core = lax.axis_index("c")
    xl = lax.axis_index("xl")
    z = lax.axis_index("z")
    section = lax.axis_index(SECTION)
    quarter = xl * 2 + core
    at = jnp.stack([core, section, xl, quarter]).astype(jnp.int32)
    ids = example_ids[0]
    w_in = adapter_in[0]
    w_out = adapter_out[0]

    send, row, own_cols, start = pl.pallas_call(
        pack_kernel,
        grid_spec=pltpu.PrefetchScalarGridSpec(
            num_scalar_prefetch=2,
            grid=(2,),
            in_specs=[
                pl.BlockSpec((64, wide), lambda i, at, ids: (0, i)),
                pl.BlockSpec((64, wide), lambda i, at, ids: (0, i)),
                pl.BlockSpec((32, wide), lambda i, at, ids: (at[3], i)),
                pl.BlockSpec(
                    (1, 4, 1, 8, 32, R),
                    lambda i, at, ids: (i, at[3] % 2, at[3] // 2, 0, 0, 0),
                ),
                pl.BlockSpec(
                    (1, 4, 1, 2, BLK), lambda i, at, ids: (i, at[3] % 2, at[3] // 2, 0, 0)
                ),
                pl.BlockSpec((MIC, 32, wide), lambda i, at, ids: (0, 0, i)),
                pl.BlockSpec((R, wide), lambda i, at, ids: (0, i)),
                pl.BlockSpec((wide, R), lambda i, at, ids: (i, 0)),
                pl.BlockSpec((1, wide), lambda i, at, ids: (0, i)),
            ],
            out_specs=[
                pl.BlockSpec((8, 32, SENT), lambda i, at, ids: (i, 0, 0)),
                pl.BlockSpec((MIC * TOK, BLK), lambda i, at, ids: (0, 0)),
                pl.BlockSpec((1, R, cols), lambda i, at, ids: ((i + at[2]) % 2, 0, 0)),
                pl.BlockSpec((NS * TOK, 8 * BLK), lambda i, at, ids: (0, 0)),
            ],
            scratch_shapes=[pltpu.VMEM((R, 2 * R), F32)],
        ),
        out_shape=(
            jax.ShapeDtypeStruct((16, 32, SENT), BF16),
            jax.ShapeDtypeStruct((MIC * TOK, BLK), F32),
            jax.ShapeDtypeStruct((2, R, cols), BF16),
            jax.ShapeDtypeStruct((NS * TOK, 8 * BLK), F32),
        ),
        compiler_params=LARGE,
        name="pack",
    )(
        at,
        ids,
        in_store.reshape(64, width),
        out_store.reshape(64, width),
        w_out,
        w_in.reshape(2, 8, 2, 8, 32, R),
        norm_gain.reshape(2, 8, 2, 2, BLK),
        first_input,
        w_out,
        w_in,
        norm_gain,
    )
    other_ids = lax.ppermute(ids, "xl", SWAP)
    other_cols = lax.ppermute(own_cols[1], "xl", SWAP)
    got = lax.all_to_all(send, PLANE, 0, 0, tiled=True)
    other = lax.ppermute(got[:, :, W_LANE:], "c", SWAP)
    parts, out_w, in_w, first = pl.pallas_call(
        project_kernel,
        out_shape=(
            jax.ShapeDtypeStruct((16, 2 * TOK, SPLIT * BLK), BF16),
            jax.ShapeDtypeStruct((NS, R, cols), BF16),
            jax.ShapeDtypeStruct((NS, cols, R), BF16),
            jax.ShapeDtypeStruct((16, MIC * TOK, cols), BF16),
        ),
        in_specs=[SMEM, SMEM, SMEM, VMEM, VMEM, VMEM, VMEM, VMEM],
        out_specs=(VMEM, VMEM, VMEM, VMEM),
        scratch_shapes=[pltpu.VMEM((R, 2 * SPLIT * BLK), F32)],
        compiler_params=PARAMS,
        name="project",
    )(at, ids, other_ids, got, other, own_cols[0], other_cols, start)
    parts = lax.all_to_all(parts, PLANE, 0, 0, tiled=True)

    first_gram = (GRAM - SPLIT) * BLK
    gram = parts[:, TOK:, first_gram : first_gram + GRAMS * BLK].astype(F32)
    gram = jnp.sum(gram, 0).astype(BF16)
    gram = lax.all_to_all(
        jnp.broadcast_to(gram, (16,) + gram.shape), PLANE, 0, 0, tiled=True
    ).reshape(R, GRAMS * BLK)
    other = lax.ppermute(gram, "c", SWAP)

    latent = pl.pallas_call(
        functools.partial(chain_kernel, width),
        out_shape=jax.ShapeDtypeStruct((16, MIC * TOK, 17 * BLK), BF16),
        in_specs=[SMEM, VMEM, VMEM, VMEM, VMEM],
        out_specs=VMEM,
        scratch_shapes=[
            pltpu.VMEM((TOK, START * BLK), F32),
            pltpu.VMEM((R, OO * BLK), BF16),
            pltpu.VMEM((R, OI * BLK), BF16),
        ],
        compiler_params=PARAMS,
        name="chain",
    )(at, parts, row, gram, other)
    latent = lax.all_to_all(latent, PLANE, 0, 0, tiled=True).reshape(16 * MIC * TOK, 17 * BLK)

    def grads(own):
        def side(at):
            return at[0] if own else 1 - at[0]

        return pl.pallas_call(
            grads_kernel,
            grid_spec=pltpu.PrefetchScalarGridSpec(
                num_scalar_prefetch=1,
                grid=(1,),
                in_specs=[
                    pl.BlockSpec((16, 32, HALF), lambda i, at: (0, 0, side(at))),
                    pl.BlockSpec((16, MIC * TOK, half), lambda i, at: (0, 0, side(at))),
                    pl.BlockSpec((NS, R, half), lambda i, at: (0, 0, side(at))),
                    pl.BlockSpec((NS, half, R), lambda i, at: (0, side(at), 0)),
                    pl.BlockSpec((16 * MIC * TOK, 17 * BLK), lambda i, at: (0, 0)),
                ],
                out_specs=pl.BlockSpec((8, NS, 32, 2 * R), lambda i, at: (0, 0, 0, 0)),
                scratch_shapes=[pltpu.VMEM((NS, 16 * MIC * TOK, half), F32)],
            ),
            out_shape=jax.ShapeDtypeStruct((8, NS, 32, 2 * R), F32 if own else BF16),
            compiler_params=PARAMS,
            name="grads_own" if own else "grads_other",
        )(at, got, first, out_w, in_w, latent)

    swapped = lax.ppermute(grads(False), "c", SWAP)
    total = (grads(True) + swapped.astype(F32)).astype(BF16).reshape(64, 32, 2 * R)
    block = (xl * NS + z) * 2 + core
    gain = lax.dynamic_slice_in_dim(norm_gain[0], block * half, half, 0)
    total, gain = lax.optimization_barrier((total, gain))
    total = lax.all_to_all(total, ("z",) + SECTION, 0, 0, tiled=True)
    grad_in, grad_out = pl.pallas_call(
        final_kernel,
        out_shape=(
            jax.ShapeDtypeStruct((half, R), F32),
            jax.ShapeDtypeStruct((R, half), F32),
        ),
        in_specs=[VMEM, VMEM],
        out_specs=(VMEM, VMEM),
        compiler_params=PARAMS,
        name="final",
    )(total.reshape(8, 8, 32, 2 * R), gain.reshape(2, BLK))
    return (grad_in[None], grad_out[None])


def solution(mesh):
    fine = Mesh(mesh.devices.reshape(2, 8, 2, 4, 2), ("xl", "z", "c", "y", "xh"))
    dp = ("xl", "z", "c")
    placed = (
        P(None, dp, None),
        P(dp, None, None),
        P(SECTION, dp, None, None),
        P(SECTION, dp, None, None),
        P(SECTION, None),
        P(SECTION, None, None),
        P(SECTION, None, None),
    )
    return jax.shard_map(
        body,
        mesh=fine,
        in_specs=placed,
        out_specs=(P(SECTION, dp, None), P(SECTION, None, dp)),
        check_vma=False,
    )
```

```python
import functools

import jax
import jax.numpy as jnp
from jax import lax
from jax.experimental import pallas as pl
from jax.experimental.pallas import tpu as pltpu
from jax.sharding import Mesh, PartitionSpec as P

F32 = jnp.float32
BF16 = jnp.bfloat16
EPS = 1e-05
PLANE = ("xl", "y", "xh")
SECTION = ("y", "xh")
SWAP = [(0, 1), (1, 0)]
NS = 8
R = 128
TOK = 8
MIC = 4
BLK = 128
HALF = 1024
W_LANE = 2 * HALF
SENT = 3072
PROJ = 29
NORM = 36
START = 37
GRAM = 45
GRAMS = 32
SPLIT = 39
OO = 36
OI = 28
LARGE = pltpu.CompilerParams(vmem_limit_bytes=56 * 1024 * 1024)
PARAMS = pltpu.CompilerParams(vmem_limit_bytes=16 * 1024 * 1024)
VMEM = pl.BlockSpec(memory_space=pltpu.VMEM)
SMEM = pl.BlockSpec(memory_space=pltpu.SMEM)


def gram_at(t):
    return sum(NS - i for i in range(t))


def cross_at(t):
    return sum(NS - 1 - i for i in range(t))


def proj_at(s):
    return s * (s - 1) // 2


def dot_t(a, b):
    return lax.dot_general(a, b, (((1,), (1,)), ((), ())), preferred_element_type=F32)


def dot_rows(a, b):
    return lax.dot_general(a, b, (((0,), (0,)), ((), ())), preferred_element_type=F32)


def dot(a, b):
    return jnp.dot(a, b, preferred_element_type=F32)


def split(x):
    high = x.astype(BF16)
    return high, (x - high.astype(F32)).astype(BF16)


def pack_kernel(
    at_ref, in_ref, out_ref, w_out_ref, w_in_ref, gain_ref, first_ref,
    send_ref, cols_ref, give_ref, turn_ref,
):
    section = at_ref[1]

    @pl.when(pl.program_id(0) == 0)
    def _():
        shape = (4 * BLK, 4 * BLK)
        row = lax.broadcasted_iota(jnp.int32, shape, 0)
        col = lax.broadcasted_iota(jnp.int32, shape, 1)
        same = (row // BLK == col % BLK // 32) & (row % BLK // 32 == col // BLK)
        same = same & (row % 32 == col % 32)
        turn_ref[...] = jnp.where(same, 1.0, 0.0).astype(BF16)

    gain = gain_ref[...].reshape(8, BLK).T
    for s in range(NS):
        for j in range(4):
            column = 2 * j + s // 4
            scale = gain[(s % 4) * 32 : (s % 4) * 32 + 32, column : column + 1]
            to = W_LANE + 512 + j * BLK
            send_ref[s, :, to : to + BLK] = (w_in_ref[0, j, 0, s].astype(F32) * scale).astype(BF16)

    pieces, places = [], []
    for c in range(2):
        for zq in range(2):
            to = c * 256 + zq * BLK
            for h in range(2):
                lanes = [((4 * zq + j) * 4 + c * 2 + h) * BLK for j in range(4)]
                for ref, row, at in (
                    (in_ref, 0, c * HALF + zq * BLK),
                    (in_ref, 32, c * HALF + 256 + zq * BLK),
                    (out_ref, 0, c * HALF + 512 + zq * BLK),
                    (out_ref, 32, c * HALF + 768 + zq * BLK),
                    (w_out_ref, 0, W_LANE + to),
                ):
                    pieces.append(
                        jnp.concatenate(
                            [ref[row : row + 32, lane : lane + BLK] for lane in lanes], 1
                        )
                    )
                    places.append((4 * h, at))
    turned = dot(jnp.concatenate(pieces, 0), turn_ref[...]).astype(BF16)
    for n, (first, at) in enumerate(places):
        for i in range(4):
            send_ref[first + i, :, at : at + BLK] = turned[
                32 * n : 32 * n + 32, i * BLK : (i + 1) * BLK
            ]

    pieces = []
    for c in range(2):
        for zq in range(2):
            lanes = [
                pl.multiple_of(((4 * zq + j) * 4 + c * 2 + section // 4) * BLK, BLK)
                for j in range(4)
            ]
            for m in range(MIC):
                pieces.append(
                    jnp.concatenate([first_ref[m, :, pl.ds(lane, BLK)] for lane in lanes], 1)
                )
    group = pl.multiple_of(section % 4 * BLK, BLK)
    turned = dot(jnp.concatenate(pieces, 0), turn_ref[:, pl.ds(group, BLK)]).astype(BF16)
    mine = pl.program_id(0) == at_ref[2]

    def put(ref):
        for n in range(4):
            ref[:, n * BLK : (n + 1) * BLK] = turned[n * R : (n + 1) * R]

    @pl.when(mine)
    def _():
        put(cols_ref)

    @pl.when(jnp.logical_not(mine))
    def _():
        put(give_ref)


def start_kernel(
    at_ref, ids_ref, first_ref, w_out_ref, w_in_ref, gain_ref, after_ref, row_ref, start_ref
):
    del after_ref
    section = at_ref[1]
    lane = lax.broadcasted_iota(jnp.int32, (TOK, BLK), 1)
    for m in range(MIC):
        picks = [ids_ref[m, j] == section for j in range(4)]
        block = first_ref[m].astype(F32)
        total = jnp.zeros((TOK, block.shape[1]), F32)
        for j in range(4):
            total = jnp.where(picks[j], block[j * TOK : (j + 1) * TOK], total)
        norm = jnp.sum(total * total, -1, keepdims=True)
        valid = picks[0] | picks[1] | picks[2] | picks[3]
        row_ref[m * TOK : (m + 1) * TOK, :] = jnp.where(
            lane == 0, norm, jnp.where(valid, 1.0, 0.0)
        )
    flat = first_ref[...].reshape(R, first_ref.shape[2])
    scaled = (flat.astype(F32) * gain_ref[...]).astype(BF16)
    both = jnp.concatenate([dot(scaled, w_in_ref[...]), dot_t(flat, w_out_ref[...])], 1)
    for m in range(MIC):
        blocks = [both[(4 * m + j) * TOK : (4 * m + j + 1) * TOK] for j in range(4)]
        for e in range(NS):
            total = jnp.zeros((TOK, 2 * R), F32)
            for j in range(4):
                total = jnp.where(ids_ref[m, j] == e, blocks[j], total)
            start_ref[e * TOK : (e + 1) * TOK, m * 2 * R : (m + 1) * 2 * R] = total


def stores(got_ref, s, at, cols):
    pieces = []
    for x in range(2):
        for i in range(2):
            a, b = at + i * 256, at + 512 + i * 256
            pieces.append(
                got_ref[x * NS + s, :, a : a + cols].astype(F32)
                - got_ref[x * NS + s - 1, :, b : b + cols].astype(F32)
            )
    return jnp.concatenate(pieces, 0)


def project_kernel(
    at_ref,
    ids_ref,
    other_ids_ref,
    got_ref,
    other_ref,
    cols_ref,
    other_cols_ref,
    start_ref,
    send_ref,
    out_w_ref,
    in_w_ref,
    first_ref,
    wide_ref,
):
    cols = cols_ref.shape[1]
    first_core = at_ref[0] == 0
    for s in range(NS):
        for x in range(2):
            mine = got_ref[x * NS + s, :, W_LANE:SENT]
            theirs = other_ref[x * NS + s]
            for c in range(2):
                part = jnp.where(first_core == (c == 0), mine, theirs)
                k = 2 * x + c
                out_w_ref[s, 32 * k : 32 * k + 32, :] = part[:, :cols]
                for g in range(4):
                    row = k * BLK + g * 32
                    lane = cols + g * BLK
                    in_w_ref[s, row : row + 32, :] = part[:, lane : lane + BLK]
    first = [[] for _ in range(MIC)]
    for x in range(2):
        here = at_ref[2] == x
        rows = jnp.where(here, cols_ref[...], other_cols_ref[...]).astype(F32)
        picked = [
            [jnp.where(here, ids_ref[m, j], other_ids_ref[m, j]) for j in range(4)]
            for m in range(MIC)
        ]
        for e in range(NS):
            blocks = []
            for m in range(MIC):
                total = jnp.zeros((TOK, cols), F32)
                for j in range(4):
                    at = (4 * m + j) * TOK
                    total = jnp.where(picked[m][j] == e, rows[at : at + TOK], total)
                blocks.append(total)
                first[m].append(total)
            first_ref[x * NS + e] = jnp.concatenate(blocks, 0).astype(BF16)
    first = [2.0 * jnp.concatenate(blocks, 0) for blocks in first]
    running = None
    lane = lax.broadcasted_iota(jnp.int32, (R, BLK), 1)
    norms = jnp.zeros((R, BLK), F32)
    for s in range(1, NS):
        step = jnp.concatenate(
            [stores(got_ref, s, 0, cols // 2), stores(got_ref, s, HALF, cols // 2)], 1
        )
        running = step if running is None else running + step
        rounded = running.astype(BF16)
        count = s if s < NS - 1 else NS
        at = proj_at(s) * BLK
        wide_ref[:, at : at + count * BLK] = dot_t(
            rounded, out_w_ref[0:count].reshape(count * R, cols)
        )
        at = (PROJ + s - 1) * BLK
        wide_ref[:, at : at + BLK] = dot(rounded, in_w_ref[s])
        for m in range(MIC):
            part = jnp.sum(running * (running + first[m]), -1, keepdims=True)
            norms = jnp.where(lane == m * NS + s, part, norms)
    high = norms.astype(BF16).astype(F32)
    wide_ref[:, NORM * BLK : (NORM + 1) * BLK] = jnp.where(
        lane < 32, high, pltpu.roll(norms - high, 32, 1)
    )
    wide_ref[0:64, START * BLK : GRAM * BLK] = start_ref[...]
    wide_ref[64:128, START * BLK : GRAM * BLK] = start_ref[...]
    wide_ref[:, (GRAM + GRAMS) * BLK :] = jnp.zeros((R, BLK), F32)

    square = [(t, s) for t in range(NS) for s in range(t, NS)]

    @pl.when(first_core)
    def _():
        for t in range(5):
            at = (GRAM + gram_at(t)) * BLK
            wide_ref[:, at : at + (NS - t) * BLK] = dot_t(
                out_w_ref[t], out_w_ref[t:NS].reshape((NS - t) * R, cols)
            )
        for i in range(gram_at(5), GRAMS):
            t, s = square[i]
            at = (GRAM + i) * BLK
            wide_ref[:, at : at + BLK] = dot_t(out_w_ref[t], out_w_ref[s])

    @pl.when(jnp.logical_not(first_core))
    def _():
        for t in range(NS - 1):
            for s in range(t + 1, NS):
                at = (GRAM + cross_at(t) + s - t - 1) * BLK
                wide_ref[:, at : at + BLK] = dot(out_w_ref[t], in_w_ref[s])
        for i in range(GRAMS, OO):
            t, s = square[i]
            at = (GRAM + OI + i - GRAMS) * BLK
            wide_ref[:, at : at + BLK] = dot_t(out_w_ref[t], out_w_ref[s])

    for b in range(SPLIT):
        pair = [
            wide_ref[:, at * BLK : (at + 1) * BLK].reshape(16, TOK, BLK) for at in (b, SPLIT + b)
        ]
        send_ref[:, :, b * BLK : (b + 1) * BLK] = jnp.concatenate(pair, 1).astype(BF16)


def chain_kernel(
    width, at_ref, parts_ref, row_ref, gram_ref, other_ref, send_ref, sum_ref, oo_ref, oi_ref
):
    rows = MIC * TOK
    first_core = at_ref[0] == 0
    for b in range(0, GRAMS, 4):
        at = slice(b * BLK, (b + 4) * BLK)
        mine, theirs = gram_ref[:, at], other_ref[:, at]
        oo_ref[:, at] = jnp.where(first_core, mine, theirs)
        second = jnp.where(first_core, theirs, mine)
        if b < OI:
            oi_ref[:, at] = second
        else:
            oo_ref[:, (b + 4) * BLK : (b + 8) * BLK] = second
    for b in range(START):
        at = slice(b * BLK, (b + 1) * BLK)
        total = parts_ref[0, :, at].astype(F32)
        for q in range(1, 16):
            total = total + parts_ref[q, :, at].astype(F32)
        sum_ref[:, at] = total[:TOK]
    starts = []
    for s in range(NS):
        block = parts_ref[at_ref[2] * NS + s].astype(F32)
        pieces = []
        for m in range(MIC):
            b = START + 2 * m
            if b < SPLIT:
                pieces.append(block[:TOK, b * BLK : (b + 2) * BLK])
            else:
                pieces.append(block[TOK:, (b - SPLIT) * BLK : (b + 2 - SPLIT) * BLK])
        starts.append(jnp.concatenate(pieces, 0))

    def spread(at):
        block = sum_ref[:, at * BLK : (at + 1) * BLK]
        return jnp.concatenate([block] * MIC, 0)

    def square(t, s, count=1):
        at = (gram_at(t) + s - t) * BLK
        return oo_ref[:, at : at + count * BLK]

    def cross(t, s, count=1):
        at = (cross_at(t) + s - t - 1) * BLK
        return oi_ref[:, at : at + count * BLK]

    mask = row_ref[:, 1:2]
    own_norm = row_ref[:, 0:1]
    norm_block = sum_ref[:, NORM * BLK : (NORM + 1) * BLK]
    run_in = [start[:, :R] for start in starts]
    start_out = [start[:, R:] for start in starts]
    run_out = list(start_out)
    inners, inverses, actives, crossed = [], [], [], []
    for s in range(NS):
        norm = own_norm
        entry_out = []
        inner = run_in[s]
        if s > 0:
            inner = inner + spread(PROJ + s - 1)
            norm = norm + jnp.concatenate(
                [
                    norm_block[:, m * NS + s : m * NS + s + 1]
                    + norm_block[:, 32 + m * NS + s : 33 + m * NS + s]
                    for m in range(MIC)
                ],
                0,
            )
            total = jnp.zeros((rows, R), F32)
            for t in range(s):
                base = spread(proj_at(s) + t)
                full = base + run_out[t]
                entry_out.append(full)
                total = total + actives[t].astype(F32) * (full + base + start_out[t])
            norm = norm + jnp.sum(total, -1, keepdims=True)
        inverse = lax.rsqrt(jnp.maximum(norm, 0.0) * (1.0 / width) + EPS)
        inner = inner * inverse
        active = (inner * jax.nn.sigmoid(inner) * mask).astype(BF16)
        inners.append(inner)
        inverses.append(inverse)
        actives.append(active)
        crossed.append(entry_out)
        grown = dot(active, square(s, s, NS - s))
        for t in range(NS):
            if t >= s:
                run_out[t] = run_out[t] + grown[:, (t - s) * R : (t - s + 1) * R]
            else:
                run_out[t] = run_out[t] + dot_t(active, square(t, s))
        if s < NS - 1:
            grown = dot(active, cross(s, s + 1, NS - 1 - s))
            for t in range(s + 1, NS):
                run_in[t] = run_in[t] + grown[:, (t - s - 1) * R : (t - s) * R]
    grads = [run_out[t] + spread(proj_at(NS - 1) + t) for t in range(NS)]
    lane = lax.broadcasted_iota(jnp.int32, (rows, BLK), 1)
    scalars = jnp.zeros((rows, BLK), F32)
    d_inners = [None] * NS
    for s in range(NS - 1, -1, -1):
        inner = inners[s]
        sigm = jax.nn.sigmoid(inner)
        d_inner = (grads[s] * sigm * (1.0 + inner * (1.0 - sigm)) * mask).astype(BF16)
        d_inners[s] = d_inner
        d_wide = d_inner.astype(F32)
        inverse = inverses[s]
        scale = inverse * inverse * jnp.sum(d_wide * inner, -1, keepdims=True) * (1.0 / width)
        for t in range(s):
            grads[t] = (
                grads[t] + inverse * dot_t(d_inner, cross(t, s)) - scale * crossed[s][t]
            )
        for at, value in ((s, inverse), (2 * NS + s, scale)):
            high, low = split(value)
            scalars = jnp.where(lane == at, high.astype(F32), scalars)
            scalars = jnp.where(lane == at + NS, low.astype(F32), scalars)
    for q in range(16):
        for s in range(NS):
            send_ref[q, :, s * R : (s + 1) * R] = actives[s]
            send_ref[q, :, (NS + s) * R : (NS + s + 1) * R] = d_inners[s]
        send_ref[q, :, 2 * NS * R :] = scalars.astype(BF16)


def grads_kernel(at_ref, got_ref, first_ref, out_w_ref, in_w_ref, chain_ref, result_ref, kept_ref):
    cols = first_ref.shape[2]
    rows = 16 * MIC * TOK
    scalars = chain_ref[:, 2 * NS * R :].astype(F32)
    inverses = [scalars[:, s : s + 1] + scalars[:, NS + s : NS + s + 1] for s in range(NS)]
    scales = [
        scalars[:, 2 * NS + s : 2 * NS + s + 1] + scalars[:, 3 * NS + s : 3 * NS + s + 1]
        for s in range(NS)
    ]

    def active(s):
        return chain_ref[:, s * R : (s + 1) * R]

    def d_inner(s):
        return chain_ref[:, (NS + s) * R : (NS + s + 1) * R]

    def put(s, kind, value):
        result_ref[:, s, :, kind * R : (kind + 1) * R] = value.reshape(8, 32, R).astype(
            result_ref.dtype
        )

    entry = first_ref[...].astype(F32).reshape(rows, cols)
    for s in range(NS):
        if s > 0:
            step = stores(got_ref, s, 0, cols)
            step = jnp.broadcast_to(step.reshape(16, 1, TOK, cols), (16, MIC, TOK, cols))
            entry = entry + step.reshape(rows, cols)
        kept_ref[s] = entry
        put(s, 0, dot_rows((entry * inverses[s]).astype(BF16), d_inner(s)))
        entry = entry + dot(active(s), out_w_ref[s])
    grad = entry
    for s in range(NS - 1, -1, -1):
        put(s, 1, dot_rows(grad.astype(BF16), active(s)))
        if s > 0:
            grad = grad + inverses[s] * dot_t(d_inner(s), in_w_ref[s]) - scales[s] * kept_ref[s]


def final_kernel(parts_ref, gain_ref, in_ref, out_ref):
    total = parts_ref[0].astype(F32)
    for i in range(1, 8):
        total = total + parts_ref[i].astype(F32)
    gain = gain_ref[...].T
    for j in range(8):
        scale = gain[(j % 4) * 32 : (j % 4) * 32 + 32, j // 4 : j // 4 + 1]
        in_ref[j * 32 : j * 32 + 32, :] = total[j, :, :R] * scale
    out = total[:, :, R:].reshape(2 * BLK, R)
    for i in range(2):
        out_ref[:, i * BLK : (i + 1) * BLK] = out[i * BLK : (i + 1) * BLK].T


def body(first_input, example_ids, out_store, in_store, norm_gain, adapter_in, adapter_out):
    width = first_input.shape[2]
    cols = width // 16
    half = cols // 2
    wide = width // 2
    core = lax.axis_index("c")
    xl = lax.axis_index("xl")
    z = lax.axis_index("z")
    section = lax.axis_index(SECTION)
    quarter = xl * 2 + core
    at = jnp.stack([core, section, xl, quarter]).astype(jnp.int32)
    ids = example_ids[0]
    w_in = adapter_in[0]
    w_out = adapter_out[0]

    send, own_cols, give_cols = pl.pallas_call(
        pack_kernel,
        grid_spec=pltpu.PrefetchScalarGridSpec(
            num_scalar_prefetch=1,
            grid=(2,),
            in_specs=[
                pl.BlockSpec((64, wide), lambda i, at: (0, i)),
                pl.BlockSpec((64, wide), lambda i, at: (0, i)),
                pl.BlockSpec((32, wide), lambda i, at: (at[3], i)),
                pl.BlockSpec(
                    (1, 4, 1, 8, 32, R), lambda i, at: (i, at[3] % 2, at[3] // 2, 0, 0, 0)
                ),
                pl.BlockSpec((1, 4, 1, 2, BLK), lambda i, at: (i, at[3] % 2, at[3] // 2, 0, 0)),
                pl.BlockSpec((MIC, 32, wide), lambda i, at: (0, 0, i)),
            ],
            out_specs=[
                pl.BlockSpec((8, 32, SENT), lambda i, at: (i, 0, 0)),
                pl.BlockSpec((R, cols), lambda i, at: (0, 0)),
                pl.BlockSpec((R, cols), lambda i, at: (0, 0)),
            ],
            scratch_shapes=[pltpu.VMEM((4 * BLK, 4 * BLK), BF16)],
        ),
        out_shape=(
            jax.ShapeDtypeStruct((16, 32, SENT), BF16),
            jax.ShapeDtypeStruct((R, cols), BF16),
            jax.ShapeDtypeStruct((R, cols), BF16),
        ),
        compiler_params=LARGE,
        name="pack",
    )(
        at,
        in_store.reshape(64, width),
        out_store.reshape(64, width),
        w_out,
        w_in.reshape(2, 8, 2, 8, 32, R),
        norm_gain.reshape(2, 8, 2, 2, BLK),
        first_input,
    )
    other_ids = lax.ppermute(ids, "xl", SWAP)
    other_cols = lax.ppermute(give_cols, "xl", SWAP)
    got = lax.all_to_all(send, PLANE, 0, 0, tiled=True)
    other = lax.ppermute(got[:, :, W_LANE:], "c", SWAP)
    row, start = pl.pallas_call(
        start_kernel,
        out_shape=(
            jax.ShapeDtypeStruct((MIC * TOK, BLK), F32),
            jax.ShapeDtypeStruct((NS * TOK, 8 * BLK), F32),
        ),
        in_specs=[SMEM, SMEM, VMEM, VMEM, VMEM, VMEM, pl.BlockSpec(memory_space=pl.ANY)],
        out_specs=(VMEM, VMEM),
        compiler_params=PARAMS,
        cost_estimate=pl.CostEstimate(flops=600000000, bytes_accessed=7000000, transcendentals=0),
        name="start",
    )(at, ids, first_input, w_out, w_in, norm_gain, got)
    parts, out_w, in_w, first = pl.pallas_call(
        project_kernel,
        out_shape=(
            jax.ShapeDtypeStruct((16, 2 * TOK, SPLIT * BLK), BF16),
            jax.ShapeDtypeStruct((NS, R, cols), BF16),
            jax.ShapeDtypeStruct((NS, cols, R), BF16),
            jax.ShapeDtypeStruct((16, MIC * TOK, cols), BF16),
        ),
        in_specs=[SMEM, SMEM, SMEM, VMEM, VMEM, VMEM, VMEM, VMEM],
        out_specs=(VMEM, VMEM, VMEM, VMEM),
        scratch_shapes=[pltpu.VMEM((R, 2 * SPLIT * BLK), F32)],
        compiler_params=PARAMS,
        name="project",
    )(at, ids, other_ids, got, other, own_cols, other_cols, start)
    parts = lax.all_to_all(parts, PLANE, 0, 0, tiled=True)

    first_gram = (GRAM - SPLIT) * BLK
    gram = parts[:, TOK:, first_gram : first_gram + GRAMS * BLK].astype(F32)
    gram = jnp.sum(gram, 0).astype(BF16)
    gram = lax.all_to_all(
        jnp.broadcast_to(gram, (16,) + gram.shape), PLANE, 0, 0, tiled=True
    ).reshape(R, GRAMS * BLK)
    other = lax.ppermute(gram, "c", SWAP)

    latent = pl.pallas_call(
        functools.partial(chain_kernel, width),
        out_shape=jax.ShapeDtypeStruct((16, MIC * TOK, 17 * BLK), BF16),
        in_specs=[SMEM, VMEM, VMEM, VMEM, VMEM],
        out_specs=VMEM,
        scratch_shapes=[
            pltpu.VMEM((TOK, START * BLK), F32),
            pltpu.VMEM((R, OO * BLK), BF16),
            pltpu.VMEM((R, OI * BLK), BF16),
        ],
        compiler_params=PARAMS,
        name="chain",
    )(at, parts, row, gram, other)
    latent = lax.all_to_all(latent, PLANE, 0, 0, tiled=True).reshape(16 * MIC * TOK, 17 * BLK)

    def grads(own):
        def side(at):
            return at[0] if own else 1 - at[0]

        return pl.pallas_call(
            grads_kernel,
            grid_spec=pltpu.PrefetchScalarGridSpec(
                num_scalar_prefetch=1,
                grid=(1,),
                in_specs=[
                    pl.BlockSpec((16, 32, HALF), lambda i, at: (0, 0, side(at))),
                    pl.BlockSpec((16, MIC * TOK, half), lambda i, at: (0, 0, side(at))),
                    pl.BlockSpec((NS, R, half), lambda i, at: (0, 0, side(at))),
                    pl.BlockSpec((NS, half, R), lambda i, at: (0, side(at), 0)),
                    pl.BlockSpec((16 * MIC * TOK, 17 * BLK), lambda i, at: (0, 0)),
                ],
                out_specs=pl.BlockSpec((8, NS, 32, 2 * R), lambda i, at: (0, 0, 0, 0)),
                scratch_shapes=[pltpu.VMEM((NS, 16 * MIC * TOK, half), F32)],
            ),
            out_shape=jax.ShapeDtypeStruct((8, NS, 32, 2 * R), F32 if own else BF16),
            compiler_params=PARAMS,
            name="grads_own" if own else "grads_other",
        )(at, got, first, out_w, in_w, latent)

    swapped = lax.ppermute(grads(False), "c", SWAP)
    total = (grads(True) + swapped.astype(F32)).astype(BF16).reshape(64, 32, 2 * R)
    block = (xl * NS + z) * 2 + core
    gain = lax.dynamic_slice_in_dim(norm_gain[0], block * half, half, 0)
    total, gain = lax.optimization_barrier((total, gain))
    total = lax.all_to_all(total, ("z",) + SECTION, 0, 0, tiled=True)
    grad_in, grad_out = pl.pallas_call(
        final_kernel,
        out_shape=(
            jax.ShapeDtypeStruct((half, R), F32),
            jax.ShapeDtypeStruct((R, half), F32),
        ),
        in_specs=[VMEM, VMEM],
        out_specs=(VMEM, VMEM),
        compiler_params=PARAMS,
        name="final",
    )(total.reshape(8, 8, 32, 2 * R), gain.reshape(2, BLK))
    return (grad_in[None], grad_out[None])


def solution(mesh):
    fine = Mesh(mesh.devices.reshape(2, 8, 2, 4, 2), ("xl", "z", "c", "y", "xh"))
    dp = ("xl", "z", "c")
    placed = (
        P(None, dp, None),
        P(dp, None, None),
        P(SECTION, dp, None, None),
        P(SECTION, dp, None, None),
        P(SECTION, None),
        P(SECTION, None, None),
        P(SECTION, None, None),
    )
    return jax.shard_map(
        body,
        mesh=fine,
        in_specs=placed,
        out_specs=(P(SECTION, dp, None), P(SECTION, None, dp)),
        check_vma=False,
    )
```

```python
import functools

import jax
import jax.numpy as jnp
from jax import lax
from jax.experimental import pallas as pl
from jax.experimental.pallas import tpu as pltpu
from jax.sharding import Mesh, PartitionSpec as P

F32 = jnp.float32
BF16 = jnp.bfloat16
EPS = 1e-05
PLANE = ("xl", "y", "xh")
SECTION = ("y", "xh")
SWAP = [(0, 1), (1, 0)]
NS = 8
R = 128
TOK = 8
MIC = 4
BLK = 128
HALF = 1024
W_LANE = 2 * HALF
SENT = 3072
PROJ = 29
NORM = 36
GRAM = 37
GRAMS = 32
SPLIT = 35
START = SPLIT * BLK
WIDE = START + 16 * BLK
OO = 36
OI = 28
LARGE = pltpu.CompilerParams(vmem_limit_bytes=56 * 1024 * 1024)
PARAMS = pltpu.CompilerParams(vmem_limit_bytes=16 * 1024 * 1024)
VMEM = pl.BlockSpec(memory_space=pltpu.VMEM)
SMEM = pl.BlockSpec(memory_space=pltpu.SMEM)


def gram_at(t):
    return sum(NS - i for i in range(t))


def cross_at(t):
    return sum(NS - 1 - i for i in range(t))


def proj_at(s):
    return s * (s - 1) // 2


def dot_t(a, b):
    return lax.dot_general(a, b, (((1,), (1,)), ((), ())), preferred_element_type=F32)


def dot_rows(a, b):
    return lax.dot_general(a, b, (((0,), (0,)), ((), ())), preferred_element_type=F32)


def dot(a, b):
    return jnp.dot(a, b, preferred_element_type=F32)


def split(x):
    high = x.astype(BF16)
    return high, (x - high.astype(F32)).astype(BF16)


def pack_kernel(
    at_ref, in_ref, out_ref, w_out_ref, w_in_ref, gain_ref, first_ref,
    send_ref, cols_ref, give_ref, turn_ref,
):
    section = at_ref[1]

    @pl.when(pl.program_id(0) == 0)
    def _():
        shape = (4 * BLK, 4 * BLK)
        row = lax.broadcasted_iota(jnp.int32, shape, 0)
        col = lax.broadcasted_iota(jnp.int32, shape, 1)
        same = (row // BLK == col % BLK // 32) & (row % BLK // 32 == col // BLK)
        same = same & (row % 32 == col % 32)
        turn_ref[...] = jnp.where(same, 1.0, 0.0).astype(BF16)

    gain = gain_ref[...].reshape(8, BLK).T
    for s in range(NS):
        for j in range(4):
            column = 2 * j + s // 4
            scale = gain[(s % 4) * 32 : (s % 4) * 32 + 32, column : column + 1]
            to = W_LANE + 512 + j * BLK
            send_ref[s, :, to : to + BLK] = (w_in_ref[0, j, 0, s].astype(F32) * scale).astype(BF16)

    pieces, places = [], []
    for c in range(2):
        for zq in range(2):
            to = c * 256 + zq * BLK
            for h in range(2):
                lanes = [((4 * zq + j) * 4 + c * 2 + h) * BLK for j in range(4)]
                for ref, row, at in (
                    (in_ref, 0, c * HALF + zq * BLK),
                    (in_ref, 32, c * HALF + 256 + zq * BLK),
                    (out_ref, 0, c * HALF + 512 + zq * BLK),
                    (out_ref, 32, c * HALF + 768 + zq * BLK),
                    (w_out_ref, 0, W_LANE + to),
                ):
                    pieces.append(
                        jnp.concatenate(
                            [ref[row : row + 32, lane : lane + BLK] for lane in lanes], 1
                        )
                    )
                    places.append((4 * h, at))
    turned = dot(jnp.concatenate(pieces, 0), turn_ref[...]).astype(BF16)
    for n, (first, at) in enumerate(places):
        for i in range(4):
            send_ref[first + i, :, at : at + BLK] = turned[
                32 * n : 32 * n + 32, i * BLK : (i + 1) * BLK
            ]

    pieces = []
    for c in range(2):
        for zq in range(2):
            lanes = [
                pl.multiple_of(((4 * zq + j) * 4 + c * 2 + section // 4) * BLK, BLK)
                for j in range(4)
            ]
            for m in range(MIC):
                pieces.append(
                    jnp.concatenate([first_ref[m, :, pl.ds(lane, BLK)] for lane in lanes], 1)
                )
    group = pl.multiple_of(section % 4 * BLK, BLK)
    turned = dot(jnp.concatenate(pieces, 0), turn_ref[:, pl.ds(group, BLK)]).astype(BF16)
    mine = pl.program_id(0) == at_ref[2]

    def put(ref):
        for n in range(4):
            ref[:, n * BLK : (n + 1) * BLK] = turned[n * R : (n + 1) * R]

    @pl.when(mine)
    def _():
        put(cols_ref)

    @pl.when(jnp.logical_not(mine))
    def _():
        put(give_ref)


def start_kernel(first_ref, w_out_ref, w_in_ref, gain_ref, after_ref, start_ref):
    del after_ref
    flat = first_ref[...].reshape(R, first_ref.shape[2])
    scaled = (flat.astype(F32) * gain_ref[...]).astype(BF16)
    start_ref[:, :R] = dot(scaled, w_in_ref[...]).astype(BF16)
    start_ref[:, R:] = dot_t(flat, w_out_ref[...]).astype(BF16)


def stores(got_ref, s, at, cols):
    pieces = []
    for x in range(2):
        for i in range(2):
            a, b = at + i * 256, at + 512 + i * 256
            pieces.append(
                got_ref[x * NS + s, :, pl.ds(a, cols)].astype(F32)
                - got_ref[x * NS + s - 1, :, pl.ds(b, cols)].astype(F32)
            )
    return jnp.concatenate(pieces, 0)


def picks_of(at_ref, ids_ref, other_ids_ref):
    picks = []
    for x in range(2):
        here = at_ref[2] == x
        for m in range(MIC):
            for j in range(4):
                picks.append(x * NS + jnp.where(here, ids_ref[m, j], other_ids_ref[m, j]))
    return picks


def project_kernel(
    at_ref, ids_ref, other_ids_ref, got_ref, other_ref, cols_ref, other_cols_ref, start_ref,
    send_ref, out_w_ref, in_w_ref, first_ref, wide_ref,
):
    cols = cols_ref.shape[1]
    first_core = at_ref[0] == 0
    for s in range(NS):
        for x in range(2):
            mine = got_ref[x * NS + s, :, W_LANE:SENT]
            theirs = other_ref[x * NS + s]
            for c in range(2):
                part = jnp.where(first_core == (c == 0), mine, theirs)
                k = 2 * x + c
                out_w_ref[s, 32 * k : 32 * k + 32, :] = part[:, :cols]
                for g in range(4):
                    row = k * BLK + g * 32
                    lane = cols + g * BLK
                    in_w_ref[s, row : row + 32, :] = part[:, lane : lane + BLK]
    picks = picks_of(at_ref, ids_ref, other_ids_ref)
    placed = [[] for _ in range(MIC)]
    for x in range(2):
        rows = jnp.where(at_ref[2] == x, cols_ref[...], other_cols_ref[...])
        first_ref[x * R : (x + 1) * R, :] = rows
        rows = rows.astype(F32)
        for e in range(NS):
            for m in range(MIC):
                total = jnp.zeros((TOK, cols), F32)
                for j in range(4):
                    n = 4 * m + j
                    total = jnp.where(
                        picks[16 * x + n] == x * NS + e, rows[n * TOK : (n + 1) * TOK], total
                    )
                placed[m].append(total)
    placed = [jnp.concatenate(blocks, 0) for blocks in placed]
    running = None
    lane = lax.broadcasted_iota(jnp.int32, (R, BLK), 1)
    norms = jnp.zeros((R, BLK), F32)
    for m in range(MIC):
        part = jnp.sum(placed[m] * placed[m], -1, keepdims=True)
        norms = jnp.where(lane == m * NS, part, norms)
    for s in range(1, NS):
        step = jnp.concatenate(
            [stores(got_ref, s, 0, cols // 2), stores(got_ref, s, HALF, cols // 2)], 1
        )
        running = step if running is None else running + step
        rounded = running.astype(BF16)
        count = s if s < NS - 1 else NS
        at = proj_at(s) * BLK
        wide_ref[:, at : at + count * BLK] = dot_t(
            rounded, out_w_ref[0:count].reshape(count * R, cols)
        )
        at = (PROJ + s - 1) * BLK
        wide_ref[:, at : at + BLK] = dot(rounded, in_w_ref[s])
        for m in range(MIC):
            entry = running + placed[m]
            part = jnp.sum(entry * entry, -1, keepdims=True)
            norms = jnp.where(lane == m * NS + s, part, norms)
    high = norms.astype(BF16).astype(F32)
    wide_ref[:, NORM * BLK : (NORM + 1) * BLK] = jnp.where(
        lane < 32, high, pltpu.roll(norms - high, 32, 1)
    )
    wide_ref[:, (GRAM + GRAMS) * BLK :] = jnp.zeros((R, BLK), F32)

    square = [(t, s) for t in range(NS) for s in range(t, NS)]

    @pl.when(first_core)
    def _():
        for t in range(5):
            at = (GRAM + gram_at(t)) * BLK
            wide_ref[:, at : at + (NS - t) * BLK] = dot_t(
                out_w_ref[t], out_w_ref[t:NS].reshape((NS - t) * R, cols)
            )
        for i in range(gram_at(5), GRAMS):
            t, s = square[i]
            at = (GRAM + i) * BLK
            wide_ref[:, at : at + BLK] = dot_t(out_w_ref[t], out_w_ref[s])

    @pl.when(jnp.logical_not(first_core))
    def _():
        for t in range(NS - 1):
            for s in range(t + 1, NS):
                at = (GRAM + cross_at(t) + s - t - 1) * BLK
                wide_ref[:, at : at + BLK] = dot(out_w_ref[t], in_w_ref[s])
        for i in range(GRAMS, OO):
            t, s = square[i]
            at = (GRAM + OI + i - GRAMS) * BLK
            wide_ref[:, at : at + BLK] = dot_t(out_w_ref[t], out_w_ref[s])

    for b in range(SPLIT):
        pair = [
            wide_ref[:, at * BLK : (at + 1) * BLK].reshape(16, TOK, BLK) for at in (b, SPLIT + b)
        ]
        send_ref[:, :, b * BLK : (b + 1) * BLK] = jnp.concatenate(pair, 1).astype(BF16)
    for g in range(8):
        at = START + g * 2 * R
        for q in range(16):
            send_ref[q, :, at : at + 2 * R] = start_ref[g * 16 : (g + 1) * 16, :]


def sum_kernel(parts_ref, send_ref):
    lane = lax.broadcasted_iota(jnp.int32, (2 * TOK, BLK), 1)
    row = lax.broadcasted_iota(jnp.int32, (2 * TOK, BLK), 0)
    for b in range(SPLIT):
        at = slice(b * BLK, (b + 1) * BLK)
        total = parts_ref[0, :, at].astype(F32)
        for q in range(1, 16):
            total = total + parts_ref[q, :, at].astype(F32)
        if b == NORM - SPLIT:
            norm = total + pltpu.roll(total, 96, 1)
            high = norm.astype(BF16).astype(F32)
            norm = jnp.where(lane < 32, high, pltpu.roll(norm - high, 32, 1))
            total = jnp.where(row < TOK, total, norm)
        total = total.astype(BF16)
        for q in range(16):
            send_ref[q, :, at] = total


def chain_kernel(
    width, at_ref, ids_ref, other_ids_ref, parts_ref, sums_ref, other_ref,
    latent_ref, scalar_ref, proj_ref, oo_ref, oi_ref,
):
    rows = 2 * R
    first_core = at_ref[0] == 0
    for b in range(GRAM):
        upper = b >= SPLIT
        at = (b - SPLIT * upper) * BLK
        block = sums_ref[:, :, at : at + BLK].astype(F32)
        proj_ref[:, b * BLK : (b + 1) * BLK] = block[:, TOK * upper : TOK * upper + TOK].reshape(
            R, BLK
        )
    for b in range(0, GRAMS, 4):
        at = (GRAM - SPLIT + b) * BLK
        mine = sums_ref[:, :, at : at + 4 * BLK].astype(F32)[:, TOK:]
        mine = mine.reshape(R, 4 * BLK).astype(BF16)
        at = slice(b * BLK, (b + 4) * BLK)
        theirs = other_ref[:, at]
        oo_ref[:, at] = jnp.where(first_core, mine, theirs)
        second = jnp.where(first_core, theirs, mine)
        if b < OI:
            oi_ref[:, at] = second
        else:
            oo_ref[:, (b + 4) * BLK : (b + 8) * BLK] = second
    places = [
        pl.multiple_of(pick * TOK, TOK) for pick in picks_of(at_ref, ids_ref, other_ids_ref)
    ]

    def spread(at):
        return jnp.concatenate(
            [proj_ref[pl.ds(place, TOK), at * BLK : (at + 1) * BLK] for place in places], 0
        )

    def square(t, s, count=1):
        at = (gram_at(t) + s - t) * BLK
        return oo_ref[:, at : at + count * BLK]

    def cross(t, s, count=1):
        at = (cross_at(t) + s - t - 1) * BLK
        return oi_ref[:, at : at + count * BLK]

    norms = spread(NORM)
    norms = norms + pltpu.roll(norms, 96, 1)
    pieces = []
    for n in range(32):
        m = n % 16 // 4
        piece = norms[n * TOK : (n + 1) * TOK]
        pieces.append(pltpu.roll(piece, BLK - m * NS, 1) if m else piece)
    norms = jnp.concatenate(pieces, 0)

    starts = []
    for s in range(NS):
        pieces = []
        for x in range(2):
            for g in range(8):
                at = START + g * 2 * R
                pieces.append(parts_ref[x * NS + s, :, at : at + 2 * R])
        starts.append(jnp.concatenate(pieces, 0))
    start_out = [start[:, R:].astype(F32) for start in starts]
    run_in = [start[:, :R].astype(F32) for start in starts]
    run_out = list(start_out)
    inners, inverses, actives, crossed = [], [], [], []
    for s in range(NS):
        norm = norms[:, s : s + 1]
        entry_out = []
        inner = run_in[s]
        if s > 0:
            inner = inner + spread(PROJ + s - 1)
            total = jnp.zeros((rows, R), F32)
            for t in range(s):
                base = spread(proj_at(s) + t)
                full = base + run_out[t]
                entry_out.append(full)
                total = total + actives[t].astype(F32) * (full + base + start_out[t])
            norm = norm + jnp.sum(total, -1, keepdims=True)
        inverse = lax.rsqrt(jnp.maximum(norm, 0.0) * (1.0 / width) + EPS)
        inner = inner * inverse
        active = (inner * jax.nn.sigmoid(inner)).astype(BF16)
        latent_ref[:, s * R : (s + 1) * R] = active
        inners.append(inner)
        inverses.append(inverse)
        actives.append(active)
        crossed.append(entry_out)
        grown = dot(active, square(s, s, NS - s))
        for t in range(NS):
            if t >= s:
                run_out[t] = run_out[t] + grown[:, (t - s) * R : (t - s + 1) * R]
            else:
                run_out[t] = run_out[t] + dot_t(active, square(t, s))
        if s < NS - 1:
            grown = dot(active, cross(s, s + 1, NS - 1 - s))
            for t in range(s + 1, NS):
                run_in[t] = run_in[t] + grown[:, (t - s - 1) * R : (t - s) * R]
    grads = [run_out[t] + spread(proj_at(NS - 1) + t) for t in range(NS)]
    lane = lax.broadcasted_iota(jnp.int32, (rows, BLK), 1)
    scalars = jnp.zeros((rows, BLK), F32)
    for s in range(NS - 1, -1, -1):
        inner = inners[s]
        sigm = jax.nn.sigmoid(inner)
        d_inner = (grads[s] * sigm * (1.0 + inner * (1.0 - sigm))).astype(BF16)
        latent_ref[:, (NS + s) * R : (NS + s + 1) * R] = d_inner
        inverse = inverses[s]
        total = jnp.sum(d_inner.astype(F32) * inner, -1, keepdims=True)
        scale = inverse * inverse * total * (1.0 / width)
        for t in range(s):
            grads[t] = (
                grads[t] + inverse * dot_t(d_inner, cross(t, s)) - scale * crossed[s][t]
            )
        scalars = jnp.where(lane == s, inverse, scalars)
        scalars = jnp.where(lane == NS + s, scale, scalars)
    scalar_ref[...] = scalars


def grads_kernel(
    at_ref, ids_ref, other_ids_ref, got_ref, first_ref, out_w_ref, in_w_ref, latent_ref, scalar_ref,
    give_ref, keep_ref, entry_ref, step_ref,
):
    cols = step_ref.shape[1]
    scalars = scalar_ref[...]
    inverses = [scalars[:, s : s + 1] for s in range(NS)]
    scales = [scalars[:, NS + s : NS + s + 1] for s in range(NS)]
    places = [
        pl.multiple_of(pick * TOK, TOK) for pick in picks_of(at_ref, ids_ref, other_ids_ref)
    ]

    def active(s):
        return latent_ref[:, s * R : (s + 1) * R]

    def d_inner(s):
        return latent_ref[:, (NS + s) * R : (NS + s + 1) * R]

    for side, result_ref in ((1 - at_ref[0], give_ref), (at_ref[0], keep_ref)):
        here = pl.ds(pl.multiple_of(side * cols, cols), cols)
        at = pl.multiple_of(side * HALF, HALF)

        def put(s, kind, value, result_ref=result_ref):
            result_ref[:, s, :, kind * R : (kind + 1) * R] = value.reshape(8, 32, R).astype(
                result_ref.dtype
            )

        entry = first_ref[:, here].astype(F32)
        for s in range(NS):
            if s > 0:
                step_ref[...] = stores(got_ref, s, at, cols)
                entry = entry + jnp.concatenate(
                    [step_ref[pl.ds(place, TOK), :] for place in places], 0
                )
            entry_ref[s] = entry
            put(s, 0, dot_rows((entry * inverses[s]).astype(BF16), d_inner(s)))
            entry = entry + dot(active(s), out_w_ref[s, :, here])
        grad = entry
        for s in range(NS - 1, -1, -1):
            put(s, 1, dot_rows(grad.astype(BF16), active(s)))
            if s > 0:
                grad = (
                    grad
                    + inverses[s] * dot_t(d_inner(s), in_w_ref[s, here, :])
                    - scales[s] * entry_ref[s]
                )


def final_kernel(parts_ref, gain_ref, in_ref, out_ref):
    total = parts_ref[0].astype(F32)
    for i in range(1, 8):
        total = total + parts_ref[i].astype(F32)
    gain = gain_ref[...].T
    for j in range(8):
        scale = gain[(j % 4) * 32 : (j % 4) * 32 + 32, j // 4 : j // 4 + 1]
        in_ref[j * 32 : j * 32 + 32, :] = total[j, :, :R] * scale
    out = total[:, :, R:].reshape(2 * BLK, R)
    for i in range(2):
        out_ref[:, i * BLK : (i + 1) * BLK] = out[i * BLK : (i + 1) * BLK].T


def body(first_input, example_ids, out_store, in_store, norm_gain, adapter_in, adapter_out):
    width = first_input.shape[2]
    cols = width // 16
    half = cols // 2
    wide = width // 2
    core = lax.axis_index("c")
    xl = lax.axis_index("xl")
    z = lax.axis_index("z")
    section = lax.axis_index(SECTION)
    quarter = xl * 2 + core
    at = jnp.stack([core, section, xl, quarter]).astype(jnp.int32)
    ids = example_ids[0]
    w_in = adapter_in[0]
    w_out = adapter_out[0]

    send, own_cols, give_cols = pl.pallas_call(
        pack_kernel,
        grid_spec=pltpu.PrefetchScalarGridSpec(
            num_scalar_prefetch=1,
            grid=(2,),
            in_specs=[
                pl.BlockSpec((64, wide), lambda i, at: (0, i)),
                pl.BlockSpec((64, wide), lambda i, at: (0, i)),
                pl.BlockSpec((32, wide), lambda i, at: (at[3], i)),
                pl.BlockSpec(
                    (1, 4, 1, 8, 32, R), lambda i, at: (i, at[3] % 2, at[3] // 2, 0, 0, 0)
                ),
                pl.BlockSpec((1, 4, 1, 2, BLK), lambda i, at: (i, at[3] % 2, at[3] // 2, 0, 0)),
                pl.BlockSpec((MIC, 32, wide), lambda i, at: (0, 0, i)),
            ],
            out_specs=[
                pl.BlockSpec((8, 32, SENT), lambda i, at: (i, 0, 0)),
                pl.BlockSpec((R, cols), lambda i, at: (0, 0)),
                pl.BlockSpec((R, cols), lambda i, at: (0, 0)),
            ],
            scratch_shapes=[pltpu.VMEM((4 * BLK, 4 * BLK), BF16)],
        ),
        out_shape=(
            jax.ShapeDtypeStruct((16, 32, SENT), BF16),
            jax.ShapeDtypeStruct((R, cols), BF16),
            jax.ShapeDtypeStruct((R, cols), BF16),
        ),
        compiler_params=LARGE,
        name="pack",
    )(
        at,
        in_store.reshape(64, width),
        out_store.reshape(64, width),
        w_out,
        w_in.reshape(2, 8, 2, 8, 32, R),
        norm_gain.reshape(2, 8, 2, 2, BLK),
        first_input,
    )
    other_ids = lax.ppermute(ids, "xl", SWAP)
    other_cols = lax.ppermute(give_cols, "xl", SWAP)
    got = lax.all_to_all(send, PLANE, 0, 0, tiled=True)
    other = lax.ppermute(got[:, :, W_LANE:], "c", SWAP)
    start = pl.pallas_call(
        start_kernel,
        out_shape=jax.ShapeDtypeStruct((R, 2 * R), BF16),
        in_specs=[VMEM, VMEM, VMEM, VMEM, pl.BlockSpec(memory_space=pl.ANY)],
        out_specs=VMEM,
        compiler_params=PARAMS,
        cost_estimate=pl.CostEstimate(flops=600000000, bytes_accessed=7000000, transcendentals=0),
        name="start",
    )(first_input, w_out, w_in, norm_gain, got)
    parts, out_w, in_w, first = pl.pallas_call(
        project_kernel,
        out_shape=(
            jax.ShapeDtypeStruct((16, 2 * TOK, WIDE), BF16),
            jax.ShapeDtypeStruct((NS, R, cols), BF16),
            jax.ShapeDtypeStruct((NS, cols, R), BF16),
            jax.ShapeDtypeStruct((2 * R, cols), BF16),
        ),
        in_specs=[SMEM, SMEM, SMEM, VMEM, VMEM, VMEM, VMEM, VMEM],
        out_specs=(VMEM, VMEM, VMEM, VMEM),
        scratch_shapes=[pltpu.VMEM((R, 2 * SPLIT * BLK), F32)],
        compiler_params=PARAMS,
        name="project",
    )(at, ids, other_ids, got, other, own_cols, other_cols, start)
    parts = lax.all_to_all(parts, PLANE, 0, 0, tiled=True)
    sums = pl.pallas_call(
        sum_kernel,
        out_shape=jax.ShapeDtypeStruct((16, 2 * TOK, SPLIT * BLK), BF16),
        in_specs=[VMEM],
        out_specs=VMEM,
        compiler_params=PARAMS,
        name="sums",
    )(parts)
    sums = lax.all_to_all(sums, PLANE, 0, 0, tiled=True)
    gram = sums[:, TOK:, (GRAM - SPLIT) * BLK : (GRAM - SPLIT + GRAMS) * BLK]
    other = lax.ppermute(gram.reshape(R, GRAMS * BLK), "c", SWAP)
    latent, scalars = pl.pallas_call(
        functools.partial(chain_kernel, width),
        out_shape=(
            jax.ShapeDtypeStruct((2 * R, 16 * BLK), BF16),
            jax.ShapeDtypeStruct((2 * R, BLK), F32),
        ),
        in_specs=[SMEM, SMEM, SMEM, VMEM, VMEM, VMEM],
        out_specs=(VMEM, VMEM),
        scratch_shapes=[
            pltpu.VMEM((R, GRAM * BLK), F32),
            pltpu.VMEM((R, OO * BLK), BF16),
            pltpu.VMEM((R, OI * BLK), BF16),
        ],
        compiler_params=PARAMS,
        name="chain",
    )(at, ids, other_ids, parts, sums, other)
    give, keep = pl.pallas_call(
        grads_kernel,
        out_shape=(
            jax.ShapeDtypeStruct((8, NS, 32, 2 * R), BF16),
            jax.ShapeDtypeStruct((8, NS, 32, 2 * R), F32),
        ),
        in_specs=[SMEM, SMEM, SMEM] + [VMEM] * 6,
        out_specs=(VMEM, VMEM),
        scratch_shapes=[pltpu.VMEM((NS, 2 * R, half), F32), pltpu.VMEM((R, half), F32)],
        compiler_params=PARAMS,
        name="grads",
    )(at, ids, other_ids, got, first, out_w, in_w, latent, scalars)

    swapped = lax.ppermute(give, "c", SWAP)
    total = (keep + swapped.astype(F32)).astype(BF16).reshape(64, 32, 2 * R)
    block = (xl * NS + z) * 2 + core
    gain = lax.dynamic_slice_in_dim(norm_gain[0], block * half, half, 0)
    total, gain = lax.optimization_barrier((total, gain))
    total = lax.all_to_all(total, ("z",) + SECTION, 0, 0, tiled=True)
    grad_in, grad_out = pl.pallas_call(
        final_kernel,
        out_shape=(
            jax.ShapeDtypeStruct((half, R), F32),
            jax.ShapeDtypeStruct((R, half), F32),
        ),
        in_specs=[VMEM, VMEM],
        out_specs=(VMEM, VMEM),
        compiler_params=PARAMS,
        name="final",
    )(total.reshape(8, 8, 32, 2 * R), gain.reshape(2, BLK))
    return (grad_in[None], grad_out[None])


def solution(mesh):
    fine = Mesh(mesh.devices.reshape(2, 8, 2, 4, 2), ("xl", "z", "c", "y", "xh"))
    dp = ("xl", "z", "c")
    placed = (
        P(None, dp, None),
        P(dp, None, None),
        P(SECTION, dp, None, None),
        P(SECTION, dp, None, None),
        P(SECTION, None),
        P(SECTION, None, None),
        P(SECTION, None, None),
    )
    return jax.shard_map(
        body,
        mesh=fine,
        in_specs=placed,
        out_specs=(P(SECTION, dp, None), P(SECTION, None, dp)),
        check_vma=False,
    )
```

```python
import functools

import jax
import jax.numpy as jnp
from jax import lax
from jax.experimental import pallas as pl
from jax.experimental.pallas import tpu as pltpu
from jax.sharding import Mesh, PartitionSpec as P

F32 = jnp.float32
BF16 = jnp.bfloat16
EPS = 1e-05
PLANE = ("xl", "y", "xh")
SECTION = ("y", "xh")
SWAP = [(0, 1), (1, 0)]
NS = 8
R = 128
TOK = 8
MIC = 4
BLK = 128
HALF = 1024
W_LANE = 2 * HALF
SENT = 3072
PROJ = 29
NORM = 34
GRAM = 37
GRAMS = 32
SPLIT = 35
START = SPLIT * BLK
WIDE = START + 16 * BLK
OO = 36
OI = 28
LARGE = pltpu.CompilerParams(vmem_limit_bytes=56 * 1024 * 1024)
PARAMS = pltpu.CompilerParams(vmem_limit_bytes=16 * 1024 * 1024)
VMEM = pl.BlockSpec(memory_space=pltpu.VMEM)
SMEM = pl.BlockSpec(memory_space=pltpu.SMEM)


def gram_at(t):
    return sum(NS - i for i in range(t))


def cross_at(t):
    return sum(NS - 1 - i for i in range(t))


def proj_at(s):
    return s * (s - 1) // 2


def inner_at(s):
    return PROJ + s - 1 + (PROJ + s - 1 >= NORM)


def dot_t(a, b):
    return lax.dot_general(a, b, (((1,), (1,)), ((), ())), preferred_element_type=F32)


def dot_rows(a, b):
    return lax.dot_general(a, b, (((0,), (0,)), ((), ())), preferred_element_type=F32)


def dot(a, b):
    return jnp.dot(a, b, preferred_element_type=F32)


def split(x):
    high = x.astype(BF16)
    return high, (x - high.astype(F32)).astype(BF16)


def pack_kernel(
    at_ref, in_ref, out_ref, w_out_ref, w_in_ref, gain_ref, first_ref,
    send_ref, cols_ref, give_ref, turn_ref,
):
    section = at_ref[1]

    @pl.when(pl.program_id(0) == 0)
    def _():
        shape = (4 * BLK, 4 * BLK)
        row = lax.broadcasted_iota(jnp.int32, shape, 0)
        col = lax.broadcasted_iota(jnp.int32, shape, 1)
        same = (row // BLK == col % BLK // 32) & (row % BLK // 32 == col // BLK)
        same = same & (row % 32 == col % 32)
        turn_ref[...] = jnp.where(same, 1.0, 0.0).astype(BF16)

    gain = gain_ref[...].reshape(8, BLK).T
    for s in range(NS):
        for j in range(4):
            column = 2 * j + s // 4
            scale = gain[(s % 4) * 32 : (s % 4) * 32 + 32, column : column + 1]
            to = W_LANE + 512 + j * BLK
            send_ref[s, :, to : to + BLK] = (w_in_ref[0, j, 0, s].astype(F32) * scale).astype(BF16)

    pieces, places = [], []
    for c in range(2):
        for zq in range(2):
            to = c * 256 + zq * BLK
            for h in range(2):
                lanes = [((4 * zq + j) * 4 + c * 2 + h) * BLK for j in range(4)]
                for ref, row, at in (
                    (in_ref, 0, c * HALF + zq * BLK),
                    (in_ref, 32, c * HALF + 256 + zq * BLK),
                    (out_ref, 0, c * HALF + 512 + zq * BLK),
                    (out_ref, 32, c * HALF + 768 + zq * BLK),
                    (w_out_ref, 0, W_LANE + to),
                ):
                    pieces.append(
                        jnp.concatenate(
                            [ref[row : row + 32, lane : lane + BLK] for lane in lanes], 1
                        )
                    )
                    places.append((4 * h, at))
    turned = dot(jnp.concatenate(pieces, 0), turn_ref[...]).astype(BF16)
    for n, (first, at) in enumerate(places):
        for i in range(4):
            send_ref[first + i, :, at : at + BLK] = turned[
                32 * n : 32 * n + 32, i * BLK : (i + 1) * BLK
            ]

    pieces = []
    for c in range(2):
        for zq in range(2):
            lanes = [
                pl.multiple_of(((4 * zq + j) * 4 + c * 2 + section // 4) * BLK, BLK)
                for j in range(4)
            ]
            for m in range(MIC):
                pieces.append(
                    jnp.concatenate([first_ref[m, :, pl.ds(lane, BLK)] for lane in lanes], 1)
                )
    group = pl.multiple_of(section % 4 * BLK, BLK)
    turned = dot(jnp.concatenate(pieces, 0), turn_ref[:, pl.ds(group, BLK)]).astype(BF16)
    mine = pl.program_id(0) == at_ref[2]

    def put(ref):
        for n in range(4):
            ref[:, n * BLK : (n + 1) * BLK] = turned[n * R : (n + 1) * R]

    @pl.when(mine)
    def _():
        put(cols_ref)

    @pl.when(jnp.logical_not(mine))
    def _():
        put(give_ref)


def start_kernel(first_ref, w_out_ref, w_in_ref, gain_ref, after_ref, start_ref):
    del after_ref
    flat = first_ref[...].reshape(R, first_ref.shape[2])
    scaled = (flat.astype(F32) * gain_ref[...]).astype(BF16)
    start_ref[:, :R] = dot(scaled, w_in_ref[...]).astype(BF16)
    start_ref[:, R:] = dot_t(flat, w_out_ref[...]).astype(BF16)


def stores(got_ref, s, at, cols):
    pieces = []
    for x in range(2):
        for i in range(2):
            a, b = at + i * 256, at + 512 + i * 256
            pieces.append(
                got_ref[x * NS + s, :, pl.ds(a, cols)].astype(F32)
                - got_ref[x * NS + s - 1, :, pl.ds(b, cols)].astype(F32)
            )
    return jnp.concatenate(pieces, 0)


def picks_of(at_ref, ids_ref, other_ids_ref):
    picks = []
    for x in range(2):
        here = at_ref[2] == x
        for m in range(MIC):
            for j in range(4):
                picks.append(x * NS + jnp.where(here, ids_ref[m, j], other_ids_ref[m, j]))
    return picks


def running_sums(got_ref, cols):
    running = None
    for s in range(1, NS):
        step = jnp.concatenate(
            [stores(got_ref, s, 0, cols // 2), stores(got_ref, s, HALF, cols // 2)], 1
        )
        running = step if running is None else running + step
        yield s, running


def project_kernel(
    at_ref, got_ref, other_ref, start_ref, send_ref, out_w_ref, in_w_ref, wide_ref
):
    cols = in_w_ref.shape[1]
    first_core = at_ref[0] == 0
    for s in range(NS):
        for x in range(2):
            mine = got_ref[x * NS + s, :, W_LANE:SENT]
            theirs = other_ref[x * NS + s]
            for c in range(2):
                part = jnp.where(first_core == (c == 0), mine, theirs)
                k = 2 * x + c
                out_w_ref[s, 32 * k : 32 * k + 32, :] = part[:, :cols]
                for g in range(4):
                    row = k * BLK + g * 32
                    lane = cols + g * BLK
                    in_w_ref[s, row : row + 32, :] = part[:, lane : lane + BLK]
    for s, running in running_sums(got_ref, cols):
        rounded = running.astype(BF16)
        count = s if s < NS - 1 else NS
        at = proj_at(s) * BLK
        wide_ref[:, at : at + count * BLK] = dot_t(
            rounded, out_w_ref[0:count].reshape(count * R, cols)
        )
        at = inner_at(s) * BLK
        wide_ref[:, at : at + BLK] = dot(rounded, in_w_ref[s])
    for b in (NORM, GRAM + GRAMS):
        wide_ref[:, b * BLK : (b + 1) * BLK] = jnp.zeros((R, BLK), F32)

    square = [(t, s) for t in range(NS) for s in range(t, NS)]

    @pl.when(first_core)
    def _():
        for t in range(5):
            at = (GRAM + gram_at(t)) * BLK
            wide_ref[:, at : at + (NS - t) * BLK] = dot_t(
                out_w_ref[t], out_w_ref[t:NS].reshape((NS - t) * R, cols)
            )
        for i in range(gram_at(5), GRAMS):
            t, s = square[i]
            at = (GRAM + i) * BLK
            wide_ref[:, at : at + BLK] = dot_t(out_w_ref[t], out_w_ref[s])

    @pl.when(jnp.logical_not(first_core))
    def _():
        for t in range(NS - 1):
            for s in range(t + 1, NS):
                at = (GRAM + cross_at(t) + s - t - 1) * BLK
                wide_ref[:, at : at + BLK] = dot(out_w_ref[t], in_w_ref[s])
        for i in range(GRAMS, OO):
            t, s = square[i]
            at = (GRAM + OI + i - GRAMS) * BLK
            wide_ref[:, at : at + BLK] = dot_t(out_w_ref[t], out_w_ref[s])

    for b in range(SPLIT):
        pair = [
            wide_ref[:, at * BLK : (at + 1) * BLK].reshape(16, TOK, BLK) for at in (b, SPLIT + b)
        ]
        send_ref[:, :, b * BLK : (b + 1) * BLK] = jnp.concatenate(pair, 1).astype(BF16)
    for g in range(8):
        at = START + g * 2 * R
        for q in range(16):
            send_ref[q, :, at : at + 2 * R] = start_ref[g * 16 : (g + 1) * 16, :]


def norm_kernel(
    at_ref, ids_ref, other_ids_ref, got_ref, cols_ref, other_cols_ref, before_ref,
    send_ref, first_ref, block_ref, sem,
):
    del before_ref
    cols = cols_ref.shape[1]
    picks = picks_of(at_ref, ids_ref, other_ids_ref)
    placed = [[] for _ in range(MIC)]
    for x in range(2):
        rows = jnp.where(at_ref[2] == x, cols_ref[...], other_cols_ref[...])
        first_ref[x * R : (x + 1) * R, :] = rows
        rows = rows.astype(F32)
        for e in range(NS):
            for m in range(MIC):
                total = jnp.zeros((TOK, cols), F32)
                for j in range(4):
                    n = 4 * m + j
                    total = jnp.where(
                        picks[16 * x + n] == x * NS + e, rows[n * TOK : (n + 1) * TOK], total
                    )
                placed[m].append(total)
    placed = [jnp.concatenate(blocks, 0) for blocks in placed]
    lane = lax.broadcasted_iota(jnp.int32, (R, BLK), 1)
    norms = jnp.zeros((R, BLK), F32)
    for m in range(MIC):
        part = jnp.sum(placed[m] * placed[m], -1, keepdims=True)
        norms = jnp.where(lane == m * NS, part, norms)
    for s, running in running_sums(got_ref, cols):
        for m in range(MIC):
            entry = running + placed[m]
            part = jnp.sum(entry * entry, -1, keepdims=True)
            norms = jnp.where(lane == m * NS + s, part, norms)
    high = norms.astype(BF16).astype(F32)
    norms = jnp.where(lane < 32, high, pltpu.roll(norms - high, 32, 1)).reshape(16, TOK, BLK)
    block_ref[...] = jnp.concatenate([norms, jnp.zeros_like(norms)], 1).astype(BF16)
    copy = pltpu.make_async_copy(
        block_ref, send_ref.at[:, :, NORM * BLK : (NORM + 1) * BLK], sem
    )
    copy.start()
    copy.wait()


def sum_kernel(parts_ref, send_ref):
    lane = lax.broadcasted_iota(jnp.int32, (2 * TOK, BLK), 1)
    row = lax.broadcasted_iota(jnp.int32, (2 * TOK, BLK), 0)
    for b in range(SPLIT):
        at = slice(b * BLK, (b + 1) * BLK)
        total = parts_ref[0, :, at].astype(F32)
        for q in range(1, 16):
            total = total + parts_ref[q, :, at].astype(F32)
        if b == NORM:
            norm = total + pltpu.roll(total, 96, 1)
            high = norm.astype(BF16).astype(F32)
            norm = jnp.where(lane < 32, high, pltpu.roll(norm - high, 32, 1))
            total = jnp.where(row < TOK, norm, 0.0)
        total = total.astype(BF16)
        for q in range(16):
            send_ref[q, :, at] = total


def chain_kernel(
    width, at_ref, ids_ref, other_ids_ref, parts_ref, sums_ref, other_ref,
    latent_ref, scalar_ref, proj_ref, oo_ref, oi_ref, oo_rows_ref, oi_rows_ref,
):
    rows = 2 * R
    first_core = at_ref[0] == 0
    for b in range(GRAM):
        upper = b >= SPLIT
        at = (b - SPLIT * upper) * BLK
        block = sums_ref[:, :, at : at + BLK].astype(F32)
        proj_ref[:, b * BLK : (b + 1) * BLK] = block[:, TOK * upper : TOK * upper + TOK].reshape(
            R, BLK
        )
    for b in range(0, GRAMS, 4):
        at = (GRAM - SPLIT + b) * BLK
        mine = sums_ref[:, :, at : at + 4 * BLK].astype(F32)[:, TOK:]
        mine = mine.reshape(R, 4 * BLK).astype(BF16)
        at = slice(b * BLK, (b + 4) * BLK)
        theirs = other_ref[:, at]
        oo_ref[:, at] = jnp.where(first_core, mine, theirs)
        second = jnp.where(first_core, theirs, mine)
        if b < OI:
            oi_ref[:, at] = second
        else:
            oo_ref[:, (b + 4) * BLK : (b + 8) * BLK] = second
    places = [
        pl.multiple_of(pick * TOK, TOK) for pick in picks_of(at_ref, ids_ref, other_ids_ref)
    ]

    def spread(at):
        return jnp.concatenate(
            [proj_ref[pl.ds(place, TOK), at * BLK : (at + 1) * BLK] for place in places], 0
        )

    def square(t, s, count=1):
        at = (gram_at(t) + s - t) * BLK
        return oo_ref[:, at : at + count * BLK]

    def cross(t, s, count=1):
        at = (cross_at(t) + s - t - 1) * BLK
        return oi_ref[:, at : at + count * BLK]

    for s in range(1, NS):
        for t in range(s):
            at = slice((proj_at(s) + t) * R, (proj_at(s) + t + 1) * R)
            oo_rows_ref[at, :] = square(t, s)
            oi_rows_ref[at, :] = cross(t, s)

    def above(ref, s):
        return ref[proj_at(s) * R : (proj_at(s) + s) * R, :]

    norms = spread(NORM)
    norms = norms + pltpu.roll(norms, 96, 1)
    pieces = []
    for n in range(32):
        m = n % 16 // 4
        piece = norms[n * TOK : (n + 1) * TOK]
        pieces.append(pltpu.roll(piece, BLK - m * NS, 1) if m else piece)
    norms = jnp.concatenate(pieces, 0)

    starts = []
    for s in range(NS):
        pieces = []
        for x in range(2):
            for g in range(8):
                at = START + g * 2 * R
                pieces.append(parts_ref[x * NS + s, :, at : at + 2 * R])
        starts.append(jnp.concatenate(pieces, 0))
    start_out = [start[:, R:].astype(F32) for start in starts]
    run_in = [start[:, :R].astype(F32) for start in starts]
    run_out = list(start_out)
    inners, inverses, actives, crossed = [], [], [], []
    for s in range(NS):
        norm = norms[:, s : s + 1]
        entry_out = []
        inner = run_in[s]
        if s > 0:
            inner = inner + spread(inner_at(s))
            total = jnp.zeros((rows, R), F32)
            for t in range(s):
                base = spread(proj_at(s) + t)
                full = base + run_out[t]
                entry_out.append(full)
                total = total + actives[t].astype(F32) * (full + base + start_out[t])
            norm = norm + jnp.sum(total, -1, keepdims=True)
        inverse = lax.rsqrt(jnp.maximum(norm, 0.0) * (1.0 / width) + EPS)
        inner = inner * inverse
        active = (inner * jax.nn.sigmoid(inner)).astype(BF16)
        latent_ref[:, s * R : (s + 1) * R] = active
        inners.append(inner)
        inverses.append(inverse)
        actives.append(active)
        crossed.append(entry_out)
        grown = dot(active, square(s, s, NS - s))
        if s > 0:
            grown = jnp.concatenate([dot_t(active, above(oo_rows_ref, s)), grown], 1)
        for t in range(NS):
            run_out[t] = run_out[t] + grown[:, t * R : (t + 1) * R]
        if s < NS - 1:
            grown = dot(active, cross(s, s + 1, NS - 1 - s))
            for t in range(s + 1, NS):
                run_in[t] = run_in[t] + grown[:, (t - s - 1) * R : (t - s) * R]
    grads = [run_out[t] + spread(proj_at(NS - 1) + t) for t in range(NS)]
    lane = lax.broadcasted_iota(jnp.int32, (rows, BLK), 1)
    scalars = jnp.zeros((rows, BLK), F32)
    for s in range(NS - 1, -1, -1):
        inner = inners[s]
        sigm = jax.nn.sigmoid(inner)
        d_inner = (grads[s] * sigm * (1.0 + inner * (1.0 - sigm))).astype(BF16)
        latent_ref[:, (NS + s) * R : (NS + s + 1) * R] = d_inner
        inverse = inverses[s]
        total = jnp.sum(d_inner.astype(F32) * inner, -1, keepdims=True)
        scale = inverse * inverse * total * (1.0 / width)
        if s > 0:
            back = dot_t(d_inner, above(oi_rows_ref, s))
        for t in range(s):
            grads[t] = (
                grads[t] + inverse * back[:, t * R : (t + 1) * R] - scale * crossed[s][t]
            )
        scalars = jnp.where(lane == s, inverse, scalars)
        scalars = jnp.where(lane == NS + s, scale, scalars)
    scalar_ref[...] = scalars


def grads_kernel(
    at_ref, ids_ref, other_ids_ref, got_ref, first_ref, out_w_ref, in_w_ref, latent_ref, scalar_ref,
    give_ref, keep_ref, entry_ref, step_ref,
):
    cols = step_ref.shape[1]
    scalars = scalar_ref[...]
    inverses = [scalars[:, s : s + 1] for s in range(NS)]
    scales = [scalars[:, NS + s : NS + s + 1] for s in range(NS)]
    places = [
        pl.multiple_of(pick * TOK, TOK) for pick in picks_of(at_ref, ids_ref, other_ids_ref)
    ]

    def active(s):
        return latent_ref[:, s * R : (s + 1) * R]

    def d_inner(s):
        return latent_ref[:, (NS + s) * R : (NS + s + 1) * R]

    for side, result_ref in ((1 - at_ref[0], give_ref), (at_ref[0], keep_ref)):
        here = pl.ds(pl.multiple_of(side * cols, cols), cols)
        at = pl.multiple_of(side * HALF, HALF)

        def put(s, kind, value, result_ref=result_ref):
            result_ref[:, s, :, kind * R : (kind + 1) * R] = value.reshape(8, 32, R).astype(
                result_ref.dtype
            )

        entry = first_ref[:, here].astype(F32)
        for s in range(NS):
            if s > 0:
                step_ref[...] = stores(got_ref, s, at, cols)
                entry = entry + jnp.concatenate(
                    [step_ref[pl.ds(place, TOK), :] for place in places], 0
                )
            entry_ref[s] = entry
            put(s, 0, dot_rows((entry * inverses[s]).astype(BF16), d_inner(s)))
            entry = entry + dot(active(s), out_w_ref[s, :, here])
        grad = entry
        for s in range(NS - 1, -1, -1):
            put(s, 1, dot_rows(grad.astype(BF16), active(s)))
            if s > 0:
                grad = (
                    grad
                    + inverses[s] * dot_t(d_inner(s), in_w_ref[s, here, :])
                    - scales[s] * entry_ref[s]
                )


def add_kernel(keep_ref, swapped_ref, total_ref):
    for i in range(8):
        total_ref[i] = (keep_ref[i] + swapped_ref[i].astype(F32)).astype(BF16)


def final_kernel(parts_ref, gain_ref, in_ref, out_ref):
    total = parts_ref[0].astype(F32)
    for i in range(1, 8):
        total = total + parts_ref[i].astype(F32)
    gain = gain_ref[...].T
    for j in range(8):
        scale = gain[(j % 4) * 32 : (j % 4) * 32 + 32, j // 4 : j // 4 + 1]
        in_ref[j * 32 : j * 32 + 32, :] = total[j, :, :R] * scale
    out = total[:, :, R:].reshape(2 * BLK, R)
    for i in range(2):
        out_ref[:, i * BLK : (i + 1) * BLK] = out[i * BLK : (i + 1) * BLK].T


def body(first_input, example_ids, out_store, in_store, norm_gain, adapter_in, adapter_out):
    width = first_input.shape[2]
    cols = width // 16
    half = cols // 2
    wide = width // 2
    core = lax.axis_index("c")
    xl = lax.axis_index("xl")
    z = lax.axis_index("z")
    section = lax.axis_index(SECTION)
    quarter = xl * 2 + core
    at = jnp.stack([core, section, xl, quarter]).astype(jnp.int32)
    ids = example_ids[0]
    w_in = adapter_in[0]
    w_out = adapter_out[0]

    send, own_cols, give_cols = pl.pallas_call(
        pack_kernel,
        grid_spec=pltpu.PrefetchScalarGridSpec(
            num_scalar_prefetch=1,
            grid=(2,),
            in_specs=[
                pl.BlockSpec((64, wide), lambda i, at: (0, i)),
                pl.BlockSpec((64, wide), lambda i, at: (0, i)),
                pl.BlockSpec((32, wide), lambda i, at: (at[3], i)),
                pl.BlockSpec(
                    (1, 4, 1, 8, 32, R), lambda i, at: (i, at[3] % 2, at[3] // 2, 0, 0, 0)
                ),
                pl.BlockSpec((1, 4, 1, 2, BLK), lambda i, at: (i, at[3] % 2, at[3] // 2, 0, 0)),
                pl.BlockSpec((MIC, 32, wide), lambda i, at: (0, 0, i)),
            ],
            out_specs=[
                pl.BlockSpec((8, 32, SENT), lambda i, at: (i, 0, 0)),
                pl.BlockSpec((R, cols), lambda i, at: (0, 0)),
                pl.BlockSpec((R, cols), lambda i, at: (0, 0)),
            ],
            scratch_shapes=[pltpu.VMEM((4 * BLK, 4 * BLK), BF16)],
        ),
        out_shape=(
            jax.ShapeDtypeStruct((16, 32, SENT), BF16),
            jax.ShapeDtypeStruct((R, cols), BF16),
            jax.ShapeDtypeStruct((R, cols), BF16),
        ),
        compiler_params=LARGE,
        name="pack",
    )(
        at,
        in_store.reshape(64, width),
        out_store.reshape(64, width),
        w_out,
        w_in.reshape(2, 8, 2, 8, 32, R),
        norm_gain.reshape(2, 8, 2, 2, BLK),
        first_input,
    )
    other_ids = lax.ppermute(ids, "xl", SWAP)
    other_cols = lax.ppermute(give_cols, "xl", SWAP)
    got = lax.all_to_all(send, PLANE, 0, 0, tiled=True)
    other = lax.ppermute(got[:, :, W_LANE:], "c", SWAP)
    start = pl.pallas_call(
        start_kernel,
        out_shape=jax.ShapeDtypeStruct((R, 2 * R), BF16),
        in_specs=[VMEM, VMEM, VMEM, VMEM, pl.BlockSpec(memory_space=pl.ANY)],
        out_specs=VMEM,
        compiler_params=PARAMS,
        cost_estimate=pl.CostEstimate(flops=600000000, bytes_accessed=7000000, transcendentals=0),
        name="start",
    )(first_input, w_out, w_in, norm_gain, got)
    parts, out_w, in_w = pl.pallas_call(
        project_kernel,
        out_shape=(
            jax.ShapeDtypeStruct((16, 2 * TOK, WIDE), BF16),
            jax.ShapeDtypeStruct((NS, R, cols), BF16),
            jax.ShapeDtypeStruct((NS, cols, R), BF16),
        ),
        in_specs=[SMEM, VMEM, VMEM, VMEM],
        out_specs=(VMEM, VMEM, VMEM),
        scratch_shapes=[pltpu.VMEM((R, 2 * SPLIT * BLK), F32)],
        compiler_params=PARAMS,
        cost_estimate=pl.CostEstimate(flops=2000000000, bytes_accessed=9000000, transcendentals=0),
        name="project",
    )(at, got, other, start)
    parts, first = pl.pallas_call(
        norm_kernel,
        out_shape=(
            jax.ShapeDtypeStruct((16, 2 * TOK, WIDE), BF16),
            jax.ShapeDtypeStruct((2 * R, cols), BF16),
        ),
        in_specs=[SMEM, SMEM, SMEM, VMEM, VMEM, VMEM, pl.BlockSpec(memory_space=pl.ANY)],
        out_specs=(pl.BlockSpec(memory_space=pl.ANY), VMEM),
        scratch_shapes=[pltpu.VMEM((16, 2 * TOK, BLK), BF16), pltpu.SemaphoreType.DMA],
        input_output_aliases={6: 0},
        compiler_params=PARAMS,
        name="norms",
    )(at, ids, other_ids, got, own_cols, other_cols, parts)
    parts = lax.all_to_all(parts, PLANE, 0, 0, tiled=True)
    sums = pl.pallas_call(
        sum_kernel,
        out_shape=jax.ShapeDtypeStruct((16, 2 * TOK, SPLIT * BLK), BF16),
        in_specs=[VMEM],
        out_specs=VMEM,
        compiler_params=PARAMS,
        name="sums",
    )(parts)
    sums = lax.all_to_all(sums, PLANE, 0, 0, tiled=True)
    gram = sums[:, TOK:, (GRAM - SPLIT) * BLK : (GRAM - SPLIT + GRAMS) * BLK]
    other = lax.ppermute(gram.reshape(R, GRAMS * BLK), "c", SWAP)
    latent, scalars = pl.pallas_call(
        functools.partial(chain_kernel, width),
        out_shape=(
            jax.ShapeDtypeStruct((2 * R, 16 * BLK), BF16),
            jax.ShapeDtypeStruct((2 * R, BLK), F32),
        ),
        in_specs=[SMEM, SMEM, SMEM, VMEM, VMEM, VMEM],
        out_specs=(VMEM, VMEM),
        scratch_shapes=[
            pltpu.VMEM((R, GRAM * BLK), F32),
            pltpu.VMEM((R, OO * BLK), BF16),
            pltpu.VMEM((R, OI * BLK), BF16),
            pltpu.VMEM((OI * R, R), BF16),
            pltpu.VMEM((OI * R, R), BF16),
        ],
        compiler_params=PARAMS,
        name="chain",
    )(at, ids, other_ids, parts, sums, other)
    give, keep = pl.pallas_call(
        grads_kernel,
        out_shape=(
            jax.ShapeDtypeStruct((8, NS, 32, 2 * R), BF16),
            jax.ShapeDtypeStruct((8, NS, 32, 2 * R), F32),
        ),
        in_specs=[SMEM, SMEM, SMEM] + [VMEM] * 6,
        out_specs=(VMEM, VMEM),
        scratch_shapes=[pltpu.VMEM((NS, 2 * R, half), F32), pltpu.VMEM((R, half), F32)],
        compiler_params=PARAMS,
        name="grads",
    )(at, ids, other_ids, got, first, out_w, in_w, latent, scalars)

    swapped = lax.ppermute(give, "c", SWAP)
    total = pl.pallas_call(
        add_kernel,
        out_shape=jax.ShapeDtypeStruct((8, NS, 32, 2 * R), BF16),
        in_specs=[VMEM, VMEM],
        out_specs=VMEM,
        compiler_params=PARAMS,
        name="add",
    )(keep, swapped).reshape(64, 32, 2 * R)
    block = (xl * NS + z) * 2 + core
    gain = lax.dynamic_slice_in_dim(norm_gain[0], block * half, half, 0)
    total, gain = lax.optimization_barrier((total, gain))
    total = lax.all_to_all(total, ("z",) + SECTION, 0, 0, tiled=True)
    grad_in, grad_out = pl.pallas_call(
        final_kernel,
        out_shape=(
            jax.ShapeDtypeStruct((half, R), F32),
            jax.ShapeDtypeStruct((R, half), F32),
        ),
        in_specs=[VMEM, VMEM],
        out_specs=(VMEM, VMEM),
        compiler_params=PARAMS,
        name="final",
    )(total.reshape(8, 8, 32, 2 * R), gain.reshape(2, BLK))
    return (grad_in[None], grad_out[None])


def solution(mesh):
    fine = Mesh(mesh.devices.reshape(2, 8, 2, 4, 2), ("xl", "z", "c", "y", "xh"))
    dp = ("xl", "z", "c")
    placed = (
        P(None, dp, None),
        P(dp, None, None),
        P(SECTION, dp, None, None),
        P(SECTION, dp, None, None),
        P(SECTION, None),
        P(SECTION, None, None),
        P(SECTION, None, None),
    )
    return jax.shard_map(
        body,
        mesh=fine,
        in_specs=placed,
        out_specs=(P(SECTION, dp, None), P(SECTION, None, dp)),
        check_vma=False,
    )
```

```python
import functools

import jax
import jax.numpy as jnp
from jax import lax
from jax.experimental import pallas as pl
from jax.experimental.pallas import tpu as pltpu
from jax.sharding import Mesh, PartitionSpec as P

F32 = jnp.float32
BF16 = jnp.bfloat16
EPS = 1e-05
PLANE = ("xl", "y", "xh")
SECTION = ("y", "xh")
SWAP = [(0, 1), (1, 0)]
NS = 8
R = 128
TOK = 8
MIC = 4
BLK = 128
HALF = 1024
W_LANE = 2 * HALF
SENT = 3072
PROJ = 29
NORM = 34
GRAM = 37
GRAMS = 32
SPLIT = 35
START = SPLIT * BLK
WIDE = START + 16 * BLK
OO = 36
OI = 28
LARGE = pltpu.CompilerParams(vmem_limit_bytes=56 * 1024 * 1024)
PARAMS = pltpu.CompilerParams(vmem_limit_bytes=16 * 1024 * 1024)
VMEM = pl.BlockSpec(memory_space=pltpu.VMEM)
SMEM = pl.BlockSpec(memory_space=pltpu.SMEM)


def gram_at(t):
    return sum(NS - i for i in range(t))


def cross_at(t):
    return sum(NS - 1 - i for i in range(t))


def proj_at(s):
    return s * (s - 1) // 2


def inner_at(s):
    return PROJ + s - 1 + (PROJ + s - 1 >= NORM)


def dot_t(a, b):
    return lax.dot_general(a, b, (((1,), (1,)), ((), ())), preferred_element_type=F32)


def dot_rows(a, b):
    return lax.dot_general(a, b, (((0,), (0,)), ((), ())), preferred_element_type=F32)


def dot(a, b):
    return jnp.dot(a, b, preferred_element_type=F32)


def split(x):
    high = x.astype(BF16)
    return high, (x - high.astype(F32)).astype(BF16)


def pack_kernel(
    at_ref, in_ref, out_ref, w_out_ref, w_in_ref, gain_ref, first_ref,
    send_ref, turn_ref,
):
    section = at_ref[1]

    @pl.when(pl.program_id(0) == 0)
    def _():
        shape = (4 * BLK, 4 * BLK)
        row = lax.broadcasted_iota(jnp.int32, shape, 0)
        col = lax.broadcasted_iota(jnp.int32, shape, 1)
        same = (row // BLK == col % BLK // 32) & (row % BLK // 32 == col // BLK)
        same = same & (row % 32 == col % 32)
        turn_ref[...] = jnp.where(same, 1.0, 0.0).astype(BF16)

    gain = gain_ref[...].reshape(8, BLK).T
    for s in range(NS):
        for j in range(4):
            column = 2 * j + s // 4
            scale = gain[(s % 4) * 32 : (s % 4) * 32 + 32, column : column + 1]
            to = W_LANE + 512 + j * BLK
            send_ref[s, :, to : to + BLK] = (w_in_ref[0, j, 0, s].astype(F32) * scale).astype(BF16)

    pieces, places = [], []
    for c in range(2):
        for zq in range(2):
            to = c * 256 + zq * BLK
            for h in range(2):
                lanes = [((4 * zq + j) * 4 + c * 2 + h) * BLK for j in range(4)]
                for ref, row, at, other in (
                    (in_ref, 0, c * HALF + zq * BLK, 0),
                    (in_ref, 32, c * HALF + 256 + zq * BLK, 0),
                    (out_ref, 0, c * HALF + 512 + zq * BLK, NS - 1),
                    (out_ref, 32, c * HALF + 768 + zq * BLK, NS - 1),
                    (w_out_ref, 0, W_LANE + to, None),
                ):
                    piece = jnp.concatenate(
                        [ref[row : row + 32, lane : lane + BLK] for lane in lanes], 1
                    )
                    if other is not None:
                        first = jnp.concatenate(
                            [first_ref[row // 32, :, lane : lane + BLK] for lane in lanes], 1
                        )
                        piece = jnp.where(section == other, first, piece)
                    pieces.append(piece)
                    places.append((4 * h, at))
    turned = dot(jnp.concatenate(pieces, 0), turn_ref[...]).astype(BF16)
    for n, (first, at) in enumerate(places):
        for i in range(4):
            send_ref[first + i, :, at : at + BLK] = turned[
                32 * n : 32 * n + 32, i * BLK : (i + 1) * BLK
            ]


def start_kernel(first_ref, w_out_ref, w_in_ref, gain_ref, after_ref, start_ref):
    del after_ref
    flat = first_ref[...].reshape(R, first_ref.shape[2])
    scaled = (flat.astype(F32) * gain_ref[...]).astype(BF16)
    start_ref[:, :R] = dot(scaled, w_in_ref[...]).astype(BF16)
    start_ref[:, R:] = dot_t(flat, w_out_ref[...]).astype(BF16)


def stores(got_ref, s, at, cols):
    pieces = []
    for x in range(2):
        for i in range(2):
            a, b = at + i * 256, at + 512 + i * 256
            pieces.append(
                got_ref[x * NS + s, :, pl.ds(a, cols)].astype(F32)
                - got_ref[x * NS + s - 1, :, pl.ds(b, cols)].astype(F32)
            )
    return jnp.concatenate(pieces, 0)


def first_rows(got_ref, at, cols):
    pieces = []
    for x in range(2):
        for m in range(MIC):
            q = x * NS + (0 if m < 2 else NS - 1)
            lane = at + m // 2 * 512 + m % 2 * 256
            pieces.append(got_ref[q, :, pl.ds(lane, cols)])
    return jnp.concatenate(pieces, 0).astype(F32)


def picks_of(at_ref, ids_ref, other_ids_ref):
    picks = []
    for x in range(2):
        here = at_ref[2] == x
        for m in range(MIC):
            for j in range(4):
                picks.append(x * NS + jnp.where(here, ids_ref[m, j], other_ids_ref[m, j]))
    return picks


def running_sums(got_ref, cols):
    running = None
    for s in range(1, NS):
        step = jnp.concatenate(
            [stores(got_ref, s, 0, cols // 2), stores(got_ref, s, HALF, cols // 2)], 1
        )
        running = step if running is None else running + step
        yield s, running


def project_kernel(
    at_ref, got_ref, other_ref, start_ref, send_ref, out_w_ref, in_w_ref, wide_ref
):
    cols = in_w_ref.shape[1]
    first_core = at_ref[0] == 0
    for s in range(NS):
        for x in range(2):
            mine = got_ref[x * NS + s, :, W_LANE:SENT]
            theirs = other_ref[x * NS + s]
            for c in range(2):
                part = jnp.where(first_core == (c == 0), mine, theirs)
                k = 2 * x + c
                out_w_ref[s, 32 * k : 32 * k + 32, :] = part[:, :cols]
                for g in range(4):
                    row = k * BLK + g * 32
                    lane = cols + g * BLK
                    in_w_ref[s, row : row + 32, :] = part[:, lane : lane + BLK]
    for s, running in running_sums(got_ref, cols):
        rounded = running.astype(BF16)
        count = s if s < NS - 1 else NS
        at = proj_at(s) * BLK
        wide_ref[:, at : at + count * BLK] = dot_t(
            rounded, out_w_ref[0:count].reshape(count * R, cols)
        )
        at = inner_at(s) * BLK
        wide_ref[:, at : at + BLK] = dot(rounded, in_w_ref[s])
    for b in (NORM, GRAM + GRAMS):
        wide_ref[:, b * BLK : (b + 1) * BLK] = jnp.zeros((R, BLK), F32)

    square = [(t, s) for t in range(NS) for s in range(t, NS)]

    @pl.when(first_core)
    def _():
        for t in range(5):
            at = (GRAM + gram_at(t)) * BLK
            wide_ref[:, at : at + (NS - t) * BLK] = dot_t(
                out_w_ref[t], out_w_ref[t:NS].reshape((NS - t) * R, cols)
            )
        for i in range(gram_at(5), GRAMS):
            t, s = square[i]
            at = (GRAM + i) * BLK
            wide_ref[:, at : at + BLK] = dot_t(out_w_ref[t], out_w_ref[s])

    @pl.when(jnp.logical_not(first_core))
    def _():
        for t in range(NS - 1):
            for s in range(t + 1, NS):
                at = (GRAM + cross_at(t) + s - t - 1) * BLK
                wide_ref[:, at : at + BLK] = dot(out_w_ref[t], in_w_ref[s])
        for i in range(GRAMS, OO):
            t, s = square[i]
            at = (GRAM + OI + i - GRAMS) * BLK
            wide_ref[:, at : at + BLK] = dot_t(out_w_ref[t], out_w_ref[s])

    for b in range(SPLIT):
        pair = [
            wide_ref[:, at * BLK : (at + 1) * BLK].reshape(16, TOK, BLK) for at in (b, SPLIT + b)
        ]
        send_ref[:, :, b * BLK : (b + 1) * BLK] = jnp.concatenate(pair, 1).astype(BF16)
    for g in range(8):
        at = START + g * 2 * R
        for q in range(16):
            send_ref[q, :, at : at + 2 * R] = start_ref[g * 16 : (g + 1) * 16, :]


def norm_kernel(
    cols, at_ref, ids_ref, other_ids_ref, got_ref, before_ref, send_ref, block_ref, sem
):
    del before_ref
    picks = picks_of(at_ref, ids_ref, other_ids_ref)
    placed = [[] for _ in range(MIC)]
    first = jnp.concatenate(
        [first_rows(got_ref, 0, cols // 2), first_rows(got_ref, HALF, cols // 2)], 1
    )
    for x in range(2):
        rows = first[x * R : (x + 1) * R]
        for e in range(NS):
            for m in range(MIC):
                total = jnp.zeros((TOK, cols), F32)
                for j in range(4):
                    n = 4 * m + j
                    total = jnp.where(
                        picks[16 * x + n] == x * NS + e, rows[n * TOK : (n + 1) * TOK], total
                    )
                placed[m].append(total)
    placed = [jnp.concatenate(blocks, 0) for blocks in placed]
    lane = lax.broadcasted_iota(jnp.int32, (R, BLK), 1)
    norms = jnp.zeros((R, BLK), F32)
    for m in range(MIC):
        part = jnp.sum(placed[m] * placed[m], -1, keepdims=True)
        norms = jnp.where(lane == m * NS, part, norms)
    for s, running in running_sums(got_ref, cols):
        for m in range(MIC):
            entry = running + placed[m]
            part = jnp.sum(entry * entry, -1, keepdims=True)
            norms = jnp.where(lane == m * NS + s, part, norms)
    high = norms.astype(BF16).astype(F32)
    norms = jnp.where(lane < 32, high, pltpu.roll(norms - high, 32, 1)).reshape(16, TOK, BLK)
    block_ref[...] = jnp.concatenate([norms, jnp.zeros_like(norms)], 1).astype(BF16)
    copy = pltpu.make_async_copy(
        block_ref, send_ref.at[:, :, NORM * BLK : (NORM + 1) * BLK], sem
    )
    copy.start()
    copy.wait()


def sum_kernel(parts_ref, send_ref):
    lane = lax.broadcasted_iota(jnp.int32, (2 * TOK, BLK), 1)
    row = lax.broadcasted_iota(jnp.int32, (2 * TOK, BLK), 0)
    for b in range(SPLIT):
        at = slice(b * BLK, (b + 1) * BLK)
        total = parts_ref[0, :, at].astype(F32)
        for q in range(1, 16):
            total = total + parts_ref[q, :, at].astype(F32)
        if b == NORM:
            norm = total + pltpu.roll(total, 96, 1)
            high = norm.astype(BF16).astype(F32)
            norm = jnp.where(lane < 32, high, pltpu.roll(norm - high, 32, 1))
            total = jnp.where(row < TOK, norm, 0.0)
        total = total.astype(BF16)
        for q in range(16):
            send_ref[q, :, at] = total


def gather_kernel(at_ref, ids_ref, other_ids_ref, sums_ref, base_ref, proj_ref):
    for b in range(GRAM):
        upper = b >= SPLIT
        at = (b - SPLIT * upper) * BLK
        block = sums_ref[:, :, at : at + BLK].astype(F32)
        proj_ref[:, b * BLK : (b + 1) * BLK] = block[:, TOK * upper : TOK * upper + TOK].reshape(
            R, BLK
        )
    for n, pick in enumerate(picks_of(at_ref, ids_ref, other_ids_ref)):
        rows = slice(n * TOK, (n + 1) * TOK)
        here = pl.ds(pl.multiple_of(pick * TOK, TOK), TOK)
        base_ref[rows, :] = proj_ref[here, :]
        norm = proj_ref[here, NORM * BLK : (NORM + 1) * BLK]
        norm = norm + pltpu.roll(norm, 96, 1)
        m = n % 16 // 4
        base_ref[rows, NORM * BLK : (NORM + 1) * BLK] = (
            pltpu.roll(norm, BLK - m * NS, 1) if m else norm
        )


def chain_kernel(
    width, at_ref, parts_ref, base_ref, sums_ref, other_ref,
    latent_ref, scalar_ref, oo_ref, oi_ref, oo_rows_ref, oi_rows_ref,
):
    rows = 2 * R
    first_core = at_ref[0] == 0
    for b in range(0, GRAMS, 4):
        at = (GRAM - SPLIT + b) * BLK
        mine = sums_ref[:, :, at : at + 4 * BLK].astype(F32)[:, TOK:]
        mine = mine.reshape(R, 4 * BLK).astype(BF16)
        at = slice(b * BLK, (b + 4) * BLK)
        theirs = other_ref[:, at]
        oo_ref[:, at] = jnp.where(first_core, mine, theirs)
        second = jnp.where(first_core, theirs, mine)
        if b < OI:
            oi_ref[:, at] = second
        else:
            oo_ref[:, (b + 4) * BLK : (b + 8) * BLK] = second

    def spread(at):
        return base_ref[:, at * BLK : (at + 1) * BLK]

    def square(t, s, count=1):
        at = (gram_at(t) + s - t) * BLK
        return oo_ref[:, at : at + count * BLK]

    def cross(t, s, count=1):
        at = (cross_at(t) + s - t - 1) * BLK
        return oi_ref[:, at : at + count * BLK]

    for s in range(1, NS):
        for t in range(s):
            at = slice((proj_at(s) + t) * R, (proj_at(s) + t + 1) * R)
            oo_rows_ref[at, :] = square(t, s)
            oi_rows_ref[at, :] = cross(t, s)

    def above(ref, s):
        return ref[proj_at(s) * R : (proj_at(s) + s) * R, :]

    norms = spread(NORM)
    starts = []
    for s in range(NS):
        pieces = []
        for x in range(2):
            for g in range(8):
                at = START + g * 2 * R
                pieces.append(parts_ref[x * NS + s, :, at : at + 2 * R])
        starts.append(jnp.concatenate(pieces, 0))
    start_out = [start[:, R:].astype(F32) for start in starts]
    run_in = [start[:, :R].astype(F32) for start in starts]
    run_out = list(start_out)
    inners, inverses, actives, crossed = [], [], [], []
    grown_norm = jnp.zeros((rows, R), F32)
    for s in range(NS):
        norm = norms[:, s : s + 1]
        entry_out = []
        inner = run_in[s]
        if s > 0:
            inner = inner + spread(inner_at(s))
            total = jnp.zeros((rows, R), F32)
            for t in range(s):
                base = spread(proj_at(s) + t)
                entry_out.append(base + run_out[t])
                total = total + actives[t] * base
            norm = norm + jnp.sum(2.0 * total + grown_norm, -1, keepdims=True)
        inverse = lax.rsqrt(jnp.maximum(norm, 0.0) * (1.0 / width) + EPS)
        inner = inner * inverse
        active = (inner * jax.nn.sigmoid(inner)).astype(BF16)
        latent_ref[:, s * R : (s + 1) * R] = active
        inners.append(inner)
        inverses.append(inverse)
        actives.append(active.astype(F32))
        crossed.append(entry_out)
        grown = dot(active, square(s, s, NS - s))
        if s > 0:
            grown = jnp.concatenate([dot_t(active, above(oo_rows_ref, s)), grown], 1)
        before = run_out[s]
        for t in range(NS):
            run_out[t] = run_out[t] + grown[:, t * R : (t + 1) * R]
        grown_norm = grown_norm + actives[s] * (before + run_out[s])
        if s < NS - 1:
            grown = dot(active, cross(s, s + 1, NS - 1 - s))
            for t in range(s + 1, NS):
                run_in[t] = run_in[t] + grown[:, (t - s - 1) * R : (t - s) * R]
    grads = [run_out[t] + spread(proj_at(NS - 1) + t) for t in range(NS)]
    lane = lax.broadcasted_iota(jnp.int32, (rows, BLK), 1)
    scalars = jnp.zeros((rows, BLK), F32)
    for s in range(NS - 1, -1, -1):
        inner = inners[s]
        sigm = jax.nn.sigmoid(inner)
        d_inner = (grads[s] * sigm * (1.0 + inner * (1.0 - sigm))).astype(BF16)
        latent_ref[:, (NS + s) * R : (NS + s + 1) * R] = d_inner
        inverse = inverses[s]
        total = jnp.sum(d_inner.astype(F32) * inner, -1, keepdims=True)
        scale = inverse * inverse * total * (1.0 / width)
        if s > 0:
            back = dot_t(d_inner, above(oi_rows_ref, s))
        for t in range(s):
            grads[t] = (
                grads[t] + inverse * back[:, t * R : (t + 1) * R] - scale * crossed[s][t]
            )
        scalars = jnp.where(lane == s, inverse, scalars)
        scalars = jnp.where(lane == NS + s, scale, scalars)
    scalar_ref[...] = scalars


def grads_kernel(
    own, at_ref, ids_ref, other_ids_ref, got_ref, out_w_ref, in_w_ref, latent_ref, scalar_ref,
    result_ref, entry_ref, step_ref,
):
    cols = step_ref.shape[1]
    scalars = scalar_ref[...]
    inverses = [scalars[:, s : s + 1] for s in range(NS)]
    scales = [scalars[:, NS + s : NS + s + 1] for s in range(NS)]
    places = [
        pl.multiple_of(pick * TOK, TOK) for pick in picks_of(at_ref, ids_ref, other_ids_ref)
    ]

    def active(s):
        return latent_ref[:, s * R : (s + 1) * R]

    def d_inner(s):
        return latent_ref[:, (NS + s) * R : (NS + s + 1) * R]

    side = at_ref[0] if own else 1 - at_ref[0]
    here = pl.ds(pl.multiple_of(side * cols, cols), cols)
    at = pl.multiple_of(side * HALF, HALF)

    def put(s, kind, value):
        result_ref[:, s, :, kind * R : (kind + 1) * R] = value.reshape(8, 32, R).astype(
            result_ref.dtype
        )

    entry = first_rows(got_ref, at, cols)
    for s in range(NS):
        if s > 0:
            step_ref[...] = stores(got_ref, s, at, cols)
            entry = entry + jnp.concatenate([step_ref[pl.ds(place, TOK), :] for place in places], 0)
        entry_ref[s] = entry
        put(s, 0, dot_rows((entry * inverses[s]).astype(BF16), d_inner(s)))
        entry = entry + dot(active(s), out_w_ref[s, :, here])
    grad = entry
    for s in range(NS - 1, -1, -1):
        put(s, 1, dot_rows(grad.astype(BF16), active(s)))
        if s > 0:
            back = dot_t(d_inner(s), in_w_ref[s, here, :])
            grad = grad + inverses[s] * back - scales[s] * entry_ref[s]


def add_kernel(keep_ref, swapped_ref, total_ref):
    for i in range(8):
        total_ref[i] = (keep_ref[i] + swapped_ref[i].astype(F32)).astype(BF16)


def final_kernel(parts_ref, gain_ref, in_ref, out_ref):
    total = parts_ref[0].astype(F32)
    for i in range(1, 8):
        total = total + parts_ref[i].astype(F32)
    gain = gain_ref[...].T
    for j in range(8):
        scale = gain[(j % 4) * 32 : (j % 4) * 32 + 32, j // 4 : j // 4 + 1]
        in_ref[j * 32 : j * 32 + 32, :] = total[j, :, :R] * scale
    out = total[:, :, R:].reshape(2 * BLK, R)
    for i in range(2):
        out_ref[:, i * BLK : (i + 1) * BLK] = out[i * BLK : (i + 1) * BLK].T


def body(first_input, example_ids, out_store, in_store, norm_gain, adapter_in, adapter_out):
    width = first_input.shape[2]
    cols = width // 16
    half = cols // 2
    wide = width // 2
    core = lax.axis_index("c")
    xl = lax.axis_index("xl")
    z = lax.axis_index("z")
    section = lax.axis_index(SECTION)
    quarter = xl * 2 + core
    at = jnp.stack([core, section, xl, quarter]).astype(jnp.int32)
    w_in = adapter_in[0]
    w_out = adapter_out[0]

    ids = example_ids[0]
    other_ids = lax.ppermute(ids, "xl", SWAP)
    send = pl.pallas_call(
        pack_kernel,
        grid_spec=pltpu.PrefetchScalarGridSpec(
            num_scalar_prefetch=1,
            grid=(2,),
            in_specs=[
                pl.BlockSpec((64, wide), lambda i, at: (0, i)),
                pl.BlockSpec((64, wide), lambda i, at: (0, i)),
                pl.BlockSpec((32, wide), lambda i, at: (at[3], i)),
                pl.BlockSpec(
                    (1, 4, 1, 8, 32, R), lambda i, at: (i, at[3] % 2, at[3] // 2, 0, 0, 0)
                ),
                pl.BlockSpec((1, 4, 1, 2, BLK), lambda i, at: (i, at[3] % 2, at[3] // 2, 0, 0)),
                pl.BlockSpec((2, 32, wide), lambda i, at: (at[1] // (NS - 1), 0, i)),
            ],
            out_specs=pl.BlockSpec((8, 32, SENT), lambda i, at: (i, 0, 0)),
            scratch_shapes=[pltpu.VMEM((4 * BLK, 4 * BLK), BF16)],
        ),
        out_shape=jax.ShapeDtypeStruct((16, 32, SENT), BF16),
        compiler_params=LARGE,
        name="pack",
    )(
        at,
        in_store.reshape(64, width),
        out_store.reshape(64, width),
        w_out,
        w_in.reshape(2, 8, 2, 8, 32, R),
        norm_gain.reshape(2, 8, 2, 2, BLK),
        first_input,
    )
    got = lax.all_to_all(send, PLANE, 0, 0, tiled=True)
    other = lax.ppermute(got[:, :, W_LANE:], "c", SWAP)
    start = pl.pallas_call(
        start_kernel,
        out_shape=jax.ShapeDtypeStruct((R, 2 * R), BF16),
        in_specs=[VMEM, VMEM, VMEM, VMEM, pl.BlockSpec(memory_space=pl.ANY)],
        out_specs=VMEM,
        compiler_params=PARAMS,
        cost_estimate=pl.CostEstimate(flops=600000000, bytes_accessed=7000000, transcendentals=0),
        name="start",
    )(first_input, w_out, w_in, norm_gain, got)
    parts, out_w, in_w = pl.pallas_call(
        project_kernel,
        out_shape=(
            jax.ShapeDtypeStruct((16, 2 * TOK, WIDE), BF16),
            jax.ShapeDtypeStruct((NS, R, cols), BF16),
            jax.ShapeDtypeStruct((NS, cols, R), BF16),
        ),
        in_specs=[SMEM, VMEM, VMEM, VMEM],
        out_specs=(VMEM, VMEM, VMEM),
        scratch_shapes=[pltpu.VMEM((R, 2 * SPLIT * BLK), F32)],
        compiler_params=PARAMS,
        cost_estimate=pl.CostEstimate(flops=2000000000, bytes_accessed=9000000, transcendentals=0),
        name="project",
    )(at, got, other, start)
    parts = pl.pallas_call(
        functools.partial(norm_kernel, cols),
        out_shape=jax.ShapeDtypeStruct((16, 2 * TOK, WIDE), BF16),
        in_specs=[SMEM, SMEM, SMEM, VMEM, pl.BlockSpec(memory_space=pl.ANY)],
        out_specs=pl.BlockSpec(memory_space=pl.ANY),
        scratch_shapes=[pltpu.VMEM((16, 2 * TOK, BLK), BF16), pltpu.SemaphoreType.DMA],
        input_output_aliases={4: 0},
        compiler_params=PARAMS,
        name="norms",
    )(at, ids, other_ids, got, parts)
    parts = lax.all_to_all(parts, PLANE, 0, 0, tiled=True)
    sums = pl.pallas_call(
        sum_kernel,
        out_shape=jax.ShapeDtypeStruct((16, 2 * TOK, SPLIT * BLK), BF16),
        in_specs=[VMEM],
        out_specs=VMEM,
        compiler_params=PARAMS,
        name="sums",
    )(parts)
    sums = lax.all_to_all(sums, PLANE, 0, 0, tiled=True)
    gram = sums[:, TOK:, (GRAM - SPLIT) * BLK : (GRAM - SPLIT + GRAMS) * BLK]
    other = lax.ppermute(gram.reshape(R, GRAMS * BLK), "c", SWAP)
    base = pl.pallas_call(
        gather_kernel,
        out_shape=jax.ShapeDtypeStruct((2 * R, GRAM * BLK), F32),
        in_specs=[SMEM, SMEM, SMEM, VMEM],
        out_specs=VMEM,
        scratch_shapes=[pltpu.VMEM((R, GRAM * BLK), F32)],
        compiler_params=PARAMS,
        cost_estimate=pl.CostEstimate(flops=0, bytes_accessed=7000000, transcendentals=0),
        name="gather",
    )(at, ids, other_ids, sums)
    latent, scalars = pl.pallas_call(
        functools.partial(chain_kernel, width),
        out_shape=(
            jax.ShapeDtypeStruct((2 * R, 16 * BLK), BF16),
            jax.ShapeDtypeStruct((2 * R, BLK), F32),
        ),
        in_specs=[SMEM, VMEM, VMEM, VMEM, VMEM],
        out_specs=(VMEM, VMEM),
        scratch_shapes=[
            pltpu.VMEM((R, OO * BLK), BF16),
            pltpu.VMEM((R, OI * BLK), BF16),
            pltpu.VMEM((OI * R, R), BF16),
            pltpu.VMEM((OI * R, R), BF16),
        ],
        compiler_params=PARAMS,
        name="chain",
    )(at, parts, base, sums, other)

    def grads(own):
        return pl.pallas_call(
            functools.partial(grads_kernel, own),
            out_shape=jax.ShapeDtypeStruct((8, NS, 32, 2 * R), F32 if own else BF16),
            in_specs=[SMEM, SMEM, SMEM] + [VMEM] * 5,
            out_specs=VMEM,
            scratch_shapes=[pltpu.VMEM((NS, 2 * R, half), F32), pltpu.VMEM((R, half), F32)],
            compiler_params=PARAMS,
            cost_estimate=pl.CostEstimate(
                flops=600000000, bytes_accessed=9000000, transcendentals=0
            ),
            name="grads_own" if own else "grads_other",
        )(at, ids, other_ids, got, out_w, in_w, latent, scalars)

    swapped = lax.ppermute(grads(False), "c", SWAP)
    keep = grads(True)
    total = pl.pallas_call(
        add_kernel,
        out_shape=jax.ShapeDtypeStruct((8, NS, 32, 2 * R), BF16),
        in_specs=[VMEM, VMEM],
        out_specs=VMEM,
        compiler_params=PARAMS,
        name="add",
    )(keep, swapped).reshape(64, 32, 2 * R)
    block = (xl * NS + z) * 2 + core
    gain = lax.dynamic_slice_in_dim(norm_gain[0], block * half, half, 0)
    total, gain = lax.optimization_barrier((total, gain))
    total = lax.all_to_all(total, ("z",) + SECTION, 0, 0, tiled=True)
    grad_in, grad_out = pl.pallas_call(
        final_kernel,
        out_shape=(
            jax.ShapeDtypeStruct((half, R), F32),
            jax.ShapeDtypeStruct((R, half), F32),
        ),
        in_specs=[VMEM, VMEM],
        out_specs=(VMEM, VMEM),
        compiler_params=PARAMS,
        name="final",
    )(total.reshape(8, 8, 32, 2 * R), gain.reshape(2, BLK))
    return (grad_in[None], grad_out[None])


def solution(mesh):
    fine = Mesh(mesh.devices.reshape(2, 8, 2, 4, 2), ("xl", "z", "c", "y", "xh"))
    dp = ("xl", "z", "c")
    placed = (
        P(None, dp, None),
        P(dp, None, None),
        P(SECTION, dp, None, None),
        P(SECTION, dp, None, None),
        P(SECTION, None),
        P(SECTION, None, None),
        P(SECTION, None, None),
    )
    return jax.shard_map(
        body,
        mesh=fine,
        in_specs=placed,
        out_specs=(P(SECTION, dp, None), P(SECTION, None, dp)),
        check_vma=False,
    )
```

```python
import functools

import jax
import jax.numpy as jnp
from jax import lax
from jax.experimental import pallas as pl
from jax.experimental.pallas import tpu as pltpu
from jax.sharding import Mesh, PartitionSpec as P

F32 = jnp.float32
BF16 = jnp.bfloat16
EPS = 1e-05
PLANE = ("xl", "y", "xh")
SECTION = ("y", "xh")
SWAP = [(0, 1), (1, 0)]
NS = 8
R = 128
TOK = 8
MIC = 4
BLK = 128
HALF = 1024
W_LANE = 2 * HALF
SENT = 3072
PROJ = 29
NORM = 34
GRAM = 37
GRAMS = 32
SPLIT = 35
START = SPLIT * BLK
WIDE = START + 16 * BLK
OO = 36
OI = 28
LARGE = pltpu.CompilerParams(vmem_limit_bytes=28 * 1024 * 1024)
PARAMS = pltpu.CompilerParams(vmem_limit_bytes=16 * 1024 * 1024)
VMEM = pl.BlockSpec(memory_space=pltpu.VMEM)
SMEM = pl.BlockSpec(memory_space=pltpu.SMEM)


def gram_at(t):
    return sum(NS - i for i in range(t))


def cross_at(t):
    return sum(NS - 1 - i for i in range(t))


def proj_at(s):
    return s * (s - 1) // 2


def inner_at(s):
    return PROJ + s - 1 + (PROJ + s - 1 >= NORM)


def dot_t(a, b):
    return lax.dot_general(a, b, (((1,), (1,)), ((), ())), preferred_element_type=F32)


def dot_rows(a, b):
    return lax.dot_general(a, b, (((0,), (0,)), ((), ())), preferred_element_type=F32)


def dot(a, b):
    return jnp.dot(a, b, preferred_element_type=F32)


def split(x):
    high = x.astype(BF16)
    return high, (x - high.astype(F32)).astype(BF16)


def pack_kernel(
    at_ref, in_ref, out_ref, w_out_ref, w_in_ref, gain_ref, first_ref,
    send_ref, turn_ref,
):
    section = at_ref[1]

    @pl.when(pl.program_id(0) == 0)
    def _():
        shape = (4 * BLK, 4 * BLK)
        row = lax.broadcasted_iota(jnp.int32, shape, 0)
        col = lax.broadcasted_iota(jnp.int32, shape, 1)
        same = (row // BLK == col % BLK // 32) & (row % BLK // 32 == col // BLK)
        same = same & (row % 32 == col % 32)
        turn_ref[...] = jnp.where(same, 1.0, 0.0).astype(BF16)

    gain = gain_ref[...].reshape(8, BLK).T
    for s in range(NS):
        for j in range(4):
            column = 2 * j + s // 4
            scale = gain[(s % 4) * 32 : (s % 4) * 32 + 32, column : column + 1]
            to = W_LANE + 512 + j * BLK
            send_ref[s, :, to : to + BLK] = (w_in_ref[0, j, 0, s].astype(F32) * scale).astype(BF16)

    pieces, places = [], []
    for c in range(2):
        for zq in range(2):
            to = c * 256 + zq * BLK
            for h in range(2):
                lanes = [((4 * zq + j) * 4 + c * 2 + h) * BLK for j in range(4)]
                for ref, row, at, other in (
                    (in_ref, 0, c * HALF + zq * BLK, 0),
                    (in_ref, 32, c * HALF + 256 + zq * BLK, 0),
                    (out_ref, 0, c * HALF + 512 + zq * BLK, NS - 1),
                    (out_ref, 32, c * HALF + 768 + zq * BLK, NS - 1),
                    (w_out_ref, 0, W_LANE + to, None),
                ):
                    piece = jnp.concatenate(
                        [ref[row : row + 32, lane : lane + BLK] for lane in lanes], 1
                    )
                    if other is not None:
                        first = jnp.concatenate(
                            [first_ref[row // 32, :, lane : lane + BLK] for lane in lanes], 1
                        )
                        piece = jnp.where(section == other, first, piece)
                    pieces.append(piece)
                    places.append((4 * h, at))
    turned = dot(jnp.concatenate(pieces, 0), turn_ref[...]).astype(BF16)
    for n, (first, at) in enumerate(places):
        for i in range(4):
            send_ref[first + i, :, at : at + BLK] = turned[
                32 * n : 32 * n + 32, i * BLK : (i + 1) * BLK
            ]


def start_kernel(first_ref, w_out_ref, w_in_ref, gain_ref, after_ref, start_ref):
    del after_ref
    flat = first_ref[...].reshape(R, first_ref.shape[2])
    scaled = (flat.astype(F32) * gain_ref[...]).astype(BF16)
    start_ref[:, :R] = dot(scaled, w_in_ref[...]).astype(BF16)
    start_ref[:, R:] = dot_t(flat, w_out_ref[...]).astype(BF16)


def stores(got_ref, s, at, cols):
    pieces = []
    for x in range(2):
        for i in range(2):
            a, b = at + i * 256, at + 512 + i * 256
            pieces.append(
                got_ref[x * NS + s, :, pl.ds(a, cols)].astype(F32)
                - got_ref[x * NS + s - 1, :, pl.ds(b, cols)].astype(F32)
            )
    return jnp.concatenate(pieces, 0)


def first_rows(got_ref, at, cols):
    pieces = []
    for x in range(2):
        for m in range(MIC):
            q = x * NS + (0 if m < 2 else NS - 1)
            lane = at + m // 2 * 512 + m % 2 * 256
            pieces.append(got_ref[q, :, pl.ds(lane, cols)])
    return jnp.concatenate(pieces, 0).astype(F32)


def picks_of(at_ref, ids_ref, other_ids_ref):
    picks = []
    for x in range(2):
        here = at_ref[2] == x
        for m in range(MIC):
            for j in range(4):
                picks.append(x * NS + jnp.where(here, ids_ref[m, j], other_ids_ref[m, j]))
    return picks


def running_sums(got_ref, cols):
    running = None
    for s in range(1, NS):
        step = jnp.concatenate(
            [stores(got_ref, s, 0, cols // 2), stores(got_ref, s, HALF, cols // 2)], 1
        )
        running = step if running is None else running + step
        yield s, running


def project_kernel(
    at_ref, got_ref, other_ref, start_ref, send_ref, out_w_ref, in_w_ref, wide_ref
):
    cols = in_w_ref.shape[1]
    first_core = at_ref[0] == 0
    for s in range(NS):
        for x in range(2):
            mine = got_ref[x * NS + s, :, W_LANE:SENT]
            theirs = other_ref[x * NS + s]
            for c in range(2):
                part = jnp.where(first_core == (c == 0), mine, theirs)
                k = 2 * x + c
                out_w_ref[s, 32 * k : 32 * k + 32, :] = part[:, :cols]
                for g in range(4):
                    row = k * BLK + g * 32
                    lane = cols + g * BLK
                    in_w_ref[s, row : row + 32, :] = part[:, lane : lane + BLK]
    for s, running in running_sums(got_ref, cols):
        rounded = running.astype(BF16)
        count = s if s < NS - 1 else NS
        at = proj_at(s) * BLK
        wide_ref[:, at : at + count * BLK] = dot_t(
            rounded, out_w_ref[0:count].reshape(count * R, cols)
        )
        at = inner_at(s) * BLK
        wide_ref[:, at : at + BLK] = dot(rounded, in_w_ref[s])
    for b in (NORM, GRAM + GRAMS):
        wide_ref[:, b * BLK : (b + 1) * BLK] = jnp.zeros((R, BLK), F32)

    square = [(t, s) for t in range(NS) for s in range(t, NS)]

    @pl.when(first_core)
    def _():
        for t in range(5):
            at = (GRAM + gram_at(t)) * BLK
            wide_ref[:, at : at + (NS - t) * BLK] = dot_t(
                out_w_ref[t], out_w_ref[t:NS].reshape((NS - t) * R, cols)
            )
        for i in range(gram_at(5), GRAMS):
            t, s = square[i]
            at = (GRAM + i) * BLK
            wide_ref[:, at : at + BLK] = dot_t(out_w_ref[t], out_w_ref[s])

    @pl.when(jnp.logical_not(first_core))
    def _():
        for t in range(NS - 1):
            for s in range(t + 1, NS):
                at = (GRAM + cross_at(t) + s - t - 1) * BLK
                wide_ref[:, at : at + BLK] = dot(out_w_ref[t], in_w_ref[s])
        for i in range(GRAMS, OO):
            t, s = square[i]
            at = (GRAM + OI + i - GRAMS) * BLK
            wide_ref[:, at : at + BLK] = dot_t(out_w_ref[t], out_w_ref[s])

    for b in range(SPLIT):
        pair = [
            wide_ref[:, at * BLK : (at + 1) * BLK].reshape(16, TOK, BLK) for at in (b, SPLIT + b)
        ]
        send_ref[:, :, b * BLK : (b + 1) * BLK] = jnp.concatenate(pair, 1).astype(BF16)
    for g in range(8):
        at = START + g * 2 * R
        for q in range(16):
            send_ref[q, :, at : at + 2 * R] = start_ref[g * 16 : (g + 1) * 16, :]


def norm_kernel(
    cols, at_ref, ids_ref, other_ids_ref, got_ref, before_ref, send_ref, block_ref, sem
):
    del before_ref
    picks = picks_of(at_ref, ids_ref, other_ids_ref)
    placed = [[] for _ in range(MIC)]
    first = jnp.concatenate(
        [first_rows(got_ref, 0, cols // 2), first_rows(got_ref, HALF, cols // 2)], 1
    )
    for x in range(2):
        rows = first[x * R : (x + 1) * R]
        for e in range(NS):
            for m in range(MIC):
                total = jnp.zeros((TOK, cols), F32)
                for j in range(4):
                    n = 4 * m + j
                    total = jnp.where(
                        picks[16 * x + n] == x * NS + e, rows[n * TOK : (n + 1) * TOK], total
                    )
                placed[m].append(total)
    placed = [jnp.concatenate(blocks, 0) for blocks in placed]
    lane = lax.broadcasted_iota(jnp.int32, (R, BLK), 1)
    norms = jnp.zeros((R, BLK), F32)
    for m in range(MIC):
        part = jnp.sum(placed[m] * placed[m], -1, keepdims=True)
        norms = jnp.where(lane == m * NS, part, norms)
    for s, running in running_sums(got_ref, cols):
        for m in range(MIC):
            entry = running + placed[m]
            part = jnp.sum(entry * entry, -1, keepdims=True)
            norms = jnp.where(lane == m * NS + s, part, norms)
    high = norms.astype(BF16).astype(F32)
    norms = jnp.where(lane < 32, high, pltpu.roll(norms - high, 32, 1)).reshape(16, TOK, BLK)
    block_ref[...] = jnp.concatenate([norms, jnp.zeros_like(norms)], 1).astype(BF16)
    copy = pltpu.make_async_copy(
        block_ref, send_ref.at[:, :, NORM * BLK : (NORM + 1) * BLK], sem
    )
    copy.start()
    copy.wait()


def sum_kernel(parts_ref, send_ref):
    lane = lax.broadcasted_iota(jnp.int32, (2 * TOK, BLK), 1)
    row = lax.broadcasted_iota(jnp.int32, (2 * TOK, BLK), 0)
    for b in range(SPLIT):
        at = slice(b * BLK, (b + 1) * BLK)
        total = parts_ref[0, :, at].astype(F32)
        for q in range(1, 16):
            total = total + parts_ref[q, :, at].astype(F32)
        if b == NORM:
            norm = total + pltpu.roll(total, 96, 1)
            high = norm.astype(BF16).astype(F32)
            norm = jnp.where(lane < 32, high, pltpu.roll(norm - high, 32, 1))
            total = jnp.where(row < TOK, norm, 0.0)
        total = total.astype(BF16)
        for q in range(16):
            send_ref[q, :, at] = total


def gather_kernel(at_ref, ids_ref, other_ids_ref, sums_ref, base_ref, proj_ref):
    for b in range(GRAM):
        upper = b >= SPLIT
        at = (b - SPLIT * upper) * BLK
        block = sums_ref[:, :, at : at + BLK].astype(F32)
        proj_ref[:, b * BLK : (b + 1) * BLK] = block[:, TOK * upper : TOK * upper + TOK].reshape(
            R, BLK
        )
    for n, pick in enumerate(picks_of(at_ref, ids_ref, other_ids_ref)):
        rows = slice(n * TOK, (n + 1) * TOK)
        here = pl.ds(pl.multiple_of(pick * TOK, TOK), TOK)
        base_ref[rows, :] = proj_ref[here, :]
        norm = proj_ref[here, NORM * BLK : (NORM + 1) * BLK]
        norm = norm + pltpu.roll(norm, 96, 1)
        m = n % 16 // 4
        base_ref[rows, NORM * BLK : (NORM + 1) * BLK] = (
            pltpu.roll(norm, BLK - m * NS, 1) if m else norm
        )


def chain_kernel(
    width, at_ref, parts_ref, base_ref, sums_ref, other_ref,
    latent_ref, scalar_ref, oo_ref, oi_ref, oo_rows_ref, oi_rows_ref,
):
    rows = 2 * R
    first_core = at_ref[0] == 0
    for b in range(0, GRAMS, 4):
        at = (GRAM - SPLIT + b) * BLK
        mine = sums_ref[:, :, at : at + 4 * BLK].astype(F32)[:, TOK:]
        mine = mine.reshape(R, 4 * BLK).astype(BF16)
        at = slice(b * BLK, (b + 4) * BLK)
        theirs = other_ref[:, at]
        oo_ref[:, at] = jnp.where(first_core, mine, theirs)
        second = jnp.where(first_core, theirs, mine)
        if b < OI:
            oi_ref[:, at] = second
        else:
            oo_ref[:, (b + 4) * BLK : (b + 8) * BLK] = second

    def spread(at):
        return base_ref[:, at * BLK : (at + 1) * BLK]

    def square(t, s, count=1):
        at = (gram_at(t) + s - t) * BLK
        return oo_ref[:, at : at + count * BLK]

    def cross(t, s, count=1):
        at = (cross_at(t) + s - t - 1) * BLK
        return oi_ref[:, at : at + count * BLK]

    for s in range(1, NS):
        for t in range(s):
            at = slice((proj_at(s) + t) * R, (proj_at(s) + t + 1) * R)
            oo_rows_ref[at, :] = square(t, s)
            oi_rows_ref[at, :] = cross(t, s)

    def above(ref, s):
        return ref[proj_at(s) * R : (proj_at(s) + s) * R, :]

    norms = spread(NORM)
    starts = []
    for s in range(NS):
        pieces = []
        for x in range(2):
            for g in range(8):
                at = START + g * 2 * R
                pieces.append(parts_ref[x * NS + s, :, at : at + 2 * R])
        starts.append(jnp.concatenate(pieces, 0))
    start_out = [start[:, R:].astype(F32) for start in starts]
    run_in = [start[:, :R].astype(F32) for start in starts]
    run_out = list(start_out)
    inners, inverses, actives, crossed = [], [], [], []
    grown_norm = jnp.zeros((rows, R), F32)
    for s in range(NS):
        norm = norms[:, s : s + 1]
        entry_out = []
        inner = run_in[s]
        if s > 0:
            inner = inner + spread(inner_at(s))
            total = jnp.zeros((rows, R), F32)
            for t in range(s):
                base = spread(proj_at(s) + t)
                entry_out.append(base + run_out[t])
                total = total + actives[t] * base
            norm = norm + jnp.sum(2.0 * total + grown_norm, -1, keepdims=True)
        inverse = lax.rsqrt(jnp.maximum(norm, 0.0) * (1.0 / width) + EPS)
        inner = inner * inverse
        active = (inner * jax.nn.sigmoid(inner)).astype(BF16)
        latent_ref[:, s * R : (s + 1) * R] = active
        inners.append(inner)
        inverses.append(inverse)
        actives.append(active.astype(F32))
        crossed.append(entry_out)
        grown = dot(active, square(s, s, NS - s))
        if s > 0:
            grown = jnp.concatenate([dot_t(active, above(oo_rows_ref, s)), grown], 1)
        before = run_out[s]
        for t in range(NS):
            run_out[t] = run_out[t] + grown[:, t * R : (t + 1) * R]
        grown_norm = grown_norm + actives[s] * (before + run_out[s])
        if s < NS - 1:
            grown = dot(active, cross(s, s + 1, NS - 1 - s))
            for t in range(s + 1, NS):
                run_in[t] = run_in[t] + grown[:, (t - s - 1) * R : (t - s) * R]
    grads = [run_out[t] + spread(proj_at(NS - 1) + t) for t in range(NS)]
    lane = lax.broadcasted_iota(jnp.int32, (rows, BLK), 1)
    scalars = jnp.zeros((rows, BLK), F32)
    for s in range(NS - 1, -1, -1):
        inner = inners[s]
        sigm = jax.nn.sigmoid(inner)
        d_inner = (grads[s] * sigm * (1.0 + inner * (1.0 - sigm))).astype(BF16)
        latent_ref[:, (NS + s) * R : (NS + s + 1) * R] = d_inner
        inverse = inverses[s]
        total = jnp.sum(d_inner.astype(F32) * inner, -1, keepdims=True)
        scale = inverse * inverse * total * (1.0 / width)
        if s > 0:
            back = dot_t(d_inner, above(oi_rows_ref, s))
        for t in range(s):
            grads[t] = (
                grads[t] + inverse * back[:, t * R : (t + 1) * R] - scale * crossed[s][t]
            )
        scalars = jnp.where(lane == s, inverse, scalars)
        scalars = jnp.where(lane == NS + s, scale, scalars)
    scalar_ref[...] = scalars


def grads_kernel(
    own, at_ref, ids_ref, other_ids_ref, got_ref, out_w_ref, in_w_ref, latent_ref, scalar_ref,
    result_ref, entry_ref, step_ref,
):
    cols = step_ref.shape[1]
    scalars = scalar_ref[...]
    inverses = [scalars[:, s : s + 1] for s in range(NS)]
    scales = [scalars[:, NS + s : NS + s + 1] for s in range(NS)]
    places = [
        pl.multiple_of(pick * TOK, TOK) for pick in picks_of(at_ref, ids_ref, other_ids_ref)
    ]

    def active(s):
        return latent_ref[:, s * R : (s + 1) * R]

    def d_inner(s):
        return latent_ref[:, (NS + s) * R : (NS + s + 1) * R]

    side = at_ref[0] if own else 1 - at_ref[0]
    here = pl.ds(pl.multiple_of(side * cols, cols), cols)
    at = pl.multiple_of(side * HALF, HALF)

    def put(s, kind, value):
        result_ref[:, s, :, kind * R : (kind + 1) * R] = value.reshape(8, 32, R).astype(
            result_ref.dtype
        )

    entry = first_rows(got_ref, at, cols)
    for s in range(NS):
        if s > 0:
            step_ref[...] = stores(got_ref, s, at, cols)
            entry = entry + jnp.concatenate([step_ref[pl.ds(place, TOK), :] for place in places], 0)
        entry_ref[s] = entry
        put(s, 0, dot_rows((entry * inverses[s]).astype(BF16), d_inner(s)))
        entry = entry + dot(active(s), out_w_ref[s, :, here])
    grad = entry
    for s in range(NS - 1, -1, -1):
        put(s, 1, dot_rows(grad.astype(BF16), active(s)))
        if s > 0:
            back = dot_t(d_inner(s), in_w_ref[s, here, :])
            grad = grad + inverses[s] * back - scales[s] * entry_ref[s]


def add_kernel(keep_ref, swapped_ref, total_ref):
    for i in range(8):
        total_ref[i] = (keep_ref[i] + swapped_ref[i].astype(F32)).astype(BF16)


def final_kernel(parts_ref, gain_ref, in_ref, out_ref):
    total = parts_ref[0].astype(F32)
    for i in range(1, 8):
        total = total + parts_ref[i].astype(F32)
    gain = gain_ref[...].T
    for j in range(8):
        scale = gain[(j % 4) * 32 : (j % 4) * 32 + 32, j // 4 : j // 4 + 1]
        in_ref[j * 32 : j * 32 + 32, :] = total[j, :, :R] * scale
    out = total[:, :, R:].reshape(2 * BLK, R)
    for i in range(2):
        out_ref[:, i * BLK : (i + 1) * BLK] = out[i * BLK : (i + 1) * BLK].T


def body(first_input, example_ids, out_store, in_store, norm_gain, adapter_in, adapter_out):
    width = first_input.shape[2]
    cols = width // 16
    half = cols // 2
    wide = width // 2
    core = lax.axis_index("c")
    xl = lax.axis_index("xl")
    z = lax.axis_index("z")
    section = lax.axis_index(SECTION)
    quarter = xl * 2 + core
    at = jnp.stack([core, section, xl, quarter]).astype(jnp.int32)
    w_in = adapter_in[0]
    w_out = adapter_out[0]

    ids = example_ids[0]
    other_ids = lax.ppermute(ids, "xl", SWAP)
    send = pl.pallas_call(
        pack_kernel,
        grid_spec=pltpu.PrefetchScalarGridSpec(
            num_scalar_prefetch=1,
            grid=(2,),
            in_specs=[
                pl.BlockSpec((64, wide), lambda i, at: (0, i)),
                pl.BlockSpec((64, wide), lambda i, at: (0, i)),
                pl.BlockSpec((32, wide), lambda i, at: (at[3], i)),
                pl.BlockSpec(
                    (1, 4, 1, 8, 32, R), lambda i, at: (i, at[3] % 2, at[3] // 2, 0, 0, 0)
                ),
                pl.BlockSpec((1, 4, 1, 2, BLK), lambda i, at: (i, at[3] % 2, at[3] // 2, 0, 0)),
                pl.BlockSpec((2, 32, wide), lambda i, at: (at[1] // (NS - 1), 0, i)),
            ],
            out_specs=pl.BlockSpec((8, 32, SENT), lambda i, at: (i, 0, 0)),
            scratch_shapes=[pltpu.VMEM((4 * BLK, 4 * BLK), BF16)],
        ),
        out_shape=jax.ShapeDtypeStruct((16, 32, SENT), BF16),
        compiler_params=LARGE,
        name="pack",
    )(
        at,
        in_store.reshape(64, width),
        out_store.reshape(64, width),
        w_out,
        w_in.reshape(2, 8, 2, 8, 32, R),
        norm_gain.reshape(2, 8, 2, 2, BLK),
        first_input,
    )
    got = lax.all_to_all(send, PLANE, 0, 0, tiled=True)
    other = lax.ppermute(got[:, :, W_LANE:], "c", SWAP)
    start = pl.pallas_call(
        start_kernel,
        out_shape=jax.ShapeDtypeStruct((R, 2 * R), BF16),
        in_specs=[VMEM, VMEM, VMEM, VMEM, pl.BlockSpec(memory_space=pl.ANY)],
        out_specs=VMEM,
        compiler_params=PARAMS,
        cost_estimate=pl.CostEstimate(flops=600000000, bytes_accessed=7000000, transcendentals=0),
        name="start",
    )(first_input, w_out, w_in, norm_gain, got)
    parts, out_w, in_w = pl.pallas_call(
        project_kernel,
        out_shape=(
            jax.ShapeDtypeStruct((16, 2 * TOK, WIDE), BF16),
            jax.ShapeDtypeStruct((NS, R, cols), BF16),
            jax.ShapeDtypeStruct((NS, cols, R), BF16),
        ),
        in_specs=[SMEM, VMEM, VMEM, VMEM],
        out_specs=(VMEM, VMEM, VMEM),
        scratch_shapes=[pltpu.VMEM((R, 2 * SPLIT * BLK), F32)],
        compiler_params=PARAMS,
        cost_estimate=pl.CostEstimate(flops=2000000000, bytes_accessed=9000000, transcendentals=0),
        name="project",
    )(at, got, other, start)
    parts = pl.pallas_call(
        functools.partial(norm_kernel, cols),
        out_shape=jax.ShapeDtypeStruct((16, 2 * TOK, WIDE), BF16),
        in_specs=[SMEM, SMEM, SMEM, VMEM, pl.BlockSpec(memory_space=pl.ANY)],
        out_specs=pl.BlockSpec(memory_space=pl.ANY),
        scratch_shapes=[pltpu.VMEM((16, 2 * TOK, BLK), BF16), pltpu.SemaphoreType.DMA],
        input_output_aliases={4: 0},
        compiler_params=PARAMS,
        name="norms",
    )(at, ids, other_ids, got, parts)
    parts = lax.all_to_all(parts, PLANE, 0, 0, tiled=True)
    sums = pl.pallas_call(
        sum_kernel,
        out_shape=jax.ShapeDtypeStruct((16, 2 * TOK, SPLIT * BLK), BF16),
        in_specs=[VMEM],
        out_specs=VMEM,
        compiler_params=PARAMS,
        name="sums",
    )(parts)
    sums = lax.all_to_all(sums, PLANE, 0, 0, tiled=True)
    gram = sums[:, TOK:, (GRAM - SPLIT) * BLK : (GRAM - SPLIT + GRAMS) * BLK]
    other = lax.ppermute(gram.reshape(R, GRAMS * BLK), "c", SWAP)
    base = pl.pallas_call(
        gather_kernel,
        out_shape=jax.ShapeDtypeStruct((2 * R, GRAM * BLK), F32),
        in_specs=[SMEM, SMEM, SMEM, VMEM],
        out_specs=VMEM,
        scratch_shapes=[pltpu.VMEM((R, GRAM * BLK), F32)],
        compiler_params=PARAMS,
        cost_estimate=pl.CostEstimate(flops=0, bytes_accessed=7000000, transcendentals=0),
        name="gather",
    )(at, ids, other_ids, sums)
    latent, scalars = pl.pallas_call(
        functools.partial(chain_kernel, width),
        out_shape=(
            jax.ShapeDtypeStruct((2 * R, 16 * BLK), BF16),
            jax.ShapeDtypeStruct((2 * R, BLK), F32),
        ),
        in_specs=[SMEM, VMEM, VMEM, VMEM, VMEM],
        out_specs=(VMEM, VMEM),
        scratch_shapes=[
            pltpu.VMEM((R, OO * BLK), BF16),
            pltpu.VMEM((R, OI * BLK), BF16),
            pltpu.VMEM((OI * R, R), BF16),
            pltpu.VMEM((OI * R, R), BF16),
        ],
        compiler_params=PARAMS,
        name="chain",
    )(at, parts, base, sums, other)

    def grads(own):
        return pl.pallas_call(
            functools.partial(grads_kernel, own),
            out_shape=jax.ShapeDtypeStruct((8, NS, 32, 2 * R), F32 if own else BF16),
            in_specs=[SMEM, SMEM, SMEM] + [VMEM] * 5,
            out_specs=VMEM,
            scratch_shapes=[pltpu.VMEM((NS, 2 * R, half), F32), pltpu.VMEM((R, half), F32)],
            compiler_params=PARAMS,
            cost_estimate=pl.CostEstimate(
                flops=600000000, bytes_accessed=9000000, transcendentals=0
            ),
            name="grads_own" if own else "grads_other",
        )(at, ids, other_ids, got, out_w, in_w, latent, scalars)

    swapped = lax.ppermute(grads(False), "c", SWAP)
    keep = grads(True)
    total = pl.pallas_call(
        add_kernel,
        out_shape=jax.ShapeDtypeStruct((8, NS, 32, 2 * R), BF16),
        in_specs=[VMEM, VMEM],
        out_specs=VMEM,
        compiler_params=PARAMS,
        name="add",
    )(keep, swapped).reshape(64, 32, 2 * R)
    block = (xl * NS + z) * 2 + core
    gain = lax.dynamic_slice_in_dim(norm_gain[0], block * half, half, 0)
    total, gain = lax.optimization_barrier((total, gain))
    total = lax.all_to_all(total, ("z",) + SECTION, 0, 0, tiled=True)
    grad_in, grad_out = pl.pallas_call(
        final_kernel,
        out_shape=(
            jax.ShapeDtypeStruct((half, R), F32),
            jax.ShapeDtypeStruct((R, half), F32),
        ),
        in_specs=[VMEM, VMEM],
        out_specs=(VMEM, VMEM),
        compiler_params=PARAMS,
        name="final",
    )(total.reshape(8, 8, 32, 2 * R), gain.reshape(2, BLK))
    return (grad_in[None], grad_out[None])


def solution(mesh):
    fine = Mesh(mesh.devices.reshape(2, 8, 2, 4, 2), ("xl", "z", "c", "y", "xh"))
    dp = ("xl", "z", "c")
    placed = (
        P(None, dp, None),
        P(dp, None, None),
        P(SECTION, dp, None, None),
        P(SECTION, dp, None, None),
        P(SECTION, None),
        P(SECTION, None, None),
        P(SECTION, None, None),
    )
    return jax.shard_map(
        body,
        mesh=fine,
        in_specs=placed,
        out_specs=(P(SECTION, dp, None), P(SECTION, None, dp)),
        check_vma=False,
    )
```

```python
import functools

import jax
import jax.numpy as jnp
from jax import lax
from jax.experimental import pallas as pl
from jax.experimental.pallas import tpu as pltpu
from jax.sharding import Mesh, PartitionSpec as P

F32 = jnp.float32
BF16 = jnp.bfloat16
EPS = 1e-05
PLANE = ("xl", "y", "xh")
SECTION = ("y", "xh")
SWAP = [(0, 1), (1, 0)]
NS = 8
R = 128
TOK = 8
MIC = 4
BLK = 128
HALF = 1024
W_LANE = 2 * HALF
SENT = 3072
PROJ = 29
NORM = 34
GRAM = 37
GRAMS = 32
SPLIT = 35
START = SPLIT * BLK
WIDE = START + 16 * BLK
OO = 36
OI = 28
LARGE = pltpu.CompilerParams(vmem_limit_bytes=56 * 1024 * 1024)
PARAMS = pltpu.CompilerParams(vmem_limit_bytes=16 * 1024 * 1024)
VMEM = pl.BlockSpec(memory_space=pltpu.VMEM)
SMEM = pl.BlockSpec(memory_space=pltpu.SMEM)


def gram_at(t):
    return sum(NS - i for i in range(t))


def cross_at(t):
    return sum(NS - 1 - i for i in range(t))


def proj_at(s):
    return s * (s - 1) // 2


def inner_at(s):
    return PROJ + s - 1 + (PROJ + s - 1 >= NORM)


def dot_t(a, b):
    return lax.dot_general(a, b, (((1,), (1,)), ((), ())), preferred_element_type=F32)


def dot_rows(a, b):
    return lax.dot_general(a, b, (((0,), (0,)), ((), ())), preferred_element_type=F32)


def dot(a, b):
    return jnp.dot(a, b, preferred_element_type=F32)


def split(x):
    high = x.astype(BF16)
    return high, (x - high.astype(F32)).astype(BF16)


def pack_kernel(
    at_ref, in_ref, out_ref, w_out_ref, w_in_ref, gain_ref, first_ref,
    send_ref, turn_ref,
):
    section = at_ref[1]

    @pl.when(pl.program_id(0) == 0)
    def _():
        shape = (4 * BLK, 4 * BLK)
        row = lax.broadcasted_iota(jnp.int32, shape, 0)
        col = lax.broadcasted_iota(jnp.int32, shape, 1)
        same = (row // BLK == col % BLK // 32) & (row % BLK // 32 == col // BLK)
        same = same & (row % 32 == col % 32)
        turn_ref[...] = jnp.where(same, 1.0, 0.0).astype(BF16)

    gain = gain_ref[...].reshape(8, BLK).T
    for s in range(NS):
        for j in range(4):
            column = 2 * j + s // 4
            scale = gain[(s % 4) * 32 : (s % 4) * 32 + 32, column : column + 1]
            to = W_LANE + 512 + j * BLK
            send_ref[s, :, to : to + BLK] = (w_in_ref[0, j, 0, s].astype(F32) * scale).astype(BF16)

    pieces, places = [], []
    for c in range(2):
        for zq in range(2):
            to = c * 256 + zq * BLK
            for h in range(2):
                lanes = [((4 * zq + j) * 4 + c * 2 + h) * BLK for j in range(4)]
                for ref, row, at, other in (
                    (in_ref, 0, c * HALF + zq * BLK, 0),
                    (in_ref, 32, c * HALF + 256 + zq * BLK, 0),
                    (out_ref, 0, c * HALF + 512 + zq * BLK, NS - 1),
                    (out_ref, 32, c * HALF + 768 + zq * BLK, NS - 1),
                    (w_out_ref, 0, W_LANE + to, None),
                ):
                    piece = jnp.concatenate(
                        [ref[row : row + 32, lane : lane + BLK] for lane in lanes], 1
                    )
                    if other is not None:
                        first = jnp.concatenate(
                            [first_ref[row // 32, :, lane : lane + BLK] for lane in lanes], 1
                        )
                        piece = jnp.where(section == other, first, piece)
                    pieces.append(piece)
                    places.append((4 * h, at))
    turned = dot(jnp.concatenate(pieces, 0), turn_ref[...]).astype(BF16)
    for n, (first, at) in enumerate(places):
        for i in range(4):
            send_ref[first + i, :, at : at + BLK] = turned[
                32 * n : 32 * n + 32, i * BLK : (i + 1) * BLK
            ]


def start_kernel(first_ref, w_out_ref, w_in_ref, gain_ref, after_ref, start_ref):
    del after_ref
    flat = first_ref[...].reshape(R, first_ref.shape[2])
    scaled = (flat.astype(F32) * gain_ref[...]).astype(BF16)
    start_ref[:, :R] = dot(scaled, w_in_ref[...]).astype(BF16)
    start_ref[:, R:] = dot_t(flat, w_out_ref[...]).astype(BF16)


def stores(got_ref, s, at, cols):
    pieces = []
    for x in range(2):
        for i in range(2):
            a, b = at + i * 256, at + 512 + i * 256
            pieces.append(
                got_ref[x * NS + s, :, pl.ds(a, cols)].astype(F32)
                - got_ref[x * NS + s - 1, :, pl.ds(b, cols)].astype(F32)
            )
    return jnp.concatenate(pieces, 0)


def first_rows(got_ref, at, cols):
    pieces = []
    for x in range(2):
        for m in range(MIC):
            q = x * NS + (0 if m < 2 else NS - 1)
            lane = at + m // 2 * 512 + m % 2 * 256
            pieces.append(got_ref[q, :, pl.ds(lane, cols)])
    return jnp.concatenate(pieces, 0).astype(F32)


def picks_of(at_ref, ids_ref, other_ids_ref):
    picks = []
    for x in range(2):
        here = at_ref[2] == x
        for m in range(MIC):
            for j in range(4):
                picks.append(x * NS + jnp.where(here, ids_ref[m, j], other_ids_ref[m, j]))
    return picks


def running_sums(got_ref, cols):
    running = None
    for s in range(1, NS):
        step = jnp.concatenate(
            [stores(got_ref, s, 0, cols // 2), stores(got_ref, s, HALF, cols // 2)], 1
        )
        running = step if running is None else running + step
        yield s, running


def project_kernel(
    at_ref, got_ref, other_ref, start_ref, send_ref, out_give_ref, in_give_ref,
    out_keep_ref, in_keep_ref, wide_ref, out_w_ref, in_w_ref,
):
    cols = in_w_ref.shape[1]
    half = cols // 2
    first_core = at_ref[0] == 0
    for s in range(NS):
        for x in range(2):
            mine = got_ref[x * NS + s, :, W_LANE:SENT]
            theirs = other_ref[x * NS + s]
            for c in range(2):
                part = jnp.where(first_core == (c == 0), mine, theirs)
                k = 2 * x + c
                out_w_ref[s, 32 * k : 32 * k + 32, :] = part[:, :cols]
                for g in range(4):
                    row = k * BLK + g * 32
                    lane = cols + g * BLK
                    in_w_ref[s, row : row + 32, :] = part[:, lane : lane + BLK]
    for out_half_ref, in_half_ref, side in (
        (out_give_ref, in_give_ref, 1 - at_ref[0]),
        (out_keep_ref, in_keep_ref, at_ref[0]),
    ):
        here = pl.ds(pl.multiple_of(side * half, half), half)
        out_half_ref[...] = out_w_ref[:, :, here]
        in_half_ref[...] = in_w_ref[:, here, :]
    for s, running in running_sums(got_ref, cols):
        rounded = running.astype(BF16)
        count = s if s < NS - 1 else NS
        at = proj_at(s) * BLK
        wide_ref[:, at : at + count * BLK] = dot_t(
            rounded, out_w_ref[0:count].reshape(count * R, cols)
        )
        at = inner_at(s) * BLK
        wide_ref[:, at : at + BLK] = dot(rounded, in_w_ref[s])
    for b in (NORM, GRAM + GRAMS):
        wide_ref[:, b * BLK : (b + 1) * BLK] = jnp.zeros((R, BLK), F32)

    square = [(t, s) for t in range(NS) for s in range(t, NS)]

    @pl.when(first_core)
    def _():
        for t in range(5):
            at = (GRAM + gram_at(t)) * BLK
            wide_ref[:, at : at + (NS - t) * BLK] = dot_t(
                out_w_ref[t], out_w_ref[t:NS].reshape((NS - t) * R, cols)
            )
        for i in range(gram_at(5), GRAMS):
            t, s = square[i]
            at = (GRAM + i) * BLK
            wide_ref[:, at : at + BLK] = dot_t(out_w_ref[t], out_w_ref[s])

    @pl.when(jnp.logical_not(first_core))
    def _():
        for t in range(NS - 1):
            for s in range(t + 1, NS):
                at = (GRAM + cross_at(t) + s - t - 1) * BLK
                wide_ref[:, at : at + BLK] = dot(out_w_ref[t], in_w_ref[s])
        for i in range(GRAMS, OO):
            t, s = square[i]
            at = (GRAM + OI + i - GRAMS) * BLK
            wide_ref[:, at : at + BLK] = dot_t(out_w_ref[t], out_w_ref[s])

    for b in range(SPLIT):
        pair = [
            wide_ref[:, at * BLK : (at + 1) * BLK].reshape(16, TOK, BLK) for at in (b, SPLIT + b)
        ]
        send_ref[:, :, b * BLK : (b + 1) * BLK] = jnp.concatenate(pair, 1).astype(BF16)
    for g in range(8):
        at = START + g * 2 * R
        for q in range(16):
            send_ref[q, :, at : at + 2 * R] = start_ref[g * 16 : (g + 1) * 16, :]


def norm_kernel(
    cols, at_ref, ids_ref, other_ids_ref, got_ref, before_ref, send_ref, block_ref, sem
):
    del before_ref
    picks = picks_of(at_ref, ids_ref, other_ids_ref)
    placed = [[] for _ in range(MIC)]
    first = jnp.concatenate(
        [first_rows(got_ref, 0, cols // 2), first_rows(got_ref, HALF, cols // 2)], 1
    )
    for x in range(2):
        rows = first[x * R : (x + 1) * R]
        for e in range(NS):
            for m in range(MIC):
                total = jnp.zeros((TOK, cols), F32)
                for j in range(4):
                    n = 4 * m + j
                    total = jnp.where(
                        picks[16 * x + n] == x * NS + e, rows[n * TOK : (n + 1) * TOK], total
                    )
                placed[m].append(total)
    placed = [jnp.concatenate(blocks, 0) for blocks in placed]
    lane = lax.broadcasted_iota(jnp.int32, (R, BLK), 1)
    norms = jnp.zeros((R, BLK), F32)
    for m in range(MIC):
        part = jnp.sum(placed[m] * placed[m], -1, keepdims=True)
        norms = jnp.where(lane == m * NS, part, norms)
    for s, running in running_sums(got_ref, cols):
        for m in range(MIC):
            entry = running + placed[m]
            part = jnp.sum(entry * entry, -1, keepdims=True)
            norms = jnp.where(lane == m * NS + s, part, norms)
    high = norms.astype(BF16).astype(F32)
    norms = jnp.where(lane < 32, high, pltpu.roll(norms - high, 32, 1)).reshape(16, TOK, BLK)
    block_ref[...] = jnp.concatenate([norms, jnp.zeros_like(norms)], 1).astype(BF16)
    copy = pltpu.make_async_copy(
        block_ref, send_ref.at[:, :, NORM * BLK : (NORM + 1) * BLK], sem
    )
    copy.start()
    copy.wait()


def sum_kernel(parts_ref, send_ref):
    lane = lax.broadcasted_iota(jnp.int32, (2 * TOK, BLK), 1)
    row = lax.broadcasted_iota(jnp.int32, (2 * TOK, BLK), 0)
    for b in range(SPLIT):
        at = slice(b * BLK, (b + 1) * BLK)
        total = parts_ref[0, :, at].astype(F32)
        for q in range(1, 16):
            total = total + parts_ref[q, :, at].astype(F32)
        if b == NORM:
            norm = total + pltpu.roll(total, 96, 1)
            high = norm.astype(BF16).astype(F32)
            norm = jnp.where(lane < 32, high, pltpu.roll(norm - high, 32, 1))
            total = jnp.where(row < TOK, norm, 0.0)
        total = total.astype(BF16)
        for q in range(16):
            send_ref[q, :, at] = total


def gather_kernel(at_ref, ids_ref, other_ids_ref, sums_ref, base_ref, proj_ref):
    for b in range(GRAM):
        upper = b >= SPLIT
        at = (b - SPLIT * upper) * BLK
        block = sums_ref[:, :, at : at + BLK].astype(F32)
        proj_ref[:, b * BLK : (b + 1) * BLK] = block[:, TOK * upper : TOK * upper + TOK].reshape(
            R, BLK
        )
    for n, pick in enumerate(picks_of(at_ref, ids_ref, other_ids_ref)):
        rows = slice(n * TOK, (n + 1) * TOK)
        here = pl.ds(pl.multiple_of(pick * TOK, TOK), TOK)
        base_ref[rows, :] = proj_ref[here, :]
        norm = proj_ref[here, NORM * BLK : (NORM + 1) * BLK]
        norm = norm + pltpu.roll(norm, 96, 1)
        m = n % 16 // 4
        base_ref[rows, NORM * BLK : (NORM + 1) * BLK] = (
            pltpu.roll(norm, BLK - m * NS, 1) if m else norm
        )


def chain_kernel(
    width, at_ref, parts_ref, base_ref, sums_ref, other_ref,
    latent_ref, scalar_ref, again_ref, scalar_again_ref, oo_ref, oi_ref, oo_rows_ref, oi_rows_ref,
):
    rows = 2 * R
    first_core = at_ref[0] == 0
    for b in range(0, GRAMS, 4):
        at = (GRAM - SPLIT + b) * BLK
        mine = sums_ref[:, :, at : at + 4 * BLK].astype(F32)[:, TOK:]
        mine = mine.reshape(R, 4 * BLK).astype(BF16)
        at = slice(b * BLK, (b + 4) * BLK)
        theirs = other_ref[:, at]
        oo_ref[:, at] = jnp.where(first_core, mine, theirs)
        second = jnp.where(first_core, theirs, mine)
        if b < OI:
            oi_ref[:, at] = second
        else:
            oo_ref[:, (b + 4) * BLK : (b + 8) * BLK] = second

    def spread(at):
        return base_ref[:, at * BLK : (at + 1) * BLK]

    def square(t, s, count=1):
        at = (gram_at(t) + s - t) * BLK
        return oo_ref[:, at : at + count * BLK]

    def cross(t, s, count=1):
        at = (cross_at(t) + s - t - 1) * BLK
        return oi_ref[:, at : at + count * BLK]

    for s in range(1, NS):
        for t in range(s):
            at = slice((proj_at(s) + t) * R, (proj_at(s) + t + 1) * R)
            oo_rows_ref[at, :] = square(t, s)
            oi_rows_ref[at, :] = cross(t, s)

    def above(ref, s):
        return ref[proj_at(s) * R : (proj_at(s) + s) * R, :]

    norms = spread(NORM)
    starts = []
    for s in range(NS):
        pieces = []
        for x in range(2):
            for g in range(8):
                at = START + g * 2 * R
                pieces.append(parts_ref[x * NS + s, :, at : at + 2 * R])
        starts.append(jnp.concatenate(pieces, 0))
    start_out = [start[:, R:].astype(F32) for start in starts]
    run_in = [start[:, :R].astype(F32) for start in starts]
    run_out = list(start_out)
    inners, inverses, actives, crossed = [], [], [], []
    grown_norm = jnp.zeros((rows, R), F32)
    for s in range(NS):
        norm = norms[:, s : s + 1]
        entry_out = []
        inner = run_in[s]
        if s > 0:
            inner = inner + spread(inner_at(s))
            total = jnp.zeros((rows, R), F32)
            for t in range(s):
                base = spread(proj_at(s) + t)
                entry_out.append(base + run_out[t])
                total = total + actives[t] * base
            norm = norm + jnp.sum(2.0 * total + grown_norm, -1, keepdims=True)
        inverse = lax.rsqrt(jnp.maximum(norm, 0.0) * (1.0 / width) + EPS)
        inner = inner * inverse
        active = (inner * jax.nn.sigmoid(inner)).astype(BF16)
        latent_ref[:, s * R : (s + 1) * R] = active
        again_ref[:, s * R : (s + 1) * R] = active
        inners.append(inner)
        inverses.append(inverse)
        actives.append(active.astype(F32))
        crossed.append(entry_out)
        grown = dot(active, square(s, s, NS - s))
        if s > 0:
            grown = jnp.concatenate([dot_t(active, above(oo_rows_ref, s)), grown], 1)
        before = run_out[s]
        for t in range(NS):
            run_out[t] = run_out[t] + grown[:, t * R : (t + 1) * R]
        grown_norm = grown_norm + actives[s] * (before + run_out[s])
        if s < NS - 1:
            grown = dot(active, cross(s, s + 1, NS - 1 - s))
            for t in range(s + 1, NS):
                run_in[t] = run_in[t] + grown[:, (t - s - 1) * R : (t - s) * R]
    grads = [run_out[t] + spread(proj_at(NS - 1) + t) for t in range(NS)]
    lane = lax.broadcasted_iota(jnp.int32, (rows, BLK), 1)
    scalars = jnp.zeros((rows, BLK), F32)
    for s in range(NS - 1, -1, -1):
        inner = inners[s]
        sigm = jax.nn.sigmoid(inner)
        d_inner = (grads[s] * sigm * (1.0 + inner * (1.0 - sigm))).astype(BF16)
        latent_ref[:, (NS + s) * R : (NS + s + 1) * R] = d_inner
        again_ref[:, (NS + s) * R : (NS + s + 1) * R] = d_inner
        inverse = inverses[s]
        total = jnp.sum(d_inner.astype(F32) * inner, -1, keepdims=True)
        scale = inverse * inverse * total * (1.0 / width)
        if s > 0:
            back = dot_t(d_inner, above(oi_rows_ref, s))
        for t in range(s):
            grads[t] = (
                grads[t] + inverse * back[:, t * R : (t + 1) * R] - scale * crossed[s][t]
            )
        scalars = jnp.where(lane == s, inverse, scalars)
        scalars = jnp.where(lane == NS + s, scale, scalars)
    scalar_ref[...] = scalars
    scalar_again_ref[...] = scalars


def grads_kernel(
    own, at_ref, ids_ref, other_ids_ref, got_ref, out_w_ref, in_w_ref, latent_ref, scalar_ref,
    result_ref, entry_ref, step_ref,
):
    cols = step_ref.shape[1]
    scalars = scalar_ref[...]
    inverses = [scalars[:, s : s + 1] for s in range(NS)]
    scales = [scalars[:, NS + s : NS + s + 1] for s in range(NS)]
    places = [
        pl.multiple_of(pick * TOK, TOK) for pick in picks_of(at_ref, ids_ref, other_ids_ref)
    ]

    def active(s):
        return latent_ref[:, s * R : (s + 1) * R]

    def d_inner(s):
        return latent_ref[:, (NS + s) * R : (NS + s + 1) * R]

    side = at_ref[0] if own else 1 - at_ref[0]
    at = pl.multiple_of(side * HALF, HALF)

    def put(s, kind, value):
        result_ref[:, s, :, kind * R : (kind + 1) * R] = value.reshape(8, 32, R).astype(
            result_ref.dtype
        )

    entry = first_rows(got_ref, at, cols)
    for s in range(NS):
        if s > 0:
            step_ref[...] = stores(got_ref, s, at, cols)
            entry = entry + jnp.concatenate([step_ref[pl.ds(place, TOK), :] for place in places], 0)
        entry_ref[s] = entry
        put(s, 0, dot_rows((entry * inverses[s]).astype(BF16), d_inner(s)))
        entry = entry + dot(active(s), out_w_ref[s])
    grad = entry
    for s in range(NS - 1, -1, -1):
        put(s, 1, dot_rows(grad.astype(BF16), active(s)))
        if s > 0:
            back = dot_t(d_inner(s), in_w_ref[s])
            grad = grad + inverses[s] * back - scales[s] * entry_ref[s]


def add_kernel(keep_ref, swapped_ref, total_ref):
    for i in range(8):
        total_ref[i] = (keep_ref[i] + swapped_ref[i].astype(F32)).astype(BF16)


def final_kernel(parts_ref, gain_ref, in_ref, out_ref):
    total = parts_ref[0].astype(F32)
    for i in range(1, 8):
        total = total + parts_ref[i].astype(F32)
    gain = gain_ref[...].T
    for j in range(8):
        scale = gain[(j % 4) * 32 : (j % 4) * 32 + 32, j // 4 : j // 4 + 1]
        in_ref[j * 32 : j * 32 + 32, :] = total[j, :, :R] * scale
    out = total[:, :, R:].reshape(2 * BLK, R)
    for i in range(2):
        out_ref[:, i * BLK : (i + 1) * BLK] = out[i * BLK : (i + 1) * BLK].T


def body(first_input, example_ids, out_store, in_store, norm_gain, adapter_in, adapter_out):
    width = first_input.shape[2]
    cols = width // 16
    half = cols // 2
    wide = width // 2
    core = lax.axis_index("c")
    xl = lax.axis_index("xl")
    z = lax.axis_index("z")
    section = lax.axis_index(SECTION)
    quarter = xl * 2 + core
    at = jnp.stack([core, section, xl, quarter]).astype(jnp.int32)
    w_in = adapter_in[0]
    w_out = adapter_out[0]

    ids = example_ids[0]
    other_ids = lax.ppermute(ids, "xl", SWAP)
    send = pl.pallas_call(
        pack_kernel,
        grid_spec=pltpu.PrefetchScalarGridSpec(
            num_scalar_prefetch=1,
            grid=(2,),
            in_specs=[
                pl.BlockSpec((64, wide), lambda i, at: (0, i)),
                pl.BlockSpec((64, wide), lambda i, at: (0, i)),
                pl.BlockSpec((32, wide), lambda i, at: (at[3], i)),
                pl.BlockSpec(
                    (1, 4, 1, 8, 32, R), lambda i, at: (i, at[3] % 2, at[3] // 2, 0, 0, 0)
                ),
                pl.BlockSpec((1, 4, 1, 2, BLK), lambda i, at: (i, at[3] % 2, at[3] // 2, 0, 0)),
                pl.BlockSpec((2, 32, wide), lambda i, at: (at[1] // (NS - 1), 0, i)),
            ],
            out_specs=pl.BlockSpec((8, 32, SENT), lambda i, at: (i, 0, 0)),
            scratch_shapes=[pltpu.VMEM((4 * BLK, 4 * BLK), BF16)],
        ),
        out_shape=jax.ShapeDtypeStruct((16, 32, SENT), BF16),
        compiler_params=LARGE,
        name="pack",
    )(
        at,
        in_store.reshape(64, width),
        out_store.reshape(64, width),
        w_out,
        w_in.reshape(2, 8, 2, 8, 32, R),
        norm_gain.reshape(2, 8, 2, 2, BLK),
        first_input,
    )
    got = lax.all_to_all(send, PLANE, 0, 0, tiled=True)
    other = lax.ppermute(got[:, :, W_LANE:], "c", SWAP)
    start = pl.pallas_call(
        start_kernel,
        out_shape=jax.ShapeDtypeStruct((R, 2 * R), BF16),
        in_specs=[VMEM, VMEM, VMEM, VMEM, pl.BlockSpec(memory_space=pl.ANY)],
        out_specs=VMEM,
        compiler_params=PARAMS,
        cost_estimate=pl.CostEstimate(flops=600000000, bytes_accessed=7000000, transcendentals=0),
        name="start",
    )(first_input, w_out, w_in, norm_gain, got)
    parts, *weights = pl.pallas_call(
        project_kernel,
        out_shape=(jax.ShapeDtypeStruct((16, 2 * TOK, WIDE), BF16),)
        + (
            jax.ShapeDtypeStruct((NS, R, half), BF16),
            jax.ShapeDtypeStruct((NS, half, R), BF16),
        )
        * 2,
        in_specs=[SMEM, VMEM, VMEM, VMEM],
        out_specs=(VMEM,) * 5,
        scratch_shapes=[
            pltpu.VMEM((R, 2 * SPLIT * BLK), F32),
            pltpu.VMEM((NS, R, cols), BF16),
            pltpu.VMEM((NS, cols, R), BF16),
        ],
        compiler_params=PARAMS,
        cost_estimate=pl.CostEstimate(flops=2000000000, bytes_accessed=9000000, transcendentals=0),
        name="project",
    )(at, got, other, start)
    parts = pl.pallas_call(
        functools.partial(norm_kernel, cols),
        out_shape=jax.ShapeDtypeStruct((16, 2 * TOK, WIDE), BF16),
        in_specs=[SMEM, SMEM, SMEM, VMEM, pl.BlockSpec(memory_space=pl.ANY)],
        out_specs=pl.BlockSpec(memory_space=pl.ANY),
        scratch_shapes=[pltpu.VMEM((16, 2 * TOK, BLK), BF16), pltpu.SemaphoreType.DMA],
        input_output_aliases={4: 0},
        compiler_params=PARAMS,
        name="norms",
    )(at, ids, other_ids, got, parts)
    parts = lax.all_to_all(parts, PLANE, 0, 0, tiled=True)
    sums = pl.pallas_call(
        sum_kernel,
        out_shape=jax.ShapeDtypeStruct((16, 2 * TOK, SPLIT * BLK), BF16),
        in_specs=[VMEM],
        out_specs=VMEM,
        compiler_params=PARAMS,
        name="sums",
    )(parts)
    sums = lax.all_to_all(sums, PLANE, 0, 0, tiled=True)
    gram = sums[:, TOK:, (GRAM - SPLIT) * BLK : (GRAM - SPLIT + GRAMS) * BLK]
    other = lax.ppermute(gram.reshape(R, GRAMS * BLK), "c", SWAP)
    base = pl.pallas_call(
        gather_kernel,
        out_shape=jax.ShapeDtypeStruct((2 * R, GRAM * BLK), F32),
        in_specs=[SMEM, SMEM, SMEM, VMEM],
        out_specs=VMEM,
        scratch_shapes=[pltpu.VMEM((R, GRAM * BLK), F32)],
        compiler_params=PARAMS,
        cost_estimate=pl.CostEstimate(flops=0, bytes_accessed=7000000, transcendentals=0),
        name="gather",
    )(at, ids, other_ids, sums)
    latents = pl.pallas_call(
        functools.partial(chain_kernel, width),
        out_shape=(
            jax.ShapeDtypeStruct((2 * R, 16 * BLK), BF16),
            jax.ShapeDtypeStruct((2 * R, BLK), F32),
        )
        * 2,
        in_specs=[SMEM, VMEM, VMEM, VMEM, VMEM],
        out_specs=(VMEM,) * 4,
        scratch_shapes=[
            pltpu.VMEM((R, OO * BLK), BF16),
            pltpu.VMEM((R, OI * BLK), BF16),
            pltpu.VMEM((OI * R, R), BF16),
            pltpu.VMEM((OI * R, R), BF16),
        ],
        compiler_params=PARAMS,
        name="chain",
    )(at, parts, base, sums, other)

    def grads(own):
        return pl.pallas_call(
            functools.partial(grads_kernel, own),
            out_shape=jax.ShapeDtypeStruct((8, NS, 32, 2 * R), F32 if own else BF16),
            in_specs=[SMEM, SMEM, SMEM] + [VMEM] * 5,
            out_specs=VMEM,
            scratch_shapes=[pltpu.VMEM((NS, 2 * R, half), F32), pltpu.VMEM((R, half), F32)],
            compiler_params=PARAMS,
            cost_estimate=pl.CostEstimate(
                flops=600000000, bytes_accessed=9000000, transcendentals=0
            ),
            name="grads_own" if own else "grads_other",
        )(at, ids, other_ids, got, *weights[2 * own : 2 * own + 2], *latents[2 * own : 2 * own + 2])

    swapped = lax.ppermute(grads(False), "c", SWAP)
    keep = grads(True)
    total = pl.pallas_call(
        add_kernel,
        out_shape=jax.ShapeDtypeStruct((8, NS, 32, 2 * R), BF16),
        in_specs=[VMEM, VMEM],
        out_specs=VMEM,
        compiler_params=PARAMS,
        name="add",
    )(keep, swapped).reshape(64, 32, 2 * R)
    block = (xl * NS + z) * 2 + core
    gain = lax.dynamic_slice_in_dim(norm_gain[0], block * half, half, 0)
    total, gain = lax.optimization_barrier((total, gain))
    total = lax.all_to_all(total, ("z",) + SECTION, 0, 0, tiled=True)
    grad_in, grad_out = pl.pallas_call(
        final_kernel,
        out_shape=(
            jax.ShapeDtypeStruct((half, R), F32),
            jax.ShapeDtypeStruct((R, half), F32),
        ),
        in_specs=[VMEM, VMEM],
        out_specs=(VMEM, VMEM),
        compiler_params=PARAMS,
        name="final",
    )(total.reshape(8, 8, 32, 2 * R), gain.reshape(2, BLK))
    return (grad_in[None], grad_out[None])


def solution(mesh):
    fine = Mesh(mesh.devices.reshape(2, 8, 2, 4, 2), ("xl", "z", "c", "y", "xh"))
    dp = ("xl", "z", "c")
    placed = (
        P(None, dp, None),
        P(dp, None, None),
        P(SECTION, dp, None, None),
        P(SECTION, dp, None, None),
        P(SECTION, None),
        P(SECTION, None, None),
        P(SECTION, None, None),
    )
    return jax.shard_map(
        body,
        mesh=fine,
        in_specs=placed,
        out_specs=(P(SECTION, dp, None), P(SECTION, None, dp)),
        check_vma=False,
    )
```

```python
import functools

import jax
import jax.numpy as jnp
from jax import lax
from jax.experimental import pallas as pl
from jax.experimental.pallas import tpu as pltpu
from jax.sharding import Mesh, PartitionSpec as P

F32 = jnp.float32
BF16 = jnp.bfloat16
EPS = 1e-05
PLANE = ("xl", "y", "xh")
SECTION = ("y", "xh")
SWAP = [(0, 1), (1, 0)]
NS = 8
R = 128
TOK = 8
MIC = 4
BLK = 128
HALF = 1024
W_LANE = 2 * HALF
SENT = 3072
PROJ = 29
NORM = 34
GRAM = 37
GRAMS = 32
SPLIT = 35
START = SPLIT * BLK
WIDE = START + 16 * BLK
OO = 36
OI = 28
LARGE = pltpu.CompilerParams(vmem_limit_bytes=56 * 1024 * 1024)
PARAMS = pltpu.CompilerParams(vmem_limit_bytes=16 * 1024 * 1024)
VMEM = pl.BlockSpec(memory_space=pltpu.VMEM)
SMEM = pl.BlockSpec(memory_space=pltpu.SMEM)


def gram_at(t):
    return sum(NS - i for i in range(t))


def cross_at(t):
    return sum(NS - 1 - i for i in range(t))


def proj_at(s):
    return s * (s - 1) // 2


def inner_at(s):
    return PROJ + s - 1 + (PROJ + s - 1 >= NORM)


def dot_t(a, b):
    return lax.dot_general(a, b, (((1,), (1,)), ((), ())), preferred_element_type=F32)


def dot_rows(a, b):
    return lax.dot_general(a, b, (((0,), (0,)), ((), ())), preferred_element_type=F32)


def dot(a, b):
    return jnp.dot(a, b, preferred_element_type=F32)


def split(x):
    high = x.astype(BF16)
    return high, (x - high.astype(F32)).astype(BF16)


def pack_kernel(
    at_ref, in_ref, out_ref, w_out_ref, w_in_ref, gain_ref, first_ref,
    send_ref, turn_ref,
):
    section = at_ref[1]

    @pl.when(pl.program_id(0) == 0)
    def _():
        shape = (4 * BLK, 4 * BLK)
        row = lax.broadcasted_iota(jnp.int32, shape, 0)
        col = lax.broadcasted_iota(jnp.int32, shape, 1)
        same = (row // BLK == col % BLK // 32) & (row % BLK // 32 == col // BLK)
        same = same & (row % 32 == col % 32)
        turn_ref[...] = jnp.where(same, 1.0, 0.0).astype(BF16)

    gain = gain_ref[...].reshape(8, BLK).T
    for s in range(NS):
        for j in range(4):
            column = 2 * j + s // 4
            scale = gain[(s % 4) * 32 : (s % 4) * 32 + 32, column : column + 1]
            to = W_LANE + 512 + j * BLK
            send_ref[s, :, to : to + BLK] = (w_in_ref[0, j, 0, s].astype(F32) * scale).astype(BF16)

    pieces, places = [], []
    for c in range(2):
        for zq in range(2):
            to = c * 256 + zq * BLK
            for h in range(2):
                lanes = [((4 * zq + j) * 4 + c * 2 + h) * BLK for j in range(4)]
                for ref, row, at, other in (
                    (in_ref, 0, c * HALF + zq * BLK, 0),
                    (in_ref, 32, c * HALF + 256 + zq * BLK, 0),
                    (out_ref, 0, c * HALF + 512 + zq * BLK, NS - 1),
                    (out_ref, 32, c * HALF + 768 + zq * BLK, NS - 1),
                    (w_out_ref, 0, W_LANE + to, None),
                ):
                    piece = jnp.concatenate(
                        [ref[row : row + 32, lane : lane + BLK] for lane in lanes], 1
                    )
                    if other is not None:
                        first = jnp.concatenate(
                            [first_ref[row // 32, :, lane : lane + BLK] for lane in lanes], 1
                        )
                        piece = jnp.where(section == other, first, piece)
                    pieces.append(piece)
                    places.append((4 * h, at))
    turned = dot(jnp.concatenate(pieces, 0), turn_ref[...]).astype(BF16)
    for n, (first, at) in enumerate(places):
        for i in range(4):
            send_ref[first + i, :, at : at + BLK] = turned[
                32 * n : 32 * n + 32, i * BLK : (i + 1) * BLK
            ]


def start_kernel(first_ref, w_out_ref, w_in_ref, gain_ref, after_ref, start_ref):
    del after_ref
    flat = first_ref[...].reshape(R, first_ref.shape[2])
    scaled = (flat.astype(F32) * gain_ref[...]).astype(BF16)
    start_ref[:, :R] = dot(scaled, w_in_ref[...]).astype(BF16)
    start_ref[:, R:] = dot_t(flat, w_out_ref[...]).astype(BF16)


def stores(got_ref, s, at, cols):
    pieces = []
    for x in range(2):
        for i in range(2):
            a, b = at + i * 256, at + 512 + i * 256
            pieces.append(
                got_ref[x * NS + s, :, pl.ds(a, cols)].astype(F32)
                - got_ref[x * NS + s - 1, :, pl.ds(b, cols)].astype(F32)
            )
    return jnp.concatenate(pieces, 0)


def first_rows(got_ref, at, cols):
    pieces = []
    for x in range(2):
        for m in range(MIC):
            q = x * NS + (0 if m < 2 else NS - 1)
            lane = at + m // 2 * 512 + m % 2 * 256
            pieces.append(got_ref[q, :, pl.ds(lane, cols)])
    return jnp.concatenate(pieces, 0).astype(F32)


def picks_of(at_ref, ids_ref, other_ids_ref):
    picks = []
    for x in range(2):
        here = at_ref[2] == x
        for m in range(MIC):
            for j in range(4):
                picks.append(x * NS + jnp.where(here, ids_ref[m, j], other_ids_ref[m, j]))
    return picks


def running_sums(got_ref, cols):
    running = None
    for s in range(1, NS):
        step = jnp.concatenate(
            [stores(got_ref, s, 0, cols // 2), stores(got_ref, s, HALF, cols // 2)], 1
        )
        running = step if running is None else running + step
        yield s, running


def project_kernel(
    at_ref, got_ref, other_ref, start_ref, send_ref, out_w_ref, in_w_ref, wide_ref
):
    cols = in_w_ref.shape[1]
    first_core = at_ref[0] == 0
    for s in range(NS):
        for x in range(2):
            mine = got_ref[x * NS + s, :, W_LANE:SENT]
            theirs = other_ref[x * NS + s]
            for c in range(2):
                part = jnp.where(first_core == (c == 0), mine, theirs)
                k = 2 * x + c
                out_w_ref[s, 32 * k : 32 * k + 32, :] = part[:, :cols]
                for g in range(4):
                    row = k * BLK + g * 32
                    lane = cols + g * BLK
                    in_w_ref[s, row : row + 32, :] = part[:, lane : lane + BLK]
    for s, running in running_sums(got_ref, cols):
        rounded = running.astype(BF16)
        count = s if s < NS - 1 else NS
        at = proj_at(s) * BLK
        wide_ref[:, at : at + count * BLK] = dot_t(
            rounded, out_w_ref[0:count].reshape(count * R, cols)
        )
        at = inner_at(s) * BLK
        wide_ref[:, at : at + BLK] = dot(rounded, in_w_ref[s])
    for b in (NORM, GRAM + GRAMS):
        wide_ref[:, b * BLK : (b + 1) * BLK] = jnp.zeros((R, BLK), F32)

    square = [(t, s) for t in range(NS) for s in range(t, NS)]

    @pl.when(first_core)
    def _():
        for t in range(5):
            at = (GRAM + gram_at(t)) * BLK
            wide_ref[:, at : at + (NS - t) * BLK] = dot_t(
                out_w_ref[t], out_w_ref[t:NS].reshape((NS - t) * R, cols)
            )
        for i in range(gram_at(5), GRAMS):
            t, s = square[i]
            at = (GRAM + i) * BLK
            wide_ref[:, at : at + BLK] = dot_t(out_w_ref[t], out_w_ref[s])

    @pl.when(jnp.logical_not(first_core))
    def _():
        for t in range(NS - 1):
            for s in range(t + 1, NS):
                at = (GRAM + cross_at(t) + s - t - 1) * BLK
                wide_ref[:, at : at + BLK] = dot(out_w_ref[t], in_w_ref[s])
        for i in range(GRAMS, OO):
            t, s = square[i]
            at = (GRAM + OI + i - GRAMS) * BLK
            wide_ref[:, at : at + BLK] = dot_t(out_w_ref[t], out_w_ref[s])

    for b in range(SPLIT):
        pair = [
            wide_ref[:, at * BLK : (at + 1) * BLK].reshape(16, TOK, BLK) for at in (b, SPLIT + b)
        ]
        send_ref[:, :, b * BLK : (b + 1) * BLK] = jnp.concatenate(pair, 1).astype(BF16)
    for g in range(8):
        at = START + g * 2 * R
        for q in range(16):
            send_ref[q, :, at : at + 2 * R] = start_ref[g * 16 : (g + 1) * 16, :]


def norm_kernel(
    cols, at_ref, ids_ref, other_ids_ref, got_ref, before_ref, send_ref, block_ref, sem
):
    del before_ref
    picks = picks_of(at_ref, ids_ref, other_ids_ref)
    placed = [[] for _ in range(MIC)]
    first = jnp.concatenate(
        [first_rows(got_ref, 0, cols // 2), first_rows(got_ref, HALF, cols // 2)], 1
    )
    for x in range(2):
        rows = first[x * R : (x + 1) * R]
        for e in range(NS):
            for m in range(MIC):
                total = jnp.zeros((TOK, cols), F32)
                for j in range(4):
                    n = 4 * m + j
                    total = jnp.where(
                        picks[16 * x + n] == x * NS + e, rows[n * TOK : (n + 1) * TOK], total
                    )
                placed[m].append(total)
    placed = [jnp.concatenate(blocks, 0) for blocks in placed]
    lane = lax.broadcasted_iota(jnp.int32, (R, BLK), 1)
    norms = jnp.zeros((R, BLK), F32)
    for m in range(MIC):
        part = jnp.sum(placed[m] * placed[m], -1, keepdims=True)
        norms = jnp.where(lane == m * NS, part, norms)
    for s, running in running_sums(got_ref, cols):
        for m in range(MIC):
            entry = running + placed[m]
            part = jnp.sum(entry * entry, -1, keepdims=True)
            norms = jnp.where(lane == m * NS + s, part, norms)
    high = norms.astype(BF16).astype(F32)
    norms = jnp.where(lane < 32, high, pltpu.roll(norms - high, 32, 1)).reshape(16, TOK, BLK)
    block_ref[...] = jnp.concatenate([norms, jnp.zeros_like(norms)], 1).astype(BF16)
    copy = pltpu.make_async_copy(
        block_ref, send_ref.at[:, :, NORM * BLK : (NORM + 1) * BLK], sem
    )
    copy.start()
    copy.wait()


def sum_kernel(parts_ref, send_ref):
    lane = lax.broadcasted_iota(jnp.int32, (2 * TOK, BLK), 1)
    row = lax.broadcasted_iota(jnp.int32, (2 * TOK, BLK), 0)
    for b in range(SPLIT):
        at = slice(b * BLK, (b + 1) * BLK)
        total = parts_ref[0, :, at].astype(F32)
        for q in range(1, 16):
            total = total + parts_ref[q, :, at].astype(F32)
        if b == NORM:
            norm = total + pltpu.roll(total, 96, 1)
            high = norm.astype(BF16).astype(F32)
            norm = jnp.where(lane < 32, high, pltpu.roll(norm - high, 32, 1))
            total = jnp.where(row < TOK, norm, 0.0)
        total = total.astype(BF16)
        for q in range(16):
            send_ref[q, :, at] = total


def gather_kernel(at_ref, ids_ref, other_ids_ref, sums_ref, base_ref, proj_ref):
    for b in range(GRAM):
        upper = b >= SPLIT
        at = (b - SPLIT * upper) * BLK
        block = sums_ref[:, :, at : at + BLK].astype(F32)
        proj_ref[:, b * BLK : (b + 1) * BLK] = block[:, TOK * upper : TOK * upper + TOK].reshape(
            R, BLK
        )
    for n, pick in enumerate(picks_of(at_ref, ids_ref, other_ids_ref)):
        rows = slice(n * TOK, (n + 1) * TOK)
        here = pl.ds(pl.multiple_of(pick * TOK, TOK), TOK)
        base_ref[rows, :] = proj_ref[here, :]
        norm = proj_ref[here, NORM * BLK : (NORM + 1) * BLK]
        norm = norm + pltpu.roll(norm, 96, 1)
        m = n % 16 // 4
        base_ref[rows, NORM * BLK : (NORM + 1) * BLK] = (
            pltpu.roll(norm, BLK - m * NS, 1) if m else norm
        )


def chain_kernel(
    width, at_ref, parts_ref, base_ref, gram_ref, other_ref,
    latent_ref, scalar_ref, oo_ref, oi_ref, oo_rows_ref, oi_rows_ref,
):
    rows = 2 * R
    first_core = at_ref[0] == 0
    for b in range(0, GRAMS, 4):
        at = slice(b * BLK, (b + 4) * BLK)
        mine, theirs = gram_ref[:, at], other_ref[:, at]
        oo_ref[:, at] = jnp.where(first_core, mine, theirs)
        second = jnp.where(first_core, theirs, mine)
        if b < OI:
            oi_ref[:, at] = second
        else:
            oo_ref[:, (b + 4) * BLK : (b + 8) * BLK] = second

    def spread(at):
        return base_ref[:, at * BLK : (at + 1) * BLK]

    def square(t, s, count=1):
        at = (gram_at(t) + s - t) * BLK
        return oo_ref[:, at : at + count * BLK]

    def cross(t, s, count=1):
        at = (cross_at(t) + s - t - 1) * BLK
        return oi_ref[:, at : at + count * BLK]

    for s in range(1, NS):
        for t in range(s):
            at = slice((proj_at(s) + t) * R, (proj_at(s) + t + 1) * R)
            oo_rows_ref[at, :] = square(t, s)
            oi_rows_ref[at, :] = cross(t, s)

    def above(ref, s):
        return ref[proj_at(s) * R : (proj_at(s) + s) * R, :]

    norms = spread(NORM)
    starts = []
    for s in range(NS):
        pieces = []
        for x in range(2):
            for g in range(8):
                at = START + g * 2 * R
                pieces.append(parts_ref[x * NS + s, :, at : at + 2 * R])
        starts.append(jnp.concatenate(pieces, 0))
    start_out = [start[:, R:].astype(F32) for start in starts]
    run_in = [start[:, :R].astype(F32) for start in starts]
    run_out = list(start_out)
    inners, inverses, actives, crossed = [], [], [], []
    grown_norm = jnp.zeros((rows, R), F32)
    for s in range(NS):
        norm = norms[:, s : s + 1]
        entry_out = []
        inner = run_in[s]
        if s > 0:
            inner = inner + spread(inner_at(s))
            total = jnp.zeros((rows, R), F32)
            for t in range(s):
                base = spread(proj_at(s) + t)
                entry_out.append(base + run_out[t])
                total = total + actives[t] * base
            norm = norm + jnp.sum(2.0 * total + grown_norm, -1, keepdims=True)
        inverse = lax.rsqrt(jnp.maximum(norm, 0.0) * (1.0 / width) + EPS)
        inner = inner * inverse
        active = (inner * jax.nn.sigmoid(inner)).astype(BF16)
        latent_ref[:, s * R : (s + 1) * R] = active
        inners.append(inner)
        inverses.append(inverse)
        actives.append(active.astype(F32))
        crossed.append(entry_out)
        grown = dot(active, square(s, s, NS - s))
        if s > 0:
            grown = jnp.concatenate([dot_t(active, above(oo_rows_ref, s)), grown], 1)
        before = run_out[s]
        for t in range(NS):
            run_out[t] = run_out[t] + grown[:, t * R : (t + 1) * R]
        grown_norm = grown_norm + actives[s] * (before + run_out[s])
        if s < NS - 1:
            grown = dot(active, cross(s, s + 1, NS - 1 - s))
            for t in range(s + 1, NS):
                run_in[t] = run_in[t] + grown[:, (t - s - 1) * R : (t - s) * R]
    grads = [run_out[t] + spread(proj_at(NS - 1) + t) for t in range(NS)]
    lane = lax.broadcasted_iota(jnp.int32, (rows, BLK), 1)
    scalars = jnp.zeros((rows, BLK), F32)
    for s in range(NS - 1, -1, -1):
        inner = inners[s]
        sigm = jax.nn.sigmoid(inner)
        d_inner = (grads[s] * sigm * (1.0 + inner * (1.0 - sigm))).astype(BF16)
        latent_ref[:, (NS + s) * R : (NS + s + 1) * R] = d_inner
        inverse = inverses[s]
        total = jnp.sum(d_inner.astype(F32) * inner, -1, keepdims=True)
        scale = inverse * inverse * total * (1.0 / width)
        if s > 0:
            back = dot_t(d_inner, above(oi_rows_ref, s))
        for t in range(s):
            grads[t] = (
                grads[t] + inverse * back[:, t * R : (t + 1) * R] - scale * crossed[s][t]
            )
        scalars = jnp.where(lane == s, inverse, scalars)
        scalars = jnp.where(lane == NS + s, scale, scalars)
    scalar_ref[...] = scalars


def grads_kernel(
    at_ref, ids_ref, other_ids_ref, got_ref, out_w_ref, in_w_ref, latent_ref, scalar_ref,
    give_ref, keep_ref, entry_ref, step_ref,
):
    cols = step_ref.shape[1]
    half = cols // 2
    first_core = at_ref[0] == 0
    scalars = scalar_ref[...]
    inverses = [scalars[:, s : s + 1] for s in range(NS)]
    scales = [scalars[:, NS + s : NS + s + 1] for s in range(NS)]
    places = [
        pl.multiple_of(pick * TOK, TOK) for pick in picks_of(at_ref, ids_ref, other_ids_ref)
    ]

    def active(s):
        return latent_ref[:, s * R : (s + 1) * R]

    def d_inner(s):
        return latent_ref[:, (NS + s) * R : (NS + s + 1) * R]

    def put(s, kind, value):
        low, high = value[:half].reshape(8, 32, R), value[half:].reshape(8, 32, R)
        at = slice(kind * R, (kind + 1) * R)
        give_ref[:, s, :, at] = jnp.where(first_core, high, low).astype(BF16)
        keep_ref[:, s, :, at] = jnp.where(first_core, low, high)

    def both(part, *args):
        return jnp.concatenate(
            [part(got_ref, *args, 0, half), part(got_ref, *args, HALF, half)], 1
        )

    entry = both(first_rows)
    for s in range(NS):
        if s > 0:
            step_ref[...] = both(stores, s)
            entry = entry + jnp.concatenate([step_ref[pl.ds(place, TOK), :] for place in places], 0)
        entry_ref[s] = entry
        put(s, 0, dot_rows((entry * inverses[s]).astype(BF16), d_inner(s)))
        entry = entry + dot(active(s), out_w_ref[s])
    grad = entry
    for s in range(NS - 1, -1, -1):
        put(s, 1, dot_rows(grad.astype(BF16), active(s)))
        if s > 0:
            back = dot_t(d_inner(s), in_w_ref[s])
            grad = grad + inverses[s] * back - scales[s] * entry_ref[s]


def add_kernel(keep_ref, swapped_ref, total_ref):
    for i in range(8):
        total_ref[i] = (keep_ref[i] + swapped_ref[i].astype(F32)).astype(BF16)


def final_kernel(parts_ref, gain_ref, in_ref, out_ref):
    total = parts_ref[0].astype(F32)
    for i in range(1, 8):
        total = total + parts_ref[i].astype(F32)
    gain = gain_ref[...].T
    for j in range(8):
        scale = gain[(j % 4) * 32 : (j % 4) * 32 + 32, j // 4 : j // 4 + 1]
        in_ref[j * 32 : j * 32 + 32, :] = total[j, :, :R] * scale
    out = total[:, :, R:].reshape(2 * BLK, R)
    for i in range(2):
        out_ref[:, i * BLK : (i + 1) * BLK] = out[i * BLK : (i + 1) * BLK].T


def body(first_input, example_ids, out_store, in_store, norm_gain, adapter_in, adapter_out):
    width = first_input.shape[2]
    cols = width // 16
    half = cols // 2
    wide = width // 2
    core = lax.axis_index("c")
    xl = lax.axis_index("xl")
    z = lax.axis_index("z")
    section = lax.axis_index(SECTION)
    quarter = xl * 2 + core
    at = jnp.stack([core, section, xl, quarter]).astype(jnp.int32)
    w_in = adapter_in[0]
    w_out = adapter_out[0]

    ids = example_ids[0]
    other_ids = lax.ppermute(ids, "xl", SWAP)
    send = pl.pallas_call(
        pack_kernel,
        grid_spec=pltpu.PrefetchScalarGridSpec(
            num_scalar_prefetch=1,
            grid=(2,),
            in_specs=[
                pl.BlockSpec((64, wide), lambda i, at: (0, i)),
                pl.BlockSpec((64, wide), lambda i, at: (0, i)),
                pl.BlockSpec((32, wide), lambda i, at: (at[3], i)),
                pl.BlockSpec(
                    (1, 4, 1, 8, 32, R), lambda i, at: (i, at[3] % 2, at[3] // 2, 0, 0, 0)
                ),
                pl.BlockSpec((1, 4, 1, 2, BLK), lambda i, at: (i, at[3] % 2, at[3] // 2, 0, 0)),
                pl.BlockSpec((2, 32, wide), lambda i, at: (at[1] // (NS - 1), 0, i)),
            ],
            out_specs=pl.BlockSpec((8, 32, SENT), lambda i, at: (i, 0, 0)),
            scratch_shapes=[pltpu.VMEM((4 * BLK, 4 * BLK), BF16)],
        ),
        out_shape=jax.ShapeDtypeStruct((16, 32, SENT), BF16),
        compiler_params=LARGE,
        name="pack",
    )(
        at,
        in_store.reshape(64, width),
        out_store.reshape(64, width),
        w_out,
        w_in.reshape(2, 8, 2, 8, 32, R),
        norm_gain.reshape(2, 8, 2, 2, BLK),
        first_input,
    )
    got = lax.all_to_all(send, PLANE, 0, 0, tiled=True)
    other = lax.ppermute(got[:, :, W_LANE:], "c", SWAP)
    start = pl.pallas_call(
        start_kernel,
        out_shape=jax.ShapeDtypeStruct((R, 2 * R), BF16),
        in_specs=[VMEM, VMEM, VMEM, VMEM, pl.BlockSpec(memory_space=pl.ANY)],
        out_specs=VMEM,
        compiler_params=PARAMS,
        cost_estimate=pl.CostEstimate(flops=600000000, bytes_accessed=7000000, transcendentals=0),
        name="start",
    )(first_input, w_out, w_in, norm_gain, got)
    parts, out_w, in_w = pl.pallas_call(
        project_kernel,
        out_shape=(
            jax.ShapeDtypeStruct((16, 2 * TOK, WIDE), BF16),
            jax.ShapeDtypeStruct((NS, R, cols), BF16),
            jax.ShapeDtypeStruct((NS, cols, R), BF16),
        ),
        in_specs=[SMEM, VMEM, VMEM, VMEM],
        out_specs=(VMEM, VMEM, VMEM),
        scratch_shapes=[pltpu.VMEM((R, 2 * SPLIT * BLK), F32)],
        compiler_params=PARAMS,
        cost_estimate=pl.CostEstimate(flops=2000000000, bytes_accessed=9000000, transcendentals=0),
        name="project",
    )(at, got, other, start)
    parts = pl.pallas_call(
        functools.partial(norm_kernel, cols),
        out_shape=jax.ShapeDtypeStruct((16, 2 * TOK, WIDE), BF16),
        in_specs=[SMEM, SMEM, SMEM, VMEM, pl.BlockSpec(memory_space=pl.ANY)],
        out_specs=pl.BlockSpec(memory_space=pl.ANY),
        scratch_shapes=[pltpu.VMEM((16, 2 * TOK, BLK), BF16), pltpu.SemaphoreType.DMA],
        input_output_aliases={4: 0},
        compiler_params=PARAMS,
        name="norms",
    )(at, ids, other_ids, got, parts)
    parts = lax.all_to_all(parts, PLANE, 0, 0, tiled=True)
    sums = pl.pallas_call(
        sum_kernel,
        out_shape=jax.ShapeDtypeStruct((16, 2 * TOK, SPLIT * BLK), BF16),
        in_specs=[VMEM],
        out_specs=VMEM,
        compiler_params=PARAMS,
        name="sums",
    )(parts)
    sums = lax.all_to_all(sums, PLANE, 0, 0, tiled=True)
    gram = sums[:, TOK:, (GRAM - SPLIT) * BLK : (GRAM - SPLIT + GRAMS) * BLK]
    gram = gram.reshape(R, GRAMS * BLK)
    other = lax.ppermute(gram, "c", SWAP)
    base = pl.pallas_call(
        gather_kernel,
        out_shape=jax.ShapeDtypeStruct((2 * R, GRAM * BLK), F32),
        in_specs=[SMEM, SMEM, SMEM, VMEM],
        out_specs=VMEM,
        scratch_shapes=[pltpu.VMEM((R, GRAM * BLK), F32)],
        compiler_params=PARAMS,
        cost_estimate=pl.CostEstimate(flops=0, bytes_accessed=7000000, transcendentals=0),
        name="gather",
    )(at, ids, other_ids, sums)
    latent, scalars = pl.pallas_call(
        functools.partial(chain_kernel, width),
        out_shape=(
            jax.ShapeDtypeStruct((2 * R, 16 * BLK), BF16),
            jax.ShapeDtypeStruct((2 * R, BLK), F32),
        ),
        in_specs=[SMEM, VMEM, VMEM, VMEM, VMEM],
        out_specs=(VMEM, VMEM),
        scratch_shapes=[
            pltpu.VMEM((R, OO * BLK), BF16),
            pltpu.VMEM((R, OI * BLK), BF16),
            pltpu.VMEM((OI * R, R), BF16),
            pltpu.VMEM((OI * R, R), BF16),
        ],
        compiler_params=PARAMS,
        name="chain",
    )(at, parts, base, gram, other)

    give, keep = pl.pallas_call(
        grads_kernel,
        out_shape=(
            jax.ShapeDtypeStruct((8, NS, 32, 2 * R), BF16),
            jax.ShapeDtypeStruct((8, NS, 32, 2 * R), F32),
        ),
        in_specs=[SMEM, SMEM, SMEM] + [VMEM] * 5,
        out_specs=(VMEM, VMEM),
        scratch_shapes=[pltpu.VMEM((NS, 2 * R, cols), F32), pltpu.VMEM((R, cols), F32)],
        compiler_params=PARAMS,
        name="grads",
    )(at, ids, other_ids, got, out_w, in_w, latent, scalars)
    swapped = lax.ppermute(give, "c", SWAP)
    total = pl.pallas_call(
        add_kernel,
        out_shape=jax.ShapeDtypeStruct((8, NS, 32, 2 * R), BF16),
        in_specs=[VMEM, VMEM],
        out_specs=VMEM,
        compiler_params=PARAMS,
        name="add",
    )(keep, swapped).reshape(64, 32, 2 * R)
    block = (xl * NS + z) * 2 + core
    gain = lax.dynamic_slice_in_dim(norm_gain[0], block * half, half, 0)
    total, gain = lax.optimization_barrier((total, gain))
    total = lax.all_to_all(total, ("z",) + SECTION, 0, 0, tiled=True)
    grad_in, grad_out = pl.pallas_call(
        final_kernel,
        out_shape=(
            jax.ShapeDtypeStruct((half, R), F32),
            jax.ShapeDtypeStruct((R, half), F32),
        ),
        in_specs=[VMEM, VMEM],
        out_specs=(VMEM, VMEM),
        compiler_params=PARAMS,
        name="final",
    )(total.reshape(8, 8, 32, 2 * R), gain.reshape(2, BLK))
    return (grad_in[None], grad_out[None])


def solution(mesh):
    fine = Mesh(mesh.devices.reshape(2, 8, 2, 4, 2), ("xl", "z", "c", "y", "xh"))
    dp = ("xl", "z", "c")
    placed = (
        P(None, dp, None),
        P(dp, None, None),
        P(SECTION, dp, None, None),
        P(SECTION, dp, None, None),
        P(SECTION, None),
        P(SECTION, None, None),
        P(SECTION, None, None),
    )
    return jax.shard_map(
        body,
        mesh=fine,
        in_specs=placed,
        out_specs=(P(SECTION, dp, None), P(SECTION, None, dp)),
        check_vma=False,
    )
```

```python
import functools

import jax
import jax.numpy as jnp
from jax import lax
from jax.experimental import pallas as pl
from jax.experimental.pallas import tpu as pltpu
from jax.sharding import Mesh, PartitionSpec as P

F32 = jnp.float32
BF16 = jnp.bfloat16
EPS = 1e-05
PLANE = ("xl", "y", "xh")
SECTION = ("y", "xh")
SWAP = [(0, 1), (1, 0)]
NS = 8
R = 128
TOK = 8
MIC = 4
BLK = 128
HALF = 1024
W_LANE = 2 * HALF
SENT = 3072
PROJ = 29
NORM = 34
GRAM = 37
GRAMS = 32
SPLIT = 35
START = SPLIT * BLK
WIDE = START + 16 * BLK
OO = 36
OI = 28
LARGE = pltpu.CompilerParams(vmem_limit_bytes=56 * 1024 * 1024)
PARAMS = pltpu.CompilerParams(vmem_limit_bytes=16 * 1024 * 1024)
VMEM = pl.BlockSpec(memory_space=pltpu.VMEM)
SMEM = pl.BlockSpec(memory_space=pltpu.SMEM)


def gram_at(t):
    return sum(NS - i for i in range(t))


def cross_at(t):
    return sum(NS - 1 - i for i in range(t))


def proj_at(s):
    return s * (s - 1) // 2


def inner_at(s):
    return PROJ + s - 1 + (PROJ + s - 1 >= NORM)


def dot_t(a, b):
    return lax.dot_general(a, b, (((1,), (1,)), ((), ())), preferred_element_type=F32)


def dot_rows(a, b):
    return lax.dot_general(a, b, (((0,), (0,)), ((), ())), preferred_element_type=F32)


def dot(a, b):
    return jnp.dot(a, b, preferred_element_type=F32)


def split(x):
    high = x.astype(BF16)
    return high, (x - high.astype(F32)).astype(BF16)


def section_here():
    return lax.axis_index("y") * 2 + lax.axis_index("xh")


def pack_kernel(in_ref, out_ref, w_out_ref, w_in_ref, gain_ref, first_ref, send_ref, turn_ref):
    section = section_here()
    quarter = lax.axis_index("xl") * 2 + lax.axis_index("c")
    zq = pl.program_id(1)

    @pl.when((pl.program_id(0) == 0) & (zq == 0))
    def _():
        shape = (4 * BLK, 4 * BLK)
        row = lax.broadcasted_iota(jnp.int32, shape, 0)
        col = lax.broadcasted_iota(jnp.int32, shape, 1)
        same = (row // BLK == col % BLK // 32) & (row % BLK // 32 == col // BLK)
        same = same & (row % 32 == col % 32)
        turn_ref[...] = jnp.where(same, 1.0, 0.0).astype(BF16)

    @pl.when(zq == 0)
    def _():
        near = quarter % 2 * 4
        gain = gain_ref[0, pl.ds(near, 4), quarter // 2].reshape(8, BLK).T
        for s in range(NS):
            for j in range(4):
                column = 2 * j + s // 4
                scale = gain[(s % 4) * 32 : (s % 4) * 32 + 32, column : column + 1]
                to = W_LANE + 512 + j * BLK
                rows = w_in_ref[0, near + j, quarter // 2, s].astype(F32)
                send_ref[s, :, to : to + BLK] = (rows * scale).astype(BF16)

    pieces, places = [], []
    micro = section // (NS - 1) * 2
    rank = pl.multiple_of(quarter * 32, 32)
    for c in range(2):
        for h in range(2):
            lanes = [(j * 4 + c * 2 + h) * BLK for j in range(4)]

            def piece_of(ref, *at, lanes=lanes):
                return jnp.concatenate([ref[*at, lane : lane + BLK] for lane in lanes], 1)

            for ref, half, at, other in (
                (in_ref, 0, c * HALF, 0),
                (in_ref, 1, c * HALF + 256, 0),
                (out_ref, 0, c * HALF + 512, NS - 1),
                (out_ref, 1, c * HALF + 768, NS - 1),
            ):
                piece = piece_of(ref, slice(half * 32, half * 32 + 32))
                first = piece_of(first_ref, micro + half, slice(None))
                pieces.append(jnp.where(section == other, first, piece))
                places.append((4 * h, at))
            pieces.append(piece_of(w_out_ref, pl.ds(rank, 32)))
            places.append((4 * h, W_LANE + c * 256))
    turned = dot(jnp.concatenate(pieces, 0), turn_ref[...]).astype(BF16)
    for n, (first, at) in enumerate(places):
        to = pl.ds(pl.multiple_of(at + zq * BLK, BLK), BLK)
        for i in range(4):
            send_ref[first + i, :, to] = turned[32 * n : 32 * n + 32, i * BLK : (i + 1) * BLK]


def start_kernel(first_ref, w_out_ref, w_in_ref, gain_ref, after_ref, start_ref):
    del after_ref
    flat = first_ref[...].reshape(R, first_ref.shape[2])
    scaled = (flat.astype(F32) * gain_ref[...]).astype(BF16)
    start_ref[:, :R] = dot(scaled, w_in_ref[...]).astype(BF16)
    start_ref[:, R:] = dot_t(flat, w_out_ref[...]).astype(BF16)


def stores(got_ref, s, at, cols):
    pieces = []
    for x in range(2):
        for i in range(2):
            a, b = at + i * 256, at + 512 + i * 256
            pieces.append(
                got_ref[x * NS + s, :, pl.ds(a, cols)].astype(F32)
                - got_ref[x * NS + s - 1, :, pl.ds(b, cols)].astype(F32)
            )
    return jnp.concatenate(pieces, 0)


def first_rows(got_ref, at, cols):
    pieces = []
    for x in range(2):
        for m in range(MIC):
            q = x * NS + (0 if m < 2 else NS - 1)
            lane = at + m // 2 * 512 + m % 2 * 256
            pieces.append(got_ref[q, :, pl.ds(lane, cols)])
    return jnp.concatenate(pieces, 0).astype(F32)


def picks_of(ids_ref, other_ids_ref):
    picks = []
    for x in range(2):
        here = lax.axis_index("xl") == x
        for m in range(MIC):
            for j in range(4):
                picks.append(x * NS + jnp.where(here, ids_ref[m, j], other_ids_ref[m, j]))
    return picks


def running_sums(got_ref, cols):
    running = None
    for s in range(1, NS):
        step = jnp.concatenate(
            [stores(got_ref, s, 0, cols // 2), stores(got_ref, s, HALF, cols // 2)], 1
        )
        running = step if running is None else running + step
        yield s, running


def project_kernel(
    got_ref, other_ref, start_ref, send_ref, out_w_ref, in_w_ref, wide_ref
):
    cols = in_w_ref.shape[1]
    first_core = lax.axis_index("c") == 0
    for s in range(NS):
        for x in range(2):
            mine = got_ref[x * NS + s, :, W_LANE:SENT]
            theirs = other_ref[x * NS + s]
            for c in range(2):
                part = jnp.where(first_core == (c == 0), mine, theirs)
                k = 2 * x + c
                out_w_ref[s, 32 * k : 32 * k + 32, :] = part[:, :cols]
                for g in range(4):
                    row = k * BLK + g * 32
                    lane = cols + g * BLK
                    in_w_ref[s, row : row + 32, :] = part[:, lane : lane + BLK]
    for s, running in running_sums(got_ref, cols):
        rounded = running.astype(BF16)
        count = s if s < NS - 1 else NS
        at = proj_at(s) * BLK
        wide_ref[:, at : at + count * BLK] = dot_t(
            rounded, out_w_ref[0:count].reshape(count * R, cols)
        )
        at = inner_at(s) * BLK
        wide_ref[:, at : at + BLK] = dot(rounded, in_w_ref[s])
    for b in (NORM, GRAM + GRAMS):
        wide_ref[:, b * BLK : (b + 1) * BLK] = jnp.zeros((R, BLK), F32)

    square = [(t, s) for t in range(NS) for s in range(t, NS)]

    @pl.when(first_core)
    def _():
        for t in range(5):
            at = (GRAM + gram_at(t)) * BLK
            wide_ref[:, at : at + (NS - t) * BLK] = dot_t(
                out_w_ref[t], out_w_ref[t:NS].reshape((NS - t) * R, cols)
            )
        for i in range(gram_at(5), GRAMS):
            t, s = square[i]
            at = (GRAM + i) * BLK
            wide_ref[:, at : at + BLK] = dot_t(out_w_ref[t], out_w_ref[s])

    @pl.when(jnp.logical_not(first_core))
    def _():
        for t in range(NS - 1):
            for s in range(t + 1, NS):
                at = (GRAM + cross_at(t) + s - t - 1) * BLK
                wide_ref[:, at : at + BLK] = dot(out_w_ref[t], in_w_ref[s])
        for i in range(GRAMS, OO):
            t, s = square[i]
            at = (GRAM + OI + i - GRAMS) * BLK
            wide_ref[:, at : at + BLK] = dot_t(out_w_ref[t], out_w_ref[s])

    for b in range(SPLIT):
        pair = [
            wide_ref[:, at * BLK : (at + 1) * BLK].reshape(16, TOK, BLK) for at in (b, SPLIT + b)
        ]
        send_ref[:, :, b * BLK : (b + 1) * BLK] = jnp.concatenate(pair, 1).astype(BF16)
    for g in range(8):
        at = START + g * 2 * R
        for q in range(16):
            send_ref[q, :, at : at + 2 * R] = start_ref[g * 16 : (g + 1) * 16, :]


def norm_kernel(
    cols, ids_ref, other_ids_ref, got_ref, before_ref, send_ref, block_ref, sem
):
    del before_ref
    picks = picks_of(ids_ref, other_ids_ref)
    placed = [[] for _ in range(MIC)]
    first = jnp.concatenate(
        [first_rows(got_ref, 0, cols // 2), first_rows(got_ref, HALF, cols // 2)], 1
    )
    for x in range(2):
        rows = first[x * R : (x + 1) * R]
        for e in range(NS):
            for m in range(MIC):
                total = jnp.zeros((TOK, cols), F32)
                for j in range(4):
                    n = 4 * m + j
                    total = jnp.where(
                        picks[16 * x + n] == x * NS + e, rows[n * TOK : (n + 1) * TOK], total
                    )
                placed[m].append(total)
    placed = [jnp.concatenate(blocks, 0) for blocks in placed]
    lane = lax.broadcasted_iota(jnp.int32, (R, BLK), 1)
    norms = jnp.zeros((R, BLK), F32)
    for m in range(MIC):
        part = jnp.sum(placed[m] * placed[m], -1, keepdims=True)
        norms = jnp.where(lane == m * NS, part, norms)
    for s, running in running_sums(got_ref, cols):
        for m in range(MIC):
            entry = running + placed[m]
            part = jnp.sum(entry * entry, -1, keepdims=True)
            norms = jnp.where(lane == m * NS + s, part, norms)
    high = norms.astype(BF16).astype(F32)
    norms = jnp.where(lane < 32, high, pltpu.roll(norms - high, 32, 1)).reshape(16, TOK, BLK)
    block_ref[...] = jnp.concatenate([norms, jnp.zeros_like(norms)], 1).astype(BF16)
    copy = pltpu.make_async_copy(
        block_ref, send_ref.at[:, :, NORM * BLK : (NORM + 1) * BLK], sem
    )
    copy.start()
    copy.wait()


def sum_kernel(parts_ref, send_ref):
    lane = lax.broadcasted_iota(jnp.int32, (2 * TOK, BLK), 1)
    row = lax.broadcasted_iota(jnp.int32, (2 * TOK, BLK), 0)
    for b in range(SPLIT):
        at = slice(b * BLK, (b + 1) * BLK)
        total = parts_ref[0, :, at].astype(F32)
        for q in range(1, 16):
            total = total + parts_ref[q, :, at].astype(F32)
        if b == NORM:
            norm = total + pltpu.roll(total, 96, 1)
            high = norm.astype(BF16).astype(F32)
            norm = jnp.where(lane < 32, high, pltpu.roll(norm - high, 32, 1))
            total = jnp.where(row < TOK, norm, 0.0)
        total = total.astype(BF16)
        for q in range(16):
            send_ref[q, :, at] = total


def gather_kernel(ids_ref, other_ids_ref, sums_ref, base_ref, proj_ref):
    for b in range(GRAM):
        upper = b >= SPLIT
        at = (b - SPLIT * upper) * BLK
        block = sums_ref[:, :, at : at + BLK].astype(F32)
        proj_ref[:, b * BLK : (b + 1) * BLK] = block[:, TOK * upper : TOK * upper + TOK].reshape(
            R, BLK
        )
    for n, pick in enumerate(picks_of(ids_ref, other_ids_ref)):
        rows = slice(n * TOK, (n + 1) * TOK)
        here = pl.ds(pl.multiple_of(pick * TOK, TOK), TOK)
        base_ref[rows, :] = proj_ref[here, :]
        norm = proj_ref[here, NORM * BLK : (NORM + 1) * BLK]
        norm = norm + pltpu.roll(norm, 96, 1)
        m = n % 16 // 4
        base_ref[rows, NORM * BLK : (NORM + 1) * BLK] = (
            pltpu.roll(norm, BLK - m * NS, 1) if m else norm
        )


def chain_kernel(
    width, parts_ref, base_ref, gram_ref, other_ref,
    latent_ref, scalar_ref, oo_ref, oi_ref, oo_rows_ref, oi_rows_ref,
):
    rows = 2 * R
    first_core = lax.axis_index("c") == 0
    for b in range(0, GRAMS, 4):
        at = slice(b * BLK, (b + 4) * BLK)
        mine, theirs = gram_ref[:, at], other_ref[:, at]
        oo_ref[:, at] = jnp.where(first_core, mine, theirs)
        second = jnp.where(first_core, theirs, mine)
        if b < OI:
            oi_ref[:, at] = second
        else:
            oo_ref[:, (b + 4) * BLK : (b + 8) * BLK] = second

    def spread(at):
        return base_ref[:, at * BLK : (at + 1) * BLK]

    def square(t, s, count=1):
        at = (gram_at(t) + s - t) * BLK
        return oo_ref[:, at : at + count * BLK]

    def cross(t, s, count=1):
        at = (cross_at(t) + s - t - 1) * BLK
        return oi_ref[:, at : at + count * BLK]

    for s in range(1, NS):
        for t in range(s):
            at = slice((proj_at(s) + t) * R, (proj_at(s) + t + 1) * R)
            oo_rows_ref[at, :] = square(t, s)
            oi_rows_ref[at, :] = cross(t, s)

    def above(ref, s):
        return ref[proj_at(s) * R : (proj_at(s) + s) * R, :]

    norms = spread(NORM)
    starts = []
    for s in range(NS):
        pieces = []
        for x in range(2):
            for g in range(8):
                at = START + g * 2 * R
                pieces.append(parts_ref[x * NS + s, :, at : at + 2 * R])
        starts.append(jnp.concatenate(pieces, 0))
    start_out = [start[:, R:].astype(F32) for start in starts]
    run_in = [start[:, :R].astype(F32) for start in starts]
    run_out = list(start_out)
    inners, inverses, actives, crossed = [], [], [], []
    grown_norm = jnp.zeros((rows, R), F32)
    for s in range(NS):
        norm = norms[:, s : s + 1]
        entry_out = []
        inner = run_in[s]
        if s > 0:
            inner = inner + spread(inner_at(s))
            total = jnp.zeros((rows, R), F32)
            for t in range(s):
                base = spread(proj_at(s) + t)
                entry_out.append(base + run_out[t])
                total = total + actives[t] * base
            norm = norm + jnp.sum(2.0 * total + grown_norm, -1, keepdims=True)
        inverse = lax.rsqrt(jnp.maximum(norm, 0.0) * (1.0 / width) + EPS)
        inner = inner * inverse
        active = (inner * jax.nn.sigmoid(inner)).astype(BF16)
        latent_ref[:, s * R : (s + 1) * R] = active
        inners.append(inner)
        inverses.append(inverse)
        actives.append(active.astype(F32))
        crossed.append(entry_out)
        grown = dot(active, square(s, s, NS - s))
        if s > 0:
            grown = jnp.concatenate([dot_t(active, above(oo_rows_ref, s)), grown], 1)
        before = run_out[s]
        for t in range(NS):
            run_out[t] = run_out[t] + grown[:, t * R : (t + 1) * R]
        grown_norm = grown_norm + actives[s] * (before + run_out[s])
        if s < NS - 1:
            grown = dot(active, cross(s, s + 1, NS - 1 - s))
            for t in range(s + 1, NS):
                run_in[t] = run_in[t] + grown[:, (t - s - 1) * R : (t - s) * R]
    grads = [run_out[t] + spread(proj_at(NS - 1) + t) for t in range(NS)]
    lane = lax.broadcasted_iota(jnp.int32, (rows, BLK), 1)
    scalars = jnp.zeros((rows, BLK), F32)
    for s in range(NS - 1, -1, -1):
        inner = inners[s]
        sigm = jax.nn.sigmoid(inner)
        d_inner = (grads[s] * sigm * (1.0 + inner * (1.0 - sigm))).astype(BF16)
        latent_ref[:, (NS + s) * R : (NS + s + 1) * R] = d_inner
        inverse = inverses[s]
        total = jnp.sum(d_inner.astype(F32) * inner, -1, keepdims=True)
        scale = inverse * inverse * total * (1.0 / width)
        if s > 0:
            back = dot_t(d_inner, above(oi_rows_ref, s))
        for t in range(s):
            grads[t] = (
                grads[t] + inverse * back[:, t * R : (t + 1) * R] - scale * crossed[s][t]
            )
        scalars = jnp.where(lane == s, inverse, scalars)
        scalars = jnp.where(lane == NS + s, scale, scalars)
    scalar_ref[...] = scalars


def grads_kernel(
    ids_ref, other_ids_ref, got_ref, out_w_ref, in_w_ref, latent_ref, scalar_ref,
    give_ref, keep_ref, entry_ref, step_ref,
):
    cols = step_ref.shape[1]
    half = cols // 2
    first_core = lax.axis_index("c") == 0
    scalars = scalar_ref[...]
    inverses = [scalars[:, s : s + 1] for s in range(NS)]
    scales = [scalars[:, NS + s : NS + s + 1] for s in range(NS)]
    places = [
        pl.multiple_of(pick * TOK, TOK) for pick in picks_of(ids_ref, other_ids_ref)
    ]

    def active(s):
        return latent_ref[:, s * R : (s + 1) * R]

    def d_inner(s):
        return latent_ref[:, (NS + s) * R : (NS + s + 1) * R]

    def put(s, kind, value):
        low, high = value[:half].reshape(8, 32, R), value[half:].reshape(8, 32, R)
        at = slice(kind * R, (kind + 1) * R)
        give_ref[:, s, :, at] = jnp.where(first_core, high, low).astype(BF16)
        keep_ref[:, s, :, at] = jnp.where(first_core, low, high)

    def both(part, *args):
        return jnp.concatenate(
            [part(got_ref, *args, 0, half), part(got_ref, *args, HALF, half)], 1
        )

    entry = both(first_rows)
    for s in range(NS):
        if s > 0:
            step_ref[...] = both(stores, s)
            entry = entry + jnp.concatenate([step_ref[pl.ds(place, TOK), :] for place in places], 0)
        entry_ref[s] = entry
        put(s, 0, dot_rows((entry * inverses[s]).astype(BF16), d_inner(s)))
        entry = entry + dot(active(s), out_w_ref[s])
    grad = entry
    for s in range(NS - 1, -1, -1):
        put(s, 1, dot_rows(grad.astype(BF16), active(s)))
        if s > 0:
            back = dot_t(d_inner(s), in_w_ref[s])
            grad = grad + inverses[s] * back - scales[s] * entry_ref[s]


def add_kernel(keep_ref, swapped_ref, total_ref):
    for i in range(8):
        total_ref[i] = (keep_ref[i] + swapped_ref[i].astype(F32)).astype(BF16)


def final_kernel(parts_ref, gain_ref, in_ref, out_ref):
    total = parts_ref[0].astype(F32)
    for i in range(1, 8):
        total = total + parts_ref[i].astype(F32)
    gain = gain_ref[...].T
    for j in range(8):
        scale = gain[(j % 4) * 32 : (j % 4) * 32 + 32, j // 4 : j // 4 + 1]
        in_ref[j * 32 : j * 32 + 32, :] = total[j, :, :R] * scale
    out = total[:, :, R:].reshape(2 * BLK, R)
    for i in range(2):
        out_ref[:, i * BLK : (i + 1) * BLK] = out[i * BLK : (i + 1) * BLK].T


def body(first_input, example_ids, out_store, in_store, norm_gain, adapter_in, adapter_out):
    width = first_input.shape[2]
    cols = width // 16
    half = cols // 2
    core = lax.axis_index("c")
    xl = lax.axis_index("xl")
    z = lax.axis_index("z")
    w_in = adapter_in[0]
    w_out = adapter_out[0]

    ids = example_ids[0]
    other_ids = lax.ppermute(ids, "xl", SWAP)
    quarter = width // 4
    send = pl.pallas_call(
        pack_kernel,
        grid=(2, 2),
        in_specs=[
            pl.BlockSpec((64, quarter), lambda i, j: (0, 2 * i + j)),
            pl.BlockSpec((64, quarter), lambda i, j: (0, 2 * i + j)),
            pl.BlockSpec((R, quarter), lambda i, j: (0, 2 * i + j)),
            pl.BlockSpec((1, 8, 2, 8, 32, R), lambda i, j: (i, 0, 0, 0, 0, 0)),
            pl.BlockSpec((1, 8, 2, 2, BLK), lambda i, j: (i, 0, 0, 0, 0)),
            pl.BlockSpec((MIC, 32, quarter), lambda i, j: (0, 0, 2 * i + j)),
        ],
        out_specs=pl.BlockSpec((8, 32, SENT), lambda i, j: (i, 0, 0)),
        scratch_shapes=[pltpu.VMEM((4 * BLK, 4 * BLK), BF16)],
        out_shape=jax.ShapeDtypeStruct((16, 32, SENT), BF16),
        compiler_params=LARGE,
        name="pack",
    )(
        in_store.reshape(64, width),
        out_store.reshape(64, width),
        w_out,
        w_in.reshape(2, 8, 2, 8, 32, R),
        norm_gain.reshape(2, 8, 2, 2, BLK),
        first_input,
    )
    got = lax.all_to_all(send, PLANE, 0, 0, tiled=True)
    other = lax.ppermute(got[:, :, W_LANE:], "c", SWAP)
    start = pl.pallas_call(
        start_kernel,
        out_shape=jax.ShapeDtypeStruct((R, 2 * R), BF16),
        in_specs=[VMEM, VMEM, VMEM, VMEM, pl.BlockSpec(memory_space=pl.ANY)],
        out_specs=VMEM,
        compiler_params=PARAMS,
        cost_estimate=pl.CostEstimate(flops=600000000, bytes_accessed=7000000, transcendentals=0),
        name="start",
    )(first_input, w_out, w_in, norm_gain, got)
    parts, out_w, in_w = pl.pallas_call(
        project_kernel,
        out_shape=(
            jax.ShapeDtypeStruct((16, 2 * TOK, WIDE), BF16),
            jax.ShapeDtypeStruct((NS, R, cols), BF16),
            jax.ShapeDtypeStruct((NS, cols, R), BF16),
        ),
        in_specs=[VMEM, VMEM, VMEM],
        out_specs=(VMEM, VMEM, VMEM),
        scratch_shapes=[pltpu.VMEM((R, 2 * SPLIT * BLK), F32)],
        compiler_params=PARAMS,
        cost_estimate=pl.CostEstimate(flops=2000000000, bytes_accessed=9000000, transcendentals=0),
        name="project",
    )(got, other, start)
    parts = pl.pallas_call(
        functools.partial(norm_kernel, cols),
        out_shape=jax.ShapeDtypeStruct((16, 2 * TOK, WIDE), BF16),
        in_specs=[SMEM, SMEM, VMEM, pl.BlockSpec(memory_space=pl.ANY)],
        out_specs=pl.BlockSpec(memory_space=pl.ANY),
        scratch_shapes=[pltpu.VMEM((16, 2 * TOK, BLK), BF16), pltpu.SemaphoreType.DMA],
        input_output_aliases={3: 0},
        compiler_params=PARAMS,
        name="norms",
    )(ids, other_ids, got, parts)
    parts = lax.all_to_all(parts, PLANE, 0, 0, tiled=True)
    sums = pl.pallas_call(
        sum_kernel,
        out_shape=jax.ShapeDtypeStruct((16, 2 * TOK, SPLIT * BLK), BF16),
        in_specs=[VMEM],
        out_specs=VMEM,
        compiler_params=PARAMS,
        name="sums",
    )(parts)
    sums = lax.all_to_all(sums, PLANE, 0, 0, tiled=True)
    gram = sums[:, TOK:, (GRAM - SPLIT) * BLK : (GRAM - SPLIT + GRAMS) * BLK]
    gram = gram.reshape(R, GRAMS * BLK)
    other = lax.ppermute(gram, "c", SWAP)
    base = pl.pallas_call(
        gather_kernel,
        out_shape=jax.ShapeDtypeStruct((2 * R, GRAM * BLK), F32),
        in_specs=[SMEM, SMEM, VMEM],
        out_specs=VMEM,
        scratch_shapes=[pltpu.VMEM((R, GRAM * BLK), F32)],
        compiler_params=PARAMS,
        cost_estimate=pl.CostEstimate(flops=0, bytes_accessed=7000000, transcendentals=0),
        name="gather",
    )(ids, other_ids, sums)
    latent, scalars = pl.pallas_call(
        functools.partial(chain_kernel, width),
        out_shape=(
            jax.ShapeDtypeStruct((2 * R, 16 * BLK), BF16),
            jax.ShapeDtypeStruct((2 * R, BLK), F32),
        ),
        in_specs=[VMEM] * 4,
        out_specs=(VMEM, VMEM),
        scratch_shapes=[
            pltpu.VMEM((R, OO * BLK), BF16),
            pltpu.VMEM((R, OI * BLK), BF16),
            pltpu.VMEM((OI * R, R), BF16),
            pltpu.VMEM((OI * R, R), BF16),
        ],
        compiler_params=PARAMS,
        name="chain",
    )(parts, base, gram, other)

    give, keep = pl.pallas_call(
        grads_kernel,
        out_shape=(
            jax.ShapeDtypeStruct((8, NS, 32, 2 * R), BF16),
            jax.ShapeDtypeStruct((8, NS, 32, 2 * R), F32),
        ),
        in_specs=[SMEM, SMEM] + [VMEM] * 5,
        out_specs=(VMEM, VMEM),
        scratch_shapes=[pltpu.VMEM((NS, 2 * R, cols), F32), pltpu.VMEM((R, cols), F32)],
        compiler_params=PARAMS,
        name="grads",
    )(ids, other_ids, got, out_w, in_w, latent, scalars)
    swapped = lax.ppermute(give, "c", SWAP)
    total = pl.pallas_call(
        add_kernel,
        out_shape=jax.ShapeDtypeStruct((8, NS, 32, 2 * R), BF16),
        in_specs=[VMEM, VMEM],
        out_specs=VMEM,
        compiler_params=PARAMS,
        name="add",
    )(keep, swapped).reshape(64, 32, 2 * R)
    block = (xl * NS + z) * 2 + core
    gain = lax.dynamic_slice_in_dim(norm_gain[0], block * half, half, 0)
    total, gain = lax.optimization_barrier((total, gain))
    total = lax.all_to_all(total, ("z",) + SECTION, 0, 0, tiled=True)
    grad_in, grad_out = pl.pallas_call(
        final_kernel,
        out_shape=(
            jax.ShapeDtypeStruct((half, R), F32),
            jax.ShapeDtypeStruct((R, half), F32),
        ),
        in_specs=[VMEM, VMEM],
        out_specs=(VMEM, VMEM),
        compiler_params=PARAMS,
        name="final",
    )(total.reshape(8, 8, 32, 2 * R), gain.reshape(2, BLK))
    return (grad_in[None], grad_out[None])


def solution(mesh):
    fine = Mesh(mesh.devices.reshape(2, 8, 2, 4, 2), ("xl", "z", "c", "y", "xh"))
    dp = ("xl", "z", "c")
    placed = (
        P(None, dp, None),
        P(dp, None, None),
        P(SECTION, dp, None, None),
        P(SECTION, dp, None, None),
        P(SECTION, None),
        P(SECTION, None, None),
        P(SECTION, None, None),
    )
    return jax.shard_map(
        body,
        mesh=fine,
        in_specs=placed,
        out_specs=(P(SECTION, dp, None), P(SECTION, None, dp)),
        check_vma=False,
    )
```

```python
import functools

import jax
import jax.numpy as jnp
from jax import lax
from jax.experimental import pallas as pl
from jax.experimental.pallas import tpu as pltpu
from jax.sharding import Mesh, PartitionSpec as P

F32 = jnp.float32
BF16 = jnp.bfloat16
EPS = 1e-05
PLANE = ("xl", "y", "xh")
SECTION = ("y", "xh")
SWAP = [(0, 1), (1, 0)]
NS = 8
R = 128
TOK = 8
MIC = 4
BLK = 128
HALF = 1024
W_LANE = 2 * HALF
SENT = 3072
PROJ = 29
NORM = 34
GRAM = 37
GRAMS = 32
SPLIT = 35
START = SPLIT * BLK
WIDE = START + 16 * BLK
OO = 36
OI = 28
LARGE = pltpu.CompilerParams(vmem_limit_bytes=56 * 1024 * 1024)
PARAMS = pltpu.CompilerParams(vmem_limit_bytes=16 * 1024 * 1024)
VMEM = pl.BlockSpec(memory_space=pltpu.VMEM)
SMEM = pl.BlockSpec(memory_space=pltpu.SMEM)


def gram_at(t):
    return sum(NS - i for i in range(t))


def cross_at(t):
    return sum(NS - 1 - i for i in range(t))


def proj_at(s):
    return s * (s - 1) // 2


def inner_at(s):
    return PROJ + s - 1 + (PROJ + s - 1 >= NORM)


def dot_t(a, b):
    return lax.dot_general(a, b, (((1,), (1,)), ((), ())), preferred_element_type=F32)


def dot_rows(a, b):
    return lax.dot_general(a, b, (((0,), (0,)), ((), ())), preferred_element_type=F32)


def dot(a, b):
    return jnp.dot(a, b, preferred_element_type=F32)


def split(x):
    high = x.astype(BF16)
    return high, (x - high.astype(F32)).astype(BF16)


def section_here():
    return lax.axis_index("y") * 2 + lax.axis_index("xh")


def pack_kernel(
    in_ref, out_ref, w_out_ref, w_in_ref, gain_ref, first_ref, send_ref, turn_ref
):
    section = section_here()

    @pl.when(pl.program_id(0) == 0)
    def _():
        shape = (4 * BLK, 4 * BLK)
        row = lax.broadcasted_iota(jnp.int32, shape, 0)
        col = lax.broadcasted_iota(jnp.int32, shape, 1)
        same = (row // BLK == col % BLK // 32) & (row % BLK // 32 == col // BLK)
        same = same & (row % 32 == col % 32)
        turn_ref[...] = jnp.where(same, 1.0, 0.0).astype(BF16)

    gain = gain_ref[...].reshape(8, BLK).T
    for s in range(NS):
        for j in range(4):
            column = 2 * j + s // 4
            scale = gain[(s % 4) * 32 : (s % 4) * 32 + 32, column : column + 1]
            to = W_LANE + 512 + j * BLK
            send_ref[s, :, to : to + BLK] = (w_in_ref[0, j, 0, s].astype(F32) * scale).astype(BF16)

    pieces, places = [], []
    for c in range(2):
        for zq in range(2):
            to = c * 256 + zq * BLK
            for h in range(2):
                lanes = [((4 * zq + j) * 4 + c * 2 + h) * BLK for j in range(4)]
                for ref, row, at, other in (
                    (in_ref, 0, c * HALF + zq * BLK, 0),
                    (in_ref, 32, c * HALF + 256 + zq * BLK, 0),
                    (out_ref, 0, c * HALF + 512 + zq * BLK, NS - 1),
                    (out_ref, 32, c * HALF + 768 + zq * BLK, NS - 1),
                    (w_out_ref, 0, W_LANE + to, None),
                ):
                    piece = jnp.concatenate(
                        [ref[row : row + 32, lane : lane + BLK] for lane in lanes], 1
                    )
                    if other is not None:
                        first = jnp.concatenate(
                            [first_ref[row // 32, :, lane : lane + BLK] for lane in lanes], 1
                        )
                        piece = jnp.where(section == other, first, piece)
                    pieces.append(piece)
                    places.append((4 * h, at))
    turned = dot(jnp.concatenate(pieces, 0), turn_ref[...]).astype(BF16)
    for n, (first, at) in enumerate(places):
        for i in range(4):
            send_ref[first + i, :, at : at + BLK] = turned[
                32 * n : 32 * n + 32, i * BLK : (i + 1) * BLK
            ]


def start_kernel(first_ref, w_out_ref, w_in_ref, gain_ref, after_ref, start_ref):
    del after_ref
    flat = first_ref[...].reshape(R, first_ref.shape[2])
    scaled = (flat.astype(F32) * gain_ref[...]).astype(BF16)
    start_ref[:, :R] = dot(scaled, w_in_ref[...]).astype(BF16)
    start_ref[:, R:] = dot_t(flat, w_out_ref[...]).astype(BF16)


def stores(got_ref, s, at, cols):
    pieces = []
    for x in range(2):
        for i in range(2):
            a, b = at + i * 256, at + 512 + i * 256
            pieces.append(
                got_ref[x * NS + s, :, pl.ds(a, cols)].astype(F32)
                - got_ref[x * NS + s - 1, :, pl.ds(b, cols)].astype(F32)
            )
    return jnp.concatenate(pieces, 0)


def first_rows(got_ref, at, cols):
    pieces = []
    for x in range(2):
        for m in range(MIC):
            q = x * NS + (0 if m < 2 else NS - 1)
            lane = at + m // 2 * 512 + m % 2 * 256
            pieces.append(got_ref[q, :, pl.ds(lane, cols)])
    return jnp.concatenate(pieces, 0).astype(F32)


def picks_of(ids_ref, other_ids_ref):
    picks = []
    for x in range(2):
        here = lax.axis_index("xl") == x
        for m in range(MIC):
            for j in range(4):
                picks.append(x * NS + jnp.where(here, ids_ref[m, j], other_ids_ref[m, j]))
    return picks


def running_sums(got_ref, cols):
    running = None
    for s in range(1, NS):
        step = jnp.concatenate(
            [stores(got_ref, s, 0, cols // 2), stores(got_ref, s, HALF, cols // 2)], 1
        )
        running = step if running is None else running + step
        yield s, running


def project_kernel(
    got_ref, other_ref, start_ref, send_ref, out_w_ref, in_w_ref, wide_ref
):
    cols = in_w_ref.shape[1]
    first_core = lax.axis_index("c") == 0
    for s in range(NS):
        for x in range(2):
            mine = got_ref[x * NS + s, :, W_LANE:SENT]
            theirs = other_ref[x * NS + s]
            for c in range(2):
                part = jnp.where(first_core == (c == 0), mine, theirs)
                k = 2 * x + c
                out_w_ref[s, 32 * k : 32 * k + 32, :] = part[:, :cols]
                for g in range(4):
                    row = k * BLK + g * 32
                    lane = cols + g * BLK
                    in_w_ref[s, row : row + 32, :] = part[:, lane : lane + BLK]
    for s, running in running_sums(got_ref, cols):
        rounded = running.astype(BF16)
        count = s if s < NS - 1 else NS
        at = proj_at(s) * BLK
        wide_ref[:, at : at + count * BLK] = dot_t(
            rounded, out_w_ref[0:count].reshape(count * R, cols)
        )
        at = inner_at(s) * BLK
        wide_ref[:, at : at + BLK] = dot(rounded, in_w_ref[s])
    for b in (NORM, GRAM + GRAMS):
        wide_ref[:, b * BLK : (b + 1) * BLK] = jnp.zeros((R, BLK), F32)

    square = [(t, s) for t in range(NS) for s in range(t, NS)]

    @pl.when(first_core)
    def _():
        for t in range(5):
            at = (GRAM + gram_at(t)) * BLK
            wide_ref[:, at : at + (NS - t) * BLK] = dot_t(
                out_w_ref[t], out_w_ref[t:NS].reshape((NS - t) * R, cols)
            )
        for i in range(gram_at(5), GRAMS):
            t, s = square[i]
            at = (GRAM + i) * BLK
            wide_ref[:, at : at + BLK] = dot_t(out_w_ref[t], out_w_ref[s])

    @pl.when(jnp.logical_not(first_core))
    def _():
        for t in range(NS - 1):
            for s in range(t + 1, NS):
                at = (GRAM + cross_at(t) + s - t - 1) * BLK
                wide_ref[:, at : at + BLK] = dot(out_w_ref[t], in_w_ref[s])
        for i in range(GRAMS, OO):
            t, s = square[i]
            at = (GRAM + OI + i - GRAMS) * BLK
            wide_ref[:, at : at + BLK] = dot_t(out_w_ref[t], out_w_ref[s])

    for b in range(SPLIT):
        pair = [
            wide_ref[:, at * BLK : (at + 1) * BLK].reshape(16, TOK, BLK) for at in (b, SPLIT + b)
        ]
        send_ref[:, :, b * BLK : (b + 1) * BLK] = jnp.concatenate(pair, 1).astype(BF16)
    for g in range(8):
        at = START + g * 2 * R
        for q in range(16):
            send_ref[q, :, at : at + 2 * R] = start_ref[g * 16 : (g + 1) * 16, :]


def norm_kernel(
    cols, ids_ref, other_ids_ref, got_ref, before_ref, send_ref, block_ref, sem
):
    del before_ref
    picks = picks_of(ids_ref, other_ids_ref)
    placed = [[] for _ in range(MIC)]
    first = jnp.concatenate(
        [first_rows(got_ref, 0, cols // 2), first_rows(got_ref, HALF, cols // 2)], 1
    )
    for x in range(2):
        rows = first[x * R : (x + 1) * R]
        for e in range(NS):
            for m in range(MIC):
                total = jnp.zeros((TOK, cols), F32)
                for j in range(4):
                    n = 4 * m + j
                    total = jnp.where(
                        picks[16 * x + n] == x * NS + e, rows[n * TOK : (n + 1) * TOK], total
                    )
                placed[m].append(total)
    placed = [jnp.concatenate(blocks, 0) for blocks in placed]
    lane = lax.broadcasted_iota(jnp.int32, (R, BLK), 1)
    norms = jnp.zeros((R, BLK), F32)
    for m in range(MIC):
        part = jnp.sum(placed[m] * placed[m], -1, keepdims=True)
        norms = jnp.where(lane == m * NS, part, norms)
    for s, running in running_sums(got_ref, cols):
        for m in range(MIC):
            entry = running + placed[m]
            part = jnp.sum(entry * entry, -1, keepdims=True)
            norms = jnp.where(lane == m * NS + s, part, norms)
    high = norms.astype(BF16).astype(F32)
    norms = jnp.where(lane < 32, high, pltpu.roll(norms - high, 32, 1)).reshape(16, TOK, BLK)
    block_ref[...] = jnp.concatenate([norms, jnp.zeros_like(norms)], 1).astype(BF16)
    copy = pltpu.make_async_copy(
        block_ref, send_ref.at[:, :, NORM * BLK : (NORM + 1) * BLK], sem
    )
    copy.start()
    copy.wait()


def sum_kernel(parts_ref, send_ref):
    lane = lax.broadcasted_iota(jnp.int32, (2 * TOK, BLK), 1)
    row = lax.broadcasted_iota(jnp.int32, (2 * TOK, BLK), 0)
    for b in range(SPLIT):
        at = slice(b * BLK, (b + 1) * BLK)
        total = parts_ref[0, :, at].astype(F32)
        for q in range(1, 16):
            total = total + parts_ref[q, :, at].astype(F32)
        if b == NORM:
            norm = total + pltpu.roll(total, 96, 1)
            high = norm.astype(BF16).astype(F32)
            norm = jnp.where(lane < 32, high, pltpu.roll(norm - high, 32, 1))
            total = jnp.where(row < TOK, norm, 0.0)
        total = total.astype(BF16)
        for q in range(16):
            send_ref[q, :, at] = total


def gather_kernel(ids_ref, other_ids_ref, sums_ref, base_ref, proj_ref):
    for b in range(GRAM):
        upper = b >= SPLIT
        at = (b - SPLIT * upper) * BLK
        block = sums_ref[:, :, at : at + BLK].astype(F32)
        proj_ref[:, b * BLK : (b + 1) * BLK] = block[:, TOK * upper : TOK * upper + TOK].reshape(
            R, BLK
        )
    for n, pick in enumerate(picks_of(ids_ref, other_ids_ref)):
        rows = slice(n * TOK, (n + 1) * TOK)
        here = pl.ds(pl.multiple_of(pick * TOK, TOK), TOK)
        base_ref[rows, :] = proj_ref[here, :]
        norm = proj_ref[here, NORM * BLK : (NORM + 1) * BLK]
        norm = norm + pltpu.roll(norm, 96, 1)
        m = n % 16 // 4
        base_ref[rows, NORM * BLK : (NORM + 1) * BLK] = (
            pltpu.roll(norm, BLK - m * NS, 1) if m else norm
        )


def chain_kernel(
    width, parts_ref, base_ref, gram_ref, other_ref,
    latent_ref, scalar_ref, oo_ref, oi_ref, oo_rows_ref, oi_rows_ref,
):
    rows = 2 * R
    first_core = lax.axis_index("c") == 0
    for b in range(0, GRAMS, 4):
        at = slice(b * BLK, (b + 4) * BLK)
        mine, theirs = gram_ref[:, at], other_ref[:, at]
        oo_ref[:, at] = jnp.where(first_core, mine, theirs)
        second = jnp.where(first_core, theirs, mine)
        if b < OI:
            oi_ref[:, at] = second
        else:
            oo_ref[:, (b + 4) * BLK : (b + 8) * BLK] = second

    def spread(at):
        return base_ref[:, at * BLK : (at + 1) * BLK]

    def square(t, s, count=1):
        at = (gram_at(t) + s - t) * BLK
        return oo_ref[:, at : at + count * BLK]

    def cross(t, s, count=1):
        at = (cross_at(t) + s - t - 1) * BLK
        return oi_ref[:, at : at + count * BLK]

    for s in range(1, NS):
        for t in range(s):
            at = slice((proj_at(s) + t) * R, (proj_at(s) + t + 1) * R)
            oo_rows_ref[at, :] = square(t, s)
            oi_rows_ref[at, :] = cross(t, s)

    def above(ref, s):
        return ref[proj_at(s) * R : (proj_at(s) + s) * R, :]

    norms = spread(NORM)
    starts = []
    for s in range(NS):
        pieces = []
        for x in range(2):
            for g in range(8):
                at = START + g * 2 * R
                pieces.append(parts_ref[x * NS + s, :, at : at + 2 * R])
        starts.append(jnp.concatenate(pieces, 0))
    start_out = [start[:, R:].astype(F32) for start in starts]
    run_in = [start[:, :R].astype(F32) for start in starts]
    run_out = list(start_out)
    inners, inverses, actives, crossed = [], [], [], []
    grown_norm = jnp.zeros((rows, R), F32)
    for s in range(NS):
        norm = norms[:, s : s + 1]
        entry_out = []
        inner = run_in[s]
        if s > 0:
            inner = inner + spread(inner_at(s))
            total = jnp.zeros((rows, R), F32)
            for t in range(s):
                base = spread(proj_at(s) + t)
                entry_out.append(base + run_out[t])
                total = total + actives[t] * base
            norm = norm + jnp.sum(2.0 * total + grown_norm, -1, keepdims=True)
        inverse = lax.rsqrt(jnp.maximum(norm, 0.0) * (1.0 / width) + EPS)
        inner = inner * inverse
        active = (inner * jax.nn.sigmoid(inner)).astype(BF16)
        latent_ref[:, s * R : (s + 1) * R] = active
        inners.append(inner)
        inverses.append(inverse)
        actives.append(active.astype(F32))
        crossed.append(entry_out)
        grown = dot(active, square(s, s, NS - s))
        if s > 0:
            grown = jnp.concatenate([dot_t(active, above(oo_rows_ref, s)), grown], 1)
        before = run_out[s]
        for t in range(NS):
            run_out[t] = run_out[t] + grown[:, t * R : (t + 1) * R]
        grown_norm = grown_norm + actives[s] * (before + run_out[s])
        if s < NS - 1:
            grown = dot(active, cross(s, s + 1, NS - 1 - s))
            for t in range(s + 1, NS):
                run_in[t] = run_in[t] + grown[:, (t - s - 1) * R : (t - s) * R]
    grads = [run_out[t] + spread(proj_at(NS - 1) + t) for t in range(NS)]
    lane = lax.broadcasted_iota(jnp.int32, (rows, BLK), 1)
    scalars = jnp.zeros((rows, BLK), F32)
    for s in range(NS - 1, -1, -1):
        inner = inners[s]
        sigm = jax.nn.sigmoid(inner)
        d_inner = (grads[s] * sigm * (1.0 + inner * (1.0 - sigm))).astype(BF16)
        latent_ref[:, (NS + s) * R : (NS + s + 1) * R] = d_inner
        inverse = inverses[s]
        total = jnp.sum(d_inner.astype(F32) * inner, -1, keepdims=True)
        scale = inverse * inverse * total * (1.0 / width)
        if s > 0:
            back = dot_t(d_inner, above(oi_rows_ref, s))
        for t in range(s):
            grads[t] = (
                grads[t] + inverse * back[:, t * R : (t + 1) * R] - scale * crossed[s][t]
            )
        scalars = jnp.where(lane == s, inverse, scalars)
        scalars = jnp.where(lane == NS + s, scale, scalars)
    scalar_ref[...] = scalars


def grads_kernel(
    ids_ref, other_ids_ref, got_ref, out_w_ref, in_w_ref, latent_ref, scalar_ref,
    give_ref, keep_ref, entry_ref, step_ref,
):
    cols = step_ref.shape[1]
    half = cols // 2
    first_core = lax.axis_index("c") == 0
    scalars = scalar_ref[...]
    inverses = [scalars[:, s : s + 1] for s in range(NS)]
    scales = [scalars[:, NS + s : NS + s + 1] for s in range(NS)]
    places = [
        pl.multiple_of(pick * TOK, TOK) for pick in picks_of(ids_ref, other_ids_ref)
    ]

    def active(s):
        return latent_ref[:, s * R : (s + 1) * R]

    def d_inner(s):
        return latent_ref[:, (NS + s) * R : (NS + s + 1) * R]

    def put(s, kind, value):
        low, high = value[:half].reshape(8, 32, R), value[half:].reshape(8, 32, R)
        at = slice(kind * R, (kind + 1) * R)
        give_ref[:, s, :, at] = jnp.where(first_core, high, low).astype(BF16)
        keep_ref[:, s, :, at] = jnp.where(first_core, low, high)

    def both(part, *args):
        return jnp.concatenate(
            [part(got_ref, *args, 0, half), part(got_ref, *args, HALF, half)], 1
        )

    entry = both(first_rows)
    for s in range(NS):
        if s > 0:
            step_ref[...] = both(stores, s)
            entry = entry + jnp.concatenate([step_ref[pl.ds(place, TOK), :] for place in places], 0)
        entry_ref[s] = entry
        put(s, 0, dot_rows((entry * inverses[s]).astype(BF16), d_inner(s)))
        entry = entry + dot(active(s), out_w_ref[s])
    grad = entry
    for s in range(NS - 1, -1, -1):
        put(s, 1, dot_rows(grad.astype(BF16), active(s)))
        if s > 0:
            back = dot_t(d_inner(s), in_w_ref[s])
            grad = grad + inverses[s] * back - scales[s] * entry_ref[s]


def add_kernel(keep_ref, swapped_ref, total_ref):
    for i in range(8):
        total_ref[i] = (keep_ref[i] + swapped_ref[i].astype(F32)).astype(BF16)


def final_kernel(parts_ref, gain_ref, in_ref, out_ref):
    total = parts_ref[0].astype(F32)
    for i in range(1, 8):
        total = total + parts_ref[i].astype(F32)
    gain = gain_ref[...].T
    for j in range(8):
        scale = gain[(j % 4) * 32 : (j % 4) * 32 + 32, j // 4 : j // 4 + 1]
        in_ref[j * 32 : j * 32 + 32, :] = total[j, :, :R] * scale
    out = total[:, :, R:].reshape(2 * BLK, R)
    for i in range(2):
        out_ref[:, i * BLK : (i + 1) * BLK] = out[i * BLK : (i + 1) * BLK].T


def body(first_input, example_ids, out_store, in_store, norm_gain, adapter_in, adapter_out):
    width = first_input.shape[2]
    cols = width // 16
    half = cols // 2
    core = lax.axis_index("c")
    xl = lax.axis_index("xl")
    z = lax.axis_index("z")
    w_in = adapter_in[0]
    w_out = adapter_out[0]

    ids = example_ids[0]
    other_ids = lax.ppermute(ids, "xl", SWAP)
    wide = width // 2

    def quarter():
        return lax.axis_index("xl") * 2 + lax.axis_index("c")

    send = pl.pallas_call(
        pack_kernel,
        grid=(2,),
        in_specs=[
            pl.BlockSpec((64, wide), lambda i: (0, i)),
            pl.BlockSpec((64, wide), lambda i: (0, i)),
            pl.BlockSpec((32, wide), lambda i: (quarter(), i)),
            pl.BlockSpec(
                (1, 4, 1, 8, 32, R), lambda i: (i, quarter() % 2, quarter() // 2, 0, 0, 0)
            ),
            pl.BlockSpec((1, 4, 1, 2, BLK), lambda i: (i, quarter() % 2, quarter() // 2, 0, 0)),
            pl.BlockSpec((2, 32, wide), lambda i: (section_here() // (NS - 1), 0, i)),
        ],
        out_specs=pl.BlockSpec((8, 32, SENT), lambda i: (i, 0, 0)),
        scratch_shapes=[pltpu.VMEM((4 * BLK, 4 * BLK), BF16)],
        out_shape=jax.ShapeDtypeStruct((16, 32, SENT), BF16),
        compiler_params=LARGE,
        name="pack",
    )(
        in_store.reshape(64, width),
        out_store.reshape(64, width),
        w_out,
        w_in.reshape(2, 8, 2, 8, 32, R),
        norm_gain.reshape(2, 8, 2, 2, BLK),
        first_input,
    )
    got = lax.all_to_all(send, PLANE, 0, 0, tiled=True)
    other = lax.ppermute(got[:, :, W_LANE:], "c", SWAP)
    start = pl.pallas_call(
        start_kernel,
        out_shape=jax.ShapeDtypeStruct((R, 2 * R), BF16),
        in_specs=[VMEM, VMEM, VMEM, VMEM, pl.BlockSpec(memory_space=pl.ANY)],
        out_specs=VMEM,
        compiler_params=PARAMS,
        cost_estimate=pl.CostEstimate(flops=600000000, bytes_accessed=7000000, transcendentals=0),
        name="start",
    )(first_input, w_out, w_in, norm_gain, got)
    parts, out_w, in_w = pl.pallas_call(
        project_kernel,
        out_shape=(
            jax.ShapeDtypeStruct((16, 2 * TOK, WIDE), BF16),
            jax.ShapeDtypeStruct((NS, R, cols), BF16),
            jax.ShapeDtypeStruct((NS, cols, R), BF16),
        ),
        in_specs=[VMEM, VMEM, VMEM],
        out_specs=(VMEM, VMEM, VMEM),
        scratch_shapes=[pltpu.VMEM((R, 2 * SPLIT * BLK), F32)],
        compiler_params=PARAMS,
        cost_estimate=pl.CostEstimate(flops=2000000000, bytes_accessed=9000000, transcendentals=0),
        name="project",
    )(got, other, start)
    parts = pl.pallas_call(
        functools.partial(norm_kernel, cols),
        out_shape=jax.ShapeDtypeStruct((16, 2 * TOK, WIDE), BF16),
        in_specs=[SMEM, SMEM, VMEM, pl.BlockSpec(memory_space=pl.ANY)],
        out_specs=pl.BlockSpec(memory_space=pl.ANY),
        scratch_shapes=[pltpu.VMEM((16, 2 * TOK, BLK), BF16), pltpu.SemaphoreType.DMA],
        input_output_aliases={3: 0},
        compiler_params=PARAMS,
        name="norms",
    )(ids, other_ids, got, parts)
    parts = lax.all_to_all(parts, PLANE, 0, 0, tiled=True)
    sums = pl.pallas_call(
        sum_kernel,
        out_shape=jax.ShapeDtypeStruct((16, 2 * TOK, SPLIT * BLK), BF16),
        in_specs=[VMEM],
        out_specs=VMEM,
        compiler_params=PARAMS,
        name="sums",
    )(parts)
    sums = lax.all_to_all(sums, PLANE, 0, 0, tiled=True)
    gram = sums[:, TOK:, (GRAM - SPLIT) * BLK : (GRAM - SPLIT + GRAMS) * BLK]
    gram = gram.reshape(R, GRAMS * BLK)
    other = lax.ppermute(gram, "c", SWAP)
    base = pl.pallas_call(
        gather_kernel,
        out_shape=jax.ShapeDtypeStruct((2 * R, GRAM * BLK), F32),
        in_specs=[SMEM, SMEM, VMEM],
        out_specs=VMEM,
        scratch_shapes=[pltpu.VMEM((R, GRAM * BLK), F32)],
        compiler_params=PARAMS,
        cost_estimate=pl.CostEstimate(flops=0, bytes_accessed=7000000, transcendentals=0),
        name="gather",
    )(ids, other_ids, sums)
    latent, scalars = pl.pallas_call(
        functools.partial(chain_kernel, width),
        out_shape=(
            jax.ShapeDtypeStruct((2 * R, 16 * BLK), BF16),
            jax.ShapeDtypeStruct((2 * R, BLK), F32),
        ),
        in_specs=[VMEM] * 4,
        out_specs=(VMEM, VMEM),
        scratch_shapes=[
            pltpu.VMEM((R, OO * BLK), BF16),
            pltpu.VMEM((R, OI * BLK), BF16),
            pltpu.VMEM((OI * R, R), BF16),
            pltpu.VMEM((OI * R, R), BF16),
        ],
        compiler_params=PARAMS,
        name="chain",
    )(parts, base, gram, other)

    give, keep = pl.pallas_call(
        grads_kernel,
        out_shape=(
            jax.ShapeDtypeStruct((8, NS, 32, 2 * R), BF16),
            jax.ShapeDtypeStruct((8, NS, 32, 2 * R), F32),
        ),
        in_specs=[SMEM, SMEM] + [VMEM] * 5,
        out_specs=(VMEM, VMEM),
        scratch_shapes=[pltpu.VMEM((NS, 2 * R, cols), F32), pltpu.VMEM((R, cols), F32)],
        compiler_params=PARAMS,
        name="grads",
    )(ids, other_ids, got, out_w, in_w, latent, scalars)
    swapped = lax.ppermute(give, "c", SWAP)
    total = pl.pallas_call(
        add_kernel,
        out_shape=jax.ShapeDtypeStruct((8, NS, 32, 2 * R), BF16),
        in_specs=[VMEM, VMEM],
        out_specs=VMEM,
        compiler_params=PARAMS,
        name="add",
    )(keep, swapped).reshape(64, 32, 2 * R)
    block = (xl * NS + z) * 2 + core
    gain = lax.dynamic_slice_in_dim(norm_gain[0], block * half, half, 0)
    total, gain = lax.optimization_barrier((total, gain))
    total = lax.all_to_all(total, ("z",) + SECTION, 0, 0, tiled=True)
    grad_in, grad_out = pl.pallas_call(
        final_kernel,
        out_shape=(
            jax.ShapeDtypeStruct((half, R), F32),
            jax.ShapeDtypeStruct((R, half), F32),
        ),
        in_specs=[VMEM, VMEM],
        out_specs=(VMEM, VMEM),
        compiler_params=PARAMS,
        name="final",
    )(total.reshape(8, 8, 32, 2 * R), gain.reshape(2, BLK))
    return (grad_in[None], grad_out[None])


def solution(mesh):
    fine = Mesh(mesh.devices.reshape(2, 8, 2, 4, 2), ("xl", "z", "c", "y", "xh"))
    dp = ("xl", "z", "c")
    placed = (
        P(None, dp, None),
        P(dp, None, None),
        P(SECTION, dp, None, None),
        P(SECTION, dp, None, None),
        P(SECTION, None),
        P(SECTION, None, None),
        P(SECTION, None, None),
    )
    return jax.shard_map(
        body,
        mesh=fine,
        in_specs=placed,
        out_specs=(P(SECTION, dp, None), P(SECTION, None, dp)),
        check_vma=False,
    )
```

```python
import functools

import jax
import jax.numpy as jnp
from jax import lax
from jax.experimental import pallas as pl
from jax.experimental.pallas import tpu as pltpu
from jax.sharding import Mesh, PartitionSpec as P

F32 = jnp.float32
BF16 = jnp.bfloat16
EPS = 1e-05
PLANE = ("xl", "y", "xh")
SECTION = ("y", "xh")
SWAP = [(0, 1), (1, 0)]
NS = 8
R = 128
TOK = 8
MIC = 4
BLK = 128
HALF = 1024
W_LANE = 2 * HALF
SENT = 3072
PROJ = 29
NORM = 34
GRAM = 37
GRAMS = 32
SPLIT = 35
START = SPLIT * BLK
WIDE = START + 16 * BLK
OO = 36
OI = 28
LARGE = pltpu.CompilerParams(vmem_limit_bytes=56 * 1024 * 1024)
PARAMS = pltpu.CompilerParams(vmem_limit_bytes=16 * 1024 * 1024)
VMEM = pl.BlockSpec(memory_space=pltpu.VMEM)
SMEM = pl.BlockSpec(memory_space=pltpu.SMEM)


def gram_at(t):
    return sum(NS - i for i in range(t))


def cross_at(t):
    return sum(NS - 1 - i for i in range(t))


def proj_at(s):
    return s * (s - 1) // 2


def inner_at(s):
    return PROJ + s - 1 + (PROJ + s - 1 >= NORM)


def dot_t(a, b):
    return lax.dot_general(a, b, (((1,), (1,)), ((), ())), preferred_element_type=F32)


def dot_rows(a, b):
    return lax.dot_general(a, b, (((0,), (0,)), ((), ())), preferred_element_type=F32)


def dot(a, b):
    return jnp.dot(a, b, preferred_element_type=F32)


def split(x):
    high = x.astype(BF16)
    return high, (x - high.astype(F32)).astype(BF16)


def section_here():
    return lax.axis_index("y") * 2 + lax.axis_index("xh")


def pack_kernel(
    in_ref, out_ref, w_out_ref, w_in_ref, gain_ref, first_ref, send_ref, turn_ref
):
    section = section_here()

    @pl.when(pl.program_id(0) == 0)
    def _():
        shape = (4 * BLK, 4 * BLK)
        row = lax.broadcasted_iota(jnp.int32, shape, 0)
        col = lax.broadcasted_iota(jnp.int32, shape, 1)
        same = (row // BLK == col % BLK // 32) & (row % BLK // 32 == col // BLK)
        same = same & (row % 32 == col % 32)
        turn_ref[...] = jnp.where(same, 1.0, 0.0).astype(BF16)

    gain = gain_ref[...].reshape(8, BLK).T
    for s in range(NS):
        for j in range(4):
            column = 2 * j + s // 4
            scale = gain[(s % 4) * 32 : (s % 4) * 32 + 32, column : column + 1]
            to = W_LANE + 512 + j * BLK
            send_ref[s, :, to : to + BLK] = (w_in_ref[0, j, 0, s].astype(F32) * scale).astype(BF16)

    pieces, places = [], []
    for c in range(2):
        for zq in range(2):
            to = c * 256 + zq * BLK
            for h in range(2):
                lanes = [((4 * zq + j) * 4 + c * 2 + h) * BLK for j in range(4)]
                for ref, row, at, other in (
                    (in_ref, 0, c * HALF + zq * BLK, 0),
                    (in_ref, 32, c * HALF + 256 + zq * BLK, 0),
                    (out_ref, 0, c * HALF + 512 + zq * BLK, NS - 1),
                    (out_ref, 32, c * HALF + 768 + zq * BLK, NS - 1),
                    (w_out_ref, 0, W_LANE + to, None),
                ):
                    piece = jnp.concatenate(
                        [ref[row : row + 32, lane : lane + BLK] for lane in lanes], 1
                    )
                    if other is not None:
                        first = jnp.concatenate(
                            [first_ref[row // 32, :, lane : lane + BLK] for lane in lanes], 1
                        )
                        piece = jnp.where(section == other, first, piece)
                    pieces.append(piece)
                    places.append((4 * h, at))
    turned = dot(jnp.concatenate(pieces, 0), turn_ref[...]).astype(BF16)
    for n, (first, at) in enumerate(places):
        for i in range(4):
            send_ref[first + i, :, at : at + BLK] = turned[
                32 * n : 32 * n + 32, i * BLK : (i + 1) * BLK
            ]


def start_kernel(first_ref, w_out_ref, w_in_ref, gain_ref, after_ref, start_ref):
    del after_ref
    flat = first_ref[...].reshape(R, first_ref.shape[2])
    scaled = (flat.astype(F32) * gain_ref[...]).astype(BF16)
    start_ref[:, :R] = dot(scaled, w_in_ref[...]).astype(BF16)
    start_ref[:, R:] = dot_t(flat, w_out_ref[...]).astype(BF16)


def stores(got_ref, s, at, cols):
    pieces = []
    for x in range(2):
        for i in range(2):
            a, b = at + i * 256, at + 512 + i * 256
            pieces.append(
                got_ref[x * NS + s, :, pl.ds(a, cols)].astype(F32)
                - got_ref[x * NS + s - 1, :, pl.ds(b, cols)].astype(F32)
            )
    return jnp.concatenate(pieces, 0)


def first_rows(got_ref, at, cols):
    pieces = []
    for x in range(2):
        for m in range(MIC):
            q = x * NS + (0 if m < 2 else NS - 1)
            lane = at + m // 2 * 512 + m % 2 * 256
            pieces.append(got_ref[q, :, pl.ds(lane, cols)])
    return jnp.concatenate(pieces, 0).astype(F32)


def picks_of(ids_ref, other_ids_ref):
    picks = []
    for x in range(2):
        here = lax.axis_index("xl") == x
        for m in range(MIC):
            for j in range(4):
                picks.append(x * NS + jnp.where(here, ids_ref[m, j], other_ids_ref[m, j]))
    return picks


def running_sums(got_ref, cols):
    running = None
    for s in range(1, NS):
        step = jnp.concatenate(
            [stores(got_ref, s, 0, cols // 2), stores(got_ref, s, HALF, cols // 2)], 1
        )
        running = step if running is None else running + step
        yield s, running


def placed_rows(ids_ref, other_ids_ref, got_ref, cols):
    picks = picks_of(ids_ref, other_ids_ref)
    placed = [[] for _ in range(MIC)]
    first = jnp.concatenate(
        [first_rows(got_ref, 0, cols // 2), first_rows(got_ref, HALF, cols // 2)], 1
    )
    for x in range(2):
        rows = first[x * R : (x + 1) * R]
        for e in range(NS):
            for m in range(MIC):
                total = jnp.zeros((TOK, cols), F32)
                for j in range(4):
                    n = 4 * m + j
                    total = jnp.where(
                        picks[16 * x + n] == x * NS + e, rows[n * TOK : (n + 1) * TOK], total
                    )
                placed[m].append(total)
    return [jnp.concatenate(blocks, 0) for blocks in placed]


def project_kernel(
    ids_ref, other_ids_ref, got_ref, other_ref, start_ref, send_ref, out_w_ref, in_w_ref, wide_ref
):
    cols = in_w_ref.shape[1]
    first_core = lax.axis_index("c") == 0
    for s in range(NS):
        for x in range(2):
            mine = got_ref[x * NS + s, :, W_LANE:SENT]
            theirs = other_ref[x * NS + s]
            for c in range(2):
                part = jnp.where(first_core == (c == 0), mine, theirs)
                k = 2 * x + c
                out_w_ref[s, 32 * k : 32 * k + 32, :] = part[:, :cols]
                for g in range(4):
                    row = k * BLK + g * 32
                    lane = cols + g * BLK
                    in_w_ref[s, row : row + 32, :] = part[:, lane : lane + BLK]
    placed = placed_rows(ids_ref, other_ids_ref, got_ref, cols)
    lane = lax.broadcasted_iota(jnp.int32, (R, BLK), 1)
    norms = jnp.zeros((R, BLK), F32)
    for m in range(MIC):
        part = jnp.sum(placed[m] * placed[m], -1, keepdims=True)
        norms = jnp.where(lane == m * NS, part, norms)
    for s, running in running_sums(got_ref, cols):
        for m in range(MIC):
            entry = running + placed[m]
            part = jnp.sum(entry * entry, -1, keepdims=True)
            norms = jnp.where(lane == m * NS + s, part, norms)
        rounded = running.astype(BF16)
        count = s if s < NS - 1 else NS
        at = proj_at(s) * BLK
        wide_ref[:, at : at + count * BLK] = dot_t(
            rounded, out_w_ref[0:count].reshape(count * R, cols)
        )
        at = inner_at(s) * BLK
        wide_ref[:, at : at + BLK] = dot(rounded, in_w_ref[s])
    high = norms.astype(BF16).astype(F32)
    wide_ref[:, NORM * BLK : (NORM + 1) * BLK] = jnp.where(
        lane < 32, high, pltpu.roll(norms - high, 32, 1)
    )
    wide_ref[:, (GRAM + GRAMS) * BLK :] = jnp.zeros((R, BLK), F32)

    square = [(t, s) for t in range(NS) for s in range(t, NS)]

    @pl.when(first_core)
    def _():
        for t in range(5):
            at = (GRAM + gram_at(t)) * BLK
            wide_ref[:, at : at + (NS - t) * BLK] = dot_t(
                out_w_ref[t], out_w_ref[t:NS].reshape((NS - t) * R, cols)
            )
        for i in range(gram_at(5), GRAMS):
            t, s = square[i]
            at = (GRAM + i) * BLK
            wide_ref[:, at : at + BLK] = dot_t(out_w_ref[t], out_w_ref[s])

    @pl.when(jnp.logical_not(first_core))
    def _():
        for t in range(NS - 1):
            for s in range(t + 1, NS):
                at = (GRAM + cross_at(t) + s - t - 1) * BLK
                wide_ref[:, at : at + BLK] = dot(out_w_ref[t], in_w_ref[s])
        for i in range(GRAMS, OO):
            t, s = square[i]
            at = (GRAM + OI + i - GRAMS) * BLK
            wide_ref[:, at : at + BLK] = dot_t(out_w_ref[t], out_w_ref[s])

    for b in range(SPLIT):
        pair = [
            wide_ref[:, at * BLK : (at + 1) * BLK].reshape(16, TOK, BLK) for at in (b, SPLIT + b)
        ]
        send_ref[:, :, b * BLK : (b + 1) * BLK] = jnp.concatenate(pair, 1).astype(BF16)
    for g in range(8):
        at = START + g * 2 * R
        for q in range(16):
            send_ref[q, :, at : at + 2 * R] = start_ref[g * 16 : (g + 1) * 16, :]


def sum_kernel(parts_ref, send_ref):
    lane = lax.broadcasted_iota(jnp.int32, (2 * TOK, BLK), 1)
    row = lax.broadcasted_iota(jnp.int32, (2 * TOK, BLK), 0)
    for b in range(SPLIT):
        at = slice(b * BLK, (b + 1) * BLK)
        total = parts_ref[0, :, at].astype(F32)
        for q in range(1, 16):
            total = total + parts_ref[q, :, at].astype(F32)
        if b == NORM:
            norm = total + pltpu.roll(total, 96, 1)
            high = norm.astype(BF16).astype(F32)
            norm = jnp.where(lane < 32, high, pltpu.roll(norm - high, 32, 1))
            total = jnp.where(row < TOK, norm, 0.0)
        total = total.astype(BF16)
        for q in range(16):
            send_ref[q, :, at] = total


def gather_kernel(ids_ref, other_ids_ref, sums_ref, base_ref, proj_ref):
    for b in range(GRAM):
        upper = b >= SPLIT
        at = (b - SPLIT * upper) * BLK
        block = sums_ref[:, :, at : at + BLK].astype(F32)
        proj_ref[:, b * BLK : (b + 1) * BLK] = block[:, TOK * upper : TOK * upper + TOK].reshape(
            R, BLK
        )
    for n, pick in enumerate(picks_of(ids_ref, other_ids_ref)):
        rows = slice(n * TOK, (n + 1) * TOK)
        here = pl.ds(pl.multiple_of(pick * TOK, TOK), TOK)
        base_ref[rows, :] = proj_ref[here, :]
        norm = proj_ref[here, NORM * BLK : (NORM + 1) * BLK]
        norm = norm + pltpu.roll(norm, 96, 1)
        m = n % 16 // 4
        base_ref[rows, NORM * BLK : (NORM + 1) * BLK] = (
            pltpu.roll(norm, BLK - m * NS, 1) if m else norm
        )


def chain_kernel(
    width, parts_ref, base_ref, gram_ref, other_ref,
    latent_ref, scalar_ref, oo_ref, oi_ref, oo_rows_ref, oi_rows_ref,
):
    rows = 2 * R
    first_core = lax.axis_index("c") == 0
    for b in range(0, GRAMS, 4):
        at = slice(b * BLK, (b + 4) * BLK)
        mine, theirs = gram_ref[:, at], other_ref[:, at]
        oo_ref[:, at] = jnp.where(first_core, mine, theirs)
        second = jnp.where(first_core, theirs, mine)
        if b < OI:
            oi_ref[:, at] = second
        else:
            oo_ref[:, (b + 4) * BLK : (b + 8) * BLK] = second

    def spread(at):
        return base_ref[:, at * BLK : (at + 1) * BLK]

    def square(t, s, count=1):
        at = (gram_at(t) + s - t) * BLK
        return oo_ref[:, at : at + count * BLK]

    def cross(t, s, count=1):
        at = (cross_at(t) + s - t - 1) * BLK
        return oi_ref[:, at : at + count * BLK]

    for s in range(1, NS):
        for t in range(s):
            at = slice((proj_at(s) + t) * R, (proj_at(s) + t + 1) * R)
            oo_rows_ref[at, :] = square(t, s)
            oi_rows_ref[at, :] = cross(t, s)

    def above(ref, s):
        return ref[proj_at(s) * R : (proj_at(s) + s) * R, :]

    norms = spread(NORM)
    starts = []
    for s in range(NS):
        pieces = []
        for x in range(2):
            for g in range(8):
                at = START + g * 2 * R
                pieces.append(parts_ref[x * NS + s, :, at : at + 2 * R])
        starts.append(jnp.concatenate(pieces, 0))
    start_out = [start[:, R:].astype(F32) for start in starts]
    run_in = [start[:, :R].astype(F32) for start in starts]
    run_out = list(start_out)
    inners, inverses, actives, crossed = [], [], [], []
    grown_norm = jnp.zeros((rows, R), F32)
    for s in range(NS):
        norm = norms[:, s : s + 1]
        entry_out = []
        inner = run_in[s]
        if s > 0:
            inner = inner + spread(inner_at(s))
            total = jnp.zeros((rows, R), F32)
            for t in range(s):
                base = spread(proj_at(s) + t)
                entry_out.append(base + run_out[t])
                total = total + actives[t] * base
            norm = norm + jnp.sum(2.0 * total + grown_norm, -1, keepdims=True)
        inverse = lax.rsqrt(jnp.maximum(norm, 0.0) * (1.0 / width) + EPS)
        inner = inner * inverse
        active = (inner * jax.nn.sigmoid(inner)).astype(BF16)
        latent_ref[:, s * R : (s + 1) * R] = active
        inners.append(inner)
        inverses.append(inverse)
        actives.append(active.astype(F32))
        crossed.append(entry_out)
        grown = dot(active, square(s, s, NS - s))
        if s > 0:
            grown = jnp.concatenate([dot_t(active, above(oo_rows_ref, s)), grown], 1)
        before = run_out[s]
        for t in range(NS):
            run_out[t] = run_out[t] + grown[:, t * R : (t + 1) * R]
        grown_norm = grown_norm + actives[s] * (before + run_out[s])
        if s < NS - 1:
            grown = dot(active, cross(s, s + 1, NS - 1 - s))
            for t in range(s + 1, NS):
                run_in[t] = run_in[t] + grown[:, (t - s - 1) * R : (t - s) * R]
    grads = [run_out[t] + spread(proj_at(NS - 1) + t) for t in range(NS)]
    lane = lax.broadcasted_iota(jnp.int32, (rows, BLK), 1)
    scalars = jnp.zeros((rows, BLK), F32)
    for s in range(NS - 1, -1, -1):
        inner = inners[s]
        sigm = jax.nn.sigmoid(inner)
        d_inner = (grads[s] * sigm * (1.0 + inner * (1.0 - sigm))).astype(BF16)
        latent_ref[:, (NS + s) * R : (NS + s + 1) * R] = d_inner
        inverse = inverses[s]
        total = jnp.sum(d_inner.astype(F32) * inner, -1, keepdims=True)
        scale = inverse * inverse * total * (1.0 / width)
        if s > 0:
            back = dot_t(d_inner, above(oi_rows_ref, s))
        for t in range(s):
            grads[t] = (
                grads[t] + inverse * back[:, t * R : (t + 1) * R] - scale * crossed[s][t]
            )
        scalars = jnp.where(lane == s, inverse, scalars)
        scalars = jnp.where(lane == NS + s, scale, scalars)
    scalar_ref[...] = scalars


def grads_kernel(
    ids_ref, other_ids_ref, got_ref, out_w_ref, in_w_ref, latent_ref, scalar_ref,
    give_ref, keep_ref, entry_ref, step_ref,
):
    cols = step_ref.shape[1]
    half = cols // 2
    first_core = lax.axis_index("c") == 0
    scalars = scalar_ref[...]
    inverses = [scalars[:, s : s + 1] for s in range(NS)]
    scales = [scalars[:, NS + s : NS + s + 1] for s in range(NS)]
    places = [
        pl.multiple_of(pick * TOK, TOK) for pick in picks_of(ids_ref, other_ids_ref)
    ]

    def active(s):
        return latent_ref[:, s * R : (s + 1) * R]

    def d_inner(s):
        return latent_ref[:, (NS + s) * R : (NS + s + 1) * R]

    def put(s, kind, value):
        low, high = value[:half].reshape(8, 32, R), value[half:].reshape(8, 32, R)
        at = slice(kind * R, (kind + 1) * R)
        give_ref[:, s, :, at] = jnp.where(first_core, high, low).astype(BF16)
        keep_ref[:, s, :, at] = jnp.where(first_core, low, high)

    def both(part, *args):
        return jnp.concatenate(
            [part(got_ref, *args, 0, half), part(got_ref, *args, HALF, half)], 1
        )

    entry = both(first_rows)
    for s in range(NS):
        if s > 0:
            step_ref[...] = both(stores, s)
            entry = entry + jnp.concatenate([step_ref[pl.ds(place, TOK), :] for place in places], 0)
        entry_ref[s] = entry
        put(s, 0, dot_rows((entry * inverses[s]).astype(BF16), d_inner(s)))
        entry = entry + dot(active(s), out_w_ref[s])
    grad = entry
    for s in range(NS - 1, -1, -1):
        put(s, 1, dot_rows(grad.astype(BF16), active(s)))
        if s > 0:
            back = dot_t(d_inner(s), in_w_ref[s])
            grad = grad + inverses[s] * back - scales[s] * entry_ref[s]


def add_kernel(keep_ref, swapped_ref, total_ref):
    for i in range(8):
        total_ref[i] = (keep_ref[i] + swapped_ref[i].astype(F32)).astype(BF16)


def final_kernel(parts_ref, gain_ref, in_ref, out_ref):
    total = parts_ref[0].astype(F32)
    for i in range(1, 8):
        total = total + parts_ref[i].astype(F32)
    gain = gain_ref[...].T
    for j in range(8):
        scale = gain[(j % 4) * 32 : (j % 4) * 32 + 32, j // 4 : j // 4 + 1]
        in_ref[j * 32 : j * 32 + 32, :] = total[j, :, :R] * scale
    out = total[:, :, R:].reshape(2 * BLK, R)
    for i in range(2):
        out_ref[:, i * BLK : (i + 1) * BLK] = out[i * BLK : (i + 1) * BLK].T


def body(first_input, example_ids, out_store, in_store, norm_gain, adapter_in, adapter_out):
    width = first_input.shape[2]
    cols = width // 16
    half = cols // 2
    core = lax.axis_index("c")
    xl = lax.axis_index("xl")
    z = lax.axis_index("z")
    w_in = adapter_in[0]
    w_out = adapter_out[0]

    ids = example_ids[0]
    other_ids = lax.ppermute(ids, "xl", SWAP)
    wide = width // 2

    def quarter():
        return lax.axis_index("xl") * 2 + lax.axis_index("c")

    send = pl.pallas_call(
        pack_kernel,
        grid=(2,),
        in_specs=[
            pl.BlockSpec((64, wide), lambda i: (0, i)),
            pl.BlockSpec((64, wide), lambda i: (0, i)),
            pl.BlockSpec((32, wide), lambda i: (quarter(), i)),
            pl.BlockSpec(
                (1, 4, 1, 8, 32, R), lambda i: (i, quarter() % 2, quarter() // 2, 0, 0, 0)
            ),
            pl.BlockSpec((1, 4, 1, 2, BLK), lambda i: (i, quarter() % 2, quarter() // 2, 0, 0)),
            pl.BlockSpec((2, 32, wide), lambda i: (section_here() // (NS - 1), 0, i)),
        ],
        out_specs=pl.BlockSpec((8, 32, SENT), lambda i: (i, 0, 0)),
        scratch_shapes=[pltpu.VMEM((4 * BLK, 4 * BLK), BF16)],
        out_shape=jax.ShapeDtypeStruct((16, 32, SENT), BF16),
        compiler_params=LARGE,
        name="pack",
    )(
        in_store.reshape(64, width),
        out_store.reshape(64, width),
        w_out,
        w_in.reshape(2, 8, 2, 8, 32, R),
        norm_gain.reshape(2, 8, 2, 2, BLK),
        first_input,
    )
    send, other_ids = lax.optimization_barrier((send, other_ids))
    got = lax.all_to_all(send, PLANE, 0, 0, tiled=True)
    other = lax.ppermute(got[:, :, W_LANE:], "c", SWAP)
    start = pl.pallas_call(
        start_kernel,
        out_shape=jax.ShapeDtypeStruct((R, 2 * R), BF16),
        in_specs=[VMEM, VMEM, VMEM, VMEM, pl.BlockSpec(memory_space=pl.ANY)],
        out_specs=VMEM,
        compiler_params=PARAMS,
        cost_estimate=pl.CostEstimate(flops=600000000, bytes_accessed=7000000, transcendentals=0),
        name="start",
    )(first_input, w_out, w_in, norm_gain, got)
    parts, out_w, in_w = pl.pallas_call(
        project_kernel,
        out_shape=(
            jax.ShapeDtypeStruct((16, 2 * TOK, WIDE), BF16),
            jax.ShapeDtypeStruct((NS, R, cols), BF16),
            jax.ShapeDtypeStruct((NS, cols, R), BF16),
        ),
        in_specs=[SMEM, SMEM, VMEM, VMEM, VMEM],
        out_specs=(VMEM, VMEM, VMEM),
        scratch_shapes=[pltpu.VMEM((R, 2 * SPLIT * BLK), F32)],
        compiler_params=PARAMS,
        cost_estimate=pl.CostEstimate(flops=2000000000, bytes_accessed=9000000, transcendentals=0),
        name="project",
    )(ids, other_ids, got, other, start)
    parts = lax.all_to_all(parts, PLANE, 0, 0, tiled=True)
    sums = pl.pallas_call(
        sum_kernel,
        out_shape=jax.ShapeDtypeStruct((16, 2 * TOK, SPLIT * BLK), BF16),
        in_specs=[VMEM],
        out_specs=VMEM,
        compiler_params=PARAMS,
        name="sums",
    )(parts)
    sums = lax.all_to_all(sums, PLANE, 0, 0, tiled=True)
    gram = sums[:, TOK:, (GRAM - SPLIT) * BLK : (GRAM - SPLIT + GRAMS) * BLK]
    gram = gram.reshape(R, GRAMS * BLK)
    other = lax.ppermute(gram, "c", SWAP)
    base = pl.pallas_call(
        gather_kernel,
        out_shape=jax.ShapeDtypeStruct((2 * R, GRAM * BLK), F32),
        in_specs=[SMEM, SMEM, VMEM],
        out_specs=VMEM,
        scratch_shapes=[pltpu.VMEM((R, GRAM * BLK), F32)],
        compiler_params=PARAMS,
        cost_estimate=pl.CostEstimate(flops=0, bytes_accessed=7000000, transcendentals=0),
        name="gather",
    )(ids, other_ids, sums)
    latent, scalars = pl.pallas_call(
        functools.partial(chain_kernel, width),
        out_shape=(
            jax.ShapeDtypeStruct((2 * R, 16 * BLK), BF16),
            jax.ShapeDtypeStruct((2 * R, BLK), F32),
        ),
        in_specs=[VMEM] * 4,
        out_specs=(VMEM, VMEM),
        scratch_shapes=[
            pltpu.VMEM((R, OO * BLK), BF16),
            pltpu.VMEM((R, OI * BLK), BF16),
            pltpu.VMEM((OI * R, R), BF16),
            pltpu.VMEM((OI * R, R), BF16),
        ],
        compiler_params=PARAMS,
        name="chain",
    )(parts, base, gram, other)

    give, keep = pl.pallas_call(
        grads_kernel,
        out_shape=(
            jax.ShapeDtypeStruct((8, NS, 32, 2 * R), BF16),
            jax.ShapeDtypeStruct((8, NS, 32, 2 * R), F32),
        ),
        in_specs=[SMEM, SMEM] + [VMEM] * 5,
        out_specs=(VMEM, VMEM),
        scratch_shapes=[pltpu.VMEM((NS, 2 * R, cols), F32), pltpu.VMEM((R, cols), F32)],
        compiler_params=PARAMS,
        name="grads",
    )(ids, other_ids, got, out_w, in_w, latent, scalars)
    swapped = lax.ppermute(give, "c", SWAP)
    total = pl.pallas_call(
        add_kernel,
        out_shape=jax.ShapeDtypeStruct((8, NS, 32, 2 * R), BF16),
        in_specs=[VMEM, VMEM],
        out_specs=VMEM,
        compiler_params=PARAMS,
        name="add",
    )(keep, swapped).reshape(64, 32, 2 * R)
    block = (xl * NS + z) * 2 + core
    gain = lax.dynamic_slice_in_dim(norm_gain[0], block * half, half, 0)
    total, gain = lax.optimization_barrier((total, gain))
    total = lax.all_to_all(total, ("z",) + SECTION, 0, 0, tiled=True)
    grad_in, grad_out = pl.pallas_call(
        final_kernel,
        out_shape=(
            jax.ShapeDtypeStruct((half, R), F32),
            jax.ShapeDtypeStruct((R, half), F32),
        ),
        in_specs=[VMEM, VMEM],
        out_specs=(VMEM, VMEM),
        compiler_params=PARAMS,
        name="final",
    )(total.reshape(8, 8, 32, 2 * R), gain.reshape(2, BLK))
    return (grad_in[None], grad_out[None])


def solution(mesh):
    fine = Mesh(mesh.devices.reshape(2, 8, 2, 4, 2), ("xl", "z", "c", "y", "xh"))
    dp = ("xl", "z", "c")
    placed = (
        P(None, dp, None),
        P(dp, None, None),
        P(SECTION, dp, None, None),
        P(SECTION, dp, None, None),
        P(SECTION, None),
        P(SECTION, None, None),
        P(SECTION, None, None),
    )
    return jax.shard_map(
        body,
        mesh=fine,
        in_specs=placed,
        out_specs=(P(SECTION, dp, None), P(SECTION, None, dp)),
        check_vma=False,
    )
```

```python
import functools

import jax
import jax.numpy as jnp
from jax import lax
from jax.experimental import pallas as pl
from jax.experimental.pallas import tpu as pltpu
from jax.sharding import Mesh, PartitionSpec as P

F32 = jnp.float32
BF16 = jnp.bfloat16
EPS = 1e-05
PLANE = ("xl", "y", "xh")
SECTION = ("y", "xh")
SWAP = [(0, 1), (1, 0)]
NS = 8
R = 128
TOK = 8
MIC = 4
BLK = 128
HALF = 1024
W_LANE = 2 * HALF
SENT = 3072
PROJ = 29
NORM = 34
GRAM = 37
GRAMS = 32
SPLIT = 35
START = SPLIT * BLK
WIDE = START + 16 * BLK
OO = 36
OI = 28
LARGE = pltpu.CompilerParams(vmem_limit_bytes=56 * 1024 * 1024)
PARAMS = pltpu.CompilerParams(vmem_limit_bytes=16 * 1024 * 1024)
VMEM = pl.BlockSpec(memory_space=pltpu.VMEM)
SMEM = pl.BlockSpec(memory_space=pltpu.SMEM)


def gram_at(t):
    return sum(NS - i for i in range(t))


def cross_at(t):
    return sum(NS - 1 - i for i in range(t))


def proj_at(s):
    return s * (s - 1) // 2


def inner_at(s):
    return PROJ + s - 1 + (PROJ + s - 1 >= NORM)


def dot_t(a, b):
    return lax.dot_general(a, b, (((1,), (1,)), ((), ())), preferred_element_type=F32)


def dot_rows(a, b):
    return lax.dot_general(a, b, (((0,), (0,)), ((), ())), preferred_element_type=F32)


def dot(a, b):
    return jnp.dot(a, b, preferred_element_type=F32)


def split(x):
    high = x.astype(BF16)
    return high, (x - high.astype(F32)).astype(BF16)


def section_here():
    return lax.axis_index("y") * 2 + lax.axis_index("xh")


def pack_kernel(
    in_ref, out_ref, w_out_ref, w_in_ref, gain_ref, first_ref, send_ref, turn_ref
):
    section = section_here()

    @pl.when(pl.program_id(0) == 0)
    def _():
        shape = (4 * BLK, 4 * BLK)
        row = lax.broadcasted_iota(jnp.int32, shape, 0)
        col = lax.broadcasted_iota(jnp.int32, shape, 1)
        same = (row // BLK == col % BLK // 32) & (row % BLK // 32 == col // BLK)
        same = same & (row % 32 == col % 32)
        turn_ref[...] = jnp.where(same, 1.0, 0.0).astype(BF16)

    gain = gain_ref[...].reshape(8, BLK).T
    for s in range(NS):
        for j in range(4):
            column = 2 * j + s // 4
            scale = gain[(s % 4) * 32 : (s % 4) * 32 + 32, column : column + 1]
            to = W_LANE + 512 + j * BLK
            send_ref[s, :, to : to + BLK] = (w_in_ref[0, j, 0, s].astype(F32) * scale).astype(BF16)

    pieces, places = [], []
    for c in range(2):
        for zq in range(2):
            to = c * 256 + zq * BLK
            for h in range(2):
                lanes = [((4 * zq + j) * 4 + c * 2 + h) * BLK for j in range(4)]
                for ref, row, at, other in (
                    (in_ref, 0, c * HALF + zq * BLK, 0),
                    (in_ref, 32, c * HALF + 256 + zq * BLK, 0),
                    (out_ref, 0, c * HALF + 512 + zq * BLK, NS - 1),
                    (out_ref, 32, c * HALF + 768 + zq * BLK, NS - 1),
                    (w_out_ref, 0, W_LANE + to, None),
                ):
                    piece = jnp.concatenate(
                        [ref[row : row + 32, lane : lane + BLK] for lane in lanes], 1
                    )
                    if other is not None:
                        first = jnp.concatenate(
                            [first_ref[row // 32, :, lane : lane + BLK] for lane in lanes], 1
                        )
                        piece = jnp.where(section == other, first, piece)
                    pieces.append(piece)
                    places.append((4 * h, at))
    turned = dot(jnp.concatenate(pieces, 0), turn_ref[...]).astype(BF16)
    for n, (first, at) in enumerate(places):
        for i in range(4):
            send_ref[first + i, :, at : at + BLK] = turned[
                32 * n : 32 * n + 32, i * BLK : (i + 1) * BLK
            ]


def start_kernel(first_ref, w_out_ref, w_in_ref, gain_ref, after_ref, start_ref, sum_ref):
    del after_ref
    flat = first_ref[...].reshape(R, first_ref.shape[2])
    scaled = (flat.astype(F32) * gain_ref[...]).astype(BF16)
    both = jnp.concatenate([dot(scaled, w_in_ref[...]), dot_t(flat, w_out_ref[...])], 1)
    sum_ref[...] = jnp.where(pl.program_id(0) == 0, 0.0, sum_ref[...]) + both
    start_ref[...] = sum_ref[...].astype(BF16)


def stores(got_ref, s, at, cols):
    pieces = []
    for x in range(2):
        for i in range(2):
            a, b = at + i * 256, at + 512 + i * 256
            pieces.append(
                got_ref[x * NS + s, :, pl.ds(a, cols)].astype(F32)
                - got_ref[x * NS + s - 1, :, pl.ds(b, cols)].astype(F32)
            )
    return jnp.concatenate(pieces, 0)


def first_rows(got_ref, at, cols):
    pieces = []
    for x in range(2):
        for m in range(MIC):
            q = x * NS + (0 if m < 2 else NS - 1)
            lane = at + m // 2 * 512 + m % 2 * 256
            pieces.append(got_ref[q, :, pl.ds(lane, cols)])
    return jnp.concatenate(pieces, 0).astype(F32)


def picks_of(ids_ref, other_ids_ref):
    picks = []
    for x in range(2):
        here = lax.axis_index("xl") == x
        for m in range(MIC):
            for j in range(4):
                picks.append(x * NS + jnp.where(here, ids_ref[m, j], other_ids_ref[m, j]))
    return picks


def running_sums(got_ref, cols):
    running = None
    for s in range(1, NS):
        step = jnp.concatenate(
            [stores(got_ref, s, 0, cols // 2), stores(got_ref, s, HALF, cols // 2)], 1
        )
        running = step if running is None else running + step
        yield s, running


def placed_rows(ids_ref, other_ids_ref, got_ref, cols):
    picks = picks_of(ids_ref, other_ids_ref)
    placed = [[] for _ in range(MIC)]
    first = jnp.concatenate(
        [first_rows(got_ref, 0, cols // 2), first_rows(got_ref, HALF, cols // 2)], 1
    )
    for x in range(2):
        rows = first[x * R : (x + 1) * R]
        for e in range(NS):
            for m in range(MIC):
                total = jnp.zeros((TOK, cols), F32)
                for j in range(4):
                    n = 4 * m + j
                    total = jnp.where(
                        picks[16 * x + n] == x * NS + e, rows[n * TOK : (n + 1) * TOK], total
                    )
                placed[m].append(total)
    return [jnp.concatenate(blocks, 0) for blocks in placed]


def project_kernel(
    ids_ref, other_ids_ref, got_ref, other_ref, start_ref, send_ref, out_w_ref, in_w_ref, wide_ref
):
    cols = in_w_ref.shape[1]
    first_core = lax.axis_index("c") == 0
    for s in range(NS):
        for x in range(2):
            mine = got_ref[x * NS + s, :, W_LANE:SENT]
            theirs = other_ref[x * NS + s]
            for c in range(2):
                part = jnp.where(first_core == (c == 0), mine, theirs)
                k = 2 * x + c
                out_w_ref[s, 32 * k : 32 * k + 32, :] = part[:, :cols]
                for g in range(4):
                    row = k * BLK + g * 32
                    lane = cols + g * BLK
                    in_w_ref[s, row : row + 32, :] = part[:, lane : lane + BLK]
    placed = placed_rows(ids_ref, other_ids_ref, got_ref, cols)
    lane = lax.broadcasted_iota(jnp.int32, (R, BLK), 1)
    norms = jnp.zeros((R, BLK), F32)
    for m in range(MIC):
        part = jnp.sum(placed[m] * placed[m], -1, keepdims=True)
        norms = jnp.where(lane == m * NS, part, norms)
    for s, running in running_sums(got_ref, cols):
        for m in range(MIC):
            entry = running + placed[m]
            part = jnp.sum(entry * entry, -1, keepdims=True)
            norms = jnp.where(lane == m * NS + s, part, norms)
        rounded = running.astype(BF16)
        count = s if s < NS - 1 else NS
        at = proj_at(s) * BLK
        wide_ref[:, at : at + count * BLK] = dot_t(
            rounded, out_w_ref[0:count].reshape(count * R, cols)
        )
        at = inner_at(s) * BLK
        wide_ref[:, at : at + BLK] = dot(rounded, in_w_ref[s])
    high = norms.astype(BF16).astype(F32)
    wide_ref[:, NORM * BLK : (NORM + 1) * BLK] = jnp.where(
        lane < 32, high, pltpu.roll(norms - high, 32, 1)
    )
    wide_ref[:, (GRAM + GRAMS) * BLK :] = jnp.zeros((R, BLK), F32)

    square = [(t, s) for t in range(NS) for s in range(t, NS)]

    @pl.when(first_core)
    def _():
        for t in range(5):
            at = (GRAM + gram_at(t)) * BLK
            wide_ref[:, at : at + (NS - t) * BLK] = dot_t(
                out_w_ref[t], out_w_ref[t:NS].reshape((NS - t) * R, cols)
            )
        for i in range(gram_at(5), GRAMS):
            t, s = square[i]
            at = (GRAM + i) * BLK
            wide_ref[:, at : at + BLK] = dot_t(out_w_ref[t], out_w_ref[s])

    @pl.when(jnp.logical_not(first_core))
    def _():
        for t in range(NS - 1):
            for s in range(t + 1, NS):
                at = (GRAM + cross_at(t) + s - t - 1) * BLK
                wide_ref[:, at : at + BLK] = dot(out_w_ref[t], in_w_ref[s])
        for i in range(GRAMS, OO):
            t, s = square[i]
            at = (GRAM + OI + i - GRAMS) * BLK
            wide_ref[:, at : at + BLK] = dot_t(out_w_ref[t], out_w_ref[s])

    for b in range(SPLIT):
        pair = [
            wide_ref[:, at * BLK : (at + 1) * BLK].reshape(16, TOK, BLK) for at in (b, SPLIT + b)
        ]
        send_ref[:, :, b * BLK : (b + 1) * BLK] = jnp.concatenate(pair, 1).astype(BF16)
    for g in range(8):
        at = START + g * 2 * R
        for q in range(16):
            send_ref[q, :, at : at + 2 * R] = start_ref[g * 16 : (g + 1) * 16, :]


def sum_kernel(parts_ref, send_ref):
    lane = lax.broadcasted_iota(jnp.int32, (2 * TOK, BLK), 1)
    row = lax.broadcasted_iota(jnp.int32, (2 * TOK, BLK), 0)
    for b in range(SPLIT):
        at = slice(b * BLK, (b + 1) * BLK)
        total = parts_ref[0, :, at].astype(F32)
        for q in range(1, 16):
            total = total + parts_ref[q, :, at].astype(F32)
        if b == NORM:
            norm = total + pltpu.roll(total, 96, 1)
            high = norm.astype(BF16).astype(F32)
            norm = jnp.where(lane < 32, high, pltpu.roll(norm - high, 32, 1))
            total = jnp.where(row < TOK, norm, 0.0)
        total = total.astype(BF16)
        for q in range(16):
            send_ref[q, :, at] = total


def gather_kernel(ids_ref, other_ids_ref, sums_ref, base_ref, proj_ref):
    for b in range(GRAM):
        upper = b >= SPLIT
        at = (b - SPLIT * upper) * BLK
        block = sums_ref[:, :, at : at + BLK].astype(F32)
        proj_ref[:, b * BLK : (b + 1) * BLK] = block[:, TOK * upper : TOK * upper + TOK].reshape(
            R, BLK
        )
    for n, pick in enumerate(picks_of(ids_ref, other_ids_ref)):
        rows = slice(n * TOK, (n + 1) * TOK)
        here = pl.ds(pl.multiple_of(pick * TOK, TOK), TOK)
        base_ref[rows, :] = proj_ref[here, :]
        norm = proj_ref[here, NORM * BLK : (NORM + 1) * BLK]
        norm = norm + pltpu.roll(norm, 96, 1)
        m = n % 16 // 4
        base_ref[rows, NORM * BLK : (NORM + 1) * BLK] = (
            pltpu.roll(norm, BLK - m * NS, 1) if m else norm
        )


def chain_kernel(
    width, parts_ref, base_ref, gram_ref, other_ref,
    latent_ref, scalar_ref, oo_ref, oi_ref, oo_rows_ref, oi_rows_ref,
):
    rows = 2 * R
    first_core = lax.axis_index("c") == 0
    for b in range(0, GRAMS, 4):
        at = slice(b * BLK, (b + 4) * BLK)
        mine, theirs = gram_ref[:, at], other_ref[:, at]
        oo_ref[:, at] = jnp.where(first_core, mine, theirs)
        second = jnp.where(first_core, theirs, mine)
        if b < OI:
            oi_ref[:, at] = second
        else:
            oo_ref[:, (b + 4) * BLK : (b + 8) * BLK] = second

    def spread(at):
        return base_ref[:, at * BLK : (at + 1) * BLK]

    def square(t, s, count=1):
        at = (gram_at(t) + s - t) * BLK
        return oo_ref[:, at : at + count * BLK]

    def cross(t, s, count=1):
        at = (cross_at(t) + s - t - 1) * BLK
        return oi_ref[:, at : at + count * BLK]

    for s in range(1, NS):
        for t in range(s):
            at = slice((proj_at(s) + t) * R, (proj_at(s) + t + 1) * R)
            oo_rows_ref[at, :] = square(t, s)
            oi_rows_ref[at, :] = cross(t, s)

    def above(ref, s):
        return ref[proj_at(s) * R : (proj_at(s) + s) * R, :]

    norms = spread(NORM)
    starts = []
    for s in range(NS):
        pieces = []
        for x in range(2):
            for g in range(8):
                at = START + g * 2 * R
                pieces.append(parts_ref[x * NS + s, :, at : at + 2 * R])
        starts.append(jnp.concatenate(pieces, 0))
    start_out = [start[:, R:].astype(F32) for start in starts]
    run_in = [start[:, :R].astype(F32) for start in starts]
    run_out = list(start_out)
    inners, inverses, actives, crossed = [], [], [], []
    grown_norm = jnp.zeros((rows, R), F32)
    for s in range(NS):
        norm = norms[:, s : s + 1]
        entry_out = []
        inner = run_in[s]
        if s > 0:
            inner = inner + spread(inner_at(s))
            total = jnp.zeros((rows, R), F32)
            for t in range(s):
                base = spread(proj_at(s) + t)
                entry_out.append(base + run_out[t])
                total = total + actives[t] * base
            norm = norm + jnp.sum(2.0 * total + grown_norm, -1, keepdims=True)
        inverse = lax.rsqrt(jnp.maximum(norm, 0.0) * (1.0 / width) + EPS)
        inner = inner * inverse
        active = (inner * jax.nn.sigmoid(inner)).astype(BF16)
        latent_ref[:, s * R : (s + 1) * R] = active
        inners.append(inner)
        inverses.append(inverse)
        actives.append(active.astype(F32))
        crossed.append(entry_out)
        grown = dot(active, square(s, s, NS - s))
        if s > 0:
            grown = jnp.concatenate([dot_t(active, above(oo_rows_ref, s)), grown], 1)
        before = run_out[s]
        for t in range(NS):
            run_out[t] = run_out[t] + grown[:, t * R : (t + 1) * R]
        grown_norm = grown_norm + actives[s] * (before + run_out[s])
        if s < NS - 1:
            grown = dot(active, cross(s, s + 1, NS - 1 - s))
            for t in range(s + 1, NS):
                run_in[t] = run_in[t] + grown[:, (t - s - 1) * R : (t - s) * R]
    grads = [run_out[t] + spread(proj_at(NS - 1) + t) for t in range(NS)]
    lane = lax.broadcasted_iota(jnp.int32, (rows, BLK), 1)
    scalars = jnp.zeros((rows, BLK), F32)
    for s in range(NS - 1, -1, -1):
        inner = inners[s]
        sigm = jax.nn.sigmoid(inner)
        d_inner = (grads[s] * sigm * (1.0 + inner * (1.0 - sigm))).astype(BF16)
        latent_ref[:, (NS + s) * R : (NS + s + 1) * R] = d_inner
        inverse = inverses[s]
        total = jnp.sum(d_inner.astype(F32) * inner, -1, keepdims=True)
        scale = inverse * inverse * total * (1.0 / width)
        if s > 0:
            back = dot_t(d_inner, above(oi_rows_ref, s))
        for t in range(s):
            grads[t] = (
                grads[t] + inverse * back[:, t * R : (t + 1) * R] - scale * crossed[s][t]
            )
        scalars = jnp.where(lane == s, inverse, scalars)
        scalars = jnp.where(lane == NS + s, scale, scalars)
    scalar_ref[...] = scalars


def grads_kernel(
    ids_ref, other_ids_ref, got_ref, out_w_ref, in_w_ref, latent_ref, scalar_ref,
    give_ref, keep_ref, entry_ref, step_ref,
):
    cols = step_ref.shape[1]
    half = cols // 2
    first_core = lax.axis_index("c") == 0
    scalars = scalar_ref[...]
    inverses = [scalars[:, s : s + 1] for s in range(NS)]
    scales = [scalars[:, NS + s : NS + s + 1] for s in range(NS)]
    places = [
        pl.multiple_of(pick * TOK, TOK) for pick in picks_of(ids_ref, other_ids_ref)
    ]

    def active(s):
        return latent_ref[:, s * R : (s + 1) * R]

    def d_inner(s):
        return latent_ref[:, (NS + s) * R : (NS + s + 1) * R]

    def put(s, kind, value):
        low, high = value[:half].reshape(8, 32, R), value[half:].reshape(8, 32, R)
        at = slice(kind * R, (kind + 1) * R)
        give_ref[:, s, :, at] = jnp.where(first_core, high, low).astype(BF16)
        keep_ref[:, s, :, at] = jnp.where(first_core, low, high)

    def both(part, *args):
        return jnp.concatenate(
            [part(got_ref, *args, 0, half), part(got_ref, *args, HALF, half)], 1
        )

    entry = both(first_rows)
    for s in range(NS):
        if s > 0:
            step_ref[...] = both(stores, s)
            entry = entry + jnp.concatenate([step_ref[pl.ds(place, TOK), :] for place in places], 0)
        entry_ref[s] = entry
        put(s, 0, dot_rows((entry * inverses[s]).astype(BF16), d_inner(s)))
        entry = entry + dot(active(s), out_w_ref[s])
    grad = entry
    for s in range(NS - 1, -1, -1):
        put(s, 1, dot_rows(grad.astype(BF16), active(s)))
        if s > 0:
            back = dot_t(d_inner(s), in_w_ref[s])
            grad = grad + inverses[s] * back - scales[s] * entry_ref[s]


def add_kernel(keep_ref, swapped_ref, total_ref):
    for i in range(8):
        total_ref[i] = (keep_ref[i] + swapped_ref[i].astype(F32)).astype(BF16)


def final_kernel(parts_ref, gain_ref, in_ref, out_ref):
    total = parts_ref[0].astype(F32)
    for i in range(1, 8):
        total = total + parts_ref[i].astype(F32)
    gain = gain_ref[...].T
    for j in range(8):
        scale = gain[(j % 4) * 32 : (j % 4) * 32 + 32, j // 4 : j // 4 + 1]
        in_ref[j * 32 : j * 32 + 32, :] = total[j, :, :R] * scale
    out = total[:, :, R:].reshape(2 * BLK, R)
    for i in range(2):
        out_ref[:, i * BLK : (i + 1) * BLK] = out[i * BLK : (i + 1) * BLK].T


def body(first_input, example_ids, out_store, in_store, norm_gain, adapter_in, adapter_out):
    width = first_input.shape[2]
    cols = width // 16
    half = cols // 2
    core = lax.axis_index("c")
    xl = lax.axis_index("xl")
    z = lax.axis_index("z")
    w_in = adapter_in[0]
    w_out = adapter_out[0]

    ids = example_ids[0]
    other_ids = lax.ppermute(ids, "xl", SWAP)
    wide = width // 2

    def quarter():
        return lax.axis_index("xl") * 2 + lax.axis_index("c")

    send = pl.pallas_call(
        pack_kernel,
        grid=(2,),
        in_specs=[
            pl.BlockSpec((64, wide), lambda i: (0, i)),
            pl.BlockSpec((64, wide), lambda i: (0, i)),
            pl.BlockSpec((32, wide), lambda i: (quarter(), i)),
            pl.BlockSpec(
                (1, 4, 1, 8, 32, R), lambda i: (i, quarter() % 2, quarter() // 2, 0, 0, 0)
            ),
            pl.BlockSpec((1, 4, 1, 2, BLK), lambda i: (i, quarter() % 2, quarter() // 2, 0, 0)),
            pl.BlockSpec((2, 32, wide), lambda i: (section_here() // (NS - 1), 0, i)),
        ],
        out_specs=pl.BlockSpec((8, 32, SENT), lambda i: (i, 0, 0)),
        scratch_shapes=[pltpu.VMEM((4 * BLK, 4 * BLK), BF16)],
        out_shape=jax.ShapeDtypeStruct((16, 32, SENT), BF16),
        compiler_params=LARGE,
        name="pack",
    )(
        in_store.reshape(64, width),
        out_store.reshape(64, width),
        w_out,
        w_in.reshape(2, 8, 2, 8, 32, R),
        norm_gain.reshape(2, 8, 2, 2, BLK),
        first_input,
    )
    send, other_ids = lax.optimization_barrier((send, other_ids))
    got = lax.all_to_all(send, PLANE, 0, 0, tiled=True)
    other = lax.ppermute(got[:, :, W_LANE:], "c", SWAP)
    run = width // 4
    start = pl.pallas_call(
        start_kernel,
        grid=(4,),
        out_shape=jax.ShapeDtypeStruct((R, 2 * R), BF16),
        in_specs=[
            pl.BlockSpec((MIC, 32, run), lambda i: (0, 0, i)),
            pl.BlockSpec((R, run), lambda i: (0, i)),
            pl.BlockSpec((run, R), lambda i: (i, 0)),
            pl.BlockSpec((1, run), lambda i: (0, i)),
            pl.BlockSpec(memory_space=pl.ANY),
        ],
        out_specs=pl.BlockSpec((R, 2 * R), lambda i: (0, 0)),
        scratch_shapes=[pltpu.VMEM((R, 2 * R), F32)],
        compiler_params=LARGE,
        cost_estimate=pl.CostEstimate(flops=600000000, bytes_accessed=7000000, transcendentals=0),
        name="start",
    )(first_input, w_out, w_in, norm_gain, got)
    parts, out_w, in_w = pl.pallas_call(
        project_kernel,
        out_shape=(
            jax.ShapeDtypeStruct((16, 2 * TOK, WIDE), BF16),
            jax.ShapeDtypeStruct((NS, R, cols), BF16),
            jax.ShapeDtypeStruct((NS, cols, R), BF16),
        ),
        in_specs=[SMEM, SMEM, VMEM, VMEM, VMEM],
        out_specs=(VMEM, VMEM, VMEM),
        scratch_shapes=[pltpu.VMEM((R, 2 * SPLIT * BLK), F32)],
        compiler_params=PARAMS,
        cost_estimate=pl.CostEstimate(flops=2000000000, bytes_accessed=9000000, transcendentals=0),
        name="project",
    )(ids, other_ids, got, other, start)
    parts = lax.all_to_all(parts, PLANE, 0, 0, tiled=True)
    sums = pl.pallas_call(
        sum_kernel,
        out_shape=jax.ShapeDtypeStruct((16, 2 * TOK, SPLIT * BLK), BF16),
        in_specs=[VMEM],
        out_specs=VMEM,
        compiler_params=PARAMS,
        name="sums",
    )(parts)
    sums = lax.all_to_all(sums, PLANE, 0, 0, tiled=True)
    gram = sums[:, TOK:, (GRAM - SPLIT) * BLK : (GRAM - SPLIT + GRAMS) * BLK]
    gram = gram.reshape(R, GRAMS * BLK)
    other = lax.ppermute(gram, "c", SWAP)
    base = pl.pallas_call(
        gather_kernel,
        out_shape=jax.ShapeDtypeStruct((2 * R, GRAM * BLK), F32),
        in_specs=[SMEM, SMEM, VMEM],
        out_specs=VMEM,
        scratch_shapes=[pltpu.VMEM((R, GRAM * BLK), F32)],
        compiler_params=PARAMS,
        cost_estimate=pl.CostEstimate(flops=0, bytes_accessed=7000000, transcendentals=0),
        name="gather",
    )(ids, other_ids, sums)
    latent, scalars = pl.pallas_call(
        functools.partial(chain_kernel, width),
        out_shape=(
            jax.ShapeDtypeStruct((2 * R, 16 * BLK), BF16),
            jax.ShapeDtypeStruct((2 * R, BLK), F32),
        ),
        in_specs=[VMEM] * 4,
        out_specs=(VMEM, VMEM),
        scratch_shapes=[
            pltpu.VMEM((R, OO * BLK), BF16),
            pltpu.VMEM((R, OI * BLK), BF16),
            pltpu.VMEM((OI * R, R), BF16),
            pltpu.VMEM((OI * R, R), BF16),
        ],
        compiler_params=PARAMS,
        name="chain",
    )(parts, base, gram, other)

    give, keep = pl.pallas_call(
        grads_kernel,
        out_shape=(
            jax.ShapeDtypeStruct((8, NS, 32, 2 * R), BF16),
            jax.ShapeDtypeStruct((8, NS, 32, 2 * R), F32),
        ),
        in_specs=[SMEM, SMEM] + [VMEM] * 5,
        out_specs=(VMEM, VMEM),
        scratch_shapes=[pltpu.VMEM((NS, 2 * R, cols), F32), pltpu.VMEM((R, cols), F32)],
        compiler_params=PARAMS,
        name="grads",
    )(ids, other_ids, got, out_w, in_w, latent, scalars)
    swapped = lax.ppermute(give, "c", SWAP)
    total = pl.pallas_call(
        add_kernel,
        out_shape=jax.ShapeDtypeStruct((8, NS, 32, 2 * R), BF16),
        in_specs=[VMEM, VMEM],
        out_specs=VMEM,
        compiler_params=PARAMS,
        name="add",
    )(keep, swapped).reshape(64, 32, 2 * R)
    block = (xl * NS + z) * 2 + core
    gain = lax.dynamic_slice_in_dim(norm_gain[0], block * half, half, 0)
    total, gain = lax.optimization_barrier((total, gain))
    total = lax.all_to_all(total, ("z",) + SECTION, 0, 0, tiled=True)
    grad_in, grad_out = pl.pallas_call(
        final_kernel,
        out_shape=(
            jax.ShapeDtypeStruct((half, R), F32),
            jax.ShapeDtypeStruct((R, half), F32),
        ),
        in_specs=[VMEM, VMEM],
        out_specs=(VMEM, VMEM),
        compiler_params=PARAMS,
        name="final",
    )(total.reshape(8, 8, 32, 2 * R), gain.reshape(2, BLK))
    return (grad_in[None], grad_out[None])


def solution(mesh):
    fine = Mesh(mesh.devices.reshape(2, 8, 2, 4, 2), ("xl", "z", "c", "y", "xh"))
    dp = ("xl", "z", "c")
    placed = (
        P(None, dp, None),
        P(dp, None, None),
        P(SECTION, dp, None, None),
        P(SECTION, dp, None, None),
        P(SECTION, None),
        P(SECTION, None, None),
        P(SECTION, None, None),
    )
    return jax.shard_map(
        body,
        mesh=fine,
        in_specs=placed,
        out_specs=(P(SECTION, dp, None), P(SECTION, None, dp)),
        check_vma=False,
    )
```

```python
import functools

import jax
import jax.numpy as jnp
from jax import lax
from jax.experimental import pallas as pl
from jax.experimental.pallas import tpu as pltpu
from jax.sharding import Mesh, PartitionSpec as P

F32 = jnp.float32
BF16 = jnp.bfloat16
EPS = 1e-05
PLANE = ("xl", "y", "xh")
SECTION = ("y", "xh")
SWAP = [(0, 1), (1, 0)]
NS = 8
R = 128
TOK = 8
MIC = 4
BLK = 128
HALF = 1024
W_LANE = 2 * HALF
SENT = 3072
PROJ = 29
NORM = 34
GRAM = 37
GRAMS = 32
SPLIT = 35
START = SPLIT * BLK
WIDE = START + 16 * BLK
OO = 36
OI = 28
LARGE = pltpu.CompilerParams(vmem_limit_bytes=56 * 1024 * 1024)
PARAMS = pltpu.CompilerParams(vmem_limit_bytes=16 * 1024 * 1024)
VMEM = pl.BlockSpec(memory_space=pltpu.VMEM)
SMEM = pl.BlockSpec(memory_space=pltpu.SMEM)


def gram_at(t):
    return sum(NS - i for i in range(t))


def cross_at(t):
    return sum(NS - 1 - i for i in range(t))


def proj_at(s):
    return s * (s - 1) // 2


def inner_at(s):
    return PROJ + s - 1 + (PROJ + s - 1 >= NORM)


def dot_t(a, b):
    return lax.dot_general(a, b, (((1,), (1,)), ((), ())), preferred_element_type=F32)


def dot_rows(a, b):
    return lax.dot_general(a, b, (((0,), (0,)), ((), ())), preferred_element_type=F32)


def dot(a, b):
    return jnp.dot(a, b, preferred_element_type=F32)


def split(x):
    high = x.astype(BF16)
    return high, (x - high.astype(F32)).astype(BF16)


def section_here():
    return lax.axis_index("y") * 2 + lax.axis_index("xh")


def pack_kernel(
    in_ref, out_ref, w_out_ref, w_in_ref, gain_ref, first_ref, send_ref, turn_ref
):
    section = section_here()

    @pl.when(pl.program_id(0) == 0)
    def _():
        shape = (4 * BLK, 4 * BLK)
        row = lax.broadcasted_iota(jnp.int32, shape, 0)
        col = lax.broadcasted_iota(jnp.int32, shape, 1)
        same = (row // BLK == col % BLK // 32) & (row % BLK // 32 == col // BLK)
        same = same & (row % 32 == col % 32)
        turn_ref[...] = jnp.where(same, 1.0, 0.0).astype(BF16)

    gain = gain_ref[...].reshape(8, BLK).T
    for s in range(NS):
        for j in range(4):
            column = 2 * j + s // 4
            scale = gain[(s % 4) * 32 : (s % 4) * 32 + 32, column : column + 1]
            to = W_LANE + 512 + j * BLK
            send_ref[s, :, to : to + BLK] = (w_in_ref[0, j, 0, s].astype(F32) * scale).astype(BF16)

    pieces, places = [], []
    for c in range(2):
        for zq in range(2):
            to = c * 256 + zq * BLK
            for h in range(2):
                lanes = [((4 * zq + j) * 4 + c * 2 + h) * BLK for j in range(4)]
                for ref, row, at, other in (
                    (in_ref, 0, c * HALF + zq * BLK, 0),
                    (in_ref, 32, c * HALF + 256 + zq * BLK, 0),
                    (out_ref, 0, c * HALF + 512 + zq * BLK, NS - 1),
                    (out_ref, 32, c * HALF + 768 + zq * BLK, NS - 1),
                    (w_out_ref, 0, W_LANE + to, None),
                ):
                    piece = jnp.concatenate(
                        [ref[row : row + 32, lane : lane + BLK] for lane in lanes], 1
                    )
                    if other is not None:
                        first = jnp.concatenate(
                            [first_ref[row // 32, :, lane : lane + BLK] for lane in lanes], 1
                        )
                        piece = jnp.where(section == other, first, piece)
                    pieces.append(piece)
                    places.append((4 * h, at))
    turned = dot(jnp.concatenate(pieces, 0), turn_ref[...]).astype(BF16)
    for n, (first, at) in enumerate(places):
        for i in range(4):
            send_ref[first + i, :, at : at + BLK] = turned[
                32 * n : 32 * n + 32, i * BLK : (i + 1) * BLK
            ]


def start_kernel(first_ref, w_out_ref, w_in_ref, gain_ref, after_ref, start_ref):
    del after_ref
    flat = first_ref[...].reshape(R, first_ref.shape[2])
    scaled = (flat.astype(F32) * gain_ref[...]).astype(BF16)
    start_ref[:, :R] = dot(scaled, w_in_ref[...]).astype(BF16)
    start_ref[:, R:] = dot_t(flat, w_out_ref[...]).astype(BF16)


def stores(got_ref, s, at, cols):
    pieces = []
    for x in range(2):
        for i in range(2):
            a, b = at + i * 256, at + 512 + i * 256
            pieces.append(
                got_ref[x * NS + s, :, pl.ds(a, cols)].astype(F32)
                - got_ref[x * NS + s - 1, :, pl.ds(b, cols)].astype(F32)
            )
    return jnp.concatenate(pieces, 0)


def first_rows(got_ref, at, cols):
    pieces = []
    for x in range(2):
        for m in range(MIC):
            q = x * NS + (0 if m < 2 else NS - 1)
            lane = at + m // 2 * 512 + m % 2 * 256
            pieces.append(got_ref[q, :, pl.ds(lane, cols)])
    return jnp.concatenate(pieces, 0).astype(F32)


def picks_of(ids_ref, other_ids_ref):
    picks = []
    for x in range(2):
        here = lax.axis_index("xl") == x
        for m in range(MIC):
            for j in range(4):
                picks.append(x * NS + jnp.where(here, ids_ref[m, j], other_ids_ref[m, j]))
    return picks


def running_sums(got_ref, cols):
    running = None
    for s in range(1, NS):
        step = jnp.concatenate(
            [stores(got_ref, s, 0, cols // 2), stores(got_ref, s, HALF, cols // 2)], 1
        )
        running = step if running is None else running + step
        yield s, running


def placed_rows(ids_ref, other_ids_ref, got_ref, cols):
    picks = picks_of(ids_ref, other_ids_ref)
    placed = [[] for _ in range(MIC)]
    first = jnp.concatenate(
        [first_rows(got_ref, 0, cols // 2), first_rows(got_ref, HALF, cols // 2)], 1
    )
    for x in range(2):
        rows = first[x * R : (x + 1) * R]
        for e in range(NS):
            for m in range(MIC):
                total = jnp.zeros((TOK, cols), F32)
                for j in range(4):
                    n = 4 * m + j
                    total = jnp.where(
                        picks[16 * x + n] == x * NS + e, rows[n * TOK : (n + 1) * TOK], total
                    )
                placed[m].append(total)
    return [jnp.concatenate(blocks, 0) for blocks in placed]


def project_kernel(
    ids_ref, other_ids_ref, got_ref, other_ref, start_ref, send_ref, out_w_ref, in_w_ref, wide_ref
):
    cols = in_w_ref.shape[1]
    first_core = lax.axis_index("c") == 0
    for s in range(NS):
        for x in range(2):
            mine = got_ref[x * NS + s, :, W_LANE:SENT]
            theirs = other_ref[x * NS + s]
            for c in range(2):
                part = jnp.where(first_core == (c == 0), mine, theirs)
                k = 2 * x + c
                out_w_ref[s, 32 * k : 32 * k + 32, :] = part[:, :cols]
                for g in range(4):
                    row = k * BLK + g * 32
                    lane = cols + g * BLK
                    in_w_ref[s, row : row + 32, :] = part[:, lane : lane + BLK]
    placed = placed_rows(ids_ref, other_ids_ref, got_ref, cols)
    lane = lax.broadcasted_iota(jnp.int32, (R, BLK), 1)
    norms = jnp.zeros((R, BLK), F32)
    for m in range(MIC):
        part = jnp.sum(placed[m] * placed[m], -1, keepdims=True)
        norms = jnp.where(lane == m * NS, part, norms)
    for s, running in running_sums(got_ref, cols):
        for m in range(MIC):
            entry = running + placed[m]
            part = jnp.sum(entry * entry, -1, keepdims=True)
            norms = jnp.where(lane == m * NS + s, part, norms)
        rounded = running.astype(BF16)
        count = s if s < NS - 1 else NS
        at = proj_at(s) * BLK
        wide_ref[:, at : at + count * BLK] = dot_t(
            rounded, out_w_ref[0:count].reshape(count * R, cols)
        )
        at = inner_at(s) * BLK
        wide_ref[:, at : at + BLK] = dot(rounded, in_w_ref[s])
    high = norms.astype(BF16).astype(F32)
    wide_ref[:, NORM * BLK : (NORM + 1) * BLK] = jnp.where(
        lane < 32, high, pltpu.roll(norms - high, 32, 1)
    )
    wide_ref[:, (GRAM + GRAMS) * BLK :] = jnp.zeros((R, BLK), F32)

    square = [(t, s) for t in range(NS) for s in range(t, NS)]

    @pl.when(first_core)
    def _():
        for t in range(5):
            at = (GRAM + gram_at(t)) * BLK
            wide_ref[:, at : at + (NS - t) * BLK] = dot_t(
                out_w_ref[t], out_w_ref[t:NS].reshape((NS - t) * R, cols)
            )
        for i in range(gram_at(5), GRAMS):
            t, s = square[i]
            at = (GRAM + i) * BLK
            wide_ref[:, at : at + BLK] = dot_t(out_w_ref[t], out_w_ref[s])

    @pl.when(jnp.logical_not(first_core))
    def _():
        for t in range(NS - 1):
            for s in range(t + 1, NS):
                at = (GRAM + cross_at(t) + s - t - 1) * BLK
                wide_ref[:, at : at + BLK] = dot(out_w_ref[t], in_w_ref[s])
        for i in range(GRAMS, OO):
            t, s = square[i]
            at = (GRAM + OI + i - GRAMS) * BLK
            wide_ref[:, at : at + BLK] = dot_t(out_w_ref[t], out_w_ref[s])

    for b in range(SPLIT):
        pair = [
            wide_ref[:, at * BLK : (at + 1) * BLK].reshape(16, TOK, BLK) for at in (b, SPLIT + b)
        ]
        send_ref[:, :, b * BLK : (b + 1) * BLK] = jnp.concatenate(pair, 1).astype(BF16)
    for g in range(8):
        at = START + g * 2 * R
        for q in range(16):
            send_ref[q, :, at : at + 2 * R] = start_ref[g * 16 : (g + 1) * 16, :]


def sum_kernel(parts_ref, send_ref):
    lane = lax.broadcasted_iota(jnp.int32, (2 * TOK, BLK), 1)
    row = lax.broadcasted_iota(jnp.int32, (2 * TOK, BLK), 0)
    for b in range(SPLIT):
        at = slice(b * BLK, (b + 1) * BLK)
        total = parts_ref[0, :, at].astype(F32)
        for q in range(1, 16):
            total = total + parts_ref[q, :, at].astype(F32)
        if b == NORM:
            norm = total + pltpu.roll(total, 96, 1)
            high = norm.astype(BF16).astype(F32)
            norm = jnp.where(lane < 32, high, pltpu.roll(norm - high, 32, 1))
            total = jnp.where(row < TOK, norm, 0.0)
        total = total.astype(BF16)
        for q in range(16):
            send_ref[q, :, at] = total


def gather_kernel(ids_ref, other_ids_ref, sums_ref, base_ref, proj_ref):
    for b in range(GRAM):
        upper = b >= SPLIT
        at = (b - SPLIT * upper) * BLK
        block = sums_ref[:, :, at : at + BLK].astype(F32)
        proj_ref[:, b * BLK : (b + 1) * BLK] = block[:, TOK * upper : TOK * upper + TOK].reshape(
            R, BLK
        )
    for n, pick in enumerate(picks_of(ids_ref, other_ids_ref)):
        rows = slice(n * TOK, (n + 1) * TOK)
        here = pl.ds(pl.multiple_of(pick * TOK, TOK), TOK)
        base_ref[rows, :] = proj_ref[here, :]
        norm = proj_ref[here, NORM * BLK : (NORM + 1) * BLK]
        norm = norm + pltpu.roll(norm, 96, 1)
        m = n % 16 // 4
        base_ref[rows, NORM * BLK : (NORM + 1) * BLK] = (
            pltpu.roll(norm, BLK - m * NS, 1) if m else norm
        )


def chain_kernel(
    width, parts_ref, base_ref, gram_ref, other_ref,
    latent_ref, scalar_ref, oo_ref, oi_ref, oo_rows_ref, oi_rows_ref,
):
    rows = 2 * R
    first_core = lax.axis_index("c") == 0
    for b in range(0, GRAMS, 4):
        at = slice(b * BLK, (b + 4) * BLK)
        mine, theirs = gram_ref[:, at], other_ref[:, at]
        oo_ref[:, at] = jnp.where(first_core, mine, theirs)
        second = jnp.where(first_core, theirs, mine)
        if b < OI:
            oi_ref[:, at] = second
        else:
            oo_ref[:, (b + 4) * BLK : (b + 8) * BLK] = second

    def spread(at):
        return base_ref[:, at * BLK : (at + 1) * BLK]

    def square(t, s, count=1):
        at = (gram_at(t) + s - t) * BLK
        return oo_ref[:, at : at + count * BLK]

    def cross(t, s, count=1):
        at = (cross_at(t) + s - t - 1) * BLK
        return oi_ref[:, at : at + count * BLK]

    for s in range(1, NS):
        for t in range(s):
            at = slice((proj_at(s) + t) * R, (proj_at(s) + t + 1) * R)
            oo_rows_ref[at, :] = square(t, s)
            oi_rows_ref[at, :] = cross(t, s)

    def above(ref, s):
        return ref[proj_at(s) * R : (proj_at(s) + s) * R, :]

    norms = spread(NORM)
    starts = []
    for s in range(NS):
        pieces = []
        for x in range(2):
            for g in range(8):
                at = START + g * 2 * R
                pieces.append(parts_ref[x * NS + s, :, at : at + 2 * R])
        starts.append(jnp.concatenate(pieces, 0))
    start_out = [start[:, R:].astype(F32) for start in starts]
    run_in = [start[:, :R].astype(F32) for start in starts]
    run_out = list(start_out)
    inners, inverses, actives, crossed = [], [], [], []
    grown_norm = jnp.zeros((rows, R), F32)
    for s in range(NS):
        norm = norms[:, s : s + 1]
        entry_out = []
        inner = run_in[s]
        if s > 0:
            inner = inner + spread(inner_at(s))
            total = jnp.zeros((rows, R), F32)
            for t in range(s):
                base = spread(proj_at(s) + t)
                entry_out.append(base + run_out[t])
                total = total + actives[t] * base
            norm = norm + jnp.sum(2.0 * total + grown_norm, -1, keepdims=True)
        inverse = lax.rsqrt(jnp.maximum(norm, 0.0) * (1.0 / width) + EPS)
        inner = inner * inverse
        active = (inner * jax.nn.sigmoid(inner)).astype(BF16)
        latent_ref[:, s * R : (s + 1) * R] = active
        inners.append(inner)
        inverses.append(inverse)
        actives.append(active.astype(F32))
        crossed.append(entry_out)
        grown = dot(active, square(s, s, NS - s))
        if s > 0:
            grown = jnp.concatenate([dot_t(active, above(oo_rows_ref, s)), grown], 1)
        before = run_out[s]
        for t in range(NS):
            run_out[t] = run_out[t] + grown[:, t * R : (t + 1) * R]
        grown_norm = grown_norm + actives[s] * (before + run_out[s])
        if s < NS - 1:
            grown = dot(active, cross(s, s + 1, NS - 1 - s))
            for t in range(s + 1, NS):
                run_in[t] = run_in[t] + grown[:, (t - s - 1) * R : (t - s) * R]
    grads = [run_out[t] + spread(proj_at(NS - 1) + t) for t in range(NS)]
    lane = lax.broadcasted_iota(jnp.int32, (rows, BLK), 1)
    scalars = jnp.zeros((rows, BLK), F32)
    for s in range(NS - 1, -1, -1):
        inner = inners[s]
        sigm = jax.nn.sigmoid(inner)
        d_inner = (grads[s] * sigm * (1.0 + inner * (1.0 - sigm))).astype(BF16)
        latent_ref[:, (NS + s) * R : (NS + s + 1) * R] = d_inner
        inverse = inverses[s]
        total = jnp.sum(d_inner.astype(F32) * inner, -1, keepdims=True)
        scale = inverse * inverse * total * (1.0 / width)
        if s > 0:
            back = dot_t(d_inner, above(oi_rows_ref, s))
        for t in range(s):
            grads[t] = (
                grads[t] + inverse * back[:, t * R : (t + 1) * R] - scale * crossed[s][t]
            )
        scalars = jnp.where(lane == s, inverse, scalars)
        scalars = jnp.where(lane == NS + s, scale, scalars)
    scalar_ref[...] = scalars


def grads_kernel(
    ids_ref, other_ids_ref, got_ref, out_w_ref, in_w_ref, latent_ref, scalar_ref,
    give_ref, keep_ref, entry_ref, step_ref,
):
    cols = step_ref.shape[1]
    half = cols // 2
    first_core = lax.axis_index("c") == 0
    scalars = scalar_ref[...]
    inverses = [scalars[:, s : s + 1] for s in range(NS)]
    scales = [scalars[:, NS + s : NS + s + 1] for s in range(NS)]
    places = [
        pl.multiple_of(pick * TOK, TOK) for pick in picks_of(ids_ref, other_ids_ref)
    ]

    def active(s):
        return latent_ref[:, s * R : (s + 1) * R]

    def d_inner(s):
        return latent_ref[:, (NS + s) * R : (NS + s + 1) * R]

    def put(s, kind, value):
        low, high = value[:half].reshape(8, 32, R), value[half:].reshape(8, 32, R)
        at = slice(kind * R, (kind + 1) * R)
        give_ref[s, :, :, at] = jnp.where(first_core, high, low).astype(BF16)
        keep_ref[s, :, :, at] = jnp.where(first_core, low, high)

    def both(part, *args):
        return jnp.concatenate(
            [part(got_ref, *args, 0, half), part(got_ref, *args, HALF, half)], 1
        )

    entry = both(first_rows)
    for s in range(NS):
        if s > 0:
            step_ref[...] = both(stores, s)
            entry = entry + jnp.concatenate([step_ref[pl.ds(place, TOK), :] for place in places], 0)
        entry_ref[s] = entry
        put(s, 0, dot_rows((entry * inverses[s]).astype(BF16), d_inner(s)))
        entry = entry + dot(active(s), out_w_ref[s])
    grad = entry
    for s in range(NS - 1, -1, -1):
        put(s, 1, dot_rows(grad.astype(BF16), active(s)))
        if s > 0:
            back = dot_t(d_inner(s), in_w_ref[s])
            grad = grad + inverses[s] * back - scales[s] * entry_ref[s]


def add_kernel(keep_ref, swapped_ref, total_ref):
    for i in range(8):
        total_ref[i] = (keep_ref[i] + swapped_ref[i].astype(F32)).astype(BF16)


def final_kernel(parts_ref, gain_ref, in_ref, out_ref):
    total = parts_ref[:, 0].astype(F32)
    for i in range(1, 8):
        total = total + parts_ref[:, i].astype(F32)
    gain = gain_ref[...].T
    for j in range(8):
        scale = gain[(j % 4) * 32 : (j % 4) * 32 + 32, j // 4 : j // 4 + 1]
        in_ref[j * 32 : j * 32 + 32, :] = total[j, :, :R] * scale
    out = total[:, :, R:].reshape(2 * BLK, R)
    for i in range(2):
        out_ref[:, i * BLK : (i + 1) * BLK] = out[i * BLK : (i + 1) * BLK].T


def body(first_input, example_ids, out_store, in_store, norm_gain, adapter_in, adapter_out):
    width = first_input.shape[2]
    cols = width // 16
    half = cols // 2
    core = lax.axis_index("c")
    xl = lax.axis_index("xl")
    z = lax.axis_index("z")
    w_in = adapter_in[0]
    w_out = adapter_out[0]

    ids = example_ids[0]
    other_ids = lax.ppermute(ids, "xl", SWAP)
    wide = width // 2

    def quarter():
        return lax.axis_index("xl") * 2 + lax.axis_index("c")

    send = pl.pallas_call(
        pack_kernel,
        grid=(2,),
        in_specs=[
            pl.BlockSpec((64, wide), lambda i: (0, i)),
            pl.BlockSpec((64, wide), lambda i: (0, i)),
            pl.BlockSpec((32, wide), lambda i: (quarter(), i)),
            pl.BlockSpec(
                (1, 4, 1, 8, 32, R), lambda i: (i, quarter() % 2, quarter() // 2, 0, 0, 0)
            ),
            pl.BlockSpec((1, 4, 1, 2, BLK), lambda i: (i, quarter() % 2, quarter() // 2, 0, 0)),
            pl.BlockSpec((2, 32, wide), lambda i: (section_here() // (NS - 1), 0, i)),
        ],
        out_specs=pl.BlockSpec((8, 32, SENT), lambda i: (i, 0, 0)),
        scratch_shapes=[pltpu.VMEM((4 * BLK, 4 * BLK), BF16)],
        out_shape=jax.ShapeDtypeStruct((16, 32, SENT), BF16),
        compiler_params=LARGE,
        name="pack",
    )(
        in_store.reshape(64, width),
        out_store.reshape(64, width),
        w_out,
        w_in.reshape(2, 8, 2, 8, 32, R),
        norm_gain.reshape(2, 8, 2, 2, BLK),
        first_input,
    )
    send, other_ids = lax.optimization_barrier((send, other_ids))
    got = lax.all_to_all(send, PLANE, 0, 0, tiled=True)
    other = lax.ppermute(got[:, :, W_LANE:], "c", SWAP)
    start = pl.pallas_call(
        start_kernel,
        out_shape=jax.ShapeDtypeStruct((R, 2 * R), BF16),
        in_specs=[VMEM, VMEM, VMEM, VMEM, pl.BlockSpec(memory_space=pl.ANY)],
        out_specs=VMEM,
        compiler_params=PARAMS,
        cost_estimate=pl.CostEstimate(flops=600000000, bytes_accessed=7000000, transcendentals=0),
        name="start",
    )(first_input, w_out, w_in, norm_gain, got)
    parts, out_w, in_w = pl.pallas_call(
        project_kernel,
        out_shape=(
            jax.ShapeDtypeStruct((16, 2 * TOK, WIDE), BF16),
            jax.ShapeDtypeStruct((NS, R, cols), BF16),
            jax.ShapeDtypeStruct((NS, cols, R), BF16),
        ),
        in_specs=[SMEM, SMEM, VMEM, VMEM, VMEM],
        out_specs=(VMEM, VMEM, VMEM),
        scratch_shapes=[pltpu.VMEM((R, 2 * SPLIT * BLK), F32)],
        compiler_params=PARAMS,
        cost_estimate=pl.CostEstimate(flops=2000000000, bytes_accessed=9000000, transcendentals=0),
        name="project",
    )(ids, other_ids, got, other, start)
    parts = lax.all_to_all(parts, PLANE, 0, 0, tiled=True)
    sums = pl.pallas_call(
        sum_kernel,
        out_shape=jax.ShapeDtypeStruct((16, 2 * TOK, SPLIT * BLK), BF16),
        in_specs=[VMEM],
        out_specs=VMEM,
        compiler_params=PARAMS,
        name="sums",
    )(parts)
    sums = lax.all_to_all(sums, PLANE, 0, 0, tiled=True)
    gram = sums[:, TOK:, (GRAM - SPLIT) * BLK : (GRAM - SPLIT + GRAMS) * BLK]
    gram = gram.reshape(R, GRAMS * BLK)
    other = lax.ppermute(gram, "c", SWAP)
    base = pl.pallas_call(
        gather_kernel,
        out_shape=jax.ShapeDtypeStruct((2 * R, GRAM * BLK), F32),
        in_specs=[SMEM, SMEM, VMEM],
        out_specs=VMEM,
        scratch_shapes=[pltpu.VMEM((R, GRAM * BLK), F32)],
        compiler_params=PARAMS,
        cost_estimate=pl.CostEstimate(flops=0, bytes_accessed=7000000, transcendentals=0),
        name="gather",
    )(ids, other_ids, sums)
    latent, scalars = pl.pallas_call(
        functools.partial(chain_kernel, width),
        out_shape=(
            jax.ShapeDtypeStruct((2 * R, 16 * BLK), BF16),
            jax.ShapeDtypeStruct((2 * R, BLK), F32),
        ),
        in_specs=[VMEM] * 4,
        out_specs=(VMEM, VMEM),
        scratch_shapes=[
            pltpu.VMEM((R, OO * BLK), BF16),
            pltpu.VMEM((R, OI * BLK), BF16),
            pltpu.VMEM((OI * R, R), BF16),
            pltpu.VMEM((OI * R, R), BF16),
        ],
        compiler_params=PARAMS,
        name="chain",
    )(parts, base, gram, other)

    give, keep = pl.pallas_call(
        grads_kernel,
        out_shape=(
            jax.ShapeDtypeStruct((NS, 8, 32, 2 * R), BF16),
            jax.ShapeDtypeStruct((NS, 8, 32, 2 * R), F32),
        ),
        in_specs=[SMEM, SMEM] + [VMEM] * 5,
        out_specs=(VMEM, VMEM),
        scratch_shapes=[pltpu.VMEM((NS, 2 * R, cols), F32), pltpu.VMEM((R, cols), F32)],
        compiler_params=PARAMS,
        name="grads",
    )(ids, other_ids, got, out_w, in_w, latent, scalars)
    swapped = lax.ppermute(give, "c", SWAP)
    total = pl.pallas_call(
        add_kernel,
        out_shape=jax.ShapeDtypeStruct((NS, 8, 32, 2 * R), BF16),
        in_specs=[VMEM, VMEM],
        out_specs=VMEM,
        compiler_params=PARAMS,
        name="add",
    )(keep, swapped).reshape(64, 32, 2 * R)
    block = (xl * NS + z) * 2 + core
    gain = lax.dynamic_slice_in_dim(norm_gain[0], block * half, half, 0)
    total, gain = lax.optimization_barrier((total, gain))
    total = lax.all_to_all(total, SECTION + ("z",), 0, 0, tiled=True)
    grad_in, grad_out = pl.pallas_call(
        final_kernel,
        out_shape=(
            jax.ShapeDtypeStruct((half, R), F32),
            jax.ShapeDtypeStruct((R, half), F32),
        ),
        in_specs=[VMEM, VMEM],
        out_specs=(VMEM, VMEM),
        compiler_params=PARAMS,
        name="final",
    )(total.reshape(8, 8, 32, 2 * R), gain.reshape(2, BLK))
    return (grad_in[None], grad_out[None])


def solution(mesh):
    fine = Mesh(mesh.devices.reshape(2, 8, 2, 4, 2), ("xl", "z", "c", "y", "xh"))
    dp = ("xl", "z", "c")
    placed = (
        P(None, dp, None),
        P(dp, None, None),
        P(SECTION, dp, None, None),
        P(SECTION, dp, None, None),
        P(SECTION, None),
        P(SECTION, None, None),
        P(SECTION, None, None),
    )
    return jax.shard_map(
        body,
        mesh=fine,
        in_specs=placed,
        out_specs=(P(SECTION, dp, None), P(SECTION, None, dp)),
        check_vma=False,
    )
```

```python
import functools

import jax
import jax.numpy as jnp
from jax import lax
from jax.experimental import pallas as pl
from jax.experimental.pallas import tpu as pltpu
from jax.sharding import Mesh, PartitionSpec as P

F32 = jnp.float32
BF16 = jnp.bfloat16
EPS = 1e-05
PLANE = ("xl", "y", "xh")
SECTION = ("y", "xh")
SWAP = [(0, 1), (1, 0)]
NS = 8
R = 128
TOK = 8
MIC = 4
BLK = 128
HALF = 1024
W_LANE = 2 * HALF
SENT = 3072
PROJ = 29
NORM = 34
GRAM = 37
GRAMS = 32
SPLIT = 35
START = SPLIT * BLK
WIDE = START + 16 * BLK
OO = 36
OI = 28
LARGE = pltpu.CompilerParams(vmem_limit_bytes=56 * 1024 * 1024)
PARAMS = pltpu.CompilerParams(vmem_limit_bytes=16 * 1024 * 1024)
VMEM = pl.BlockSpec(memory_space=pltpu.VMEM)
SMEM = pl.BlockSpec(memory_space=pltpu.SMEM)


def gram_at(t):
    return sum(NS - i for i in range(t))


def cross_at(t):
    return sum(NS - 1 - i for i in range(t))


def proj_at(s):
    return s * (s - 1) // 2


def inner_at(s):
    return PROJ + s - 1 + (PROJ + s - 1 >= NORM)


def dot_t(a, b):
    return lax.dot_general(a, b, (((1,), (1,)), ((), ())), preferred_element_type=F32)


def dot_rows(a, b):
    return lax.dot_general(a, b, (((0,), (0,)), ((), ())), preferred_element_type=F32)


def dot(a, b):
    return jnp.dot(a, b, preferred_element_type=F32)


def split(x):
    high = x.astype(BF16)
    return high, (x - high.astype(F32)).astype(BF16)


def section_here():
    return lax.axis_index("y") * 2 + lax.axis_index("xh")


def pack_kernel(
    in_ref, out_ref, w_out_ref, w_in_ref, gain_ref, first_ref, send_ref, turn_ref
):
    section = section_here()

    @pl.when(pl.program_id(0) == 0)
    def _():
        shape = (4 * BLK, 4 * BLK)
        row = lax.broadcasted_iota(jnp.int32, shape, 0)
        col = lax.broadcasted_iota(jnp.int32, shape, 1)
        same = (row // BLK == col % BLK // 32) & (row % BLK // 32 == col // BLK)
        same = same & (row % 32 == col % 32)
        turn_ref[...] = jnp.where(same, 1.0, 0.0).astype(BF16)

    gain = gain_ref[...].reshape(8, BLK).T
    for s in range(NS):
        for j in range(4):
            column = 2 * j + s // 4
            scale = gain[(s % 4) * 32 : (s % 4) * 32 + 32, column : column + 1]
            to = W_LANE + 512 + j * BLK
            send_ref[s, :, to : to + BLK] = (w_in_ref[0, j, 0, s].astype(F32) * scale).astype(BF16)

    pieces, places = [], []
    for c in range(2):
        for zq in range(2):
            to = c * 256 + zq * BLK
            for h in range(2):
                lanes = [((4 * zq + j) * 4 + c * 2 + h) * BLK for j in range(4)]
                for ref, row, at, other in (
                    (in_ref, 0, c * HALF + zq * BLK, 0),
                    (in_ref, 32, c * HALF + 256 + zq * BLK, 0),
                    (out_ref, 0, c * HALF + 512 + zq * BLK, NS - 1),
                    (out_ref, 32, c * HALF + 768 + zq * BLK, NS - 1),
                    (w_out_ref, 0, W_LANE + to, None),
                ):
                    piece = jnp.concatenate(
                        [ref[row : row + 32, lane : lane + BLK] for lane in lanes], 1
                    )
                    if other is not None:
                        first = jnp.concatenate(
                            [first_ref[row // 32, :, lane : lane + BLK] for lane in lanes], 1
                        )
                        piece = jnp.where(section == other, first, piece)
                    pieces.append(piece)
                    places.append((4 * h, at))
    turned = dot(jnp.concatenate(pieces, 0), turn_ref[...]).astype(BF16)
    for n, (first, at) in enumerate(places):
        for i in range(4):
            send_ref[first + i, :, at : at + BLK] = turned[
                32 * n : 32 * n + 32, i * BLK : (i + 1) * BLK
            ]


def start_in_kernel(first_ref, w_in_ref, gain_ref, after_ref, start_ref):
    del after_ref
    flat = first_ref[...].reshape(R, first_ref.shape[2])
    scaled = (flat.astype(F32) * gain_ref[...]).astype(BF16)
    start_ref[...] = dot(scaled, w_in_ref[...]).astype(BF16)


def start_out_kernel(first_ref, w_out_ref, after_ref, start_ref):
    del after_ref
    flat = first_ref[...].reshape(R, first_ref.shape[2])
    start_ref[...] = dot_t(flat, w_out_ref[...]).astype(BF16)


def stores(got_ref, s, at, cols):
    pieces = []
    for x in range(2):
        for i in range(2):
            a, b = at + i * 256, at + 512 + i * 256
            pieces.append(
                got_ref[x * NS + s, :, pl.ds(a, cols)].astype(F32)
                - got_ref[x * NS + s - 1, :, pl.ds(b, cols)].astype(F32)
            )
    return jnp.concatenate(pieces, 0)


def first_rows(got_ref, at, cols):
    pieces = []
    for x in range(2):
        for m in range(MIC):
            q = x * NS + (0 if m < 2 else NS - 1)
            lane = at + m // 2 * 512 + m % 2 * 256
            pieces.append(got_ref[q, :, pl.ds(lane, cols)])
    return jnp.concatenate(pieces, 0).astype(F32)


def picks_of(ids_ref, other_ids_ref):
    picks = []
    for x in range(2):
        here = lax.axis_index("xl") == x
        for m in range(MIC):
            for j in range(4):
                picks.append(x * NS + jnp.where(here, ids_ref[m, j], other_ids_ref[m, j]))
    return picks


def running_sums(got_ref, cols):
    running = None
    for s in range(1, NS):
        step = jnp.concatenate(
            [stores(got_ref, s, 0, cols // 2), stores(got_ref, s, HALF, cols // 2)], 1
        )
        running = step if running is None else running + step
        yield s, running


def placed_rows(ids_ref, other_ids_ref, got_ref, cols):
    picks = picks_of(ids_ref, other_ids_ref)
    placed = [[] for _ in range(MIC)]
    first = jnp.concatenate(
        [first_rows(got_ref, 0, cols // 2), first_rows(got_ref, HALF, cols // 2)], 1
    )
    for x in range(2):
        rows = first[x * R : (x + 1) * R]
        for e in range(NS):
            for m in range(MIC):
                total = jnp.zeros((TOK, cols), F32)
                for j in range(4):
                    n = 4 * m + j
                    total = jnp.where(
                        picks[16 * x + n] == x * NS + e, rows[n * TOK : (n + 1) * TOK], total
                    )
                placed[m].append(total)
    return [jnp.concatenate(blocks, 0) for blocks in placed]


def project_kernel(
    ids_ref, other_ids_ref, got_ref, other_ref, start_in_ref, start_out_ref,
    send_ref, out_w_ref, in_w_ref, wide_ref,
):
    cols = in_w_ref.shape[1]
    first_core = lax.axis_index("c") == 0
    for s in range(NS):
        for x in range(2):
            mine = got_ref[x * NS + s, :, W_LANE:SENT]
            theirs = other_ref[x * NS + s]
            for c in range(2):
                part = jnp.where(first_core == (c == 0), mine, theirs)
                k = 2 * x + c
                out_w_ref[s, 32 * k : 32 * k + 32, :] = part[:, :cols]
                for g in range(4):
                    row = k * BLK + g * 32
                    lane = cols + g * BLK
                    in_w_ref[s, row : row + 32, :] = part[:, lane : lane + BLK]
    placed = placed_rows(ids_ref, other_ids_ref, got_ref, cols)
    lane = lax.broadcasted_iota(jnp.int32, (R, BLK), 1)
    norms = jnp.zeros((R, BLK), F32)
    for m in range(MIC):
        part = jnp.sum(placed[m] * placed[m], -1, keepdims=True)
        norms = jnp.where(lane == m * NS, part, norms)
    for s, running in running_sums(got_ref, cols):
        for m in range(MIC):
            entry = running + placed[m]
            part = jnp.sum(entry * entry, -1, keepdims=True)
            norms = jnp.where(lane == m * NS + s, part, norms)
        rounded = running.astype(BF16)
        count = s if s < NS - 1 else NS
        at = proj_at(s) * BLK
        wide_ref[:, at : at + count * BLK] = dot_t(
            rounded, out_w_ref[0:count].reshape(count * R, cols)
        )
        at = inner_at(s) * BLK
        wide_ref[:, at : at + BLK] = dot(rounded, in_w_ref[s])
    high = norms.astype(BF16).astype(F32)
    wide_ref[:, NORM * BLK : (NORM + 1) * BLK] = jnp.where(
        lane < 32, high, pltpu.roll(norms - high, 32, 1)
    )
    wide_ref[:, (GRAM + GRAMS) * BLK :] = jnp.zeros((R, BLK), F32)

    square = [(t, s) for t in range(NS) for s in range(t, NS)]

    @pl.when(first_core)
    def _():
        for t in range(5):
            at = (GRAM + gram_at(t)) * BLK
            wide_ref[:, at : at + (NS - t) * BLK] = dot_t(
                out_w_ref[t], out_w_ref[t:NS].reshape((NS - t) * R, cols)
            )
        for i in range(gram_at(5), GRAMS):
            t, s = square[i]
            at = (GRAM + i) * BLK
            wide_ref[:, at : at + BLK] = dot_t(out_w_ref[t], out_w_ref[s])

    @pl.when(jnp.logical_not(first_core))
    def _():
        for t in range(NS - 1):
            for s in range(t + 1, NS):
                at = (GRAM + cross_at(t) + s - t - 1) * BLK
                wide_ref[:, at : at + BLK] = dot(out_w_ref[t], in_w_ref[s])
        for i in range(GRAMS, OO):
            t, s = square[i]
            at = (GRAM + OI + i - GRAMS) * BLK
            wide_ref[:, at : at + BLK] = dot_t(out_w_ref[t], out_w_ref[s])

    for b in range(SPLIT):
        pair = [
            wide_ref[:, at * BLK : (at + 1) * BLK].reshape(16, TOK, BLK) for at in (b, SPLIT + b)
        ]
        send_ref[:, :, b * BLK : (b + 1) * BLK] = jnp.concatenate(pair, 1).astype(BF16)
    for g in range(8):
        at = START + g * 2 * R
        for q in range(16):
            send_ref[q, :, at : at + R] = start_in_ref[g * 16 : (g + 1) * 16, :]
            send_ref[q, :, at + R : at + 2 * R] = start_out_ref[g * 16 : (g + 1) * 16, :]


def sum_kernel(parts_ref, send_ref):
    lane = lax.broadcasted_iota(jnp.int32, (2 * TOK, BLK), 1)
    row = lax.broadcasted_iota(jnp.int32, (2 * TOK, BLK), 0)
    for b in range(SPLIT):
        at = slice(b * BLK, (b + 1) * BLK)
        total = parts_ref[0, :, at].astype(F32)
        for q in range(1, 16):
            total = total + parts_ref[q, :, at].astype(F32)
        if b == NORM:
            norm = total + pltpu.roll(total, 96, 1)
            high = norm.astype(BF16).astype(F32)
            norm = jnp.where(lane < 32, high, pltpu.roll(norm - high, 32, 1))
            total = jnp.where(row < TOK, norm, 0.0)
        total = total.astype(BF16)
        for q in range(16):
            send_ref[q, :, at] = total


def gather_kernel(ids_ref, other_ids_ref, sums_ref, base_ref, proj_ref):
    for b in range(GRAM):
        upper = b >= SPLIT
        at = (b - SPLIT * upper) * BLK
        block = sums_ref[:, :, at : at + BLK].astype(F32)
        proj_ref[:, b * BLK : (b + 1) * BLK] = block[:, TOK * upper : TOK * upper + TOK].reshape(
            R, BLK
        )
    for n, pick in enumerate(picks_of(ids_ref, other_ids_ref)):
        rows = slice(n * TOK, (n + 1) * TOK)
        here = pl.ds(pl.multiple_of(pick * TOK, TOK), TOK)
        base_ref[rows, :] = proj_ref[here, :]
        norm = proj_ref[here, NORM * BLK : (NORM + 1) * BLK]
        norm = norm + pltpu.roll(norm, 96, 1)
        m = n % 16 // 4
        base_ref[rows, NORM * BLK : (NORM + 1) * BLK] = (
            pltpu.roll(norm, BLK - m * NS, 1) if m else norm
        )


def chain_kernel(
    width, parts_ref, base_ref, gram_ref, other_ref,
    latent_ref, scalar_ref, oo_ref, oi_ref, oo_rows_ref, oi_rows_ref,
):
    rows = 2 * R
    first_core = lax.axis_index("c") == 0
    for b in range(0, GRAMS, 4):
        at = slice(b * BLK, (b + 4) * BLK)
        mine, theirs = gram_ref[:, at], other_ref[:, at]
        oo_ref[:, at] = jnp.where(first_core, mine, theirs)
        second = jnp.where(first_core, theirs, mine)
        if b < OI:
            oi_ref[:, at] = second
        else:
            oo_ref[:, (b + 4) * BLK : (b + 8) * BLK] = second

    def spread(at):
        return base_ref[:, at * BLK : (at + 1) * BLK]

    def square(t, s, count=1):
        at = (gram_at(t) + s - t) * BLK
        return oo_ref[:, at : at + count * BLK]

    def cross(t, s, count=1):
        at = (cross_at(t) + s - t - 1) * BLK
        return oi_ref[:, at : at + count * BLK]

    for s in range(1, NS):
        for t in range(s):
            at = slice((proj_at(s) + t) * R, (proj_at(s) + t + 1) * R)
            oo_rows_ref[at, :] = square(t, s)
            oi_rows_ref[at, :] = cross(t, s)

    def above(ref, s):
        return ref[proj_at(s) * R : (proj_at(s) + s) * R, :]

    norms = spread(NORM)
    starts = []
    for s in range(NS):
        pieces = []
        for x in range(2):
            for g in range(8):
                at = START + g * 2 * R
                pieces.append(parts_ref[x * NS + s, :, at : at + 2 * R])
        starts.append(jnp.concatenate(pieces, 0))
    start_out = [start[:, R:].astype(F32) for start in starts]
    run_in = [start[:, :R].astype(F32) for start in starts]
    run_out = list(start_out)
    inners, inverses, actives, crossed = [], [], [], []
    grown_norm = jnp.zeros((rows, R), F32)
    for s in range(NS):
        norm = norms[:, s : s + 1]
        entry_out = []
        inner = run_in[s]
        if s > 0:
            inner = inner + spread(inner_at(s))
            total = jnp.zeros((rows, R), F32)
            for t in range(s):
                base = spread(proj_at(s) + t)
                entry_out.append(base + run_out[t])
                total = total + actives[t] * base
            norm = norm + jnp.sum(2.0 * total + grown_norm, -1, keepdims=True)
        inverse = lax.rsqrt(jnp.maximum(norm, 0.0) * (1.0 / width) + EPS)
        inner = inner * inverse
        active = (inner * jax.nn.sigmoid(inner)).astype(BF16)
        latent_ref[:, s * R : (s + 1) * R] = active
        inners.append(inner)
        inverses.append(inverse)
        actives.append(active.astype(F32))
        crossed.append(entry_out)
        grown = dot(active, square(s, s, NS - s))
        if s > 0:
            grown = jnp.concatenate([dot_t(active, above(oo_rows_ref, s)), grown], 1)
        before = run_out[s]
        for t in range(NS):
            run_out[t] = run_out[t] + grown[:, t * R : (t + 1) * R]
        grown_norm = grown_norm + actives[s] * (before + run_out[s])
        if s < NS - 1:
            grown = dot(active, cross(s, s + 1, NS - 1 - s))
            for t in range(s + 1, NS):
                run_in[t] = run_in[t] + grown[:, (t - s - 1) * R : (t - s) * R]
    grads = [run_out[t] + spread(proj_at(NS - 1) + t) for t in range(NS)]
    lane = lax.broadcasted_iota(jnp.int32, (rows, BLK), 1)
    scalars = jnp.zeros((rows, BLK), F32)
    for s in range(NS - 1, -1, -1):
        inner = inners[s]
        sigm = jax.nn.sigmoid(inner)
        d_inner = (grads[s] * sigm * (1.0 + inner * (1.0 - sigm))).astype(BF16)
        latent_ref[:, (NS + s) * R : (NS + s + 1) * R] = d_inner
        inverse = inverses[s]
        total = jnp.sum(d_inner.astype(F32) * inner, -1, keepdims=True)
        scale = inverse * inverse * total * (1.0 / width)
        if s > 0:
            back = dot_t(d_inner, above(oi_rows_ref, s))
        for t in range(s):
            grads[t] = (
                grads[t] + inverse * back[:, t * R : (t + 1) * R] - scale * crossed[s][t]
            )
        scalars = jnp.where(lane == s, inverse, scalars)
        scalars = jnp.where(lane == NS + s, scale, scalars)
    scalar_ref[...] = scalars


def grads_kernel(
    ids_ref, other_ids_ref, got_ref, out_w_ref, in_w_ref, latent_ref, scalar_ref,
    give_ref, keep_ref, entry_ref, step_ref,
):
    cols = step_ref.shape[1]
    half = cols // 2
    first_core = lax.axis_index("c") == 0
    scalars = scalar_ref[...]
    inverses = [scalars[:, s : s + 1] for s in range(NS)]
    scales = [scalars[:, NS + s : NS + s + 1] for s in range(NS)]
    places = [
        pl.multiple_of(pick * TOK, TOK) for pick in picks_of(ids_ref, other_ids_ref)
    ]

    def active(s):
        return latent_ref[:, s * R : (s + 1) * R]

    def d_inner(s):
        return latent_ref[:, (NS + s) * R : (NS + s + 1) * R]

    def put(s, kind, value):
        low, high = value[:half].reshape(8, 32, R), value[half:].reshape(8, 32, R)
        at = slice(kind * R, (kind + 1) * R)
        give_ref[:, s, :, at] = jnp.where(first_core, high, low).astype(BF16)
        keep_ref[:, s, :, at] = jnp.where(first_core, low, high)

    def both(part, *args):
        return jnp.concatenate(
            [part(got_ref, *args, 0, half), part(got_ref, *args, HALF, half)], 1
        )

    entry = both(first_rows)
    for s in range(NS):
        if s > 0:
            step_ref[...] = both(stores, s)
            entry = entry + jnp.concatenate([step_ref[pl.ds(place, TOK), :] for place in places], 0)
        entry_ref[s] = entry
        put(s, 0, dot_rows((entry * inverses[s]).astype(BF16), d_inner(s)))
        entry = entry + dot(active(s), out_w_ref[s])
    grad = entry
    for s in range(NS - 1, -1, -1):
        put(s, 1, dot_rows(grad.astype(BF16), active(s)))
        if s > 0:
            back = dot_t(d_inner(s), in_w_ref[s])
            grad = grad + inverses[s] * back - scales[s] * entry_ref[s]


def add_kernel(keep_ref, swapped_ref, total_ref):
    for i in range(8):
        total_ref[i] = (keep_ref[i] + swapped_ref[i].astype(F32)).astype(BF16)


def final_kernel(parts_ref, gain_ref, in_ref, out_ref):
    total = parts_ref[0].astype(F32)
    for i in range(1, 8):
        total = total + parts_ref[i].astype(F32)
    gain = gain_ref[...].T
    for j in range(8):
        scale = gain[(j % 4) * 32 : (j % 4) * 32 + 32, j // 4 : j // 4 + 1]
        in_ref[j * 32 : j * 32 + 32, :] = total[j, :, :R] * scale
    out = total[:, :, R:].reshape(2 * BLK, R)
    for i in range(2):
        out_ref[:, i * BLK : (i + 1) * BLK] = out[i * BLK : (i + 1) * BLK].T


def body(first_input, example_ids, out_store, in_store, norm_gain, adapter_in, adapter_out):
    width = first_input.shape[2]
    cols = width // 16
    half = cols // 2
    core = lax.axis_index("c")
    xl = lax.axis_index("xl")
    z = lax.axis_index("z")
    w_in = adapter_in[0]
    w_out = adapter_out[0]

    ids = example_ids[0]
    other_ids = lax.ppermute(ids, "xl", SWAP)
    wide = width // 2

    def quarter():
        return lax.axis_index("xl") * 2 + lax.axis_index("c")

    send = pl.pallas_call(
        pack_kernel,
        grid=(2,),
        in_specs=[
            pl.BlockSpec((64, wide), lambda i: (0, i)),
            pl.BlockSpec((64, wide), lambda i: (0, i)),
            pl.BlockSpec((32, wide), lambda i: (quarter(), i)),
            pl.BlockSpec(
                (1, 4, 1, 8, 32, R), lambda i: (i, quarter() % 2, quarter() // 2, 0, 0, 0)
            ),
            pl.BlockSpec((1, 4, 1, 2, BLK), lambda i: (i, quarter() % 2, quarter() // 2, 0, 0)),
            pl.BlockSpec((2, 32, wide), lambda i: (section_here() // (NS - 1), 0, i)),
        ],
        out_specs=pl.BlockSpec((8, 32, SENT), lambda i: (i, 0, 0)),
        scratch_shapes=[pltpu.VMEM((4 * BLK, 4 * BLK), BF16)],
        out_shape=jax.ShapeDtypeStruct((16, 32, SENT), BF16),
        compiler_params=LARGE,
        name="pack",
    )(
        in_store.reshape(64, width),
        out_store.reshape(64, width),
        w_out,
        w_in.reshape(2, 8, 2, 8, 32, R),
        norm_gain.reshape(2, 8, 2, 2, BLK),
        first_input,
    )
    send, other_ids = lax.optimization_barrier((send, other_ids))
    got = lax.all_to_all(send, PLANE, 0, 0, tiled=True)
    other = lax.ppermute(got[:, :, W_LANE:], "c", SWAP)

    def start(kernel, name, *arrays):
        return pl.pallas_call(
            kernel,
            out_shape=jax.ShapeDtypeStruct((R, R), BF16),
            in_specs=[VMEM] * len(arrays) + [pl.BlockSpec(memory_space=pl.ANY)],
            out_specs=VMEM,
            compiler_params=PARAMS,
            cost_estimate=pl.CostEstimate(
                flops=300000000, bytes_accessed=4000000, transcendentals=0
            ),
            name=name,
        )(*arrays, got)

    start_in = start(start_in_kernel, "start_in", first_input, w_in, norm_gain)
    start_out = start(start_out_kernel, "start_out", first_input, w_out)
    parts, out_w, in_w = pl.pallas_call(
        project_kernel,
        out_shape=(
            jax.ShapeDtypeStruct((16, 2 * TOK, WIDE), BF16),
            jax.ShapeDtypeStruct((NS, R, cols), BF16),
            jax.ShapeDtypeStruct((NS, cols, R), BF16),
        ),
        in_specs=[SMEM, SMEM, VMEM, VMEM, VMEM, VMEM],
        out_specs=(VMEM, VMEM, VMEM),
        scratch_shapes=[pltpu.VMEM((R, 2 * SPLIT * BLK), F32)],
        compiler_params=PARAMS,
        cost_estimate=pl.CostEstimate(flops=2000000000, bytes_accessed=9000000, transcendentals=0),
        name="project",
    )(ids, other_ids, got, other, start_in, start_out)
    parts = lax.all_to_all(parts, PLANE, 0, 0, tiled=True)
    sums = pl.pallas_call(
        sum_kernel,
        out_shape=jax.ShapeDtypeStruct((16, 2 * TOK, SPLIT * BLK), BF16),
        in_specs=[VMEM],
        out_specs=VMEM,
        compiler_params=PARAMS,
        name="sums",
    )(parts)
    sums = lax.all_to_all(sums, PLANE, 0, 0, tiled=True)
    gram = sums[:, TOK:, (GRAM - SPLIT) * BLK : (GRAM - SPLIT + GRAMS) * BLK]
    gram = gram.reshape(R, GRAMS * BLK)
    other = lax.ppermute(gram, "c", SWAP)
    base = pl.pallas_call(
        gather_kernel,
        out_shape=jax.ShapeDtypeStruct((2 * R, GRAM * BLK), F32),
        in_specs=[SMEM, SMEM, VMEM],
        out_specs=VMEM,
        scratch_shapes=[pltpu.VMEM((R, GRAM * BLK), F32)],
        compiler_params=PARAMS,
        cost_estimate=pl.CostEstimate(flops=0, bytes_accessed=7000000, transcendentals=0),
        name="gather",
    )(ids, other_ids, sums)
    latent, scalars = pl.pallas_call(
        functools.partial(chain_kernel, width),
        out_shape=(
            jax.ShapeDtypeStruct((2 * R, 16 * BLK), BF16),
            jax.ShapeDtypeStruct((2 * R, BLK), F32),
        ),
        in_specs=[VMEM] * 4,
        out_specs=(VMEM, VMEM),
        scratch_shapes=[
            pltpu.VMEM((R, OO * BLK), BF16),
            pltpu.VMEM((R, OI * BLK), BF16),
            pltpu.VMEM((OI * R, R), BF16),
            pltpu.VMEM((OI * R, R), BF16),
        ],
        compiler_params=PARAMS,
        name="chain",
    )(parts, base, gram, other)

    give, keep = pl.pallas_call(
        grads_kernel,
        out_shape=(
            jax.ShapeDtypeStruct((8, NS, 32, 2 * R), BF16),
            jax.ShapeDtypeStruct((8, NS, 32, 2 * R), F32),
        ),
        in_specs=[SMEM, SMEM] + [VMEM] * 5,
        out_specs=(VMEM, VMEM),
        scratch_shapes=[pltpu.VMEM((NS, 2 * R, cols), F32), pltpu.VMEM((R, cols), F32)],
        compiler_params=PARAMS,
        name="grads",
    )(ids, other_ids, got, out_w, in_w, latent, scalars)
    swapped = lax.ppermute(give, "c", SWAP)
    total = pl.pallas_call(
        add_kernel,
        out_shape=jax.ShapeDtypeStruct((8, NS, 32, 2 * R), BF16),
        in_specs=[VMEM, VMEM],
        out_specs=VMEM,
        compiler_params=PARAMS,
        name="add",
    )(keep, swapped).reshape(64, 32, 2 * R)
    block = (xl * NS + z) * 2 + core
    gain = lax.dynamic_slice_in_dim(norm_gain[0], block * half, half, 0)
    total, gain = lax.optimization_barrier((total, gain))
    total = lax.all_to_all(total, ("z",) + SECTION, 0, 0, tiled=True)
    grad_in, grad_out = pl.pallas_call(
        final_kernel,
        out_shape=(
            jax.ShapeDtypeStruct((half, R), F32),
            jax.ShapeDtypeStruct((R, half), F32),
        ),
        in_specs=[VMEM, VMEM],
        out_specs=(VMEM, VMEM),
        compiler_params=PARAMS,
        name="final",
    )(total.reshape(8, 8, 32, 2 * R), gain.reshape(2, BLK))
    return (grad_in[None], grad_out[None])


def solution(mesh):
    fine = Mesh(mesh.devices.reshape(2, 8, 2, 4, 2), ("xl", "z", "c", "y", "xh"))
    dp = ("xl", "z", "c")
    placed = (
        P(None, dp, None),
        P(dp, None, None),
        P(SECTION, dp, None, None),
        P(SECTION, dp, None, None),
        P(SECTION, None),
        P(SECTION, None, None),
        P(SECTION, None, None),
    )
    return jax.shard_map(
        body,
        mesh=fine,
        in_specs=placed,
        out_specs=(P(SECTION, dp, None), P(SECTION, None, dp)),
        check_vma=False,
    )
```
